32 devices in a mesh: batch: 4 (over y, core), blk: 8 (over z, x).
Axes of the slice: x: 2, y: 2, z: 4, core: 2. Of those that a mesh axis runs over, the one named last changes fastest.
Arguments:
- cube_tokens: bfloat16 [16, 1536, 768], P('batch', 'blk'), may hold values from -6 to 6
- visible: int32 [16, 512], P('batch', 'blk'), may hold values from 0 to 1535, as said below
- live_counts: int32 [16, 8], P('batch', 'blk'), may hold values from 9 to 64, as said below
- block_cotangent: bfloat16 [16, 512, 768], P('batch', 'blk'), may hold values from -6 to 6
- triple_master: float32 [768, 2304], P('blk', 'batch'), may hold values from -0.21875 to 0.21875
- triple_first: float32 [768, 2304], P('blk', 'batch')
- triple_second: float32 [768, 2304], P('blk', 'batch')
- mixing_master: float32 [768, 768], P('blk', 'batch'), may hold values from -1.75 to 1.75
- mixing_first: float32 [768, 768], P('blk', 'batch')
- mixing_second: float32 [768, 768], P('blk', 'batch')
- expand_master: float32 [768, 3072], P('blk', 'batch'), may hold values from -0.21875 to 0.21875
- expand_first: float32 [768, 3072], P('blk', 'batch')
- expand_second: float32 [768, 3072], P('blk', 'batch')
- shrink_master: float32 [3072, 768], P('blk', 'batch'), may hold values from -0.109375 to 0.109375
- shrink_first: float32 [3072, 768], P('blk', 'batch')
- shrink_second: float32 [3072, 768], P('blk', 'batch')
- vector_master: float32 [12, 768], P(None, 'blk')
- vector_first: float32 [12, 768], P(None, 'blk')
- vector_second: float32 [12, 768], P(None, 'blk')
Outputs:
- block_output: bfloat16 [16, 512, 768], P('batch', 'blk')
- token_grads: bfloat16 [16, 1536, 768], P('batch', 'blk')
- triple_first_new: float32 [768, 2304], P('blk', 'batch')
- triple_second_new: float32 [768, 2304], P('blk', 'batch')
- triple_updated: float32 [768, 2304], P('blk', 'batch')
- triple_copy: bfloat16 [768, 2304], P('blk', 'batch')
- mixing_first_new: float32 [768, 768], P('blk', 'batch')
- mixing_second_new: float32 [768, 768], P('blk', 'batch')
- mixing_updated: float32 [768, 768], P('blk', 'batch')
- mixing_copy: bfloat16 [768, 768], P('blk', 'batch')
- expand_first_new: float32 [768, 3072], P('blk', 'batch')
- expand_second_new: float32 [768, 3072], P('blk', 'batch')
- expand_updated: float32 [768, 3072], P('blk', 'batch')
- expand_copy: bfloat16 [768, 3072], P('blk', 'batch')
- shrink_first_new: float32 [3072, 768], P('blk', 'batch')
- shrink_second_new: float32 [3072, 768], P('blk', 'batch')
- shrink_updated: float32 [3072, 768], P('blk', 'batch')
- shrink_copy: bfloat16 [3072, 768], P('blk', 'batch')
- vector_first_new: float32 [12, 768], P(None, 'blk')
- vector_second_new: float32 [12, 768], P(None, 'blk')
- vector_updated: float32 [12, 768], P(None, 'blk')
- vector_copy: bfloat16 [12, 768], P(None, 'blk')
The draws below stay inside these ranges and needn't reach their ends.
Inputs may be any that keep to these rules, and one draw needn't show every extreme that they name: `visible`: slots of block j of a cube (slots j * 64 to j * 64 + 63) name distinct positions of region j of that cube (positions j * 192 to j * 192 + 191). `live_counts`: the live slots of a block are its first ones; every block has one or more, and some block of some cube is full.
All inputs are finite; a program needn't handle non-finite values.
Results may differ from the reference program's by a relative error of at most 0.013.
The reference program's roundings to bfloat16 on the way count: a program that leaves them out, or rounds other values in their place, can miss the bound.
Values may be sent and summed in bfloat16 or wider, within the bound.
No kernel may reach another device: no remote copies, remote signals or barrier semaphores. Data moves between devices by JAX's collectives and lax.ppermute only.
A program may use at most 192 MiB of HBM per device.

```python
import math
import jax
import jax.numpy as jnp
from jax import lax

D = 768
HD = 64
FF = 3072
CUBE = 1536
VIS = 512
CG = 4
STEP = 10
CUBES = 16
VROWS = 12
N_BATCH = 4
N_BLK = 8


def grad_size(factor):
    return factor * math.sqrt(CG * N_BATCH * VIS / 2.0)


def first_moment(key, array_shape, factor):
    sign_key, size_key = jax.random.split(key)
    sign_flip = jnp.where(jax.random.bernoulli(sign_key, 0.5, array_shape), 1.0, -1.0)
    magnitudes = jnp.exp(jax.random.uniform(size_key, array_shape, jnp.float32, math.log(0.5), math.log(2.0)))
    return sign_flip * magnitudes * (grad_size(factor) / 9.0)


def second_moment(key, array_shape, factor):
    magnitudes = jnp.exp(jax.random.uniform(key, array_shape, jnp.float32, 0.0, math.log(4.0)))
    return magnitudes * (grad_size(factor) ** 2 / 999.0)


def draw_visible(key, part):
    key = jax.random.fold_in(key, 1)
    region = CUBE // N_BLK
    block_slots = VIS // N_BLK
    keys_all = jax.random.split(key, CUBES * N_BLK)
    chosen = jax.vmap(lambda subkey: jax.random.permutation(subkey, region)[:block_slots])(keys_all)
    offsets = jnp.arange(CUBES * N_BLK, dtype=jnp.int32) % N_BLK * region
    return (chosen.astype(jnp.int32) + offsets[:, None]).reshape(CUBES, VIS)


def draw_live_counts(key, part):
    key = jax.random.fold_in(key, 2)
    level_key, trim_key, cube_key, block_key = jax.random.split(key, 4)
    block_slots = VIS // N_BLK
    levels = jax.random.randint(level_key, (CUBES, N_BLK), 0, 4)
    ceiling = jnp.where(levels <= 1, block_slots, jnp.where(levels == 2, block_slots // 2, block_slots // 4))
    trims = jax.random.randint(trim_key, (CUBES, N_BLK), 0, 1 << 20) % jnp.maximum(ceiling // 2, 1)
    counts_drawn = jnp.maximum(ceiling - trims, 1)
    chosen_cube = jax.random.randint(cube_key, (), 0, CUBES)
    chosen_block = jax.random.randint(block_key, (), 0, N_BLK)
    return counts_drawn.at[chosen_cube, chosen_block].set(block_slots).astype(jnp.int32)


def draw_triple_first(key, part):
    key = jax.random.fold_in(key, 11)
    return first_moment(key, (D, 3 * D), 2.0)


def draw_triple_second(key, part):
    key = jax.random.fold_in(key, 12)
    return second_moment(key, (D, 3 * D), 2.0)


def draw_mixing_first(key, part):
    key = jax.random.fold_in(key, 13)
    return first_moment(key, (D, D), 0.3)


def draw_mixing_second(key, part):
    key = jax.random.fold_in(key, 14)
    return second_moment(key, (D, D), 0.3)


def draw_expand_first(key, part):
    key = jax.random.fold_in(key, 15)
    return first_moment(key, (D, FF), 0.6)


def draw_expand_second(key, part):
    key = jax.random.fold_in(key, 16)
    return second_moment(key, (D, FF), 0.6)


def draw_shrink_first(key, part):
    key = jax.random.fold_in(key, 17)
    return first_moment(key, (FF, D), 0.6)


def draw_shrink_second(key, part):
    key = jax.random.fold_in(key, 18)
    return second_moment(key, (FF, D), 0.6)


def draw_vector_master(key, part):
    key = jax.random.fold_in(key, 20)
    gain_key, shift_key = jax.random.split(key)
    row_ids = jnp.arange(VROWS)[:, None]
    is_gain = (row_ids == 0) | (row_ids == 2)
    gains = jnp.exp(0.3 * jax.random.normal(gain_key, (VROWS, D), jnp.float32))
    shifts = 0.3 * jax.random.normal(shift_key, (VROWS, D), jnp.float32)
    return jnp.where(is_gain, gains, shifts)


def draw_vector_first(key, part):
    key = jax.random.fold_in(key, 21)
    return first_moment(key, (VROWS, D), 1.0)


def draw_vector_second(key, part):
    key = jax.random.fold_in(key, 22)
    return second_moment(key, (VROWS, D), 1.0)


def steps_of(key, extent, shards, least, top_value):
    def one(axis_at, shards_of):
        heights = jax.random.uniform(jax.random.fold_in(jax.random.fold_in(key, 6), axis_at), (shards_of,), jnp.float32, least / len(shards), top_value / len(shards))
        return jnp.repeat(jnp.exp(heights), extent[axis_at] // shards_of).reshape((-1,) + (1,) * (len(extent) - axis_at - 1))

    factor_of = one(*shards[0])
    for cut in shards[1:]:
        factor_of = factor_of * one(*cut)
    return factor_of


def gaussian(key, shape, width, bound, shards=(), kind=jnp.bfloat16):
    entries = jax.random.normal(key, shape, jnp.float32) * width
    if len(shards) > 0:
        entries = steps_of(key, shape, shards, -0.22, 0.18) * entries
    return jnp.clip(entries, min=-bound, max=bound).astype(kind)


def setup_inputs(seed: int = 0) -> dict:
    streams_of = jax.random.split(jax.random.key(seed), 20)
    cube_tokens = gaussian(streams_of[0], (CUBES, CUBE, D), 1.0, 6.0, ((0, 4), (1, 8)))
    visible = draw_visible(jax.random.fold_in(streams_of[19], 71), 0)
    live_counts = draw_live_counts(jax.random.fold_in(streams_of[19], 71), 0)
    block_cotangent = gaussian(streams_of[3], (CUBES, VIS, D), 1.0, 6.0, ((0, 4), (1, 8)))
    triple_master = gaussian(streams_of[4], (D, 3 * D), D ** -0.5, 0.21875, ((0, 8), (1, 4)), jnp.float32)
    triple_first = draw_triple_first(jax.random.fold_in(streams_of[19], 71), 0)
    triple_second = draw_triple_second(jax.random.fold_in(streams_of[19], 71), 0)
    mixing_master = gaussian(streams_of[7], (D, D), (max(D // 64, 1)) ** -0.5, 1.75, ((0, 8), (1, 4)), jnp.float32)
    mixing_first = draw_mixing_first(jax.random.fold_in(streams_of[19], 71), 0)
    mixing_second = draw_mixing_second(jax.random.fold_in(streams_of[19], 71), 0)
    expand_master = gaussian(streams_of[10], (D, FF), D ** -0.5, 0.21875, ((0, 8), (1, 4)), jnp.float32)
    expand_first = draw_expand_first(jax.random.fold_in(streams_of[19], 71), 0)
    expand_second = draw_expand_second(jax.random.fold_in(streams_of[19], 71), 0)
    shrink_master = gaussian(streams_of[13], (FF, D), FF ** -0.5, 0.109375, ((0, 8), (1, 4)), jnp.float32)
    shrink_first = draw_shrink_first(jax.random.fold_in(streams_of[19], 71), 0)
    shrink_second = draw_shrink_second(jax.random.fold_in(streams_of[19], 71), 0)
    vector_master = draw_vector_master(jax.random.fold_in(streams_of[19], 71), 0)
    vector_first = draw_vector_first(jax.random.fold_in(streams_of[19], 71), 0)
    vector_second = draw_vector_second(jax.random.fold_in(streams_of[19], 71), 0)
    return {"cube_tokens": cube_tokens, "visible": visible, "live_counts": live_counts, "block_cotangent": block_cotangent, "triple_master": triple_master, "triple_first": triple_first, "triple_second": triple_second, "mixing_master": mixing_master, "mixing_first": mixing_first, "mixing_second": mixing_second, "expand_master": expand_master, "expand_first": expand_first, "expand_second": expand_second, "shrink_master": shrink_master, "shrink_first": shrink_first, "shrink_second": shrink_second, "vector_master": vector_master, "vector_first": vector_first, "vector_second": vector_second}


@jax.custom_vjp
def low(v):
    return lax.optimization_barrier(v.astype(jnp.bfloat16)).astype(jnp.float32)

@jax.custom_vjp
def low_back(v):
    return v

def low_keep(v):
    return (low(v), None)

def low_pass(kept, grad):
    return (grad,)

def back_keep(v):
    return (v, None)

def back_low(kept, grad):
    return (low(grad),)
low.defvjp(low_keep, low_pass)
low_back.defvjp(back_keep, back_low)
RATES = (0.04, 0.3, 0.04, 0.02, 0.25)
DECAYS = (0.05, 0.05, 0.05, 0.05, 0.0)

def rounded(master):
    return lax.optimization_barrier(master.astype(jnp.bfloat16)).astype(jnp.float32)

def matmul(left, right):
    return jnp.dot(left, right, precision=lax.Precision.HIGHEST, preferred_element_type=jnp.float32)

def layer_norm(rows, gain, shift):
    center = rows - lax.optimization_barrier(jnp.mean(rows, axis=-1, keepdims=True))
    spread = lax.rsqrt(lax.optimization_barrier(jnp.mean(center * center, axis=-1, keepdims=True)) + 1e-06)
    return center * spread * gain + shift

def group_layer(weights, cube_group, visible, counts):
    triple_w, mixing_w, expand_w, shrink_w, vector_w = weights
    groups, slots = visible.shape
    features = cube_group.shape[2]
    block_cap = slots // counts.shape[1]
    tokens = jnp.take_along_axis(cube_group, visible[:, :, None], axis=1).reshape(groups * slots, features)
    slot_ids = jnp.arange(slots, dtype=jnp.int32) % block_cap
    live_mask = slot_ids[None, :] < jnp.repeat(counts, block_cap, axis=1)
    normed1 = low(layer_norm(tokens, vector_w[0], vector_w[1]))
    zero_bias = jnp.zeros((features,), jnp.float32)
    triple_bias = jnp.concatenate([vector_w[4], zero_bias, vector_w[5]])
    triple = low(low_back(matmul(normed1, triple_w) + triple_bias))
    head_count = features // HD
    triple = triple.reshape(groups, slots, 3, head_count, HD)
    queries = triple[:, :, 0]
    key_rows = triple[:, :, 1]
    value_rows = triple[:, :, 2]
    raw = jnp.einsum('gshe,gthe->ghst', queries, key_rows, precision=lax.Precision.HIGHEST) * (1.0 / math.sqrt(HD))
    scores = jnp.where(live_mask[:, None, None, :], low_back(raw), -1e+30)
    peak = lax.optimization_barrier(jnp.max(scores, axis=-1, keepdims=True))
    expo = jnp.exp(scores - peak)
    probs = low(expo / lax.optimization_barrier(jnp.sum(expo, axis=-1, keepdims=True)))
    mixed = jnp.einsum('ghst,gthe->gshe', probs, value_rows, precision=lax.Precision.HIGHEST)
    mixed = low(low_back(mixed.reshape(groups * slots, features)))
    attended = tokens + low_back(matmul(mixed, mixing_w) + vector_w[6])
    normed2 = low(layer_norm(attended, vector_w[2], vector_w[3]))
    preact = low_back(matmul(normed2, expand_w) + vector_w[8:].reshape(-1))
    activation = low(jax.nn.gelu(preact, approximate=False))
    result = attended + low_back(matmul(activation, shrink_w) + vector_w[7])
    result = jnp.where(live_mask.reshape(groups * slots, 1), result, 0.0)
    return result.reshape(groups, slots, features)

def adamw(master, first, second, grad, rate, decay):
    first_new = 0.9 * first + 0.1 * grad
    second_new = 0.999 * second + 0.001 * grad * grad
    corrected = first_new / (1.0 - 0.9 ** STEP) / (jnp.sqrt(second_new / (1.0 - 0.999 ** STEP)) + 1e-08)
    master_new = master - rate * (corrected + decay * master)
    return (first_new, second_new, master_new, master_new.astype(jnp.bfloat16))

def reference(cube_tokens, visible, live_counts, block_cotangent, triple_master, triple_first, triple_second, mixing_master, mixing_first, mixing_second, expand_master, expand_first, expand_second, shrink_master, shrink_first, shrink_second, vector_master, vector_first, vector_second):
    masters = (triple_master, mixing_master, expand_master, shrink_master, vector_master)
    firsts = (triple_first, mixing_first, expand_first, shrink_first, vector_first)
    seconds = (triple_second, mixing_second, expand_second, shrink_second, vector_second)
    weights = tuple((rounded(master) for master in masters))
    cubes = cube_tokens.astype(jnp.float32)
    cube_count = cubes.shape[0]
    group_steps = cube_count // CG
    visible_groups = visible.reshape(group_steps, CG, VIS)
    count_groups = live_counts.reshape(group_steps, CG, -1)

    def whole_layer(weights, cubes):

        def one_group(pieces):
            return group_layer(weights, pieces[0], pieces[1], pieces[2])
        stacked = (cubes.reshape(group_steps, CG, CUBE, D), visible_groups, count_groups)
        return lax.map(jax.checkpoint(one_group), stacked).reshape(cube_count, VIS, D)
    result, pullback = jax.vjp(whole_layer, weights, cubes)
    weight_grads, cube_grads = pullback(block_cotangent.astype(jnp.float32))
    outputs = [result.astype(jnp.bfloat16), cube_grads.astype(jnp.bfloat16)]
    for master, first, second, grad, rate, decay in zip(masters, firsts, seconds, weight_grads, RATES, DECAYS):
        outputs.extend(adamw(master, first, second, grad, rate, decay))
    return tuple(outputs)
```

```python
from functools import partial
import math

import jax
import jax.numpy as jnp
from jax import lax
from jax.experimental import pallas as pl
from jax.experimental.pallas import tpu as pltpu
from jax.sharding import Mesh, PartitionSpec as P

HD = 64
STEP = 10
BF = jnp.bfloat16
F32 = jnp.float32

RATES = (0.04, 0.3, 0.04, 0.02, 0.25)
DECAYS = (0.05, 0.05, 0.05, 0.05, 0.0)


def adamw(master, first, second, grad, rate, decay):
    first_new = 0.9 * first + 0.1 * grad
    second_new = 0.999 * second + 0.001 * grad * grad
    corrected = first_new / (1.0 - 0.9**STEP) / (jnp.sqrt(second_new / (1.0 - 0.999**STEP)) + 1e-08)
    master_new = master - rate * (corrected + decay * master)
    return (first_new, second_new, master_new, master_new.astype(BF))


FINE = ("y", "core", "blk")


def place(y, c, b):
    return (y * 2 + c) * 8 + b


def swap(x, dy=0, dc=0, db=0):
    pairs = [
        (place(y, c, b), place(y ^ dy, c ^ dc, b ^ db))
        for y in range(2)
        for c in range(2)
        for b in range(8)
    ]
    return lax.ppermute(x, FINE, pairs)


def cube_pairs(step, back):
    pairs = []
    for y in range(2):
        for c in range(2):
            for b in range(8):
                r, q = b // 4, b % 4
                far = place(y, r, 4 * c + (q + step) % 4)
                near = place(y, c, b)
                pairs.append((far, near) if back else (near, far))
    return pairs


def pick(x, index, axis):
    return lax.dynamic_index_in_dim(x, index, axis, keepdims=False)


def add_low(a, b):
    return (a.astype(F32) + b.astype(F32)).astype(BF)


def chip_sum(part_a, part_b, bits):
    my, mx, mz0, mz1 = bits
    ra, cols = part_a.shape[2:]
    rb = part_b.shape[2]
    a = part_a.reshape(2, 4, 2, ra, cols)
    a_in = swap(pick(a, 1 - mx, 2), db=1)
    b_in = swap(pick(part_b, 1 - my, 0), dy=1)
    a = add_low(pick(a, mx, 2), a_in)
    b = add_low(pick(part_b, my, 0), b_in).reshape(4, 2, rb, cols)
    a_in = swap(pick(a, 1 - my, 0), dy=1)
    b_in = swap(pick(b, 1 - mx, 1), db=1)
    a = add_low(pick(a, my, 0), a_in)
    b = add_low(pick(b, mx, 1), b_in)
    both = jnp.concatenate([a, b], axis=1).reshape(2, 2, ra + rb, cols)
    z_in = swap(pick(both, 1 - mz0, 1), db=2)
    both = add_low(pick(both, mz0, 1), z_in)
    z_in = swap(pick(both, 1 - mz1, 0), db=4)
    both = pick(both, mz1, 0).astype(F32) + z_in.astype(F32)
    return both[:ra], both[ra:]


def dot_nn(a, b):
    return jnp.dot(a, b, preferred_element_type=F32)


def dot_nt(a, b):
    return lax.dot_general(a, b, (((1,), (1,)), ((), ())), preferred_element_type=F32)


def dot_tn(a, b):
    return lax.dot_general(a, b, (((0,), (0,)), ((), ())), preferred_element_type=F32)


def call(kernel, outs, name, flops=0, moved=0, **kw):
    return pl.pallas_call(
        kernel,
        out_shape=outs,
        name=name,
        cost_estimate=pl.CostEstimate(flops=int(flops), bytes_accessed=int(moved), transcendentals=0),
        compiler_params=pltpu.CompilerParams(vmem_limit_bytes=50 * 2**20),
        **kw,
    )


def shape(*dims, dtype=F32):
    return jax.ShapeDtypeStruct(dims, dtype)


VM = pl.BlockSpec(memory_space=pltpu.VMEM)
SM = pl.BlockSpec(memory_space=pltpu.SMEM)


def normalize(rows):
    center = rows - jnp.mean(rows, axis=-1, keepdims=True)
    spread = lax.rsqrt(jnp.mean(center * center, axis=-1, keepdims=True) + 1e-06)
    return center * spread, spread


def norm_back(xhat, spread, gain, grad):
    q = grad * gain
    mean_q = jnp.mean(q, axis=-1, keepdims=True)
    mean_x = jnp.mean(q * xhat, axis=-1, keepdims=True)
    return spread * (q - mean_q - xhat * mean_x)


def qkv_kernel(me, tok, vec, bias, qv, rest, n1_out, x3_out, t3_out, mix_out):
    my, mx, mz0, mz1 = me[0], me[1], me[2], me[3]
    for b in range(8):
        zr = ((b >> 1 & 1) ^ mz0) * 2 + ((b >> 2) ^ mz1)
        xr = (b & 1) ^ mx
        for y in range(2):
            yr = y ^ my
            t3_out[y, 96 * b : 96 * b + 96, :] = qv[(yr * 2 + xr) * 4 + zr]
            ib = (xr * 2 + yr) * 4 + zr
            keys = rest[ib, 0:48, :]
            t3_out[2, 96 * b : 96 * b + 48, 192 * y : 192 * y + 192] = keys[:, :192]
            t3_out[2, 96 * b + 48 : 96 * b + 96, 192 * y : 192 * y + 192] = keys[:, 192:]
            mix_out[y * 8 + b] = rest[ib, 64:112, :]
    xhat, _ = normalize(tok[...].astype(F32))
    n1 = (xhat * vec[0:1, :] + vec[1:2, :]).astype(BF)
    n1_out[...] = n1
    for j in range(3):
        x3_out[j] = (dot_nn(n1, t3_out[j]) + bias[j : j + 1, :]).astype(BF)


def head_masks():
    lane = lax.broadcasted_iota(jnp.int32, (1, 2 * HD), 1)
    return [lane < HD, lane >= HD]


def soft(keys, query, live, width):
    raw = dot_nt(keys, query) * (1.0 / math.sqrt(HD))
    raw = jnp.where(jnp.concatenate([live] * (width // 128), axis=1) > 0, raw, -1e30)
    expo = jnp.exp(raw - jnp.max(raw, axis=0, keepdims=True))
    return expo * (1.0 / jnp.sum(expo, axis=0, keepdims=True))


QB = 256


def attn_kernel(x3, live, out):
    q, v, k = x3[0], x3[1], x3[2]
    slots = q.shape[0]
    lv = live[...]
    vt = v.astype(F32).T.astype(BF)
    row = lax.broadcasted_iota(jnp.int32, (2 * HD, 1), 0)
    masks = head_masks()
    for s in range(0, slots, QB):
        total = jnp.zeros((2 * HD, QB), F32)
        for h in range(2):
            qh = jnp.where(masks[h], q[s : s + QB], jnp.zeros((), BF))
            low = soft(k, qh, lv, QB).astype(BF)
            vh = jnp.where(row < HD if h == 0 else row >= HD, vt, jnp.zeros((), BF))
            total += dot_nn(vh, low)
        out[s : s + QB, :] = total.T.astype(BF)


def attn_back_kernel(x3, gm_ref, live, d3):
    q, v, k, gm = x3[0], x3[1], x3[2], gm_ref[...]
    slots = q.shape[0]
    lv = live[...]
    kt = k.astype(F32).T.astype(BF)
    row = lax.broadcasted_iota(jnp.int32, (2 * HD, 1), 0)
    masks = head_masks()
    scale = 1.0 / math.sqrt(HD)
    zero = jnp.zeros((), BF)
    dk = jnp.zeros((slots, 2 * HD), F32)
    dv = jnp.zeros((slots, 2 * HD), F32)
    for s in range(0, slots, QB):
        dqt = jnp.zeros((2 * HD, QB), F32)
        for h in range(2):
            qh = jnp.where(masks[h], q[s : s + QB], zero)
            gh = jnp.where(masks[h], gm[s : s + QB], zero)
            probs = soft(k, qh, lv, QB)
            gp = dot_nt(v, gh)
            delta = jnp.sum(probs * gp, axis=0, keepdims=True)
            ds = (probs * (gp - delta)).astype(BF)
            kh = jnp.where(row < HD if h == 0 else row >= HD, kt, zero)
            dqt += dot_nn(kh, ds)
            dk += dot_nn(ds, qh)
            dv += dot_nn(probs.astype(BF), gh)
        d3[0, s : s + QB, :] = (dqt.T * scale).astype(BF)
    d3[1] = dv.astype(BF)
    d3[2] = (dk * scale).astype(BF)


def mid_kernel(tok, mixed, far, m_own, m_far, vec, att_out, n2_out):
    branch = dot_nn(mixed[...], m_own[...]) + dot_nn(far[...], m_far[...])
    att = tok[...].astype(F32) + (branch + vec[6:7, :])
    att_out[...] = att
    xhat, _ = normalize(att)
    n2_out[...] = (xhat * vec[2:3, :] + vec[3:4, :]).astype(BF)


def ffn_kernel(n2_ref, br_ref, e_ref, s_ref, eb, part, gn2, d_e, d_s, d_bias, n2t):
    n = pl.program_id(0)
    n2, br = n2_ref[...], br_ref[...]

    @pl.when(n == 0)
    def _():
        part[...] = jnp.zeros_like(part)
        gn2[...] = jnp.zeros_like(gn2)
        n2t[...] = n2.astype(F32).T.astype(BF)

    e = e_ref[0].reshape(768, 384)
    s0, s1 = s_ref[0].reshape(384, 384), s_ref[1].reshape(384, 384)
    b0, b1 = br[:, :384], br[:, 384:]
    pre = dot_nn(n2, e) + eb[0]
    cdf = 0.5 * (1.0 + lax.erf(pre * math.sqrt(0.5)))
    act = (pre * cdf).astype(BF)
    slope = cdf + pre * (jnp.exp(-0.5 * pre * pre) * (1.0 / math.sqrt(2.0 * math.pi)))
    part[:, :384] += dot_nn(act, s0)
    part[:, 384:] += dot_nn(act, s1)
    grad_act = dot_nt(b0, s0) + dot_nt(b1, s1)
    grad_pre = (grad_act * slope).astype(BF)
    gn2[...] += dot_nt(grad_pre, e)
    d_s[0] = dot_tn(act, b0).astype(BF)
    d_s[1] = dot_tn(act, b1).astype(BF)
    d_e[0] = dot_nn(n2t[...], grad_pre).astype(BF)
    d_bias[0] = jnp.sum(grad_pre.astype(F32), axis=0, keepdims=True)


def mid_back_kernel(gn_a, gn_b, att_ref, br_ref, mixed, far, m_own, m_far, vec, gatt, dm_own, dm_far, gm_own, gm_far, sums):
    gn = gn_a[...] + gn_b[...]
    br = br_ref[...].astype(F32)
    xhat, spread = normalize(att_ref[...])
    grad = br + norm_back(xhat, spread, vec[2:3, :], gn)
    gatt[...] = grad
    low = grad.astype(BF)
    dm_own[...] = dot_tn(mixed[...], low).astype(BF)
    dm_far[...] = dot_tn(far[...], low).astype(BF)
    gm_own[...] = dot_nt(low, m_own[...]).astype(BF)
    gm_far[...] = dot_nt(low, m_far[...]).astype(BF)
    sums[0:1] = jnp.sum(gn * xhat, axis=0, keepdims=True)
    sums[1:2] = jnp.sum(gn, axis=0, keepdims=True)
    sums[2:3] = jnp.sum(low.astype(F32), axis=0, keepdims=True)
    sums[3:4] = jnp.sum(br, axis=0, keepdims=True)
    sums[4:8] = jnp.zeros((4, sums.shape[1]), F32)


def triple_back_kernel(n1_ref, d3, t3, d_qv, d_k, gn1, sums):
    j = pl.program_id(0)
    d = d3[0]
    weight = dot_tn(n1_ref[...], d).astype(BF)
    part = dot_nt(d, t3[0])
    sums[0] = jnp.sum(d.astype(F32), axis=0, keepdims=True)

    @pl.when(j == 0)
    def _():
        gn1[...] = part

    @pl.when(j > 0)
    def _():
        gn1[...] += part

    @pl.when(j < 2)
    def _():
        d_qv[0] = weight

    @pl.when(j == 2)
    def _():
        d_k[...] = weight


def first_back_kernel(gn_a, gn_b, tok, gatt, vec, out, sums):
    gn = gn_a[...] + gn_b[...]
    xhat, spread = normalize(tok[...].astype(F32))
    out[...] = (gatt[...] + norm_back(xhat, spread, vec[0:1, :], gn)).astype(BF)
    sums[0:1] = jnp.sum(gn * xhat, axis=0, keepdims=True)
    sums[1:2] = jnp.sum(gn, axis=0, keepdims=True)
    sums[2:8] = jnp.zeros((6, sums.shape[1]), F32)


def by_core(c, own, far):
    return jnp.where(c == 0, jnp.stack([own, far]), jnp.stack([far, own]))


def per_device(
    cube_tokens, visible, live_counts, block_cotangent,
    triple_master, triple_first, triple_second,
    mixing_master, mixing_first, mixing_second,
    expand_master, expand_first, expand_second,
    shrink_master, shrink_first, shrink_second,
    vector_master, vector_first, vector_second,
):
    y, c, b = lax.axis_index("y"), lax.axis_index("core"), lax.axis_index("blk")
    bits = (y, b & 1, b >> 1 & 1, b >> 2)
    turn = b % 4
    region, feats = cube_tokens.shape[1:]
    slots = visible.shape[1]
    slot_axis = jnp.arange(slots, dtype=jnp.int32)

    t_low, m_low, e_low, s_low, v_low = [
        w.astype(BF) for w in (triple_master, mixing_master, expand_master, shrink_master, vector_master)
    ]
    t0, t1, t2 = t_low[:, :192], t_low[:, 192:384], t_low[:, 384:]
    e4 = e_low.reshape(96, 2, 2, 192)
    s2 = s_low.reshape(2, 192, 192)
    e_mine = jnp.concatenate([pick(e4, c, 2)[:, 0], pick(e4, c, 2)[:, 1]], axis=1)
    e_send = pick(e4, 1 - c, 2)
    give = jnp.concatenate([e_send[:, 0], e_send[:, 1], pick(s2, 1 - c, 0), t1], axis=0)
    took = swap(give, dc=1)
    e_far = jnp.concatenate([took[:96], took[96:192]], axis=1)
    s_far, t_far = took[192:384], took[384:480]
    e_blob = by_core(c, e_mine, e_far).reshape(192, 384)
    s_both = by_core(c, pick(s2, c, 0), s_far)
    s_blob = jnp.concatenate([s_both[0], s_both[1]], axis=1)
    es = lax.all_gather(jnp.concatenate([e_blob, s_blob], axis=0), ("y", "blk"), axis=0, tiled=False)
    es = es.reshape(2, 8, 384, 384)

    t_id = 2 * y + c
    qv_blob = jnp.concatenate(
        [jnp.where(t_id == 1, t_far, jnp.where(t_id == 2, t2, t0)),
         jnp.where(t_id == 1, t0, jnp.where(t_id == 2, t_far, t2))], axis=1)
    k_unit = jnp.where(t_id == 1, t2, jnp.where(t_id == 2, t0, t_far))
    k_blob = jnp.concatenate([k_unit[:48], k_unit[48:]], axis=1)
    m_blob = jnp.concatenate([m_low[:48], m_low[48:]], axis=1)
    v_blob = jnp.concatenate([v_low.reshape(3, 384), jnp.zeros((13, 384), BF)], axis=0)
    blob = jnp.concatenate([qv_blob, k_blob, v_blob, m_blob], axis=0)
    blob = jnp.stack([blob, swap(blob, db=4)])
    blob = jnp.stack([blob, swap(blob, db=2)])
    qv, rest = blob[:, :, :96], blob[:, :, 96:]
    qv_x, rest_y = swap(qv, db=1), swap(rest, dy=1)
    qv = jnp.stack([qv, qv_x])
    rest = jnp.stack([rest, rest_y])
    qv_y, rest_x = swap(qv, dy=1), swap(rest, db=1)
    qv = jnp.stack([qv, qv_y]).reshape(16, 96, 384)
    rest = jnp.stack([rest, rest_x])

    order = (turn + jnp.arange(4, dtype=jnp.int32)) % 4
    local = visible % region
    flat_index = jnp.take(local + region * jnp.arange(4, dtype=jnp.int32)[:, None], order, axis=0)
    picked = jnp.take(cube_tokens.reshape(-1, feats), flat_index.reshape(-1), axis=0).reshape(4, slots, feats)
    live_here = slot_axis[None, :] < live_counts
    masked = jnp.where(live_here[:, :, None], block_cotangent, jnp.zeros((), BF))
    masked = lax.dynamic_slice_in_dim(jnp.concatenate([masked, masked]), turn, 4, 0)
    counts = jnp.broadcast_to(jnp.take(live_counts, order, axis=0)[:, :, None].astype(BF), (4, 16, feats))
    packet = jnp.concatenate([picked, masked, counts], axis=1)
    own = jnp.stack([lax.ppermute(packet[s], FINE, cube_pairs(s, False)) for s in range(4)])
    far = swap(own, dc=1)
    rows = 4 * slots
    tok_own = own[:, :slots].reshape(rows, feats)
    br_own = own[:, slots : 2 * slots].reshape(rows, feats)
    tok_all = jnp.concatenate([tok_own, far[:, :slots].reshape(rows, feats)])
    br_all = jnp.concatenate([br_own, far[:, slots : 2 * slots].reshape(rows, feats)])
    cnt = jnp.concatenate([own[:, 2 * slots, :1], far[:, 2 * slots, :1]]).astype(jnp.int32)
    live = (slot_axis[None, :] < cnt).reshape(2 * rows, 1)
    live_cols = jnp.broadcast_to(live.astype(F32), (2 * rows, 128))

    ids = jnp.arange(8, dtype=jnp.int32)
    rel = ((ids & 1) ^ bits[1]) * 4 + ((ids >> 1 & 1) ^ bits[2]) * 2 + ((ids >> 2) ^ bits[3])
    vec = rest[:, 0, :, :, 48:51].reshape(8, 1152)
    vec = jnp.take(vec, rel, axis=0).reshape(8, 12, 96).transpose(1, 0, 2).reshape(12, feats).astype(F32)
    qb = pick(vec[4].reshape(2, 2, 192), c, 1).reshape(1, 384)
    vb = pick(vec[5].reshape(2, 2, 192), c, 1).reshape(1, 384)
    bias = jnp.concatenate([qb, vb, jnp.zeros((6, 384), F32)])
    e_bias = pick(vec[8:].reshape(4, 2, 2, 192), c, 2).reshape(4, 1, 384)

    me = jnp.stack(bits).astype(jnp.int32)
    n1, x3, t3, mix = call(
        qkv_kernel,
        (shape(2 * rows, feats, dtype=BF), shape(3, 2 * rows, 384, dtype=BF), shape(3, feats, 384, dtype=BF), shape(16, 48, 384, dtype=BF)),
        "qkv", 2 * 512 * 768 * 1152, 8e6,
        in_specs=[SM, VM, VM, VM, VM, VM], out_specs=(VM, VM, VM, VM),
    )(me, tok_all, vec, bias, qv, rest.reshape(16, 112, 384))

    pairs3 = pl.BlockSpec((3, 2 * rows, 128), lambda i: (0, 0, i))
    col = pl.BlockSpec((2 * rows, 128), lambda i: (0, i))
    same = pl.BlockSpec((2 * rows, 128), lambda i: (0, 0))
    mixed = call(
        attn_kernel, shape(2 * rows, 384, dtype=BF), "attention", 4 * 512 * 512 * 768, 20e6,
        grid=(3,), in_specs=[pairs3, same], out_specs=col,
    )(x3, live_cols)

    mix = by_core(c, mix, swap(mix, dc=1)).reshape(2, 2, 8, 48, 2, 192)
    mix = mix.transpose(2, 4, 3, 1, 0, 5).reshape(feats, feats)
    m4 = mix.reshape(2, 2, 192, feats)
    m_own, m_far = pick(m4, c, 1).reshape(384, feats), pick(m4, 1 - c, 1).reshape(384, feats)

    mixed_own = mixed[:rows]
    mixed_far = swap(mixed[rows:], dc=1)
    att, n2 = call(
        mid_kernel, (shape(rows, feats), shape(rows, feats, dtype=BF)), "mixing", 2 * 256 * 768 * 768, 5e6,
        in_specs=[VM] * 6, out_specs=(VM, VM),
    )(tok_own, mixed_own, mixed_far, m_own, m_far, vec)

    n2_all = jnp.concatenate([n2, swap(n2, dc=1)])
    whole = pl.BlockSpec((2 * rows, feats), lambda n: (0, 0))
    part, gn2, d_e, d_s, d_bias = call(
        ffn_kernel,
        (shape(2 * rows, feats), shape(2 * rows, feats), shape(2, feats, 768, dtype=BF), shape(2, 1536, 384, dtype=BF), shape(4, 1, 384)),
        "feed_forward", 12 * 512 * 768 * 1536, 30e6,
        grid=(4,),
        in_specs=[
            whole, whole,
            pl.BlockSpec((1, 8, 96, 384), lambda n: (n // 2, 0, n % 2, 0)),
            pl.BlockSpec((2, 2, 192, 384), lambda n: (0, n, 1, 0)),
            pl.BlockSpec((1, 1, 384), lambda n: (n, 0, 0)),
        ],
        out_specs=(
            whole, whole,
            pl.BlockSpec((1, feats, 384), lambda n: (n // 2, 0, n % 2)),
            pl.BlockSpec((2, 384, 384), lambda n: (0, n, 0)),
            pl.BlockSpec((1, 1, 384), lambda n: (n, 0, 0)),
        ),
        scratch_shapes=[pltpu.VMEM((feats, 2 * rows), BF)],
    )(n2_all, br_all, es, es, e_bias)

    part_far = swap(part[rows:], dc=1)
    result = att + (part[:rows] + part_far + vec[7])
    result = jnp.where(live[:rows], result, 0.0).astype(BF).reshape(4, slots, feats)
    back = jnp.stack([lax.ppermute(result[s], FINE, cube_pairs(s, True)) for s in range(4)])
    unturn = (4 - turn) % 4
    block_output = lax.dynamic_slice_in_dim(jnp.concatenate([back, back]), unturn, 4, 0)

    gn2_far = swap(gn2[rows:], dc=1)
    gatt, dm_own, dm_far, gm_own, gm_far, sums2 = call(
        mid_back_kernel,
        (shape(rows, feats), shape(384, feats, dtype=BF), shape(384, feats, dtype=BF),
         shape(rows, 384, dtype=BF), shape(rows, 384, dtype=BF), shape(8, feats)),
        "mixing_back", 4 * 256 * 768 * 768, 8e6,
        in_specs=[VM] * 9, out_specs=(VM,) * 6,
    )(gn2[:rows], gn2_far, att, br_own, mixed_own, mixed_far, m_own, m_far, vec)
    gm_all = jnp.concatenate([gm_own, swap(gm_far, dc=1)])

    d3 = call(
        attn_back_kernel, shape(3, 2 * rows, 384, dtype=BF), "attention_back", 10 * 512 * 512 * 768, 30e6,
        grid=(3,), in_specs=[pairs3, col, same], out_specs=pairs3,
    )(x3, gm_all, live_cols)

    third = pl.BlockSpec((1, 2 * rows, 384), lambda j: (j, 0, 0))
    d_qv, d_k, gn1, sums1 = call(
        triple_back_kernel,
        (shape(2, feats, 384, dtype=BF), shape(feats, 384, dtype=BF), shape(2 * rows, feats), shape(3, 1, 384)),
        "triple_back", 4 * 512 * 768 * 1152, 10e6,
        grid=(3,),
        in_specs=[pl.BlockSpec((2 * rows, feats), lambda j: (0, 0)), third, pl.BlockSpec((1, feats, 384), lambda j: (j, 0, 0))],
        out_specs=(
            pl.BlockSpec((1, feats, 384), lambda j: (jnp.minimum(j, 1), 0, 0)),
            pl.BlockSpec((feats, 384), lambda j: (0, 0)),
            pl.BlockSpec((2 * rows, feats), lambda j: (0, 0)),
            pl.BlockSpec((1, 1, 384), lambda j: (j, 0, 0)),
        ),
    )(n1, d3, t3)

    gn1_far = swap(gn1[rows:], dc=1)
    grad_tok, sums0 = call(
        first_back_kernel, (shape(rows, feats, dtype=BF), shape(8, feats)), "first_back", 0, 4e6,
        in_specs=[VM] * 5, out_specs=(VM, VM),
    )(gn1[:rows], gn1_far, tok_own, gatt, vec)
    grad_tok = grad_tok.reshape(4, slots, feats)
    back = jnp.stack([lax.ppermute(grad_tok[s], FINE, cube_pairs(s, True)) for s in range(4)])
    back = lax.dynamic_slice_in_dim(jnp.concatenate([back, back]), unturn, 4, 0)
    spread = (jnp.arange(region, dtype=jnp.int32)[None, :, None] == local[:, None, :]).astype(BF)
    token_grads = jnp.einsum("grs,gsf->grf", spread, back, preferred_element_type=F32).astype(BF)

    e_sum, s_sum = chip_sum(d_e.reshape(2, 8, 96, 2, 384).transpose(0, 1, 3, 2, 4).reshape(2, 8, 192, 384), d_s.reshape(2, 8, 192, 384), bits)
    dm = by_core(c, dm_own.reshape(2, 192, feats), dm_far.reshape(2, 192, feats))
    dm = dm.transpose(1, 0, 2, 3).reshape(8, 2, 48, 2, 2, 192)
    dm = dm.transpose(4, 3, 0, 2, 1, 5).reshape(2, 2, 8, 48, 384)
    dm = add_low(pick(dm, c, 0), swap(pick(dm, 1 - c, 0), dc=1))
    d_k = d_k.reshape(8, 2, 48, 2, 192).transpose(3, 0, 2, 1, 4).reshape(2, 8, 48, 384)
    qv_sum, km_sum = chip_sum(d_qv.reshape(2, 8, 96, 384), jnp.concatenate([d_k, dm], axis=2), bits)

    e_sum = e_sum.reshape(2, 96, 384)
    s_sum = s_sum.reshape(192, 2, 192)
    k_sum = jnp.concatenate([km_sum[:48, :192], km_sum[:48, 192:]], axis=0)
    m_grad = jnp.concatenate([km_sum[48:, :192], km_sum[48:, 192:]], axis=0)
    qa, qb2 = qv_sum[:, :192], qv_sum[:, 192:]
    give_e = pick(e_sum, 1 - c, 0)
    give = jnp.concatenate([give_e[:, :192], give_e[:, 192:], pick(s_sum, 1 - c, 1)], axis=0)
    took = swap(give, dc=1)
    t_took = swap(jnp.where(t_id == 1, qa, jnp.where(t_id == 2, qb2, k_sum)), dc=1)
    e_own = pick(e_sum, c, 0).reshape(96, 2, 192)
    e_took = jnp.stack([took[:96], took[96:192]], axis=1)
    e_pair = by_core(c, e_own, e_took)
    e_grad = e_pair.transpose(1, 2, 0, 3).reshape(96, 768)
    s_grad = by_core(c, pick(s_sum, c, 1), took[192:]).reshape(384, 192)
    p0 = jnp.where(t_id == 1, qb2, jnp.where(t_id == 2, k_sum, qa))
    p2 = jnp.where(t_id == 1, k_sum, jnp.where(t_id == 2, qa, qb2))
    t_grad = jnp.concatenate([p0, t_took, p2], axis=1)

    mine = jnp.arange(2)[None, :, None] == c

    def spread_units(sums):
        return jnp.where(mine, sums.reshape(-1, 1, 192), 0.0).reshape(-1, feats)

    table = jnp.concatenate(
        [sums0[:2], sums2[:2], spread_units(sums1[0]), spread_units(sums1[1]), sums2[2:4], spread_units(d_bias)]
    )
    table = table + swap(table, dc=1)
    table = table + swap(table, dy=1)
    table = table + swap(table, db=1)
    table = table + swap(table, db=2)
    table = table + swap(table, db=4)
    v_grad = lax.dynamic_slice_in_dim(table, b * vector_master.shape[1], vector_master.shape[1], 1)

    masters = (triple_master, mixing_master, expand_master, shrink_master, vector_master)
    firsts = (triple_first, mixing_first, expand_first, shrink_first, vector_first)
    seconds = (triple_second, mixing_second, expand_second, shrink_second, vector_second)
    grads = (t_grad, m_grad, e_grad, s_grad, v_grad)
    outputs = [block_output, token_grads]
    for master, first, second, grad, rate, decay in zip(masters, firsts, seconds, grads, RATES, DECAYS):
        outputs.extend(adamw(master, first, second, grad, rate, decay))
    return tuple(outputs)


def layer_norm(rows, gain, shift):
    center = rows - jnp.mean(rows, axis=-1, keepdims=True)
    spread = lax.rsqrt(jnp.mean(center * center, axis=-1, keepdims=True) + 1e-06)
    return center * spread * gain + shift


def outer_sum(left, right):
    return lax.dot_general(
        left, right, (((0,), (0,)), ((), ())), preferred_element_type=jnp.float32
    )


def back_product(grads, weight):
    return lax.dot_general(
        grads, weight, (((1,), (1,)), ((), ())), preferred_element_type=jnp.float32
    )


def masked_scores(queries, key_all, live_all):
    raw = jnp.einsum("gshe,gthe->ghst", queries, key_all, preferred_element_type=jnp.float32) * (
        1.0 / math.sqrt(HD)
    )
    return jnp.where(live_all[:, None, None, :] > 0, raw, -1e30)


def cycle_section(triple_grad, mixing_grad, expand_grad, shrink_grad, vector_grad):
    summed = (
        lax.psum_scatter(triple_grad, "blk", scatter_dimension=0, tiled=True),
        lax.psum_scatter(mixing_grad, "blk", scatter_dimension=0, tiled=True),
        lax.psum_scatter(expand_grad, "blk", scatter_dimension=0, tiled=True),
        lax.psum_scatter(shrink_grad, "blk", scatter_dimension=0, tiled=True),
        lax.psum_scatter(vector_grad, "blk", scatter_dimension=1, tiled=True),
    )
    return (summed[0], summed[1], summed[2], summed[3], summed[4])


def group_section(triple_grad, mixing_grad, expand_grad, shrink_grad, vector_grad):
    summed = (
        lax.psum_scatter(triple_grad, "batch", scatter_dimension=1, tiled=True),
        lax.psum_scatter(mixing_grad, "batch", scatter_dimension=1, tiled=True),
        lax.psum_scatter(expand_grad, "batch", scatter_dimension=1, tiled=True),
        lax.psum_scatter(shrink_grad, "batch", scatter_dimension=1, tiled=True),
    )
    vector_sum = lax.psum(vector_grad, "batch")
    return (summed[0], summed[1], summed[2], summed[3], vector_sum)


def per_device_any(
    cube_tokens,
    visible,
    live_counts,
    block_cotangent,
    triple_master,
    triple_first,
    triple_second,
    mixing_master,
    mixing_first,
    mixing_second,
    expand_master,
    expand_first,
    expand_second,
    shrink_master,
    shrink_first,
    shrink_second,
    vector_master,
    vector_first,
    vector_second,
):
    low_copies = (
        lax.all_gather(triple_master.astype(jnp.bfloat16), "blk", axis=0, tiled=True),
        lax.all_gather(mixing_master.astype(jnp.bfloat16), "blk", axis=0, tiled=True),
        lax.all_gather(expand_master.astype(jnp.bfloat16), "blk", axis=0, tiled=True),
        lax.all_gather(shrink_master.astype(jnp.bfloat16), "blk", axis=0, tiled=True),
        lax.all_gather(vector_master.astype(jnp.bfloat16), "blk", axis=1, tiled=True),
    )
    triple_w, mixing_w, expand_w, shrink_w = (
        lax.all_gather(low_copies[0], "batch", axis=1, tiled=True),
        lax.all_gather(low_copies[1], "batch", axis=1, tiled=True),
        lax.all_gather(low_copies[2], "batch", axis=1, tiled=True),
        lax.all_gather(low_copies[3], "batch", axis=1, tiled=True),
    )
    vector_w = low_copies[4].astype(jnp.float32)
    groups, slot_count = visible.shape
    region = cube_tokens.shape[1]
    features = cube_tokens.shape[2]
    row_count = groups * slot_count
    head_count = features // HD
    local_index = visible % region
    tokens = jnp.take_along_axis(cube_tokens, local_index[:, :, None], axis=1).astype(jnp.float32)
    flat_tokens = tokens.reshape(row_count, features)
    live_mask = jnp.arange(slot_count, dtype=jnp.int32)[None, :] < live_counts
    live_rows = live_mask.reshape(row_count, 1)
    normed1 = layer_norm(flat_tokens, vector_w[0], vector_w[1]).astype(jnp.bfloat16)
    zero_bias = jnp.zeros((features,), jnp.float32)
    triple_bias = jnp.concatenate([vector_w[4], zero_bias, vector_w[5]])
    triple = (jnp.dot(normed1, triple_w, preferred_element_type=jnp.float32) + triple_bias).astype(
        jnp.bfloat16
    )
    triple = triple.reshape(groups, slot_count, 3 * features)
    query_flat = triple[:, :, :features]
    queries = query_flat.reshape(groups, slot_count, head_count, HD)
    key_rows = triple[:, :, features : 2 * features]
    value_rows = triple[:, :, 2 * features :]
    key_all, value_all, live_all = (
        lax.all_gather(key_rows, "blk", axis=1, tiled=True),
        lax.all_gather(value_rows, "blk", axis=1, tiled=True),
        lax.all_gather(live_mask.astype(jnp.bfloat16), "blk", axis=1, tiled=True),
    )
    key_all = key_all.reshape(groups, -1, head_count, HD)
    value_all = value_all.reshape(groups, -1, head_count, HD)
    scores = masked_scores(queries, key_all, live_all)
    peak = jnp.max(scores, axis=-1, keepdims=True)
    expo = jnp.exp(scores - peak)
    total = jnp.sum(expo, axis=-1, keepdims=True)
    prob_low = (expo / total).astype(jnp.bfloat16)
    mixed = jnp.einsum("ghst,gthe->gshe", prob_low, value_all, preferred_element_type=jnp.float32)
    mixed = mixed.astype(jnp.bfloat16).reshape(row_count, features)
    attended = flat_tokens + (
        jnp.dot(mixed, mixing_w, preferred_element_type=jnp.float32) + vector_w[6]
    )
    normed2 = layer_norm(attended, vector_w[2], vector_w[3]).astype(jnp.bfloat16)
    preact = jnp.dot(normed2, expand_w, preferred_element_type=jnp.float32) + vector_w[8:].reshape(
        -1
    )
    activation = jax.nn.gelu(preact, approximate=False).astype(jnp.bfloat16)
    result = attended + (
        jnp.dot(activation, shrink_w, preferred_element_type=jnp.float32) + vector_w[7]
    )
    result = jnp.where(live_rows, result, 0.0)
    block_output = result.astype(jnp.bfloat16).reshape(groups, slot_count, features)
    grad_out = jnp.where(
        live_rows, block_cotangent.reshape(row_count, features).astype(jnp.float32), 0.0
    )
    branch_low = grad_out.astype(jnp.bfloat16)
    shrink_grad = outer_sum(activation, branch_low)
    shrink_bias_grad = jnp.sum(branch_low.astype(jnp.float32), axis=0)
    grad_act = back_product(branch_low, shrink_w)
    gelu_value, gelu_back = jax.vjp(partial(jax.nn.gelu, approximate=False), preact)
    grad_pre = gelu_back(grad_act)[0].astype(jnp.bfloat16)
    expand_grad = outer_sum(normed2, grad_pre)
    expand_bias_grad = jnp.sum(grad_pre.astype(jnp.float32), axis=0)
    grad_normed2 = back_product(grad_pre, expand_w)
    norm2_value, norm2_back = jax.vjp(layer_norm, attended, vector_w[2], vector_w[3])
    grad_through2, gain2_grad, shift2_grad = norm2_back(grad_normed2)
    grad_attended = grad_out + grad_through2
    mix_low = grad_attended.astype(jnp.bfloat16)
    mixing_grad = outer_sum(mixed, mix_low)
    mixing_bias_grad = jnp.sum(mix_low.astype(jnp.float32), axis=0)
    grad_mixed_flat = (
        back_product(mix_low, mixing_w).astype(jnp.bfloat16).reshape(groups, slot_count, features)
    )
    grad_mixed = grad_mixed_flat.reshape(groups, slot_count, head_count, HD)
    scores = masked_scores(queries, key_all, live_all)
    probs = jnp.exp(scores - peak) / total
    prob_low = probs.astype(jnp.bfloat16)
    grad_probs = jnp.einsum(
        "gshe,gthe->ghst", grad_mixed, value_all, preferred_element_type=jnp.float32
    )
    delta = jnp.sum(probs * grad_probs, axis=-1, keepdims=True)
    grad_scores = (probs * (grad_probs - delta)).astype(jnp.bfloat16)
    score_scale = 1.0 / math.sqrt(HD)
    grad_queries = (
        jnp.einsum("ghst,gthe->gshe", grad_scores, key_all, preferred_element_type=jnp.float32)
        * score_scale
    )
    term_keys = (
        jnp.einsum("ghst,gshe->gthe", grad_scores, queries, preferred_element_type=jnp.float32)
        * score_scale
    )
    term_values = jnp.einsum(
        "ghst,gshe->gthe", prob_low, grad_mixed, preferred_element_type=jnp.float32
    )
    grad_keys, grad_values = (
        lax.psum_scatter(
            term_keys.reshape(groups, -1, features), "blk", scatter_dimension=1, tiled=True
        ),
        lax.psum_scatter(
            term_values.reshape(groups, -1, features), "blk", scatter_dimension=1, tiled=True
        ),
    )
    grad_triple = jnp.concatenate(
        [
            grad_queries.reshape(row_count, features),
            grad_keys.reshape(row_count, features),
            grad_values.reshape(row_count, features),
        ],
        axis=1,
    ).astype(jnp.bfloat16)
    triple_grad = outer_sum(normed1, grad_triple)
    triple_sums = jnp.sum(grad_triple.astype(jnp.float32), axis=0)
    grad_normed1 = back_product(grad_triple, triple_w)
    norm1_value, norm1_back = jax.vjp(layer_norm, flat_tokens, vector_w[0], vector_w[1])
    grad_through1, gain1_grad, shift1_grad = norm1_back(grad_normed1)
    grad_tokens = (grad_attended + grad_through1).reshape(groups, slot_count, features)
    cube_rows = jnp.arange(groups, dtype=jnp.int32)[:, None]
    token_grads = (
        jnp.zeros(cube_tokens.shape, jnp.float32)
        .at[cube_rows, local_index]
        .add(grad_tokens)
        .astype(jnp.bfloat16)
    )
    leading_rows = jnp.stack(
        [
            gain1_grad,
            shift1_grad,
            gain2_grad,
            shift2_grad,
            triple_sums[:features],
            triple_sums[2 * features :],
            mixing_bias_grad,
            shrink_bias_grad,
        ]
    )
    vector_grad = jnp.concatenate([leading_rows, expand_bias_grad.reshape(-1, features)], axis=0)
    reduced = group_section(triple_grad, mixing_grad, expand_grad, shrink_grad, vector_grad)
    reduced = cycle_section(reduced[0], reduced[1], reduced[2], reduced[3], reduced[4])
    masters = (triple_master, mixing_master, expand_master, shrink_master, vector_master)
    firsts = (triple_first, mixing_first, expand_first, shrink_first, vector_first)
    seconds = (triple_second, mixing_second, expand_second, shrink_second, vector_second)
    outputs = [block_output, token_grads]
    for master, first, second, grad, rate, decay in zip(
        masters, firsts, seconds, reduced, RATES, DECAYS
    ):
        outputs.extend(adamw(master, first, second, grad, rate, decay))
    return tuple(outputs)


def solution(mesh):
    groups, blocks = mesh.shape["batch"], mesh.shape["blk"]
    if (groups, blocks) == (4, 8):
        mesh = Mesh(mesh.devices.reshape(2, 2, 8), FINE)
        batch, body = ("y", "core"), per_device
    else:
        batch, body = "batch", per_device_any
    rows = P(batch, "blk", None)
    part = P("blk", batch)
    table = P(None, "blk")
    in_specs = (rows, P(batch, "blk"), P(batch, "blk"), rows) + (part,) * 12 + (table,) * 3
    out_specs = (rows, rows) + (part,) * 16 + (table,) * 4
    return jax.shard_map(body, mesh=mesh, in_specs=in_specs, out_specs=out_specs, check_vma=False)
```

```python
from functools import partial
import math

import jax
import jax.numpy as jnp
from jax import lax
from jax.experimental import pallas as pl
from jax.experimental.pallas import tpu as pltpu
from jax.sharding import Mesh, PartitionSpec as P

HD = 64
STEP = 10
BF = jnp.bfloat16
F32 = jnp.float32

RATES = (0.04, 0.3, 0.04, 0.02, 0.25)
DECAYS = (0.05, 0.05, 0.05, 0.05, 0.0)


def adamw(master, first, second, grad, rate, decay):
    first_new = 0.9 * first + 0.1 * grad
    second_new = 0.999 * second + 0.001 * grad * grad
    corrected = first_new / (1.0 - 0.9**STEP) / (jnp.sqrt(second_new / (1.0 - 0.999**STEP)) + 1e-08)
    master_new = master - rate * (corrected + decay * master)
    return (first_new, second_new, master_new, master_new.astype(BF))


FINE = ("y", "core", "blk")


def place(y, c, b):
    return (y * 2 + c) * 8 + b


def swap(x, dy=0, dc=0, db=0):
    pairs = [
        (place(y, c, b), place(y ^ dy, c ^ dc, b ^ db))
        for y in range(2)
        for c in range(2)
        for b in range(8)
    ]
    return lax.ppermute(x, FINE, pairs)


def cube_pairs(step, back):
    pairs = []
    for y in range(2):
        for c in range(2):
            for b in range(8):
                r, q = b // 4, b % 4
                far = place(y, r, 4 * c + (q + step) % 4)
                near = place(y, c, b)
                pairs.append((far, near) if back else (near, far))
    return pairs


def pick(x, index, axis):
    return lax.dynamic_index_in_dim(x, index, axis, keepdims=False)


def add_low(a, b):
    return (a.astype(F32) + b.astype(F32)).astype(BF)


def tie(*parts):
    return lax.optimization_barrier(parts)


def dot_nn(a, b):
    return jnp.dot(a, b, preferred_element_type=F32)


def dot_nt(a, b):
    return lax.dot_general(a, b, (((1,), (1,)), ((), ())), preferred_element_type=F32)


def dot_tn(a, b):
    return lax.dot_general(a, b, (((0,), (0,)), ((), ())), preferred_element_type=F32)


def call(kernel, outs, name, flops=0, moved=0, **kw):
    return pl.pallas_call(
        kernel,
        out_shape=outs,
        name=name,
        cost_estimate=pl.CostEstimate(flops=int(flops), bytes_accessed=int(moved), transcendentals=0),
        compiler_params=pltpu.CompilerParams(vmem_limit_bytes=50 * 2**20),
        **kw,
    )


def shape(*dims, dtype=F32):
    return jax.ShapeDtypeStruct(dims, dtype)


VM = pl.BlockSpec(memory_space=pltpu.VMEM)
SM = pl.BlockSpec(memory_space=pltpu.SMEM)


def normalize(rows):
    center = rows - jnp.mean(rows, axis=-1, keepdims=True)
    spread = lax.rsqrt(jnp.mean(center * center, axis=-1, keepdims=True) + 1e-06)
    return center * spread, spread


def norm_back(xhat, spread, gain, grad):
    q = grad * gain
    mean_q = jnp.mean(q, axis=-1, keepdims=True)
    mean_x = jnp.mean(q * xhat, axis=-1, keepdims=True)
    return spread * (q - mean_q - xhat * mean_x)


def lanes(ref_rows, unit):
    return ref_rows[:, 192 * unit : 192 * unit + 192]


def give_kernel(ids, triple, expand, shrink_t, give):
    first = ids[0] == 0
    e = expand[...].astype(BF)
    give[0:96] = jnp.where(first, lanes(e, 1), lanes(e, 0))
    give[96:192] = jnp.where(first, lanes(e, 3), lanes(e, 2))
    s = shrink_t[...].T.astype(BF)
    give[192:384] = jnp.where(first, s[192:], s[:192])
    give[384:480] = lanes(triple, 1).astype(BF)


def pack_kernel(ids, triple, mixing, expand, shrink_t, vector, took, tvm, e_out, s_out):
    first, t = ids[0] == 0, ids[1]
    e = expand[...].astype(BF)
    for j in range(2):
        mine = jnp.where(first, lanes(e, 2 * j), lanes(e, 2 * j + 1))
        far = took[96 * j : 96 * j + 96]
        e_out[0:96, 192 * j : 192 * j + 192] = jnp.where(first, mine, far)
        e_out[96:192, 192 * j : 192 * j + 192] = jnp.where(first, far, mine)
    s = shrink_t[...].T.astype(BF)
    mine, far = jnp.where(first, s[:192], s[192:]), took[192:384]
    s_out[:, :192] = jnp.where(first, mine, far)
    s_out[:, 192:] = jnp.where(first, far, mine)
    low = triple[...].astype(BF)
    t0, t2, far = lanes(low, 0), lanes(low, 2), took[384:480]
    tvm[0:96, :192] = jnp.where(t == 1, far, jnp.where(t == 2, t2, t0))
    tvm[0:96, 192:] = jnp.where(t == 1, t0, jnp.where(t == 2, far, t2))
    key = jnp.where(t == 1, t2, jnp.where(t == 2, t0, far))
    tvm[96:144, :192] = key[:48]
    tvm[96:144, 192:] = key[48:]
    m = mixing[...].astype(BF)
    tvm[144:192, :192] = m[:48]
    tvm[144:192, 192:] = m[48:]
    tvm[192:208] = jnp.zeros((16, 384), BF)
    tvm[192:204, 0:96] = vector[...].astype(BF)


def qkv_kernel(ids, tok_own, tok_far, qv_own, qv_far, rest_own, rest_far,
               n1_out, x3_out, t3_out, mix_out, vec_out, eb_out, bias):
    first, my, mx, mz = ids[0] == 0, ids[2], ids[3], ids[4]
    for b in range(8):
        iz = ((b >> 1 & 1) ^ (mz & 1)) * 2 + ((b >> 2) ^ (mz >> 1))
        here = (b & 1) ^ mx
        for y in range(2):
            there = y ^ my
            iq, ir = here * 4 + iz, there * 4 + iz
            t3_out[y, 96 * b : 96 * b + 96, :] = jnp.where(there == 0, qv_own[iq], qv_far[iq])
            block = jnp.where(here == 0, rest_own[ir], rest_far[ir])
            t3_out[2, 96 * b : 96 * b + 48, 192 * y : 192 * y + 192] = block[0:48, :192]
            t3_out[2, 96 * b + 48 : 96 * b + 96, 192 * y : 192 * y + 192] = block[0:48, 192:]
            mix_out[y * 8 + b] = block[48:96]
            if y == 0:
                vec_out[0:16, 96 * b : 96 * b + 96] = block[96:112, 0:96].astype(F32)
    half = tok_own.shape[0]
    for at, tok in ((0, tok_own), (half, tok_far)):
        xhat, _ = normalize(tok[...].astype(F32))
        n1_out[at : at + half, :] = (xhat * vec_out[0:1, :] + vec_out[1:2, :]).astype(BF)
    bias[...] = jnp.zeros_like(bias)
    for j in range(2):
        for k in range(2):
            row = vec_out[4 + j : 5 + j, 384 * k : 384 * k + 384]
            bias[j : j + 1, 192 * k : 192 * k + 192] = jnp.where(first, lanes(row, 0), lanes(row, 1))
    for n in range(4):
        for k in range(2):
            row = vec_out[8 + n : 9 + n, 384 * k : 384 * k + 384]
            eb_out[n, 0:1, 192 * k : 192 * k + 192] = jnp.where(first, lanes(row, 0), lanes(row, 1))
    for j in range(3):
        x3_out[j] = (dot_nn(n1_out[...], t3_out[j]) + bias[j : j + 1, :]).astype(BF)


def head_masks():
    lane = lax.broadcasted_iota(jnp.int32, (1, 2 * HD), 1)
    return [lane < HD, lane >= HD]


def soft(keys, query, live, width):
    raw = dot_nt(keys, query) * (1.0 / math.sqrt(HD))
    raw = jnp.where(jnp.concatenate([live] * (width // 128), axis=1) > 0, raw, -1e30)
    expo = jnp.exp(raw - jnp.max(raw, axis=0, keepdims=True))
    return expo * (1.0 / jnp.sum(expo, axis=0, keepdims=True))


QB = 256


def attn_kernel(x3, live, own, far):
    q, v, k = x3[0], x3[1], x3[2]
    lv = live[...]
    vt = v.astype(F32).T.astype(BF)
    row = lax.broadcasted_iota(jnp.int32, (2 * HD, 1), 0)
    masks = head_masks()
    for s, out in ((0, own), (QB, far)):
        total = jnp.zeros((2 * HD, QB), F32)
        for h in range(2):
            qh = jnp.where(masks[h], q[s : s + QB], jnp.zeros((), BF))
            low = soft(k, qh, lv, QB).astype(BF)
            vh = jnp.where(row < HD if h == 0 else row >= HD, vt, jnp.zeros((), BF))
            total += dot_nn(vh, low)
        out[...] = total.T.astype(BF)


def attn_back_kernel(x3, gm_own, gm_far, live, d3):
    q, v, k = x3[0], x3[1], x3[2]
    slots = q.shape[0]
    lv = live[...]
    kt = k.astype(F32).T.astype(BF)
    row = lax.broadcasted_iota(jnp.int32, (2 * HD, 1), 0)
    masks = head_masks()
    scale = 1.0 / math.sqrt(HD)
    zero = jnp.zeros((), BF)
    dk = jnp.zeros((slots, 2 * HD), F32)
    dv = jnp.zeros((slots, 2 * HD), F32)
    for s, gm in ((0, gm_own), (QB, gm_far)):
        dqt = jnp.zeros((2 * HD, QB), F32)
        for h in range(2):
            qh = jnp.where(masks[h], q[s : s + QB], zero)
            gh = jnp.where(masks[h], gm[...], zero)
            probs = soft(k, qh, lv, QB)
            gp = dot_nt(v, gh)
            delta = jnp.sum(probs * gp, axis=0, keepdims=True)
            ds = (probs * (gp - delta)).astype(BF)
            kh = jnp.where(row < HD if h == 0 else row >= HD, kt, zero)
            dqt += dot_nn(kh, ds)
            dk += dot_nn(ds, qh)
            dv += dot_nn(probs.astype(BF), gh)
        d3[0, s : s + QB, :] = (dqt.T * scale).astype(BF)
    d3[1] = dv.astype(BF)
    d3[2] = (dk * scale).astype(BF)


def mid_kernel(ids, tok, own, far, mix_own, mix_far, vec, att_out, n2_out, m_out, mixed_out):
    first = ids[0] == 0
    for y in range(2):
        for b in range(8):
            a, f = mix_own[y * 8 + b], mix_far[y * 8 + b]
            for p, block in ((0, jnp.where(first, a, f)), (1, jnp.where(first, f, a))):
                at = 192 * (2 * y + p)
                m_out[96 * b : 96 * b + 48, at : at + 192] = block[:, :192]
                m_out[96 * b + 48 : 96 * b + 96, at : at + 192] = block[:, 192:]
    for k in range(2):
        a, f = lanes(own, k), lanes(far, k)
        mixed_out[:, 384 * k : 384 * k + 192] = jnp.where(first, a, f)
        mixed_out[:, 384 * k + 192 : 384 * k + 384] = jnp.where(first, f, a)
    att = tok[...].astype(F32) + (dot_nn(mixed_out[...], m_out[...]) + vec[6:7, :])
    att_out[...] = att
    xhat, _ = normalize(att)
    n2_out[...] = (xhat * vec[2:3, :] + vec[3:4, :]).astype(BF)


def ffn_kernel(ids, n2_own, n2_far, br_own, br_far, ea, ea_far, eb, eb_far, sa, sa_far, sb, sb_far, bias,
               part_own, part_far, gn_own, gn_far, d_e, d_s, d_bias, n2, n2t, br, e_ref, s_ref):
    my, mx, mz = ids[2], ids[3], ids[4]
    n = pl.program_id(0)
    ny, np_ = n // 2, n % 2

    def layer(z):
        return (((z & 1) ^ (mz & 1)) * 2 + ((z >> 1) ^ (mz >> 1))) * 2

    def at_x_first(near, far, y, x, z):
        i = layer(z) + (x ^ mx)
        return jnp.where(y == my, near[i], far[i])

    def at_y_first(near, far, y, x, z):
        i = layer(z) + (y ^ my)
        return jnp.where(x == mx, near[i], far[i])

    @pl.when(np_ == 0)
    def _():
        for b in range(8):
            e_ref[96 * b : 96 * b + 96] = at_x_first(ea, ea_far, ny, b & 1, b >> 1)

    @pl.when(np_ == 1)
    def _():
        for b in range(8):
            e_ref[96 * b : 96 * b + 96] = at_y_first(eb, eb_far, ny, b & 1, b >> 1)

    for y in range(2):
        for x in range(2):
            s_ref[y, 192 * x : 192 * x + 96] = at_x_first(sa, sa_far, y, x, n)
            s_ref[y, 192 * x + 96 : 192 * x + 192] = at_y_first(sb, sb_far, y, x, n)
    half = n2_own.shape[0]

    @pl.when(pl.program_id(0) == 0)
    def _():
        for out in (part_own, part_far, gn_own, gn_far):
            out[...] = jnp.zeros_like(out)
        n2[0:half], n2[half:] = n2_own[...], n2_far[...]
        br[0:half], br[half:] = br_own[...], br_far[...]
        n2t[:, 0:half] = n2_own[...].astype(F32).T.astype(BF)
        n2t[:, half:] = n2_far[...].astype(F32).T.astype(BF)

    e, s0, s1 = e_ref[...], s_ref[0], s_ref[1]
    b0, b1 = br[:, :384], br[:, 384:]
    pre = dot_nn(n2[...], e) + bias[0]
    cdf = 0.5 * (1.0 + lax.erf(pre * math.sqrt(0.5)))
    act = (pre * cdf).astype(BF)
    slope = cdf + pre * (jnp.exp(-0.5 * pre * pre) * (1.0 / math.sqrt(2.0 * math.pi)))
    for k, sk in ((0, s0), (1, s1)):
        y = dot_nn(act, sk)
        part_own[:, 384 * k : 384 * k + 384] += y[:half]
        part_far[:, 384 * k : 384 * k + 384] += y[half:]
    grad_act = dot_nt(b0, s0) + dot_nt(b1, s1)
    grad_pre = (grad_act * slope).astype(BF)
    gn = dot_nt(grad_pre, e)
    gn_own[...] += gn[:half]
    gn_far[...] += gn[half:]
    d_s[0, 0] = dot_tn(act, b0).astype(BF).reshape(2, 192, 384)
    d_s[1, 0] = dot_tn(act, b1).astype(BF).reshape(2, 192, 384)
    d_e[0, :, 0] = dot_nn(n2t[...], grad_pre).astype(BF).reshape(8, 96, 384)
    d_bias[0] = jnp.sum(grad_pre.astype(F32), axis=0, keepdims=True)


def mid_back_kernel(ids, gn_a, gn_b, att_ref, br_ref, mixed, m, vec, gatt, dm, gm_own, gm_far, sums):
    first, c = ids[0] == 0, ids[0]
    gn = gn_a[...] + gn_b[...]
    br = br_ref[...].astype(F32)
    xhat, spread = normalize(att_ref[...])
    grad = br + norm_back(xhat, spread, vec[2:3, :], gn)
    gatt[...] = grad
    low = grad.astype(BF)
    gm = dot_nt(low, m[...]).astype(BF)
    for k in range(2):
        u, v = lanes(gm, 2 * k), lanes(gm, 2 * k + 1)
        gm_own[:, 192 * k : 192 * k + 192] = jnp.where(first, u, v)
        gm_far[:, 192 * k : 192 * k + 192] = jnp.where(first, v, u)
    weight = dot_tn(mixed[...], low).astype(BF)
    for y in range(2):
        for b in range(8):
            for p in range(2):
                at = 192 * (2 * y + p)
                dm[p ^ c, y * 8 + b, :, :192] = weight[96 * b : 96 * b + 48, at : at + 192]
                dm[p ^ c, y * 8 + b, :, 192:] = weight[96 * b + 48 : 96 * b + 96, at : at + 192]
    sums[0:1] = jnp.sum(gn * xhat, axis=0, keepdims=True)
    sums[1:2] = jnp.sum(gn, axis=0, keepdims=True)
    sums[2:3] = jnp.sum(low.astype(F32), axis=0, keepdims=True)
    sums[3:4] = jnp.sum(br, axis=0, keepdims=True)
    sums[4:8] = jnp.zeros((4, sums.shape[1]), F32)


def triple_back_kernel(n1_ref, d3, t3, d_qv, d_k, gn_own, gn_far, sums):
    j = pl.program_id(0)
    d = d3[0]
    half = gn_own.shape[0]
    weight = dot_tn(n1_ref[...], d).astype(BF)
    part = dot_nt(d, t3[0])
    sums[0] = jnp.sum(d.astype(F32), axis=0, keepdims=True)

    @pl.when(j == 0)
    def _():
        gn_own[...] = part[:half]
        gn_far[...] = part[half:]

    @pl.when(j > 0)
    def _():
        gn_own[...] += part[:half]
        gn_far[...] += part[half:]

    @pl.when(j < 2)
    def _():
        d_qv[0] = weight

    @pl.when(j == 2)
    def _():
        for b in range(8):
            for y in range(2):
                d_k[y, b, :, :192] = weight[96 * b : 96 * b + 48, 192 * y : 192 * y + 192]
                d_k[y, b, :, 192:] = weight[96 * b + 48 : 96 * b + 96, 192 * y : 192 * y + 192]


def first_back_kernel(gn_a, gn_b, tok, gatt, vec, out, sums):
    gn = gn_a[...] + gn_b[...]
    xhat, spread = normalize(tok[...].astype(F32))
    out[...] = (gatt[...] + norm_back(xhat, spread, vec[0:1, :], gn)).astype(BF)
    sums[0:1] = jnp.sum(gn * xhat, axis=0, keepdims=True)
    sums[1:2] = jnp.sum(gn, axis=0, keepdims=True)
    sums[2:8] = jnp.zeros((6, sums.shape[1]), F32)


def by_core(c, own, far):
    return jnp.where(c == 0, jnp.stack([own, far]), jnp.stack([far, own]))


def per_device(
    cube_tokens, visible, live_counts, block_cotangent,
    triple_master, triple_first, triple_second,
    mixing_master, mixing_first, mixing_second,
    expand_master, expand_first, expand_second,
    shrink_master, shrink_first, shrink_second,
    vector_master, vector_first, vector_second,
):
    y, c, b = lax.axis_index("y"), lax.axis_index("core"), lax.axis_index("blk")
    bits = (y, b & 1, b >> 1 & 1, b >> 2)
    turn = b % 4
    unturn = (4 - turn) % 4
    region, feats = cube_tokens.shape[1:]
    slots = visible.shape[1]
    slot_axis = jnp.arange(slots, dtype=jnp.int32)

    t_id = 2 * y + c
    ids = jnp.stack([c, t_id, y, bits[1], b >> 1]).astype(jnp.int32)
    shrink_t = shrink_master.T
    took = swap(call(
        give_kernel, shape(480, 192, dtype=BF), "give", 1e6, 1e6, in_specs=[SM, VM, VM, VM], out_specs=VM,
    )(ids, triple_master, expand_master, shrink_t), dc=1)
    tvm, e_low, s_low = call(
        pack_kernel, (shape(208, 384, dtype=BF), shape(192, 384, dtype=BF), shape(192, 384, dtype=BF)), "pack", 1e6, 2e6,
        in_specs=[SM] + [VM] * 6, out_specs=(VM, VM, VM),
    )(ids, triple_master, mixing_master, expand_master, shrink_t, vector_master, took)
    order = (turn + jnp.arange(4, dtype=jnp.int32)) % 4
    local = visible % region
    flat_index = jnp.take(local + region * jnp.arange(4, dtype=jnp.int32)[:, None], order, axis=0)
    picked = jnp.take(cube_tokens.reshape(-1, feats), flat_index.reshape(-1), axis=0).reshape(4, slots, feats)
    counts = jnp.broadcast_to(jnp.take(live_counts, order, axis=0)[:, :, None].astype(BF), (4, 16, feats))
    packet = jnp.concatenate([picked, counts], axis=1)
    live_here = slot_axis[None, :] < live_counts
    masked = jnp.where(live_here[:, :, None], block_cotangent, jnp.zeros((), BF))
    masked = lax.dynamic_slice_in_dim(jnp.concatenate([masked, masked]), turn, 4, 0)

    t_far = swap(tvm, db=4)
    ea, eb, sa, sb = e_low[:96], e_low[96:], s_low[:96], s_low[96:]
    ea_in, eb_in = swap(ea, db=1), swap(eb, dy=1)
    own = [lax.ppermute(packet[s], FINE, cube_pairs(s, False)) for s in range(4)]

    t_far, ea_in, eb_in, sa, sb = tie(t_far, ea_in, eb_in, sa, sb)
    tvm = jnp.stack([tvm, t_far])
    t_far = swap(tvm, db=2)
    e4 = jnp.stack([ea, ea_in, eb, eb_in])
    e_far = swap(e4, db=4)
    sa_in, sb_in = swap(sa, db=1), swap(sb, dy=1)

    t_far, e_far, sa_in, sb_in, own = tie(t_far, e_far, sa_in, sb_in, own)
    tvm = jnp.stack([tvm, t_far]).reshape(4, 208, 384)
    qv, rest = tvm[:, :96], tvm[:, 96:]
    qv_x, rest_y = swap(qv, db=1), swap(rest, dy=1)
    e8 = jnp.stack([e4, e_far])
    e_far = swap(e8, db=2)
    s4 = jnp.stack([sa, sa_in, sb, sb_in])
    s_far = swap(s4, db=4)
    own = jnp.stack(own)
    far = swap(own, dc=1)

    qv_x, rest_y, e_far, s_far, far = tie(qv_x, rest_y, e_far, s_far, far)
    qv = jnp.stack([qv, qv_x]).reshape(8, 96, 384)
    rest = jnp.stack([rest, rest_y]).reshape(8, 112, 384)
    qv_far, rest_far = swap(qv, dy=1), swap(rest, db=1)
    s8 = jnp.stack([s4, s_far])
    s_far = swap(s8, db=2)
    e16 = jnp.stack([e8, e_far])
    ea, eb = e16[:, :, :2].reshape(8, 96, 384), e16[:, :, 2:].reshape(8, 96, 384)
    ea_far, eb_far = swap(ea, dy=1), swap(eb, db=1)

    qv_far, rest_far, s_far = tie(qv_far, rest_far, s_far)
    s16 = jnp.stack([s8, s_far])
    sa, sb = s16[:, :, :2].reshape(8, 96, 384), s16[:, :, 2:].reshape(8, 96, 384)
    sa_far, sb_far = swap(sa, dy=1), swap(sb, db=1)

    def cotangent(s, after):
        return lax.ppermute(tie(masked[s], after)[0], FINE, cube_pairs(s, False))

    rows = 4 * slots
    tok_own, tok_far = own[:, :slots].reshape(rows, feats), far[:, :slots].reshape(rows, feats)
    cnt = jnp.concatenate([own[:, slots, :1], far[:, slots, :1]]).astype(jnp.int32)
    live = (slot_axis[None, :] < cnt).reshape(2 * rows, 1)
    live_cols = jnp.broadcast_to(live.astype(F32), (2 * rows, 128))

    n1, x3, t3, mix, vec, e_bias = call(
        qkv_kernel,
        (shape(2 * rows, feats, dtype=BF), shape(3, 2 * rows, 384, dtype=BF), shape(3, feats, 384, dtype=BF),
         shape(16, 48, 384, dtype=BF), shape(16, feats), shape(4, 1, 384)),
        "qkv", 2 * 512 * 768 * 1152, 8e6,
        in_specs=[SM] + [VM] * 6, out_specs=(VM,) * 6, scratch_shapes=[pltpu.VMEM((8, 384), F32)],
    )(ids, tok_own, tok_far, qv, qv_far, rest, rest_far)
    mix_far = swap(mix, dc=1)
    br = [cotangent(0, qv_far), cotangent(1, n1)]

    pairs3 = pl.BlockSpec((3, 2 * rows, 128), lambda i: (0, 0, i))
    col = pl.BlockSpec((rows, 128), lambda i: (0, i))
    same = pl.BlockSpec((2 * rows, 128), lambda i: (0, 0))
    mixed_own, mixed_give = call(
        attn_kernel, (shape(rows, 384, dtype=BF),) * 2, "attention", 6e9, 2e6,
        grid=(3,), in_specs=[pairs3, same], out_specs=(col, col),
    )(x3, live_cols)

    mixed_far = swap(mixed_give, dc=1)
    br += [cotangent(2, mixed_own)]
    att, n2, mix, mixed = call(
        mid_kernel,
        (shape(rows, feats), shape(rows, feats, dtype=BF), shape(feats, feats, dtype=BF), shape(rows, feats, dtype=BF)),
        "mixing", 2e9, 5e6,
        in_specs=[SM] + [VM] * 6, out_specs=(VM,) * 4,
    )(ids, tok_own, mixed_own, mixed_far, mix, mix_far, vec)

    n2_far = swap(n2, dc=1)
    br += [cotangent(3, n2)]
    br_own = jnp.concatenate(br)
    br_far = swap(br_own, dc=1)
    whole = pl.BlockSpec((rows, feats), lambda i: (0, 0))

    gathered = pl.BlockSpec((8, 96, 384), lambda n: (0, 0, 0))
    part_own, part_give, gn2_own, gn2_give, d_e, d_s, d_b = call(
        ffn_kernel,
        (shape(rows, feats),) * 4
        + (shape(2, 8, 2, 96, 384, dtype=BF), shape(2, 4, 2, 192, 384, dtype=BF), shape(4, 1, 384)),
        "feed_forward", 18e9, 20e6,
        grid=(4,),
        in_specs=[SM] + [whole] * 4 + [gathered] * 8 + [pl.BlockSpec((1, 1, 384), lambda n: (n, 0, 0))],
        out_specs=(whole,) * 4 + (
            pl.BlockSpec((1, 8, 1, 96, 384), lambda n: (n // 2, 0, n % 2, 0, 0)),
            pl.BlockSpec((2, 1, 2, 192, 384), lambda n: (0, n, 0, 0, 0)),
            pl.BlockSpec((1, 1, 384), lambda n: (n, 0, 0)),
        ),
        scratch_shapes=[pltpu.VMEM((2 * rows, feats), BF), pltpu.VMEM((feats, 2 * rows), BF), pltpu.VMEM((2 * rows, feats), BF),
                        pltpu.VMEM((feats, 384), BF), pltpu.VMEM((2, 384, 384), BF)],
    )(ids, n2, n2_far, br_own, br_far, ea, ea_far, eb, eb_far, sa, sa_far, sb, sb_far, e_bias)

    z0, z1 = bits[2], bits[3]
    gn2_far = swap(gn2_give, dc=1)
    d_e = d_e.reshape(2, 4, 2, 192, 384)
    e_in = swap(pick(d_e, 1 - bits[1], 2), db=1)
    s_in = swap(pick(d_s, 1 - y, 0), dy=1)
    gatt, dm, gm_own, gm_give, sums2 = call(
        mid_back_kernel,
        (shape(rows, feats), shape(2, 16, 48, 384, dtype=BF), shape(rows, 384, dtype=BF), shape(rows, 384, dtype=BF), shape(8, feats)),
        "mixing_back", 4e9, 8e6,
        in_specs=[SM] + [VM] * 7, out_specs=(VM,) * 5,
    )(ids, gn2_own, gn2_far, att, br_own, mixed, mix, vec)
    gm_far = swap(gm_give, dc=1)

    part_give, gatt = tie(part_give, gatt)
    part_far = swap(part_give, dc=1)
    result = att + (part_own + part_far + vec[7])
    result = jnp.where(live[:rows], result, 0.0).astype(BF).reshape(4, slots, feats)
    back = [lax.ppermute(result[s], FINE, cube_pairs(s, True)) for s in range(3)]

    d3 = call(
        attn_back_kernel, shape(3, 2 * rows, 384, dtype=BF), "attention_back", 9e9, 5e6,
        grid=(3,), in_specs=[pairs3, col, col, same], out_specs=pairs3,
    )(x3, gm_own, gm_far, live_cols)
    result, back, d3 = tie(result, back, d3)
    back = back + [lax.ppermute(result[3], FINE, cube_pairs(3, True))]
    dm = add_low(dm[0], swap(dm[1], dc=1)).reshape(2, 8, 48, 384)

    third = pl.BlockSpec((1, 2 * rows, 384), lambda j: (j, 0, 0))
    d_qv, d_k, gn1_own, gn1_give, sums1 = call(
        triple_back_kernel,
        (shape(2, feats, 384, dtype=BF), shape(2, 8, 48, 384, dtype=BF), shape(rows, feats), shape(rows, feats), shape(3, 1, 384)),
        "triple_back", 5e9, 5e6,
        grid=(3,),
        in_specs=[pl.BlockSpec((2 * rows, feats), lambda j: (0, 0)), third, pl.BlockSpec((1, feats, 384), lambda j: (j, 0, 0))],
        out_specs=(
            pl.BlockSpec((1, feats, 384), lambda j: (jnp.minimum(j, 1), 0, 0)),
            pl.BlockSpec((2, 8, 48, 384), lambda j: (0, 0, 0, 0)),
            whole, whole,
            pl.BlockSpec((1, 1, 384), lambda j: (j, 0, 0)),
        ),
    )(n1, d3, t3)

    d_qv, d_k, gn1_own, gn1_give, back, dm = tie(d_qv, d_k, gn1_own, gn1_give, back, dm)
    gn1_far = swap(gn1_give, dc=1)
    d_qv = d_qv.reshape(2, 4, 2, 96, 384)
    d_km = jnp.concatenate([d_k, dm], axis=2).reshape(2, 4, 2, 96, 384)
    qv_in = swap(pick(d_qv, 1 - bits[1], 2), db=1)
    km_in = swap(pick(d_km, 1 - y, 0), dy=1)
    back = jnp.stack(back)
    block_output = lax.dynamic_slice_in_dim(jnp.concatenate([back, back]), unturn, 4, 0)
    grad_tok, sums0 = call(
        first_back_kernel, (shape(rows, feats, dtype=BF), shape(8, feats)), "first_back", 1e9, 1e6,
        in_specs=[VM] * 5, out_specs=(VM, VM),
    )(gn1_own, gn1_far, tok_own, gatt, vec)
    grad_tok = grad_tok.reshape(4, slots, feats)

    e_in, s_in, grad_tok, sums0, block_output = tie(e_in, s_in, grad_tok, sums0, block_output)
    d_e = add_low(pick(d_e, bits[1], 2), e_in)
    d_s = add_low(pick(d_s, y, 0), s_in)
    e_in = swap(pick(d_e, 1 - y, 0), dy=1)
    s_in = swap(pick(d_s, 1 - bits[1], 1), db=1)
    back = [lax.ppermute(grad_tok[s], FINE, cube_pairs(s, True)) for s in range(2)]

    mine = jnp.arange(2)[None, :, None] == c

    def spread_units(sums):
        return jnp.where(mine, sums.reshape(-1, 1, 192), 0.0).reshape(-1, feats)

    table = jnp.concatenate(
        [sums0[:2], sums2[:2], spread_units(sums1[0]), spread_units(sums1[1]), sums2[2:4], spread_units(d_b)]
    )
    table = table + swap(table, dc=1)

    qv_in, km_in, back, table, grad_tok = tie(qv_in, km_in, back, table, grad_tok)
    d_qv = add_low(pick(d_qv, bits[1], 2), qv_in)
    d_km = add_low(pick(d_km, y, 0), km_in)
    qv_in = swap(pick(d_qv, 1 - y, 0), dy=1)
    km_in = swap(pick(d_km, 1 - bits[1], 1), db=1)
    back = back + [lax.ppermute(grad_tok[2], FINE, cube_pairs(2, True))]
    table = table + swap(table, dy=1)

    e_in, s_in, back, grad_tok, table = tie(e_in, s_in, back, grad_tok, table)
    d_es = jnp.concatenate(
        [add_low(pick(d_e, y, 0), e_in), add_low(pick(d_s, bits[1], 1), s_in)], axis=1
    ).reshape(2, 2, 384, 384)
    es_in = swap(pick(d_es, 1 - z0, 1), db=2)
    back = back + [lax.ppermute(grad_tok[3], FINE, cube_pairs(3, True))]
    table = table + swap(table, db=1)

    qv_in, km_in, back, table = tie(qv_in, km_in, back, table)
    d_t = jnp.concatenate(
        [add_low(pick(d_qv, y, 0), qv_in), add_low(pick(d_km, bits[1], 1), km_in)], axis=1
    ).reshape(2, 2, 192, 384)
    t_in = swap(pick(d_t, 1 - z0, 1), db=2)
    back = jnp.stack(back)
    back = lax.dynamic_slice_in_dim(jnp.concatenate([back, back]), unturn, 4, 0)
    spread = (jnp.arange(region, dtype=jnp.int32)[None, :, None] == local[:, None, :]).astype(BF)
    token_grads = jnp.einsum("grs,gsf->grf", spread, back, preferred_element_type=F32).astype(BF)
    table = table + swap(table, db=2)

    es_in, t_in, table, token_grads = tie(es_in, t_in, table, token_grads)
    d_es = add_low(pick(d_es, z0, 1), es_in)
    es_in = swap(pick(d_es, 1 - z1, 0), db=4)
    d_t = add_low(pick(d_t, z0, 1), t_in)
    t_in = swap(pick(d_t, 1 - z1, 0), db=4)
    table = table + swap(table, db=4)
    v_grad = lax.dynamic_slice_in_dim(table, b * vector_master.shape[1], vector_master.shape[1], 1)
    es_sum = pick(d_es, z1, 0).astype(F32) + es_in.astype(F32)
    e_sum, s_sum = es_sum[:192], es_sum[192:]
    t_sum = pick(d_t, z1, 0).astype(F32) + t_in.astype(F32)
    qv_sum, km_sum = t_sum[:96], t_sum[96:]

    e_sum = e_sum.reshape(2, 96, 384)
    s_sum = s_sum.reshape(192, 2, 192)
    k_sum = jnp.concatenate([km_sum[:48, :192], km_sum[:48, 192:]], axis=0)
    m_grad = jnp.concatenate([km_sum[48:, :192], km_sum[48:, 192:]], axis=0)
    qa, qb2 = qv_sum[:, :192], qv_sum[:, 192:]
    give_e = pick(e_sum, 1 - c, 0)
    give = jnp.concatenate([give_e[:, :192], give_e[:, 192:], pick(s_sum, 1 - c, 1)], axis=0)
    took = swap(give, dc=1)
    t_took = swap(jnp.where(t_id == 1, qa, jnp.where(t_id == 2, qb2, k_sum)), dc=1)
    e_own = pick(e_sum, c, 0).reshape(96, 2, 192)
    e_took = jnp.stack([took[:96], took[96:192]], axis=1)
    e_pair = by_core(c, e_own, e_took)
    e_grad = e_pair.transpose(1, 2, 0, 3).reshape(96, 768)
    s_grad = by_core(c, pick(s_sum, c, 1), took[192:]).reshape(384, 192)
    p0 = jnp.where(t_id == 1, qb2, jnp.where(t_id == 2, k_sum, qa))
    p2 = jnp.where(t_id == 1, k_sum, jnp.where(t_id == 2, qa, qb2))
    t_grad = jnp.concatenate([p0, t_took, p2], axis=1)

    masters = (triple_master, mixing_master, expand_master, shrink_master, vector_master)
    firsts = (triple_first, mixing_first, expand_first, shrink_first, vector_first)
    seconds = (triple_second, mixing_second, expand_second, shrink_second, vector_second)
    grads = (t_grad, m_grad, e_grad, s_grad, v_grad)
    outputs = [block_output, token_grads]
    for master, first, second, grad, rate, decay in zip(masters, firsts, seconds, grads, RATES, DECAYS):
        outputs.extend(adamw(master, first, second, grad, rate, decay))
    return tuple(outputs)


def layer_norm(rows, gain, shift):
    center = rows - jnp.mean(rows, axis=-1, keepdims=True)
    spread = lax.rsqrt(jnp.mean(center * center, axis=-1, keepdims=True) + 1e-06)
    return center * spread * gain + shift


def outer_sum(left, right):
    return lax.dot_general(
        left, right, (((0,), (0,)), ((), ())), preferred_element_type=jnp.float32
    )


def back_product(grads, weight):
    return lax.dot_general(
        grads, weight, (((1,), (1,)), ((), ())), preferred_element_type=jnp.float32
    )


def masked_scores(queries, key_all, live_all):
    raw = jnp.einsum("gshe,gthe->ghst", queries, key_all, preferred_element_type=jnp.float32) * (
        1.0 / math.sqrt(HD)
    )
    return jnp.where(live_all[:, None, None, :] > 0, raw, -1e30)


def cycle_section(triple_grad, mixing_grad, expand_grad, shrink_grad, vector_grad):
    summed = (
        lax.psum_scatter(triple_grad, "blk", scatter_dimension=0, tiled=True),
        lax.psum_scatter(mixing_grad, "blk", scatter_dimension=0, tiled=True),
        lax.psum_scatter(expand_grad, "blk", scatter_dimension=0, tiled=True),
        lax.psum_scatter(shrink_grad, "blk", scatter_dimension=0, tiled=True),
        lax.psum_scatter(vector_grad, "blk", scatter_dimension=1, tiled=True),
    )
    return (summed[0], summed[1], summed[2], summed[3], summed[4])


def group_section(triple_grad, mixing_grad, expand_grad, shrink_grad, vector_grad):
    summed = (
        lax.psum_scatter(triple_grad, "batch", scatter_dimension=1, tiled=True),
        lax.psum_scatter(mixing_grad, "batch", scatter_dimension=1, tiled=True),
        lax.psum_scatter(expand_grad, "batch", scatter_dimension=1, tiled=True),
        lax.psum_scatter(shrink_grad, "batch", scatter_dimension=1, tiled=True),
    )
    vector_sum = lax.psum(vector_grad, "batch")
    return (summed[0], summed[1], summed[2], summed[3], vector_sum)


def per_device_any(
    cube_tokens,
    visible,
    live_counts,
    block_cotangent,
    triple_master,
    triple_first,
    triple_second,
    mixing_master,
    mixing_first,
    mixing_second,
    expand_master,
    expand_first,
    expand_second,
    shrink_master,
    shrink_first,
    shrink_second,
    vector_master,
    vector_first,
    vector_second,
):
    low_copies = (
        lax.all_gather(triple_master.astype(jnp.bfloat16), "blk", axis=0, tiled=True),
        lax.all_gather(mixing_master.astype(jnp.bfloat16), "blk", axis=0, tiled=True),
        lax.all_gather(expand_master.astype(jnp.bfloat16), "blk", axis=0, tiled=True),
        lax.all_gather(shrink_master.astype(jnp.bfloat16), "blk", axis=0, tiled=True),
        lax.all_gather(vector_master.astype(jnp.bfloat16), "blk", axis=1, tiled=True),
    )
    triple_w, mixing_w, expand_w, shrink_w = (
        lax.all_gather(low_copies[0], "batch", axis=1, tiled=True),
        lax.all_gather(low_copies[1], "batch", axis=1, tiled=True),
        lax.all_gather(low_copies[2], "batch", axis=1, tiled=True),
        lax.all_gather(low_copies[3], "batch", axis=1, tiled=True),
    )
    vector_w = low_copies[4].astype(jnp.float32)
    groups, slot_count = visible.shape
    region = cube_tokens.shape[1]
    features = cube_tokens.shape[2]
    row_count = groups * slot_count
    head_count = features // HD
    local_index = visible % region
    tokens = jnp.take_along_axis(cube_tokens, local_index[:, :, None], axis=1).astype(jnp.float32)
    flat_tokens = tokens.reshape(row_count, features)
    live_mask = jnp.arange(slot_count, dtype=jnp.int32)[None, :] < live_counts
    live_rows = live_mask.reshape(row_count, 1)
    normed1 = layer_norm(flat_tokens, vector_w[0], vector_w[1]).astype(jnp.bfloat16)
    zero_bias = jnp.zeros((features,), jnp.float32)
    triple_bias = jnp.concatenate([vector_w[4], zero_bias, vector_w[5]])
    triple = (jnp.dot(normed1, triple_w, preferred_element_type=jnp.float32) + triple_bias).astype(
        jnp.bfloat16
    )
    triple = triple.reshape(groups, slot_count, 3 * features)
    query_flat = triple[:, :, :features]
    queries = query_flat.reshape(groups, slot_count, head_count, HD)
    key_rows = triple[:, :, features : 2 * features]
    value_rows = triple[:, :, 2 * features :]
    key_all, value_all, live_all = (
        lax.all_gather(key_rows, "blk", axis=1, tiled=True),
        lax.all_gather(value_rows, "blk", axis=1, tiled=True),
        lax.all_gather(live_mask.astype(jnp.bfloat16), "blk", axis=1, tiled=True),
    )
    key_all = key_all.reshape(groups, -1, head_count, HD)
    value_all = value_all.reshape(groups, -1, head_count, HD)
    scores = masked_scores(queries, key_all, live_all)
    peak = jnp.max(scores, axis=-1, keepdims=True)
    expo = jnp.exp(scores - peak)
    total = jnp.sum(expo, axis=-1, keepdims=True)
    prob_low = (expo / total).astype(jnp.bfloat16)
    mixed = jnp.einsum("ghst,gthe->gshe", prob_low, value_all, preferred_element_type=jnp.float32)
    mixed = mixed.astype(jnp.bfloat16).reshape(row_count, features)
    attended = flat_tokens + (
        jnp.dot(mixed, mixing_w, preferred_element_type=jnp.float32) + vector_w[6]
    )
    normed2 = layer_norm(attended, vector_w[2], vector_w[3]).astype(jnp.bfloat16)
    preact = jnp.dot(normed2, expand_w, preferred_element_type=jnp.float32) + vector_w[8:].reshape(
        -1
    )
    activation = jax.nn.gelu(preact, approximate=False).astype(jnp.bfloat16)
    result = attended + (
        jnp.dot(activation, shrink_w, preferred_element_type=jnp.float32) + vector_w[7]
    )
    result = jnp.where(live_rows, result, 0.0)
    block_output = result.astype(jnp.bfloat16).reshape(groups, slot_count, features)
    grad_out = jnp.where(
        live_rows, block_cotangent.reshape(row_count, features).astype(jnp.float32), 0.0
    )
    branch_low = grad_out.astype(jnp.bfloat16)
    shrink_grad = outer_sum(activation, branch_low)
    shrink_bias_grad = jnp.sum(branch_low.astype(jnp.float32), axis=0)
    grad_act = back_product(branch_low, shrink_w)
    gelu_value, gelu_back = jax.vjp(partial(jax.nn.gelu, approximate=False), preact)
    grad_pre = gelu_back(grad_act)[0].astype(jnp.bfloat16)
    expand_grad = outer_sum(normed2, grad_pre)
    expand_bias_grad = jnp.sum(grad_pre.astype(jnp.float32), axis=0)
    grad_normed2 = back_product(grad_pre, expand_w)
    norm2_value, norm2_back = jax.vjp(layer_norm, attended, vector_w[2], vector_w[3])
    grad_through2, gain2_grad, shift2_grad = norm2_back(grad_normed2)
    grad_attended = grad_out + grad_through2
    mix_low = grad_attended.astype(jnp.bfloat16)
    mixing_grad = outer_sum(mixed, mix_low)
    mixing_bias_grad = jnp.sum(mix_low.astype(jnp.float32), axis=0)
    grad_mixed_flat = (
        back_product(mix_low, mixing_w).astype(jnp.bfloat16).reshape(groups, slot_count, features)
    )
    grad_mixed = grad_mixed_flat.reshape(groups, slot_count, head_count, HD)
    scores = masked_scores(queries, key_all, live_all)
    probs = jnp.exp(scores - peak) / total
    prob_low = probs.astype(jnp.bfloat16)
    grad_probs = jnp.einsum(
        "gshe,gthe->ghst", grad_mixed, value_all, preferred_element_type=jnp.float32
    )
    delta = jnp.sum(probs * grad_probs, axis=-1, keepdims=True)
    grad_scores = (probs * (grad_probs - delta)).astype(jnp.bfloat16)
    score_scale = 1.0 / math.sqrt(HD)
    grad_queries = (
        jnp.einsum("ghst,gthe->gshe", grad_scores, key_all, preferred_element_type=jnp.float32)
        * score_scale
    )
    term_keys = (
        jnp.einsum("ghst,gshe->gthe", grad_scores, queries, preferred_element_type=jnp.float32)
        * score_scale
    )
    term_values = jnp.einsum(
        "ghst,gshe->gthe", prob_low, grad_mixed, preferred_element_type=jnp.float32
    )
    grad_keys, grad_values = (
        lax.psum_scatter(
            term_keys.reshape(groups, -1, features), "blk", scatter_dimension=1, tiled=True
        ),
        lax.psum_scatter(
            term_values.reshape(groups, -1, features), "blk", scatter_dimension=1, tiled=True
        ),
    )
    grad_triple = jnp.concatenate(
        [
            grad_queries.reshape(row_count, features),
            grad_keys.reshape(row_count, features),
            grad_values.reshape(row_count, features),
        ],
        axis=1,
    ).astype(jnp.bfloat16)
    triple_grad = outer_sum(normed1, grad_triple)
    triple_sums = jnp.sum(grad_triple.astype(jnp.float32), axis=0)
    grad_normed1 = back_product(grad_triple, triple_w)
    norm1_value, norm1_back = jax.vjp(layer_norm, flat_tokens, vector_w[0], vector_w[1])
    grad_through1, gain1_grad, shift1_grad = norm1_back(grad_normed1)
    grad_tokens = (grad_attended + grad_through1).reshape(groups, slot_count, features)
    cube_rows = jnp.arange(groups, dtype=jnp.int32)[:, None]
    token_grads = (
        jnp.zeros(cube_tokens.shape, jnp.float32)
        .at[cube_rows, local_index]
        .add(grad_tokens)
        .astype(jnp.bfloat16)
    )
    leading_rows = jnp.stack(
        [
            gain1_grad,
            shift1_grad,
            gain2_grad,
            shift2_grad,
            triple_sums[:features],
            triple_sums[2 * features :],
            mixing_bias_grad,
            shrink_bias_grad,
        ]
    )
    vector_grad = jnp.concatenate([leading_rows, expand_bias_grad.reshape(-1, features)], axis=0)
    reduced = group_section(triple_grad, mixing_grad, expand_grad, shrink_grad, vector_grad)
    reduced = cycle_section(reduced[0], reduced[1], reduced[2], reduced[3], reduced[4])
    masters = (triple_master, mixing_master, expand_master, shrink_master, vector_master)
    firsts = (triple_first, mixing_first, expand_first, shrink_first, vector_first)
    seconds = (triple_second, mixing_second, expand_second, shrink_second, vector_second)
    outputs = [block_output, token_grads]
    for master, first, second, grad, rate, decay in zip(
        masters, firsts, seconds, reduced, RATES, DECAYS
    ):
        outputs.extend(adamw(master, first, second, grad, rate, decay))
    return tuple(outputs)


def solution(mesh):
    groups, blocks = mesh.shape["batch"], mesh.shape["blk"]
    if (groups, blocks) == (4, 8):
        mesh = Mesh(mesh.devices.reshape(2, 2, 8), FINE)
        batch, body = ("y", "core"), per_device
    else:
        batch, body = "batch", per_device_any
    rows = P(batch, "blk", None)
    part = P("blk", batch)
    table = P(None, "blk")
    in_specs = (rows, P(batch, "blk"), P(batch, "blk"), rows) + (part,) * 12 + (table,) * 3
    out_specs = (rows, rows) + (part,) * 16 + (table,) * 4
    return jax.shard_map(body, mesh=mesh, in_specs=in_specs, out_specs=out_specs, check_vma=False)
```

```python
from functools import partial
import math

import jax
import jax.numpy as jnp
from jax import lax
from jax.experimental import pallas as pl
from jax.experimental.pallas import tpu as pltpu
from jax.sharding import Mesh, PartitionSpec as P

HD = 64
STEP = 10
BF = jnp.bfloat16
F32 = jnp.float32

RATES = (0.04, 0.3, 0.04, 0.02, 0.25)
DECAYS = (0.05, 0.05, 0.05, 0.05, 0.0)


def adamw(master, first, second, grad, rate, decay):
    first_new = 0.9 * first + 0.1 * grad
    second_new = 0.999 * second + 0.001 * grad * grad
    corrected = first_new / (1.0 - 0.9**STEP) / (jnp.sqrt(second_new / (1.0 - 0.999**STEP)) + 1e-08)
    master_new = master - rate * (corrected + decay * master)
    return (first_new, second_new, master_new, master_new.astype(BF))


FINE = ("y", "core", "blk")


def place(y, c, b):
    return (y * 2 + c) * 8 + b


def swap(x, dy=0, dc=0, db=0):
    pairs = [
        (place(y, c, b), place(y ^ dy, c ^ dc, b ^ db))
        for y in range(2)
        for c in range(2)
        for b in range(8)
    ]
    return lax.ppermute(x, FINE, pairs)


def trade(x):
    return lax.all_to_all(x, "core", 0, 0, tiled=True)


def cube_pairs(step, back):
    pairs = []
    for y in range(2):
        for c in range(2):
            for b in range(8):
                r, q = b // 4, b % 4
                far = place(y, r, 4 * c + (q + step) % 4)
                near = place(y, c, b)
                pairs.append((far, near) if back else (near, far))
    return pairs


def pick(x, index, axis):
    return lax.dynamic_index_in_dim(x, index, axis, keepdims=False)


def add_low(a, b):
    return (a.astype(F32) + b.astype(F32)).astype(BF)


def tie(*parts):
    return lax.optimization_barrier(parts)


def dot_nn(a, b):
    return jnp.dot(a, b, preferred_element_type=F32)


def dot_nt(a, b):
    return lax.dot_general(a, b, (((1,), (1,)), ((), ())), preferred_element_type=F32)


def dot_tn(a, b):
    return lax.dot_general(a, b, (((0,), (0,)), ((), ())), preferred_element_type=F32)


def call(kernel, outs, name, flops=0, moved=0, **kw):
    return pl.pallas_call(
        kernel,
        out_shape=outs,
        name=name,
        cost_estimate=pl.CostEstimate(flops=int(flops), bytes_accessed=int(moved), transcendentals=0),
        compiler_params=pltpu.CompilerParams(vmem_limit_bytes=50 * 2**20),
        **kw,
    )


def shape(*dims, dtype=F32):
    return jax.ShapeDtypeStruct(dims, dtype)


VM = pl.BlockSpec(memory_space=pltpu.VMEM)
SM = pl.BlockSpec(memory_space=pltpu.SMEM)


def normalize(rows):
    center = rows - jnp.mean(rows, axis=-1, keepdims=True)
    spread = lax.rsqrt(jnp.mean(center * center, axis=-1, keepdims=True) + 1e-06)
    return center * spread, spread


def norm_back(xhat, spread, gain, grad):
    q = grad * gain
    mean_q = jnp.mean(q, axis=-1, keepdims=True)
    mean_x = jnp.mean(q * xhat, axis=-1, keepdims=True)
    return spread * (q - mean_q - xhat * mean_x)


def lanes(ref_rows, unit):
    return ref_rows[:, 192 * unit : 192 * unit + 192]


def give_kernel(ids, triple, expand, shrink_t, give):
    first = ids[0] == 0
    e = expand[...].astype(BF)
    give[0:96] = jnp.where(first, lanes(e, 1), lanes(e, 0))
    give[96:192] = jnp.where(first, lanes(e, 3), lanes(e, 2))
    s = shrink_t[...].T.astype(BF)
    give[192:384] = jnp.where(first, s[192:], s[:192])
    give[384:480] = lanes(triple, 1).astype(BF)


def pack_kernel(ids, took, triple, mixing, expand, shrink_t, vector, tvm, es):
    first, t = ids[0] == 0, ids[1]
    e = expand[...].astype(BF)
    for j in range(2):
        mine = jnp.where(first, lanes(e, 2 * j), lanes(e, 2 * j + 1))
        far = took[96 * j : 96 * j + 96]
        es[0:96, 192 * j : 192 * j + 192] = jnp.where(first, mine, far)
        es[192:288, 192 * j : 192 * j + 192] = jnp.where(first, far, mine)
    s = shrink_t[...].T.astype(BF)
    mine, far = jnp.where(first, s[:192], s[192:]), took[192:384]
    left, right = jnp.where(first, mine, far), jnp.where(first, far, mine)
    for at, rows in ((96, slice(0, 96)), (288, slice(96, 192))):
        es[at : at + 96, :192] = left[rows]
        es[at : at + 96, 192:] = right[rows]
    low = triple[...].astype(BF)
    t0, t2, far = lanes(low, 0), lanes(low, 2), took[384:480]
    tvm[0:96, :192] = jnp.where(t == 1, far, jnp.where(t == 2, t2, t0))
    tvm[0:96, 192:] = jnp.where(t == 1, t0, jnp.where(t == 2, far, t2))
    key = jnp.where(t == 1, t2, jnp.where(t == 2, t0, far))
    tvm[96:144, :192] = key[:48]
    tvm[96:144, 192:] = key[48:]
    m = mixing[...].astype(BF)
    tvm[144:192, :192] = m[:48]
    tvm[144:192, 192:] = m[48:]
    tvm[192:208] = jnp.zeros((16, 384), BF)
    tvm[192:204, 0:96] = vector[...].astype(BF)


def qkv_kernel(ids, tok_own, tok_far, qv_own, qv_far, rest_own, rest_far,
               n1_out, x3_out, t3_out, mix_out, vec_out, eb_out, bias, n1):
    first, my, mx, mz = ids[0] == 0, ids[2], ids[3], ids[4]
    for b in range(8):
        iz = ((b >> 1 & 1) ^ (mz & 1)) * 2 + ((b >> 2) ^ (mz >> 1))
        here = (b & 1) ^ mx
        for y in range(2):
            there = y ^ my
            iq, ir = here * 4 + iz, there * 4 + iz
            t3_out[y, 96 * b : 96 * b + 96, :] = jnp.where(there == 0, qv_own[iq], qv_far[iq])
            block = jnp.where(here == 0, rest_own[ir], rest_far[ir])
            t3_out[2, 96 * b : 96 * b + 48, 192 * y : 192 * y + 192] = block[0:48, :192]
            t3_out[2, 96 * b + 48 : 96 * b + 96, 192 * y : 192 * y + 192] = block[0:48, 192:]
            at = 2 * QB + 48 * (y * 8 + b)
            mix_out[0, at : at + 48] = block[48:96]
            mix_out[1, at : at + 48] = block[48:96]
            if y == 0:
                vec_out[0:16, 96 * b : 96 * b + 96] = block[96:112, 0:96].astype(F32)
    half = tok_own.shape[0]
    for at, tok in ((0, tok_own), (half, tok_far)):
        xhat, _ = normalize(tok[...].astype(F32))
        low = (xhat * vec_out[0:1, :] + vec_out[1:2, :]).astype(BF)
        n1[at : at + half, :] = low
        n1_out[:, at : at + half] = low.astype(F32).T.astype(BF)
    mix_out[:, 0 : 2 * QB] = jnp.zeros((2, 2 * QB, 384), BF)
    bias[...] = jnp.zeros_like(bias)
    for j in range(2):
        for k in range(2):
            row = vec_out[4 + j : 5 + j, 384 * k : 384 * k + 384]
            bias[j : j + 1, 192 * k : 192 * k + 192] = jnp.where(first, lanes(row, 0), lanes(row, 1))
    for n in range(4):
        for k in range(2):
            row = vec_out[8 + n : 9 + n, 384 * k : 384 * k + 384]
            eb_out[n, 0:1, 192 * k : 192 * k + 192] = jnp.where(first, lanes(row, 0), lanes(row, 1))
    for j in range(3):
        x3_out[j] = (dot_nn(n1[...], t3_out[j]) + bias[j : j + 1, :]).astype(BF)


def head_masks():
    lane = lax.broadcasted_iota(jnp.int32, (1, 2 * HD), 1)
    return [lane < HD, lane >= HD]


def soft(keys, query, live, width):
    raw = dot_nt(keys, query) * (1.0 / math.sqrt(HD))
    raw = jnp.where(jnp.concatenate([live] * (width // 128), axis=1) > 0, raw, -1e30)
    expo = jnp.exp(raw - jnp.max(raw, axis=0, keepdims=True))
    return expo * (1.0 / jnp.sum(expo, axis=0, keepdims=True))


QB = 256


def attn_kernel(ids, x3, live, _, out):
    q, v, k = x3[0], x3[1], x3[2]
    c = ids[0]
    lv = live[...]
    vt = v.astype(F32).T.astype(BF)
    row = lax.broadcasted_iota(jnp.int32, (2 * HD, 1), 0)
    masks = head_masks()
    for s, core in ((0, c), (QB, 1 - c)):
        total = jnp.zeros((2 * HD, QB), F32)
        for h in range(2):
            qh = jnp.where(masks[h], q[s : s + QB], jnp.zeros((), BF))
            low = soft(k, qh, lv, QB).astype(BF)
            vh = jnp.where(row < HD if h == 0 else row >= HD, vt, jnp.zeros((), BF))
            total += dot_nn(vh, low)
        mixed = total.T.astype(BF)
        at = pl.ds(pl.multiple_of(core * QB, QB), QB)
        out[0, at, :] = mixed
        out[1, at, :] = mixed


def attn_back_kernel(x3, gm_ref, live, d3):
    q, v, k = x3[0], x3[1], x3[2]
    slots = q.shape[0]
    lv = live[...]
    kt = k.astype(F32).T.astype(BF)
    row = lax.broadcasted_iota(jnp.int32, (2 * HD, 1), 0)
    masks = head_masks()
    scale = 1.0 / math.sqrt(HD)
    zero = jnp.zeros((), BF)
    dk = jnp.zeros((slots, 2 * HD), F32)
    dv = jnp.zeros((slots, 2 * HD), F32)
    for s in range(0, slots, QB):
        gm = gm_ref[s : s + QB, :]
        dqt = jnp.zeros((2 * HD, QB), F32)
        for h in range(2):
            qh = jnp.where(masks[h], q[s : s + QB], zero)
            gh = jnp.where(masks[h], gm, zero)
            probs = soft(k, qh, lv, QB)
            gp = dot_nt(v, gh)
            delta = jnp.sum(probs * gp, axis=0, keepdims=True)
            ds = (probs * (gp - delta)).astype(BF)
            kh = jnp.where(row < HD if h == 0 else row >= HD, kt, zero)
            dqt += dot_nn(kh, ds)
            dk += dot_nn(ds, qh)
            dv += dot_nn(probs.astype(BF), gh)
        d3[0, s : s + QB, :] = (dqt.T * scale).astype(BF)
    d3[1] = dv.astype(BF)
    d3[2] = (dk * scale).astype(BF)


def mid_kernel(ids, tok_own, tok_far, traded, vec, att_own, att_far, n2_out, n2t_out, m_out, mixed_t, mixed_out):
    c = ids[0]
    half = tok_own.shape[0]
    for p in range(2):
        for y in range(2):
            at = 192 * (2 * y + p)
            for b in range(8):
                block = traded[p, 2 * half + 48 * (y * 8 + b) : 2 * half + 48 * (y * 8 + b) + 48]
                m_out[96 * b : 96 * b + 48, at : at + 192] = block[:, :192]
                m_out[96 * b + 48 : 96 * b + 96, at : at + 192] = block[:, 192:]
            for to, core in ((0, c), (half, 1 - c)):
                rows = traded[p, pl.ds(pl.multiple_of(core * half, half), half), :]
                mixed_out[to : to + half, at : at + 192] = lanes(rows, y)
    for to, tok, out in ((0, tok_own, att_own), (half, tok_far, att_far)):
        att = tok[...].astype(F32) + (dot_nn(mixed_out[to : to + half, :], m_out[...]) + vec[6:7, :])
        out[...] = att
        xhat, _ = normalize(att)
        n2 = (xhat * vec[2:3, :] + vec[3:4, :]).astype(BF)
        n2_out[to : to + half, :] = n2
        n2t_out[:, to : to + half] = n2.astype(F32).T.astype(BF)
        mixed_t[:, to : to + half] = mixed_out[to : to + half, :].astype(F32).T.astype(BF)


def ffn_kernel(ids, n2, n2t, br_own, br_far, ea, ea_far, eb, eb_far, bias,
               part_own, part_far, gn2, d_e, d_s, d_bias, br, e_ref, s_ref):
    my, mx, mz = ids[2], ids[3], ids[4]
    n = pl.program_id(0)
    ny, np_ = n // 2, n % 2

    def layer(z):
        return ((z & 1) ^ (mz & 1)) * 2 + ((z >> 1) ^ (mz >> 1))

    def x_first(at, y, x, z):
        i, rows = (x ^ mx) * 4 + layer(z), pl.ds(at, 96)
        return jnp.where(y == my, ea[i, rows, :], ea_far[i, rows, :])

    def y_first(at, y, x, z):
        i, rows = (y ^ my) * 4 + layer(z), pl.ds(at, 96)
        return jnp.where(x == mx, eb[i, rows, :], eb_far[i, rows, :])

    @pl.when(np_ == 0)
    def _():
        for b in range(8):
            e_ref[96 * b : 96 * b + 96] = x_first(0, ny, b & 1, b >> 1)

    @pl.when(np_ == 1)
    def _():
        for b in range(8):
            e_ref[96 * b : 96 * b + 96] = y_first(0, ny, b & 1, b >> 1)

    for y in range(2):
        for x in range(2):
            s_ref[y, 192 * x : 192 * x + 96] = x_first(96, y, x, n)
            s_ref[y, 192 * x + 96 : 192 * x + 192] = y_first(96, y, x, n)
    half = br_own.shape[0]

    @pl.when(pl.program_id(0) == 0)
    def _():
        for out in (part_own, part_far, gn2):
            out[...] = jnp.zeros_like(out)
        br[0:half], br[half:] = br_own[...], br_far[...]

    e, s0, s1 = e_ref[...], s_ref[0], s_ref[1]
    b0, b1 = br[:, :384], br[:, 384:]
    pre = dot_nn(n2[...], e) + bias[0]
    cdf = 0.5 * (1.0 + lax.erf(pre * math.sqrt(0.5)))
    act = (pre * cdf).astype(BF)
    slope = cdf + pre * (jnp.exp(-0.5 * pre * pre) * (1.0 / math.sqrt(2.0 * math.pi)))
    for k, sk in ((0, s0), (1, s1)):
        y = dot_nn(act, sk)
        part_own[:, 384 * k : 384 * k + 384] += y[:half]
        part_far[:, 384 * k : 384 * k + 384] += y[half:]
    grad_act = dot_nt(b0, s0) + dot_nt(b1, s1)
    grad_pre = (grad_act * slope).astype(BF)
    gn2[...] += dot_nt(grad_pre, e)
    act_t = act.astype(F32).T.astype(BF)
    d_s[0, 0] = dot_nn(act_t, b0).astype(BF).reshape(2, 192, 384)
    d_s[1, 0] = dot_nn(act_t, b1).astype(BF).reshape(2, 192, 384)
    d_e[0, :, 0] = dot_nn(n2t[...], grad_pre).astype(BF).reshape(8, 96, 384)
    d_bias[0] = jnp.sum(grad_pre.astype(F32), axis=0, keepdims=True)


def mid_back_kernel(ids, gn_here, gn_there, att_own, att_far, br_own, br_far, mixed_t, m, vec, gatt, gm, dm, sums, low):
    first, c = ids[0] == 0, ids[0]
    half = att_own.shape[0]
    for to, att, br_ref in ((0, att_own, br_own), (half, att_far, br_far)):
        gn = gn_here[to : to + half, :] + gn_there[half - to : 2 * half - to, :]
        br = br_ref[...].astype(F32)
        xhat, spread = normalize(att[...])
        grad = br + norm_back(xhat, spread, vec[2:3, :], gn)
        low[to : to + half, :] = grad.astype(BF)
        if to == 0:
            gatt[...] = grad
            sums[0:1] = jnp.sum(gn * xhat, axis=0, keepdims=True)
            sums[1:2] = jnp.sum(gn, axis=0, keepdims=True)
            sums[2:3] = jnp.sum(grad.astype(BF).astype(F32), axis=0, keepdims=True)
            sums[3:4] = jnp.sum(br, axis=0, keepdims=True)
            sums[4:8] = jnp.zeros((4, sums.shape[1]), F32)
    for k in range(2):
        rows = m[pl.ds(pl.multiple_of(192 * (2 * k + c), 192), 192), :]
        gm[:, 192 * k : 192 * k + 192] = dot_nt(low[...], rows).astype(BF)
        both = low[:, 384 * k : 384 * k + 384]
        mine = jnp.where(first, lanes(both, 0), lanes(both, 1))
        weight = dot_nn(mixed_t[...], mine).astype(BF)
        for b in range(8):
            dm[8 * k + b, :, :192] = weight[96 * b : 96 * b + 48]
            dm[8 * k + b, :, 192:] = weight[96 * b + 48 : 96 * b + 96]


def triple_back_kernel(ids, n1_ref, d3, t3, d_qv, d_k, gn, sums):
    c = ids[0]
    j = pl.program_id(0)
    d = d3[0]
    half = gn.shape[1]
    weight = dot_nn(n1_ref[...], d).astype(BF)
    part = dot_nt(d, t3[0])
    sums[0] = jnp.sum(d.astype(F32), axis=0, keepdims=True)

    @pl.when(j == 0)
    def _():
        gn[c] = part[:half]
        gn[1 - c] = part[half:]

    @pl.when(j > 0)
    def _():
        gn[c] += part[:half]
        gn[1 - c] += part[half:]

    @pl.when(j < 2)
    def _():
        d_qv[0] = weight

    @pl.when(j == 2)
    def _():
        for b in range(8):
            for y in range(2):
                d_k[y, b, :, :192] = weight[96 * b : 96 * b + 48, 192 * y : 192 * y + 192]
                d_k[y, b, :, 192:] = weight[96 * b + 48 : 96 * b + 96, 192 * y : 192 * y + 192]


def first_back_kernel(ids, gn_both, tok, gatt, vec, sums2, sums1, d_bias, out, blocks, table):
    c = ids[0]
    gn = gn_both[0] + gn_both[1]
    xhat, spread = normalize(tok[...].astype(F32))
    out[...] = (gatt[...] + norm_back(xhat, spread, vec[0:1, :], gn)).astype(BF)
    table[12:16] = jnp.zeros((4, table.shape[1]), F32)
    table[0:1] = jnp.sum(gn * xhat, axis=0, keepdims=True)
    table[1:2] = jnp.sum(gn, axis=0, keepdims=True)
    table[2:4] = sums2[0:2]
    table[6:8] = sums2[2:4]
    for row, sums in [(4, sums1[0]), (5, sums1[1])] + [(8 + n, d_bias[n]) for n in range(4)]:
        for k in range(2):
            for p in range(2):
                at = 192 * (2 * k + p)
                table[row : row + 1, at : at + 192] = jnp.where(c == p, lanes(sums, k), 0.0)
    blocks[...] = jnp.zeros_like(blocks)
    for b in range(8):
        blocks[b, :, 0:96] = table[:, 96 * b : 96 * b + 96].astype(BF)


def halves(rows):
    return rows[:, :192], rows[:, 192:]


def fetch(refs, places, sems):
    copies = [pltpu.make_async_copy(ref, place, sems.at[i]) for i, (ref, place) in enumerate(zip(refs, places))]
    for copy in copies:
        copy.start()
    for copy in copies:
        copy.wait()


def adam_into(state, outs, rate, decay, at, grad):
    new = adamw(state[0][at], state[1][at], state[2][at], grad, rate, decay)
    for out, value in zip(outs, new):
        out[at] = value


def triple_units(t, total):
    a, b = halves(total[0:96])
    k = jnp.concatenate(halves(total[96:144]), axis=0)
    return a, b, k


def triple_give_kernel(ids, own, far, give):
    t = ids[1]
    total = own[...].astype(F32) + far[...].astype(F32)
    a, b, k = triple_units(t, total)
    give[0:96] = jnp.where(t == 1, a, jnp.where(t == 2, b, k))
    give[96:112] = jnp.zeros((16, 192), F32)
    give[96:112, 0:96] = total[192:208, 0:96]


def triple_end_kernel(ids, own, far, took, *refs):
    outs, state, sems = refs[9:21], refs[21:30], refs[30]
    fetch(refs[:9], state, sems)
    t = ids[1]
    total = own[...].astype(F32) + far[...].astype(F32)
    a, b, k = triple_units(t, total)
    units = (
        jnp.where(t == 1, b, jnp.where(t == 2, k, a)),
        took[0:96],
        jnp.where(t == 1, k, jnp.where(t == 2, a, b)),
    )
    every = slice(None)
    for i, unit in enumerate(units):
        adam_into(state[0:3], outs[0:4], RATES[0], DECAYS[0], (every, slice(192 * i, 192 * i + 192)), unit)
    for i, part in enumerate(halves(total[144:192])):
        adam_into(state[3:6], outs[4:8], RATES[1], DECAYS[1], (slice(48 * i, 48 * i + 48), every), part)
    adam_into(state[6:9], outs[8:12], RATES[4], DECAYS[4], (every, every), total[192:204, 0:96] + took[96:108, 0:96])


def forward_give_kernel(ids, own, far, give):
    first = ids[0] == 0
    total = own[...].astype(F32) + far[...].astype(F32)
    e = jnp.where(first, total[96:192], total[0:96])
    give[0:96], give[96:192] = halves(e)
    s0, s1 = halves(total[192:])
    give[192:384] = jnp.where(first, s1, s0)


def forward_end_kernel(ids, own, far, took, *refs):
    outs, state, sems = refs[6:14], refs[14:20], refs[20]
    fetch(refs[:6], state, sems)
    first, c = ids[0] == 0, ids[0]
    total = own[...].astype(F32) + far[...].astype(F32)
    e = halves(jnp.where(first, total[0:96], total[96:192]))
    s0, s1 = halves(total[192:])
    s = jnp.where(first, s0, s1)
    every = slice(None)
    for p in range(2):
        for j in range(2):
            grad = jnp.where(c == p, e[j], took[96 * j : 96 * j + 96])
            at = 384 * j + 192 * p
            adam_into(state[0:3], outs[0:4], RATES[2], DECAYS[2], (every, slice(at, at + 192)), grad)
        grad = jnp.where(c == p, s, took[192:384]).T
        adam_into(state[3:6], outs[4:8], RATES[3], DECAYS[3], (every, slice(192 * p, 192 * p + 192)), grad)


def by_core(c, own, far):
    return jnp.where(c == 0, jnp.stack([own, far]), jnp.stack([far, own]))


def per_device(
    cube_tokens, visible, live_counts, block_cotangent,
    triple_master, triple_first, triple_second,
    mixing_master, mixing_first, mixing_second,
    expand_master, expand_first, expand_second,
    shrink_master, shrink_first, shrink_second,
    vector_master, vector_first, vector_second,
):
    y, c, b = lax.axis_index("y"), lax.axis_index("core"), lax.axis_index("blk")
    bits = (y, b & 1, b >> 1 & 1, b >> 2)
    turn = b % 4
    unturn = (4 - turn) % 4
    region, feats = cube_tokens.shape[1:]
    slots = visible.shape[1]
    slot_axis = jnp.arange(slots, dtype=jnp.int32)

    t_id = 2 * y + c
    ids = jnp.stack([c, t_id, y, bits[1], b >> 1]).astype(jnp.int32)
    shrink_t = shrink_master.T
    took = swap(call(
        give_kernel, shape(480, 192, dtype=BF), "give", 1e10, 1e3, in_specs=[SM, VM, VM, VM], out_specs=VM,
    )(ids, triple_master, expand_master, shrink_t), dc=1)
    tvm, es = call(
        pack_kernel, (shape(208, 384, dtype=BF), shape(384, 384, dtype=BF)), "pack", 1e10, 1e3,
        in_specs=[SM] + [VM] * 6, out_specs=(VM, VM),
    )(ids, took, triple_master, mixing_master, expand_master, shrink_t, vector_master)

    t_far = swap(tvm, db=4)

    visible, block_cotangent, tvm, es = tie(visible, block_cotangent, tvm, es)
    def turned(x):
        return lax.dynamic_slice_in_dim(jnp.concatenate([x, x]), turn, 4, 0)

    local = visible % region
    flat_index = turned(local + region * jnp.arange(4, dtype=jnp.int32)[:, None])
    picked = jnp.take(cube_tokens.reshape(-1, feats), flat_index.reshape(-1), axis=0).reshape(4, slots, feats)
    counts = jnp.broadcast_to(turned(live_counts)[:, :, None].astype(BF), (4, 16, feats))
    live_here = slot_axis[None, :] < live_counts
    masked = turned(jnp.where(live_here[:, :, None], block_cotangent, jnp.zeros((), BF)))
    packet = jnp.concatenate([picked, masked, counts], axis=1)

    def packets(*steps):
        return [lax.ppermute(packet[s], FINE, cube_pairs(s, False)) for s in steps]

    t_far, packet, es = tie(t_far, packet, es)
    tvm = jnp.stack([tvm, t_far])
    t_far = swap(tvm, db=2)
    es_far = swap(es, db=4)
    own = packets(0, 1)

    t_far, packet = tie(t_far, packet)
    tvm = jnp.stack([tvm, t_far]).reshape(4, 208, 384)
    qv, rest = tvm[:, :96], tvm[:, 96:]
    qv_x, rest_y = swap(qv, db=1), swap(rest, dy=1)

    qv_x, rest_y, es_far, own, packet = tie(qv_x, rest_y, es_far, own, packet)
    qv = jnp.stack([qv, qv_x]).reshape(8, 96, 384)
    rest = jnp.stack([rest, rest_y]).reshape(8, 112, 384)
    qv_far, rest_far = swap(qv, dy=1), swap(rest, db=1)
    es = jnp.stack([es, es_far])
    es_far = swap(es, db=2)
    own = own + packets(2, 3)

    qv_far, rest_far, es_far, own = tie(qv_far, rest_far, es_far, own)
    es = jnp.stack([es, es_far]).reshape(4, 384, 384)
    ea, eb = es[:, :192], es[:, 192:]
    ea_in, eb_in = swap(ea, db=1), swap(eb, dy=1)
    own = jnp.stack(own)
    far = swap(own, dc=1)

    rows = 4 * slots
    tok_own, tok_far = [p[:, :slots].reshape(rows, feats) for p in (own, far)]
    br_own, br_far = [p[:, slots : 2 * slots].reshape(rows, feats) for p in (own, far)]
    cnt = jnp.concatenate([own[:, 2 * slots, :1], far[:, 2 * slots, :1]]).astype(jnp.int32)
    live = (slot_axis[None, :] < cnt).reshape(2 * rows, 1)
    live_cols = jnp.broadcast_to(live.astype(F32), (2 * rows, 128))

    n1, x3, t3, mix, vec, e_bias = call(
        qkv_kernel,
        (shape(feats, 2 * rows, dtype=BF), shape(3, 2 * rows, 384, dtype=BF), shape(3, feats, 384, dtype=BF),
         shape(2, 2 * rows + feats, 384, dtype=BF), shape(16, feats), shape(4, 1, 384)),
        "qkv", 2 * 512 * 768 * 1152, 8e6,
        in_specs=[SM] + [VM] * 6, out_specs=(VM,) * 6, scratch_shapes=[pltpu.VMEM((8, 384), F32), pltpu.VMEM((2 * rows, feats), BF)],
    )(ids, tok_own, tok_far, qv, qv_far, rest, rest_far)
    x3, mix, ea_in, eb_in = tie(x3, mix, ea_in, eb_in)
    ea = jnp.stack([ea, ea_in]).reshape(8, 192, 384)
    eb = jnp.stack([eb, eb_in]).reshape(8, 192, 384)
    ea_far, eb_far = swap(ea, dy=1), swap(eb, db=1)

    pairs3 = pl.BlockSpec((3, 2 * rows, 128), lambda i: (0, 0, i))
    col = pl.BlockSpec((2 * rows, 128), lambda i: (0, i))
    same = pl.BlockSpec((2 * rows, 128), lambda i: (0, 0))
    traded = trade(call(
        attn_kernel, shape(2, 2 * rows + feats, 384, dtype=BF), "attention", 6e9, 2e6,
        grid=(3,), in_specs=[SM, pairs3, same, pl.BlockSpec(memory_space=pl.ANY)],
        out_specs=pl.BlockSpec((2, 2 * rows, 128), lambda i: (0, 0, i)), input_output_aliases={3: 0},
    )(ids, x3, live_cols, mix))
    att, att_far, n2, n2t, mix, mixed = call(
        mid_kernel,
        (shape(rows, feats), shape(rows, feats), shape(2 * rows, feats, dtype=BF), shape(feats, 2 * rows, dtype=BF),
         shape(feats, feats, dtype=BF), shape(feats, 2 * rows, dtype=BF)),
        "mixing", 3e9, 5e6, in_specs=[SM] + [VM] * 4, out_specs=(VM,) * 6,
        scratch_shapes=[pltpu.VMEM((2 * rows, feats), BF)],
    )(ids, tok_own, tok_far, traded, vec)

    whole = pl.BlockSpec((rows, feats), lambda i: (0, 0))

    gathered = pl.BlockSpec((8, 192, 384), lambda n: (0, 0, 0))
    every = pl.BlockSpec((2 * rows, feats), lambda i: (0, 0))
    part_own, part_give, gn2, d_e, d_s, d_b = call(
        ffn_kernel,
        (shape(rows, feats),) * 2
        + (shape(2 * rows, feats), shape(2, 8, 2, 96, 384, dtype=BF), shape(2, 4, 2, 192, 384, dtype=BF), shape(4, 1, 384)),
        "feed_forward", 18e9, 20e6,
        grid=(4,),
        in_specs=[SM, every, pl.BlockSpec((feats, 2 * rows), lambda n: (0, 0))] + [whole] * 2 + [gathered] * 4 + [pl.BlockSpec((1, 1, 384), lambda n: (n, 0, 0))],
        out_specs=(
            whole, whole, every,
            pl.BlockSpec((1, 8, 1, 96, 384), lambda n: (n // 2, 0, n % 2, 0, 0)),
            pl.BlockSpec((2, 1, 2, 192, 384), lambda n: (0, n, 0, 0, 0)),
            pl.BlockSpec((1, 1, 384), lambda n: (n, 0, 0)),
        ),
        scratch_shapes=[pltpu.VMEM((2 * rows, feats), BF),
                        pltpu.VMEM((feats, 384), BF), pltpu.VMEM((2, 384, 384), BF)],
    )(ids, n2, n2t, br_own, br_far, ea, ea_far, eb, eb_far, e_bias)

    z0, z1 = bits[2], bits[3]
    gn2_far = swap(gn2, dc=1)
    d_e = d_e.reshape(2, 4, 2, 192, 384)
    e_in = swap(pick(d_e, 1 - bits[1], 2), db=1)
    s_in = swap(pick(d_s, 1 - y, 0), dy=1)

    gatt, gm, dm, sums2 = call(
        mid_back_kernel,
        (shape(rows, feats), shape(2 * rows, 384, dtype=BF), shape(16, 48, 384, dtype=BF), shape(8, feats)),
        "mixing_back", 6e9, 8e6, in_specs=[SM] + [VM] * 9, out_specs=(VM,) * 4,
        scratch_shapes=[pltpu.VMEM((2 * rows, feats), BF)],
    )(ids, gn2, gn2_far, att, att_far, br_own, br_far, mixed, mix, vec)
    d3 = call(
        attn_back_kernel, shape(3, 2 * rows, 384, dtype=BF), "attention_back", 9e9, 5e6,
        grid=(3,), in_specs=[pairs3, col, same], out_specs=pairs3,
    )(x3, gm, live_cols)

    third = pl.BlockSpec((1, 2 * rows, 384), lambda j: (j, 0, 0))
    d_qv, d_k, gn1, sums1 = call(
        triple_back_kernel,
        (shape(2, feats, 384, dtype=BF), shape(2, 8, 48, 384, dtype=BF), shape(2, rows, feats), shape(3, 1, 384)),
        "triple_back", 5e9, 5e6,
        grid=(3,),
        in_specs=[SM, pl.BlockSpec((feats, 2 * rows), lambda j: (0, 0)), third, pl.BlockSpec((1, feats, 384), lambda j: (j, 0, 0))],
        out_specs=(
            pl.BlockSpec((1, feats, 384), lambda j: (jnp.minimum(j, 1), 0, 0)),
            pl.BlockSpec((2, 8, 48, 384), lambda j: (0, 0, 0, 0)),
            pl.BlockSpec((2, rows, feats), lambda j: (0, 0, 0)),
            pl.BlockSpec((1, 1, 384), lambda j: (j, 0, 0)),
        ),
    )(ids, n1, d3, t3)

    gn1 = trade(gn1)
    grad_tok, blocks = call(
        first_back_kernel, (shape(rows, feats, dtype=BF), shape(8, 16, 384, dtype=BF)), "first_back", 1e9, 1e6,
        in_specs=[SM] + [VM] * 7, out_specs=(VM, VM), scratch_shapes=[pltpu.VMEM((16, feats), F32)],
    )(ids, gn1, tok_own, gatt, vec, sums2, sums1, d_b)

    blocks = jnp.broadcast_to(blocks, (2, 8, 16, 384))
    d_qv = d_qv.reshape(2, 4, 2, 96, 384)
    d_km = jnp.concatenate([d_k, dm.reshape(2, 8, 48, 384), blocks], axis=2).reshape(2, 4, 2, 112, 384)
    qv_in = swap(pick(d_qv, 1 - bits[1], 2), db=1)
    km_in = swap(pick(d_km, 1 - y, 0), dy=1)

    e_in, s_in, grad_tok, part_give = tie(e_in, s_in, grad_tok, part_give)
    d_e = add_low(pick(d_e, bits[1], 2), e_in)
    d_s = add_low(pick(d_s, y, 0), s_in)
    e_in = swap(pick(d_e, 1 - y, 0), dy=1)
    s_in = swap(pick(d_s, 1 - bits[1], 1), db=1)

    part_far = swap(part_give, dc=1)
    result = att + (part_own + part_far + vec[7])
    result = jnp.where(live[:rows], result, 0.0).astype(BF).reshape(4, slots, feats)
    packet = jnp.concatenate([result, grad_tok.reshape(4, slots, feats)], axis=1)

    def go_back(step, *after):
        part = tie(packet[step], *after)[0]
        return lax.ppermute(part, FINE, cube_pairs(step, True))

    back = [go_back(0)]
    back += [go_back(1, back[0])]

    qv_in, km_in, back, packet = tie(qv_in, km_in, back, packet)
    d_qv = add_low(pick(d_qv, bits[1], 2), qv_in)
    d_km = add_low(pick(d_km, y, 0), km_in)
    qv_in = swap(pick(d_qv, 1 - y, 0), dy=1)
    km_in = swap(pick(d_km, 1 - bits[1], 1), db=1)
    back += [go_back(2)]

    e_in, s_in, back, packet = tie(e_in, s_in, back, packet)
    d_es = jnp.concatenate(
        [add_low(pick(d_e, y, 0), e_in), add_low(pick(d_s, bits[1], 1), s_in)], axis=1
    ).reshape(2, 2, 384, 384)
    es_in = swap(pick(d_es, 1 - z0, 1), db=2)
    back += [go_back(3)]

    qv_in, km_in = tie(qv_in, km_in)
    d_t = jnp.concatenate(
        [add_low(pick(d_qv, y, 0), qv_in), add_low(pick(d_km, bits[1], 1), km_in)], axis=1
    ).reshape(2, 2, 208, 384)
    t_in = swap(pick(d_t, 1 - z0, 1), db=2)

    es_in, qv_in = tie(es_in, qv_in)
    d_es = add_low(pick(d_es, z0, 1), es_in)
    es_in = swap(pick(d_es, 1 - z1, 0), db=4)
    d_t = add_low(pick(d_t, z0, 1), t_in)
    t_in = swap(pick(d_t, 1 - z1, 0), db=4)

    t_in, back = tie(t_in, back)
    back = jnp.stack(back)
    back = lax.dynamic_slice_in_dim(jnp.concatenate([back, back]), unturn, 4, 0)
    block_output = back[:, :slots]
    spread = (jnp.arange(region, dtype=jnp.int32)[None, :, None] == local[:, None, :]).astype(BF)
    token_grads = jnp.einsum("grs,gsf->grf", spread, back[:, slots:], preferred_element_type=F32).astype(BF)

    def whole_of(a):
        return pl.BlockSpec(a.shape, lambda i: (0,) * len(a.shape))

    def update(kernel, name, given, state, copies):
        outs = tuple(shape(*a.shape, dtype=d) for a in copies for d in (F32, F32, F32, BF))
        return call(
            kernel, outs, name, 1e8, 4e6, grid=(1,),
            in_specs=[SM if a is ids else whole_of(a) for a in given] + [pl.BlockSpec(memory_space=pltpu.HBM)] * len(state),
            out_specs=tuple(whole_of(o) for o in outs),
            scratch_shapes=[pltpu.VMEM(a.shape, F32) for a in state] + [pltpu.SemaphoreType.DMA((len(state),))],
        )(*given, *state)

    d_t = pick(d_t, z1, 0)
    took = swap(call(
        triple_give_kernel, shape(112, 192), "triple_give", 1e6, 1e6, in_specs=[SM, VM, VM], out_specs=VM,
    )(ids, d_t, t_in), dc=1)
    t_state = (triple_master, triple_first, triple_second, mixing_master, mixing_first, mixing_second,
               vector_master, vector_first, vector_second)
    t_new = update(triple_end_kernel, "triple_update", (ids, d_t, t_in, took), t_state, (triple_master, mixing_master, vector_master))
    es_in, t_new, token_grads, block_output = tie(es_in, t_new, token_grads, block_output)
    d_es = pick(d_es, z1, 0)
    took = swap(call(
        forward_give_kernel, shape(384, 192), "expand_shrink_give", 1e6, 1e6, in_specs=[SM, VM, VM], out_specs=VM,
    )(ids, d_es, es_in), dc=1)
    es_state = (expand_master, expand_first, expand_second, shrink_t, shrink_first.T, shrink_second.T)
    es_new = update(forward_end_kernel, "expand_shrink_update", (ids, d_es, es_in, took), es_state, (expand_master, shrink_t))
    return (block_output, token_grads, *t_new[:8], *es_new[:4], *(o.T for o in es_new[4:]), *t_new[8:])


def layer_norm(rows, gain, shift):
    center = rows - jnp.mean(rows, axis=-1, keepdims=True)
    spread = lax.rsqrt(jnp.mean(center * center, axis=-1, keepdims=True) + 1e-06)
    return center * spread * gain + shift


def outer_sum(left, right):
    return lax.dot_general(
        left, right, (((0,), (0,)), ((), ())), preferred_element_type=jnp.float32
    )


def back_product(grads, weight):
    return lax.dot_general(
        grads, weight, (((1,), (1,)), ((), ())), preferred_element_type=jnp.float32
    )


def masked_scores(queries, key_all, live_all):
    raw = jnp.einsum("gshe,gthe->ghst", queries, key_all, preferred_element_type=jnp.float32) * (
        1.0 / math.sqrt(HD)
    )
    return jnp.where(live_all[:, None, None, :] > 0, raw, -1e30)


def cycle_section(triple_grad, mixing_grad, expand_grad, shrink_grad, vector_grad):
    summed = (
        lax.psum_scatter(triple_grad, "blk", scatter_dimension=0, tiled=True),
        lax.psum_scatter(mixing_grad, "blk", scatter_dimension=0, tiled=True),
        lax.psum_scatter(expand_grad, "blk", scatter_dimension=0, tiled=True),
        lax.psum_scatter(shrink_grad, "blk", scatter_dimension=0, tiled=True),
        lax.psum_scatter(vector_grad, "blk", scatter_dimension=1, tiled=True),
    )
    return (summed[0], summed[1], summed[2], summed[3], summed[4])


def group_section(triple_grad, mixing_grad, expand_grad, shrink_grad, vector_grad):
    summed = (
        lax.psum_scatter(triple_grad, "batch", scatter_dimension=1, tiled=True),
        lax.psum_scatter(mixing_grad, "batch", scatter_dimension=1, tiled=True),
        lax.psum_scatter(expand_grad, "batch", scatter_dimension=1, tiled=True),
        lax.psum_scatter(shrink_grad, "batch", scatter_dimension=1, tiled=True),
    )
    vector_sum = lax.psum(vector_grad, "batch")
    return (summed[0], summed[1], summed[2], summed[3], vector_sum)


def per_device_any(
    cube_tokens,
    visible,
    live_counts,
    block_cotangent,
    triple_master,
    triple_first,
    triple_second,
    mixing_master,
    mixing_first,
    mixing_second,
    expand_master,
    expand_first,
    expand_second,
    shrink_master,
    shrink_first,
    shrink_second,
    vector_master,
    vector_first,
    vector_second,
):
    low_copies = (
        lax.all_gather(triple_master.astype(jnp.bfloat16), "blk", axis=0, tiled=True),
        lax.all_gather(mixing_master.astype(jnp.bfloat16), "blk", axis=0, tiled=True),
        lax.all_gather(expand_master.astype(jnp.bfloat16), "blk", axis=0, tiled=True),
        lax.all_gather(shrink_master.astype(jnp.bfloat16), "blk", axis=0, tiled=True),
        lax.all_gather(vector_master.astype(jnp.bfloat16), "blk", axis=1, tiled=True),
    )
    triple_w, mixing_w, expand_w, shrink_w = (
        lax.all_gather(low_copies[0], "batch", axis=1, tiled=True),
        lax.all_gather(low_copies[1], "batch", axis=1, tiled=True),
        lax.all_gather(low_copies[2], "batch", axis=1, tiled=True),
        lax.all_gather(low_copies[3], "batch", axis=1, tiled=True),
    )
    vector_w = low_copies[4].astype(jnp.float32)
    groups, slot_count = visible.shape
    region = cube_tokens.shape[1]
    features = cube_tokens.shape[2]
    row_count = groups * slot_count
    head_count = features // HD
    local_index = visible % region
    tokens = jnp.take_along_axis(cube_tokens, local_index[:, :, None], axis=1).astype(jnp.float32)
    flat_tokens = tokens.reshape(row_count, features)
    live_mask = jnp.arange(slot_count, dtype=jnp.int32)[None, :] < live_counts
    live_rows = live_mask.reshape(row_count, 1)
    normed1 = layer_norm(flat_tokens, vector_w[0], vector_w[1]).astype(jnp.bfloat16)
    zero_bias = jnp.zeros((features,), jnp.float32)
    triple_bias = jnp.concatenate([vector_w[4], zero_bias, vector_w[5]])
    triple = (jnp.dot(normed1, triple_w, preferred_element_type=jnp.float32) + triple_bias).astype(
        jnp.bfloat16
    )
    triple = triple.reshape(groups, slot_count, 3 * features)
    query_flat = triple[:, :, :features]
    queries = query_flat.reshape(groups, slot_count, head_count, HD)
    key_rows = triple[:, :, features : 2 * features]
    value_rows = triple[:, :, 2 * features :]
    key_all, value_all, live_all = (
        lax.all_gather(key_rows, "blk", axis=1, tiled=True),
        lax.all_gather(value_rows, "blk", axis=1, tiled=True),
        lax.all_gather(live_mask.astype(jnp.bfloat16), "blk", axis=1, tiled=True),
    )
    key_all = key_all.reshape(groups, -1, head_count, HD)
    value_all = value_all.reshape(groups, -1, head_count, HD)
    scores = masked_scores(queries, key_all, live_all)
    peak = jnp.max(scores, axis=-1, keepdims=True)
    expo = jnp.exp(scores - peak)
    total = jnp.sum(expo, axis=-1, keepdims=True)
    prob_low = (expo / total).astype(jnp.bfloat16)
    mixed = jnp.einsum("ghst,gthe->gshe", prob_low, value_all, preferred_element_type=jnp.float32)
    mixed = mixed.astype(jnp.bfloat16).reshape(row_count, features)
    attended = flat_tokens + (
        jnp.dot(mixed, mixing_w, preferred_element_type=jnp.float32) + vector_w[6]
    )
    normed2 = layer_norm(attended, vector_w[2], vector_w[3]).astype(jnp.bfloat16)
    preact = jnp.dot(normed2, expand_w, preferred_element_type=jnp.float32) + vector_w[8:].reshape(
        -1
    )
    activation = jax.nn.gelu(preact, approximate=False).astype(jnp.bfloat16)
    result = attended + (
        jnp.dot(activation, shrink_w, preferred_element_type=jnp.float32) + vector_w[7]
    )
    result = jnp.where(live_rows, result, 0.0)
    block_output = result.astype(jnp.bfloat16).reshape(groups, slot_count, features)
    grad_out = jnp.where(
        live_rows, block_cotangent.reshape(row_count, features).astype(jnp.float32), 0.0
    )
    branch_low = grad_out.astype(jnp.bfloat16)
    shrink_grad = outer_sum(activation, branch_low)
    shrink_bias_grad = jnp.sum(branch_low.astype(jnp.float32), axis=0)
    grad_act = back_product(branch_low, shrink_w)
    gelu_value, gelu_back = jax.vjp(partial(jax.nn.gelu, approximate=False), preact)
    grad_pre = gelu_back(grad_act)[0].astype(jnp.bfloat16)
    expand_grad = outer_sum(normed2, grad_pre)
    expand_bias_grad = jnp.sum(grad_pre.astype(jnp.float32), axis=0)
    grad_normed2 = back_product(grad_pre, expand_w)
    norm2_value, norm2_back = jax.vjp(layer_norm, attended, vector_w[2], vector_w[3])
    grad_through2, gain2_grad, shift2_grad = norm2_back(grad_normed2)
    grad_attended = grad_out + grad_through2
    mix_low = grad_attended.astype(jnp.bfloat16)
    mixing_grad = outer_sum(mixed, mix_low)
    mixing_bias_grad = jnp.sum(mix_low.astype(jnp.float32), axis=0)
    grad_mixed_flat = (
        back_product(mix_low, mixing_w).astype(jnp.bfloat16).reshape(groups, slot_count, features)
    )
    grad_mixed = grad_mixed_flat.reshape(groups, slot_count, head_count, HD)
    scores = masked_scores(queries, key_all, live_all)
    probs = jnp.exp(scores - peak) / total
    prob_low = probs.astype(jnp.bfloat16)
    grad_probs = jnp.einsum(
        "gshe,gthe->ghst", grad_mixed, value_all, preferred_element_type=jnp.float32
    )
    delta = jnp.sum(probs * grad_probs, axis=-1, keepdims=True)
    grad_scores = (probs * (grad_probs - delta)).astype(jnp.bfloat16)
    score_scale = 1.0 / math.sqrt(HD)
    grad_queries = (
        jnp.einsum("ghst,gthe->gshe", grad_scores, key_all, preferred_element_type=jnp.float32)
        * score_scale
    )
    term_keys = (
        jnp.einsum("ghst,gshe->gthe", grad_scores, queries, preferred_element_type=jnp.float32)
        * score_scale
    )
    term_values = jnp.einsum(
        "ghst,gshe->gthe", prob_low, grad_mixed, preferred_element_type=jnp.float32
    )
    grad_keys, grad_values = (
        lax.psum_scatter(
            term_keys.reshape(groups, -1, features), "blk", scatter_dimension=1, tiled=True
        ),
        lax.psum_scatter(
            term_values.reshape(groups, -1, features), "blk", scatter_dimension=1, tiled=True
        ),
    )
    grad_triple = jnp.concatenate(
        [
            grad_queries.reshape(row_count, features),
            grad_keys.reshape(row_count, features),
            grad_values.reshape(row_count, features),
        ],
        axis=1,
    ).astype(jnp.bfloat16)
    triple_grad = outer_sum(normed1, grad_triple)
    triple_sums = jnp.sum(grad_triple.astype(jnp.float32), axis=0)
    grad_normed1 = back_product(grad_triple, triple_w)
    norm1_value, norm1_back = jax.vjp(layer_norm, flat_tokens, vector_w[0], vector_w[1])
    grad_through1, gain1_grad, shift1_grad = norm1_back(grad_normed1)
    grad_tokens = (grad_attended + grad_through1).reshape(groups, slot_count, features)
    cube_rows = jnp.arange(groups, dtype=jnp.int32)[:, None]
    token_grads = (
        jnp.zeros(cube_tokens.shape, jnp.float32)
        .at[cube_rows, local_index]
        .add(grad_tokens)
        .astype(jnp.bfloat16)
    )
    leading_rows = jnp.stack(
        [
            gain1_grad,
            shift1_grad,
            gain2_grad,
            shift2_grad,
            triple_sums[:features],
            triple_sums[2 * features :],
            mixing_bias_grad,
            shrink_bias_grad,
        ]
    )
    vector_grad = jnp.concatenate([leading_rows, expand_bias_grad.reshape(-1, features)], axis=0)
    reduced = group_section(triple_grad, mixing_grad, expand_grad, shrink_grad, vector_grad)
    reduced = cycle_section(reduced[0], reduced[1], reduced[2], reduced[3], reduced[4])
    masters = (triple_master, mixing_master, expand_master, shrink_master, vector_master)
    firsts = (triple_first, mixing_first, expand_first, shrink_first, vector_first)
    seconds = (triple_second, mixing_second, expand_second, shrink_second, vector_second)
    outputs = [block_output, token_grads]
    for master, first, second, grad, rate, decay in zip(
        masters, firsts, seconds, reduced, RATES, DECAYS
    ):
        outputs.extend(adamw(master, first, second, grad, rate, decay))
    return tuple(outputs)


def solution(mesh):
    groups, blocks = mesh.shape["batch"], mesh.shape["blk"]
    if (groups, blocks) == (4, 8):
        mesh = Mesh(mesh.devices.reshape(2, 2, 8), FINE)
        batch, body = ("y", "core"), per_device
    else:
        batch, body = "batch", per_device_any
    rows = P(batch, "blk", None)
    part = P("blk", batch)
    table = P(None, "blk")
    in_specs = (rows, P(batch, "blk"), P(batch, "blk"), rows) + (part,) * 12 + (table,) * 3
    out_specs = (rows, rows) + (part,) * 16 + (table,) * 4
    return jax.shard_map(body, mesh=mesh, in_specs=in_specs, out_specs=out_specs, check_vma=False)
```

```python
from functools import partial
import math

import jax
import jax.numpy as jnp
from jax import lax
from jax.experimental import pallas as pl
from jax.experimental.pallas import tpu as pltpu
from jax.sharding import Mesh, PartitionSpec as P

HD = 64
STEP = 10
BF = jnp.bfloat16
F32 = jnp.float32

RATES = (0.04, 0.3, 0.04, 0.02, 0.25)
DECAYS = (0.05, 0.05, 0.05, 0.05, 0.0)


def adamw(master, first, second, grad, rate, decay):
    first_new = 0.9 * first + 0.1 * grad
    second_new = 0.999 * second + 0.001 * grad * grad
    corrected = first_new / (1.0 - 0.9**STEP) / (jnp.sqrt(second_new / (1.0 - 0.999**STEP)) + 1e-08)
    master_new = master - rate * (corrected + decay * master)
    return (first_new, second_new, master_new, master_new.astype(BF))


FINE = ("y", "core", "blk")


def place(y, c, b):
    return (y * 2 + c) * 8 + b


def swap(x, dy=0, dc=0, db=0):
    pairs = [
        (place(y, c, b), place(y ^ dy, c ^ dc, b ^ db))
        for y in range(2)
        for c in range(2)
        for b in range(8)
    ]
    return lax.ppermute(x, FINE, pairs)


def trade(x):
    return lax.all_to_all(x, "core", 0, 0, tiled=True)


def cube_pairs(step, back):
    pairs = []
    for y in range(2):
        for c in range(2):
            for b in range(8):
                r, q = b // 4, b % 4
                far = place(y, r, 4 * c + (q + step) % 4)
                near = place(y, c, b)
                pairs.append((far, near) if back else (near, far))
    return pairs


def pick(x, index, axis):
    return lax.dynamic_index_in_dim(x, index, axis, keepdims=False)


def add_low(a, b):
    return (a.astype(F32) + b.astype(F32)).astype(BF)


def tie(*parts):
    return lax.optimization_barrier(parts)


def dot_nn(a, b):
    return jnp.dot(a, b, preferred_element_type=F32)


def dot_nt(a, b):
    return lax.dot_general(a, b, (((1,), (1,)), ((), ())), preferred_element_type=F32)


def dot_tn(a, b):
    return lax.dot_general(a, b, (((0,), (0,)), ((), ())), preferred_element_type=F32)


def call(kernel, outs, name, flops=0, moved=0, vmem=16, **kw):
    return pl.pallas_call(
        kernel,
        out_shape=outs,
        name=name,
        cost_estimate=pl.CostEstimate(flops=int(flops), bytes_accessed=int(moved), transcendentals=0),
        compiler_params=pltpu.CompilerParams(vmem_limit_bytes=vmem * 2**20),
        **kw,
    )


def shape(*dims, dtype=F32):
    return jax.ShapeDtypeStruct(dims, dtype)


VM = pl.BlockSpec(memory_space=pltpu.VMEM)
SM = pl.BlockSpec(memory_space=pltpu.SMEM)


def normalize(rows):
    center = rows - jnp.mean(rows, axis=-1, keepdims=True)
    spread = lax.rsqrt(jnp.mean(center * center, axis=-1, keepdims=True) + 1e-06)
    return center * spread, spread


def norm_back(xhat, spread, gain, grad):
    q = grad * gain
    mean_q = jnp.mean(q, axis=-1, keepdims=True)
    mean_x = jnp.mean(q * xhat, axis=-1, keepdims=True)
    return spread * (q - mean_q - xhat * mean_x)


def lanes(ref_rows, unit):
    return ref_rows[:, 192 * unit : 192 * unit + 192]


def give_kernel(ids, triple, expand, shrink_t, give):
    first = ids[0] == 0
    e = expand[...].astype(BF)
    give[0:96] = jnp.where(first, lanes(e, 1), lanes(e, 0))
    give[96:192] = jnp.where(first, lanes(e, 3), lanes(e, 2))
    s = shrink_t[...].T.astype(BF)
    give[192:384] = jnp.where(first, s[192:], s[:192])
    give[384:480] = lanes(triple, 1).astype(BF)


def pack_kernel(ids, took, triple, mixing, expand, shrink_t, vector, tvm, es, last):
    first, t = ids[0] == 0, ids[1]
    e = expand[...].astype(BF)
    for j in range(2):
        mine = jnp.where(first, lanes(e, 2 * j), lanes(e, 2 * j + 1))
        far = took[96 * j : 96 * j + 96]
        es[0:96, 192 * j : 192 * j + 192] = jnp.where(first, mine, far)
        es[144:240, 192 * j : 192 * j + 192] = jnp.where(first, far, mine)
    s = shrink_t[...].T.astype(BF)
    mine, far = jnp.where(first, s[:192], s[192:]), took[192:384]
    left, right = jnp.where(first, mine, far), jnp.where(first, far, mine)
    for out, at, rows in ((es, 96, slice(0, 48)), (es, 240, slice(48, 96)), (last, 0, slice(96, 192))):
        to = slice(at, at + rows.stop - rows.start)
        out[to, :192] = left[rows]
        out[to, 192:] = right[rows]
    low = triple[...].astype(BF)
    t0, t2, far = lanes(low, 0), lanes(low, 2), took[384:480]
    tvm[0:96, :192] = jnp.where(t == 1, far, jnp.where(t == 2, t2, t0))
    tvm[0:96, 192:] = jnp.where(t == 1, t0, jnp.where(t == 2, far, t2))
    key = jnp.where(t == 1, t2, jnp.where(t == 2, t0, far))
    tvm[96:144, :192] = key[:48]
    tvm[96:144, 192:] = key[48:]
    m = mixing[...].astype(BF)
    tvm[144:192, :192] = m[:48]
    tvm[144:192, 192:] = m[48:]
    tvm[192:208] = jnp.zeros((16, 384), BF)
    tvm[192:204, 0:96] = vector[...].astype(BF)


def qkv_kernel(ids, tok_own, tok_far, qv_own, qv_far, rest_own, rest_far,
               n1_out, x3_out, t3_out, mix_out, vec_out, eb_out, bias, n1):
    first, my, mx, mz = ids[0] == 0, ids[2], ids[3], ids[4]
    for b in range(8):
        iz = ((b >> 1 & 1) ^ (mz & 1)) * 2 + ((b >> 2) ^ (mz >> 1))
        here = (b & 1) ^ mx
        for y in range(2):
            there = y ^ my
            iq, ir = here * 4 + iz, there * 4 + iz
            t3_out[y, 96 * b : 96 * b + 96, :] = jnp.where(there == 0, qv_own[iq], qv_far[iq])
            block = jnp.where(here == 0, rest_own[ir], rest_far[ir])
            t3_out[2, 96 * b : 96 * b + 48, 192 * y : 192 * y + 192] = block[0:48, :192]
            t3_out[2, 96 * b + 48 : 96 * b + 96, 192 * y : 192 * y + 192] = block[0:48, 192:]
            at = 2 * QB + 48 * (y * 8 + b)
            mix_out[0, at : at + 48] = block[48:96]
            mix_out[1, at : at + 48] = block[48:96]
            if y == 0:
                vec_out[0:16, 96 * b : 96 * b + 96] = block[96:112, 0:96].astype(F32)
    half = tok_own.shape[0]
    for at, tok in ((0, tok_own), (half, tok_far)):
        xhat, _ = normalize(tok[...].astype(F32))
        low = (xhat * vec_out[0:1, :] + vec_out[1:2, :]).astype(BF)
        n1[at : at + half, :] = low
        n1_out[:, at : at + half] = low.astype(F32).T.astype(BF)
    mix_out[:, 0 : 2 * QB] = jnp.zeros((2, 2 * QB, 384), BF)
    bias[...] = jnp.zeros_like(bias)
    for j in range(2):
        for k in range(2):
            row = vec_out[4 + j : 5 + j, 384 * k : 384 * k + 384]
            bias[j : j + 1, 192 * k : 192 * k + 192] = jnp.where(first, lanes(row, 0), lanes(row, 1))
    for n in range(4):
        for k in range(2):
            row = vec_out[8 + n : 9 + n, 384 * k : 384 * k + 384]
            eb_out[n, 0:1, 192 * k : 192 * k + 192] = jnp.where(first, lanes(row, 0), lanes(row, 1))
    for j in range(3):
        x3_out[j] = (dot_nn(n1[...], t3_out[j]) + bias[j : j + 1, :]).astype(BF)


def head_masks():
    lane = lax.broadcasted_iota(jnp.int32, (1, 2 * HD), 1)
    return [lane < HD, lane >= HD]


def soft(keys, query, live, width):
    raw = dot_nt(keys, query) * (1.0 / math.sqrt(HD))
    raw = jnp.where(jnp.concatenate([live] * (width // 128), axis=1) > 0, raw, -1e30)
    expo = jnp.exp(raw - jnp.max(raw, axis=0, keepdims=True))
    return expo * (1.0 / jnp.sum(expo, axis=0, keepdims=True))


QB = 256


def attn_kernel(ids, x3, live, _, out):
    q, v, k = x3[0], x3[1], x3[2]
    c = ids[0]
    lv = live[...]
    vt = v.astype(F32).T.astype(BF)
    row = lax.broadcasted_iota(jnp.int32, (2 * HD, 1), 0)
    masks = head_masks()
    for s, core in ((0, c), (QB, 1 - c)):
        total = jnp.zeros((2 * HD, QB), F32)
        for h in range(2):
            qh = jnp.where(masks[h], q[s : s + QB], jnp.zeros((), BF))
            low = soft(k, qh, lv, QB).astype(BF)
            vh = jnp.where(row < HD if h == 0 else row >= HD, vt, jnp.zeros((), BF))
            total += dot_nn(vh, low)
        mixed = total.T.astype(BF)
        at = pl.ds(pl.multiple_of(core * QB, QB), QB)
        out[0, at, :] = mixed
        out[1, at, :] = mixed


def attn_back_kernel(x3, gm_ref, live, d3):
    q, v, k = x3[0], x3[1], x3[2]
    slots = q.shape[0]
    lv = live[...]
    kt = k.astype(F32).T.astype(BF)
    row = lax.broadcasted_iota(jnp.int32, (2 * HD, 1), 0)
    masks = head_masks()
    scale = 1.0 / math.sqrt(HD)
    zero = jnp.zeros((), BF)
    dk = jnp.zeros((slots, 2 * HD), F32)
    dv = jnp.zeros((slots, 2 * HD), F32)
    for s in range(0, slots, QB):
        gm = gm_ref[s : s + QB, :]
        dqt = jnp.zeros((2 * HD, QB), F32)
        for h in range(2):
            qh = jnp.where(masks[h], q[s : s + QB], zero)
            gh = jnp.where(masks[h], gm, zero)
            probs = soft(k, qh, lv, QB)
            gp = dot_nt(v, gh)
            delta = jnp.sum(probs * gp, axis=0, keepdims=True)
            ds = (probs * (gp - delta)).astype(BF)
            kh = jnp.where(row < HD if h == 0 else row >= HD, kt, zero)
            dqt += dot_nn(kh, ds)
            dk += dot_nn(ds, qh)
            dv += dot_nn(probs.astype(BF), gh)
        d3[0, s : s + QB, :] = (dqt.T * scale).astype(BF)
    d3[1] = dv.astype(BF)
    d3[2] = (dk * scale).astype(BF)


def mid_kernel(ids, tok_own, tok_far, traded, vec, att_own, att_far, n2_out, n2t_out, m_out, mixed_t, mixed_out):
    c = ids[0]
    half = tok_own.shape[0]
    for p in range(2):
        for y in range(2):
            at = 192 * (2 * y + p)
            for b in range(8):
                block = traded[p, 2 * half + 48 * (y * 8 + b) : 2 * half + 48 * (y * 8 + b) + 48]
                m_out[96 * b : 96 * b + 48, at : at + 192] = block[:, :192]
                m_out[96 * b + 48 : 96 * b + 96, at : at + 192] = block[:, 192:]
            for to, core in ((0, c), (half, 1 - c)):
                rows = traded[p, pl.ds(pl.multiple_of(core * half, half), half), :]
                mixed_out[to : to + half, at : at + 192] = lanes(rows, y)
    for to, tok, out in ((0, tok_own, att_own), (half, tok_far, att_far)):
        att = tok[...].astype(F32) + (dot_nn(mixed_out[to : to + half, :], m_out[...]) + vec[6:7, :])
        out[...] = att
        xhat, _ = normalize(att)
        n2 = (xhat * vec[2:3, :] + vec[3:4, :]).astype(BF)
        n2_out[to : to + half, :] = n2
        n2t_out[:, to : to + half] = n2.astype(F32).T.astype(BF)
        mixed_t[:, to : to + half] = mixed_out[to : to + half, :].astype(F32).T.astype(BF)


def ffn_kernel(ids, n2, n2t, br_own, br_far, ea, ea_far, eb, eb_far, el, el_far, bias,
               part_own, part_far, gn2, d_e, d_s, d_bias, br, e_ref, s_ref):
    my, mx, mz = ids[2], ids[3], ids[4]
    n = pl.program_id(0)

    def layer(z):
        return ((z & 1) ^ (mz & 1)) * 2 + ((z >> 1) ^ (mz >> 1))

    def x_first(at, y, x, z):
        i, rows = (x ^ mx) * 4 + layer(z), pl.ds(at, 96 if at == 0 else 48)
        return jnp.where(y == my, ea[i, rows, :], ea_far[i, rows, :])

    def y_first(at, y, x, z):
        i, rows = (y ^ my) * 4 + layer(z), pl.ds(at, 96 if at == 0 else 48)
        return jnp.where(x == mx, eb[i, rows, :], eb_far[i, rows, :])

    def z_last(y, x, z):
        i = (((z >> 1) ^ (mz >> 1)) * 2 + (y ^ my)) * 2 + (x ^ mx)
        return jnp.where((z & 1) == (mz & 1), el[i], el_far[i])

    for b in range(8):
        e_ref[96 * b : 96 * b + 96, :384] = x_first(0, n, b & 1, b >> 1)
        e_ref[96 * b : 96 * b + 96, 384:] = y_first(0, n, b & 1, b >> 1)
    for y in range(2):
        for k in range(2):
            for x in range(2):
                at = 384 * k + 192 * x
                s_ref[at : at + 48, 384 * y : 384 * y + 384] = x_first(96, y, x, 2 * n + k)
                s_ref[at + 48 : at + 96, 384 * y : 384 * y + 384] = y_first(96, y, x, 2 * n + k)
                s_ref[at + 96 : at + 192, 384 * y : 384 * y + 384] = z_last(y, x, 2 * n + k)
    half = br_own.shape[0]

    @pl.when(pl.program_id(0) == 0)
    def _():
        for out in (part_own, part_far, gn2):
            out[...] = jnp.zeros_like(out)
        br[0:half], br[half:] = br_own[...], br_far[...]

    e, s = e_ref[...], s_ref[...]
    pre = dot_nn(n2[...], e) + bias[0]
    grad_act = dot_nt(br[...], s)
    cdf = 0.5 * (1.0 + lax.erf(pre * math.sqrt(0.5)))
    act = (pre * cdf).astype(BF)
    slope = cdf + pre * (jnp.exp(-0.5 * pre * pre) * (1.0 / math.sqrt(2.0 * math.pi)))
    grad_pre = (grad_act * slope).astype(BF)
    y = dot_nn(act, s)
    part_own[...] += y[:half]
    part_far[...] += y[half:]
    gn2[...] += dot_nt(grad_pre, e)
    grad = dot_nn(act.astype(F32).T.astype(BF), br[...]).astype(BF)
    for y in range(2):
        d_s[y] = grad[:, 384 * y : 384 * y + 384].reshape(2, 2, 192, 384)
    grad = dot_nn(n2t[...], grad_pre).astype(BF)
    for p in range(2):
        d_e[0, :, p] = grad[:, 384 * p : 384 * p + 384].reshape(8, 96, 384)
    d_bias[0] = jnp.sum(grad_pre.astype(F32), axis=0, keepdims=True)


def mid_back_kernel(ids, gn_here, gn_there, att_own, att_far, br_own, br_far, mixed_t, m, vec, gatt, gm, dm, sums, low):
    first, c = ids[0] == 0, ids[0]
    half = att_own.shape[0]
    for to, att, br_ref in ((0, att_own, br_own), (half, att_far, br_far)):
        gn = gn_here[to : to + half, :] + gn_there[half - to : 2 * half - to, :]
        br = br_ref[...].astype(F32)
        xhat, spread = normalize(att[...])
        grad = br + norm_back(xhat, spread, vec[2:3, :], gn)
        low[to : to + half, :] = grad.astype(BF)
        if to == 0:
            gatt[...] = grad
            sums[0:1] = jnp.sum(gn * xhat, axis=0, keepdims=True)
            sums[1:2] = jnp.sum(gn, axis=0, keepdims=True)
            sums[2:3] = jnp.sum(grad.astype(BF).astype(F32), axis=0, keepdims=True)
            sums[3:4] = jnp.sum(br, axis=0, keepdims=True)
            sums[4:8] = jnp.zeros((4, sums.shape[1]), F32)
    for k in range(2):
        rows = m[pl.ds(pl.multiple_of(192 * (2 * k + c), 192), 192), :]
        gm[:, 192 * k : 192 * k + 192] = dot_nt(low[...], rows).astype(BF)
        both = low[:, 384 * k : 384 * k + 384]
        mine = jnp.where(first, lanes(both, 0), lanes(both, 1))
        weight = dot_nn(mixed_t[...], mine).astype(BF)
        for b in range(8):
            dm[8 * k + b, :, :192] = weight[96 * b : 96 * b + 48]
            dm[8 * k + b, :, 192:] = weight[96 * b + 48 : 96 * b + 96]


def triple_back_kernel(ids, n1_ref, d3, t3, d_qv, d_k, gn, sums):
    c = ids[0]
    j = pl.program_id(0)
    d = d3[0]
    half = gn.shape[1]
    weight = dot_nn(n1_ref[...], d).astype(BF)
    part = dot_nt(d, t3[0])
    sums[0] = jnp.sum(d.astype(F32), axis=0, keepdims=True)

    @pl.when(j == 0)
    def _():
        gn[c] = part[:half]
        gn[1 - c] = part[half:]

    @pl.when(j > 0)
    def _():
        gn[c] += part[:half]
        gn[1 - c] += part[half:]

    @pl.when(j < 2)
    def _():
        d_qv[0] = weight

    @pl.when(j == 2)
    def _():
        for b in range(8):
            for y in range(2):
                d_k[y, b, :, :192] = weight[96 * b : 96 * b + 48, 192 * y : 192 * y + 192]
                d_k[y, b, :, 192:] = weight[96 * b + 48 : 96 * b + 96, 192 * y : 192 * y + 192]


def first_back_kernel(ids, gn_both, tok, gatt, vec, sums2, sums1, d_bias, out, blocks, table):
    c = ids[0]
    gn = gn_both[0] + gn_both[1]
    xhat, spread = normalize(tok[...].astype(F32))
    out[...] = (gatt[...] + norm_back(xhat, spread, vec[0:1, :], gn)).astype(BF)
    table[12:16] = jnp.zeros((4, table.shape[1]), F32)
    table[0:1] = jnp.sum(gn * xhat, axis=0, keepdims=True)
    table[1:2] = jnp.sum(gn, axis=0, keepdims=True)
    table[2:4] = sums2[0:2]
    table[6:8] = sums2[2:4]
    for row, sums in [(4, sums1[0]), (5, sums1[1])] + [(8 + n, d_bias[n]) for n in range(4)]:
        for k in range(2):
            for p in range(2):
                at = 192 * (2 * k + p)
                table[row : row + 1, at : at + 192] = jnp.where(c == p, lanes(sums, k), 0.0)
    blocks[...] = jnp.zeros_like(blocks)
    for b in range(8):
        blocks[b, :, 0:96] = table[:, 96 * b : 96 * b + 96].astype(BF)


def halves(rows):
    return rows[:, :192], rows[:, 192:]


def fetch(refs, places, sems):
    copies = [pltpu.make_async_copy(ref, place, sems.at[i]) for i, (ref, place) in enumerate(zip(refs, places))]
    for copy in copies:
        copy.start()
    for copy in copies:
        copy.wait()


def adam_into(state, outs, rate, decay, at, grad):
    new = adamw(state[0][at], state[1][at], state[2][at], grad, rate, decay)
    for out, value in zip(outs, new):
        out[at] = value


def triple_units(t, total):
    a, b = halves(total[0:96])
    k = jnp.concatenate(halves(total[96:144]), axis=0)
    return a, b, k


def triple_give_kernel(ids, own, far, give):
    t = ids[1]
    total = own[...].astype(F32) + far[...].astype(F32)
    a, b, k = triple_units(t, total)
    give[0:96] = jnp.where(t == 1, a, jnp.where(t == 2, b, k))
    give[96:112] = jnp.zeros((16, 192), F32)
    give[96:112, 0:96] = total[192:208, 0:96]


def triple_end_kernel(ids, own, far, took, *refs):
    outs, state, sems = refs[9:21], refs[21:30], refs[30]
    fetch(refs[:9], state, sems)
    t = ids[1]
    total = own[...].astype(F32) + far[...].astype(F32)
    a, b, k = triple_units(t, total)
    units = (
        jnp.where(t == 1, b, jnp.where(t == 2, k, a)),
        took[0:96],
        jnp.where(t == 1, k, jnp.where(t == 2, a, b)),
    )
    every = slice(None)
    for i, unit in enumerate(units):
        adam_into(state[0:3], outs[0:4], RATES[0], DECAYS[0], (every, slice(192 * i, 192 * i + 192)), unit)
    for i, part in enumerate(halves(total[144:192])):
        adam_into(state[3:6], outs[4:8], RATES[1], DECAYS[1], (slice(48 * i, 48 * i + 48), every), part)
    adam_into(state[6:9], outs[8:12], RATES[4], DECAYS[4], (every, every), total[192:204, 0:96] + took[96:108, 0:96])


def forward_give_kernel(ids, own, far, give):
    first = ids[0] == 0
    total = own[...].astype(F32) + far[...].astype(F32)
    e = jnp.where(first, total[96:192], total[0:96])
    give[0:96], give[96:192] = halves(e)
    s0, s1 = halves(total[192:])
    give[192:384] = jnp.where(first, s1, s0)


def forward_end_kernel(ids, own, far, took, *refs):
    outs, state, sems = refs[6:14], refs[14:20], refs[20]
    fetch(refs[:6], state, sems)
    first, c = ids[0] == 0, ids[0]
    total = own[...].astype(F32) + far[...].astype(F32)
    e = halves(jnp.where(first, total[0:96], total[96:192]))
    s0, s1 = halves(total[192:])
    s = jnp.where(first, s0, s1)
    every = slice(None)
    for p in range(2):
        for j in range(2):
            grad = jnp.where(c == p, e[j], took[96 * j : 96 * j + 96])
            at = 384 * j + 192 * p
            adam_into(state[0:3], outs[0:4], RATES[2], DECAYS[2], (every, slice(at, at + 192)), grad)
        grad = jnp.where(c == p, s, took[192:384]).T
        adam_into(state[3:6], outs[4:8], RATES[3], DECAYS[3], (every, slice(192 * p, 192 * p + 192)), grad)


def by_core(c, own, far):
    return jnp.where(c == 0, jnp.stack([own, far]), jnp.stack([far, own]))


def per_device(
    cube_tokens, visible, live_counts, block_cotangent,
    triple_master, triple_first, triple_second,
    mixing_master, mixing_first, mixing_second,
    expand_master, expand_first, expand_second,
    shrink_master, shrink_first, shrink_second,
    vector_master, vector_first, vector_second,
):
    y, c, b = lax.axis_index("y"), lax.axis_index("core"), lax.axis_index("blk")
    bits = (y, b & 1, b >> 1 & 1, b >> 2)
    turn = b % 4
    unturn = (4 - turn) % 4
    region, feats = cube_tokens.shape[1:]
    slots = visible.shape[1]
    slot_axis = jnp.arange(slots, dtype=jnp.int32)

    t_id = 2 * y + c
    ids = jnp.stack([c, t_id, y, bits[1], b >> 1]).astype(jnp.int32)
    shrink_t = shrink_master.T
    took = swap(call(
        give_kernel, shape(480, 192, dtype=BF), "give", 1e10, 1e3, in_specs=[SM, VM, VM, VM], out_specs=VM,
    )(ids, triple_master, expand_master, shrink_t), dc=1)
    tvm, es, last = call(
        pack_kernel, (shape(208, 384, dtype=BF), shape(288, 384, dtype=BF), shape(96, 384, dtype=BF)), "pack", 1e10, 1e3,
        in_specs=[SM] + [VM] * 6, out_specs=(VM, VM, VM),
    )(ids, took, triple_master, mixing_master, expand_master, shrink_t, vector_master)

    t_far = swap(tvm, db=4)
    last_in = swap(last, db=1)

    visible, block_cotangent, tvm, es, last = tie(visible, block_cotangent, tvm, es, last)
    def turned(x):
        return lax.dynamic_slice_in_dim(jnp.concatenate([x, x]), turn, 4, 0)

    local = visible % region
    flat_index = turned(local + region * jnp.arange(4, dtype=jnp.int32)[:, None])
    picked = jnp.take(cube_tokens.reshape(-1, feats), flat_index.reshape(-1), axis=0).reshape(4, slots, feats)
    counts = jnp.broadcast_to(turned(live_counts)[:, :, None].astype(BF), (4, 16, feats))
    live_here = slot_axis[None, :] < live_counts
    masked = turned(jnp.where(live_here[:, :, None], block_cotangent, jnp.zeros((), BF)))
    packet = jnp.concatenate([picked, masked, counts], axis=1)

    def packets(*steps):
        return [lax.ppermute(packet[s], FINE, cube_pairs(s, False)) for s in steps]

    last = jnp.stack([last, last_in])
    last_in = swap(last, dy=1)
    t_far, packet, es, last_in = tie(t_far, packet, es, last_in)
    tvm = jnp.stack([tvm, t_far])
    t_far = swap(tvm, db=2)
    last = jnp.stack([last, last_in]).reshape(384, 384)
    es_far = swap(jnp.concatenate([es, last], axis=0), db=4)
    own = packets(0, 1)

    t_far, packet = tie(t_far, packet)
    tvm = jnp.stack([tvm, t_far]).reshape(4, 208, 384)
    qv, rest = tvm[:, :96], tvm[:, 96:]
    qv_x, rest_y = swap(qv, db=1), swap(rest, dy=1)

    qv_x, rest_y, own, packet = tie(qv_x, rest_y, own, packet)
    qv = jnp.stack([qv, qv_x]).reshape(8, 96, 384)
    rest = jnp.stack([rest, rest_y]).reshape(8, 112, 384)
    qv_far, rest_far = swap(qv, dy=1), swap(rest, db=1)
    es_far, last = tie(es_far, last)
    el = jnp.stack([last, es_far[288:]]).reshape(8, 96, 384)
    es = jnp.stack([es, es_far[:288]])
    es_far = swap(es, db=2)
    own = own + packets(2, 3)

    qv_far, rest_far, es_far, own = tie(qv_far, rest_far, es_far, own)
    es = jnp.stack([es, es_far]).reshape(4, 288, 384)
    ea, eb = es[:, :144], es[:, 144:]
    ea_in, eb_in = swap(ea, db=1), swap(eb, dy=1)
    el_far = swap(el, db=2)
    own = jnp.stack(own)
    far = swap(own, dc=1)

    rows = 4 * slots
    tok_own, tok_far = [p[:, :slots].reshape(rows, feats) for p in (own, far)]
    br_own, br_far = [p[:, slots : 2 * slots].reshape(rows, feats) for p in (own, far)]
    cnt = jnp.concatenate([own[:, 2 * slots, :1], far[:, 2 * slots, :1]]).astype(jnp.int32)
    live = (slot_axis[None, :] < cnt).reshape(2 * rows, 1)
    live_cols = jnp.broadcast_to(live.astype(F32), (2 * rows, 128))

    n1, x3, t3, mix, vec, e_bias = call(
        qkv_kernel,
        (shape(feats, 2 * rows, dtype=BF), shape(3, 2 * rows, 384, dtype=BF), shape(3, feats, 384, dtype=BF),
         shape(2, 2 * rows + feats, 384, dtype=BF), shape(16, feats), shape(4, 1, 384)),
        "qkv", 2 * 512 * 768 * 1152, 8e6,
        in_specs=[SM] + [VM] * 6, out_specs=(VM,) * 6, scratch_shapes=[pltpu.VMEM((8, 384), F32), pltpu.VMEM((2 * rows, feats), BF)],
    )(ids, tok_own, tok_far, qv, qv_far, rest, rest_far)
    x3, mix, ea_in, eb_in, el_far = tie(x3, mix, ea_in, eb_in, el_far)
    ea = jnp.stack([ea, ea_in]).reshape(8, 144, 384)
    eb = jnp.stack([eb, eb_in]).reshape(8, 144, 384)
    ea_far, eb_far = swap(ea, dy=1), swap(eb, db=1)

    pairs3 = pl.BlockSpec((3, 2 * rows, 128), lambda i: (0, 0, i))
    col = pl.BlockSpec((2 * rows, 128), lambda i: (0, i))
    same = pl.BlockSpec((2 * rows, 128), lambda i: (0, 0))
    traded = trade(call(
        attn_kernel, shape(2, 2 * rows + feats, 384, dtype=BF), "attention", 6e9, 2e6,
        grid=(3,), in_specs=[SM, pairs3, same, pl.BlockSpec(memory_space=pl.ANY)],
        out_specs=pl.BlockSpec((2, 2 * rows, 128), lambda i: (0, 0, i)), input_output_aliases={3: 0},
    )(ids, x3, live_cols, mix))
    att, att_far, n2, n2t, mix, mixed = call(
        mid_kernel,
        (shape(rows, feats), shape(rows, feats), shape(2 * rows, feats, dtype=BF), shape(feats, 2 * rows, dtype=BF),
         shape(feats, feats, dtype=BF), shape(feats, 2 * rows, dtype=BF)),
        "mixing", 3e9, 5e6, in_specs=[SM] + [VM] * 4, out_specs=(VM,) * 6,
        scratch_shapes=[pltpu.VMEM((2 * rows, feats), BF)],
    )(ids, tok_own, tok_far, traded, vec)

    whole = pl.BlockSpec((rows, feats), lambda i: (0, 0))

    gathered = [pl.BlockSpec((8, r, 384), lambda n: (0, 0, 0)) for r in (144, 144, 144, 144, 96, 96)]
    every = pl.BlockSpec((2 * rows, feats), lambda i: (0, 0))
    part_own, part_give, gn2, d_e, d_s, d_b = call(
        ffn_kernel,
        (shape(rows, feats),) * 2
        + (shape(2 * rows, feats), shape(2, 8, 2, 96, 384, dtype=BF), shape(2, 4, 2, 192, 384, dtype=BF), shape(2, 1, 768)),
        "feed_forward", 18e9, 20e6, 46,
        grid=(2,),
        in_specs=[SM, every, pl.BlockSpec((feats, 2 * rows), lambda n: (0, 0))] + [whole] * 2 + gathered
        + [pl.BlockSpec((1, 1, 768), lambda n: (n, 0, 0))],
        out_specs=(
            whole, whole, every,
            pl.BlockSpec((1, 8, 2, 96, 384), lambda n: (n, 0, 0, 0, 0)),
            pl.BlockSpec((2, 2, 2, 192, 384), lambda n: (0, n, 0, 0, 0)),
            pl.BlockSpec((1, 1, 768), lambda n: (n, 0, 0)),
        ),
        scratch_shapes=[pltpu.VMEM((2 * rows, feats), BF), pltpu.VMEM((feats, 768), BF), pltpu.VMEM((768, feats), BF)],
    )(ids, n2, n2t, br_own, br_far, ea, ea_far, eb, eb_far, el, el_far, e_bias.reshape(2, 1, 768))

    z0, z1 = bits[2], bits[3]
    gn2_far = swap(gn2, dc=1)
    d_e = d_e.reshape(2, 4, 2, 192, 384)
    e_in = swap(pick(d_e, 1 - bits[1], 2), db=1)
    s_in = swap(pick(d_s, 1 - y, 0), dy=1)

    gatt, gm, dm, sums2 = call(
        mid_back_kernel,
        (shape(rows, feats), shape(2 * rows, 384, dtype=BF), shape(16, 48, 384, dtype=BF), shape(8, feats)),
        "mixing_back", 6e9, 8e6, in_specs=[SM] + [VM] * 9, out_specs=(VM,) * 4,
        scratch_shapes=[pltpu.VMEM((2 * rows, feats), BF)],
    )(ids, gn2, gn2_far, att, att_far, br_own, br_far, mixed, mix, vec)
    d3 = call(
        attn_back_kernel, shape(3, 2 * rows, 384, dtype=BF), "attention_back", 9e9, 5e6,
        grid=(3,), in_specs=[pairs3, col, same], out_specs=pairs3,
    )(x3, gm, live_cols)

    third = pl.BlockSpec((1, 2 * rows, 384), lambda j: (j, 0, 0))
    d_qv, d_k, gn1, sums1 = call(
        triple_back_kernel,
        (shape(2, feats, 384, dtype=BF), shape(2, 8, 48, 384, dtype=BF), shape(2, rows, feats), shape(3, 1, 384)),
        "triple_back", 5e9, 5e6,
        grid=(3,),
        in_specs=[SM, pl.BlockSpec((feats, 2 * rows), lambda j: (0, 0)), third, pl.BlockSpec((1, feats, 384), lambda j: (j, 0, 0))],
        out_specs=(
            pl.BlockSpec((1, feats, 384), lambda j: (jnp.minimum(j, 1), 0, 0)),
            pl.BlockSpec((2, 8, 48, 384), lambda j: (0, 0, 0, 0)),
            pl.BlockSpec((2, rows, feats), lambda j: (0, 0, 0)),
            pl.BlockSpec((1, 1, 384), lambda j: (j, 0, 0)),
        ),
    )(ids, n1, d3, t3)

    gn1 = trade(gn1)
    grad_tok, blocks = call(
        first_back_kernel, (shape(rows, feats, dtype=BF), shape(8, 16, 384, dtype=BF)), "first_back", 1e9, 1e6,
        in_specs=[SM] + [VM] * 7, out_specs=(VM, VM), scratch_shapes=[pltpu.VMEM((16, feats), F32)],
    )(ids, gn1, tok_own, gatt, vec, sums2, sums1, d_b.reshape(4, 1, 384))

    blocks = jnp.broadcast_to(blocks, (2, 8, 16, 384))
    d_qv = d_qv.reshape(2, 4, 2, 96, 384)
    d_km = jnp.concatenate([d_k, dm.reshape(2, 8, 48, 384), blocks], axis=2).reshape(2, 4, 2, 112, 384)
    qv_in = swap(pick(d_qv, 1 - bits[1], 2), db=1)
    km_in = swap(pick(d_km, 1 - y, 0), dy=1)

    e_in, s_in, grad_tok, part_give = tie(e_in, s_in, grad_tok, part_give)
    d_e = add_low(pick(d_e, bits[1], 2), e_in)
    d_s = add_low(pick(d_s, y, 0), s_in)
    e_in = swap(pick(d_e, 1 - y, 0), dy=1)
    s_in = swap(pick(d_s, 1 - bits[1], 1), db=1)

    part_far = swap(part_give, dc=1)
    result = att + (part_own + part_far + vec[7])
    result = jnp.where(live[:rows], result, 0.0).astype(BF).reshape(4, slots, feats)
    packet = jnp.concatenate([result, grad_tok.reshape(4, slots, feats)], axis=1)

    def go_back(step, *after):
        part = tie(packet[step], *after)[0]
        return lax.ppermute(part, FINE, cube_pairs(step, True))

    back = [go_back(0)]
    back += [go_back(1, back[0])]

    qv_in, km_in, back, packet = tie(qv_in, km_in, back, packet)
    d_qv = add_low(pick(d_qv, bits[1], 2), qv_in)
    d_km = add_low(pick(d_km, y, 0), km_in)
    qv_in = swap(pick(d_qv, 1 - y, 0), dy=1)
    km_in = swap(pick(d_km, 1 - bits[1], 1), db=1)
    back += [go_back(2)]

    e_in, s_in, back, packet = tie(e_in, s_in, back, packet)
    d_es = jnp.concatenate(
        [add_low(pick(d_e, y, 0), e_in), add_low(pick(d_s, bits[1], 1), s_in)], axis=1
    ).reshape(2, 2, 384, 384)
    es_in = swap(pick(d_es, 1 - z0, 1), db=2)
    back += [go_back(3)]

    qv_in, km_in = tie(qv_in, km_in)
    d_t = jnp.concatenate(
        [add_low(pick(d_qv, y, 0), qv_in), add_low(pick(d_km, bits[1], 1), km_in)], axis=1
    ).reshape(2, 2, 208, 384)
    t_in = swap(pick(d_t, 1 - z0, 1), db=2)

    es_in, qv_in = tie(es_in, qv_in)
    d_es = add_low(pick(d_es, z0, 1), es_in)
    es_in = swap(pick(d_es, 1 - z1, 0), db=4)
    d_t = add_low(pick(d_t, z0, 1), t_in)
    t_in = swap(pick(d_t, 1 - z1, 0), db=4)

    t_in, back = tie(t_in, back)
    back = jnp.stack(back)
    back = lax.dynamic_slice_in_dim(jnp.concatenate([back, back]), unturn, 4, 0)
    block_output = back[:, :slots]
    spread = (jnp.arange(region, dtype=jnp.int32)[None, :, None] == local[:, None, :]).astype(BF)
    token_grads = jnp.einsum("grs,gsf->grf", spread, back[:, slots:], preferred_element_type=F32).astype(BF)

    def whole_of(a):
        return pl.BlockSpec(a.shape, lambda i: (0,) * len(a.shape))

    def update(kernel, name, given, state, copies):
        outs = tuple(shape(*a.shape, dtype=d) for a in copies for d in (F32, F32, F32, BF))
        return call(
            kernel, outs, name, 1e8, 4e6, grid=(1,),
            in_specs=[SM if a is ids else whole_of(a) for a in given] + [pl.BlockSpec(memory_space=pltpu.HBM)] * len(state),
            out_specs=tuple(whole_of(o) for o in outs),
            scratch_shapes=[pltpu.VMEM(a.shape, F32) for a in state] + [pltpu.SemaphoreType.DMA((len(state),))],
        )(*given, *state)

    d_t = pick(d_t, z1, 0)
    took = swap(call(
        triple_give_kernel, shape(112, 192), "triple_give", 1e6, 1e6, in_specs=[SM, VM, VM], out_specs=VM,
    )(ids, d_t, t_in), dc=1)
    t_state = (triple_master, triple_first, triple_second, mixing_master, mixing_first, mixing_second,
               vector_master, vector_first, vector_second)
    t_new = update(triple_end_kernel, "triple_update", (ids, d_t, t_in, took), t_state, (triple_master, mixing_master, vector_master))
    es_in, t_new, token_grads, block_output = tie(es_in, t_new, token_grads, block_output)
    d_es = pick(d_es, z1, 0)
    took = swap(call(
        forward_give_kernel, shape(384, 192), "expand_shrink_give", 1e6, 1e6, in_specs=[SM, VM, VM], out_specs=VM,
    )(ids, d_es, es_in), dc=1)
    es_state = (expand_master, expand_first, expand_second, shrink_t, shrink_first.T, shrink_second.T)
    es_new = update(forward_end_kernel, "expand_shrink_update", (ids, d_es, es_in, took), es_state, (expand_master, shrink_t))
    return (block_output, token_grads, *t_new[:8], *es_new[:4], *(o.T for o in es_new[4:]), *t_new[8:])


def layer_norm(rows, gain, shift):
    center = rows - jnp.mean(rows, axis=-1, keepdims=True)
    spread = lax.rsqrt(jnp.mean(center * center, axis=-1, keepdims=True) + 1e-06)
    return center * spread * gain + shift


def outer_sum(left, right):
    return lax.dot_general(
        left, right, (((0,), (0,)), ((), ())), preferred_element_type=jnp.float32
    )


def back_product(grads, weight):
    return lax.dot_general(
        grads, weight, (((1,), (1,)), ((), ())), preferred_element_type=jnp.float32
    )


def masked_scores(queries, key_all, live_all):
    raw = jnp.einsum("gshe,gthe->ghst", queries, key_all, preferred_element_type=jnp.float32) * (
        1.0 / math.sqrt(HD)
    )
    return jnp.where(live_all[:, None, None, :] > 0, raw, -1e30)


def cycle_section(triple_grad, mixing_grad, expand_grad, shrink_grad, vector_grad):
    summed = (
        lax.psum_scatter(triple_grad, "blk", scatter_dimension=0, tiled=True),
        lax.psum_scatter(mixing_grad, "blk", scatter_dimension=0, tiled=True),
        lax.psum_scatter(expand_grad, "blk", scatter_dimension=0, tiled=True),
        lax.psum_scatter(shrink_grad, "blk", scatter_dimension=0, tiled=True),
        lax.psum_scatter(vector_grad, "blk", scatter_dimension=1, tiled=True),
    )
    return (summed[0], summed[1], summed[2], summed[3], summed[4])


def group_section(triple_grad, mixing_grad, expand_grad, shrink_grad, vector_grad):
    summed = (
        lax.psum_scatter(triple_grad, "batch", scatter_dimension=1, tiled=True),
        lax.psum_scatter(mixing_grad, "batch", scatter_dimension=1, tiled=True),
        lax.psum_scatter(expand_grad, "batch", scatter_dimension=1, tiled=True),
        lax.psum_scatter(shrink_grad, "batch", scatter_dimension=1, tiled=True),
    )
    vector_sum = lax.psum(vector_grad, "batch")
    return (summed[0], summed[1], summed[2], summed[3], vector_sum)


def per_device_any(
    cube_tokens,
    visible,
    live_counts,
    block_cotangent,
    triple_master,
    triple_first,
    triple_second,
    mixing_master,
    mixing_first,
    mixing_second,
    expand_master,
    expand_first,
    expand_second,
    shrink_master,
    shrink_first,
    shrink_second,
    vector_master,
    vector_first,
    vector_second,
):
    low_copies = (
        lax.all_gather(triple_master.astype(jnp.bfloat16), "blk", axis=0, tiled=True),
        lax.all_gather(mixing_master.astype(jnp.bfloat16), "blk", axis=0, tiled=True),
        lax.all_gather(expand_master.astype(jnp.bfloat16), "blk", axis=0, tiled=True),
        lax.all_gather(shrink_master.astype(jnp.bfloat16), "blk", axis=0, tiled=True),
        lax.all_gather(vector_master.astype(jnp.bfloat16), "blk", axis=1, tiled=True),
    )
    triple_w, mixing_w, expand_w, shrink_w = (
        lax.all_gather(low_copies[0], "batch", axis=1, tiled=True),
        lax.all_gather(low_copies[1], "batch", axis=1, tiled=True),
        lax.all_gather(low_copies[2], "batch", axis=1, tiled=True),
        lax.all_gather(low_copies[3], "batch", axis=1, tiled=True),
    )
    vector_w = low_copies[4].astype(jnp.float32)
    groups, slot_count = visible.shape
    region = cube_tokens.shape[1]
    features = cube_tokens.shape[2]
    row_count = groups * slot_count
    head_count = features // HD
    local_index = visible % region
    tokens = jnp.take_along_axis(cube_tokens, local_index[:, :, None], axis=1).astype(jnp.float32)
    flat_tokens = tokens.reshape(row_count, features)
    live_mask = jnp.arange(slot_count, dtype=jnp.int32)[None, :] < live_counts
    live_rows = live_mask.reshape(row_count, 1)
    normed1 = layer_norm(flat_tokens, vector_w[0], vector_w[1]).astype(jnp.bfloat16)
    zero_bias = jnp.zeros((features,), jnp.float32)
    triple_bias = jnp.concatenate([vector_w[4], zero_bias, vector_w[5]])
    triple = (jnp.dot(normed1, triple_w, preferred_element_type=jnp.float32) + triple_bias).astype(
        jnp.bfloat16
    )
    triple = triple.reshape(groups, slot_count, 3 * features)
    query_flat = triple[:, :, :features]
    queries = query_flat.reshape(groups, slot_count, head_count, HD)
    key_rows = triple[:, :, features : 2 * features]
    value_rows = triple[:, :, 2 * features :]
    key_all, value_all, live_all = (
        lax.all_gather(key_rows, "blk", axis=1, tiled=True),
        lax.all_gather(value_rows, "blk", axis=1, tiled=True),
        lax.all_gather(live_mask.astype(jnp.bfloat16), "blk", axis=1, tiled=True),
    )
    key_all = key_all.reshape(groups, -1, head_count, HD)
    value_all = value_all.reshape(groups, -1, head_count, HD)
    scores = masked_scores(queries, key_all, live_all)
    peak = jnp.max(scores, axis=-1, keepdims=True)
    expo = jnp.exp(scores - peak)
    total = jnp.sum(expo, axis=-1, keepdims=True)
    prob_low = (expo / total).astype(jnp.bfloat16)
    mixed = jnp.einsum("ghst,gthe->gshe", prob_low, value_all, preferred_element_type=jnp.float32)
    mixed = mixed.astype(jnp.bfloat16).reshape(row_count, features)
    attended = flat_tokens + (
        jnp.dot(mixed, mixing_w, preferred_element_type=jnp.float32) + vector_w[6]
    )
    normed2 = layer_norm(attended, vector_w[2], vector_w[3]).astype(jnp.bfloat16)
    preact = jnp.dot(normed2, expand_w, preferred_element_type=jnp.float32) + vector_w[8:].reshape(
        -1
    )
    activation = jax.nn.gelu(preact, approximate=False).astype(jnp.bfloat16)
    result = attended + (
        jnp.dot(activation, shrink_w, preferred_element_type=jnp.float32) + vector_w[7]
    )
    result = jnp.where(live_rows, result, 0.0)
    block_output = result.astype(jnp.bfloat16).reshape(groups, slot_count, features)
    grad_out = jnp.where(
        live_rows, block_cotangent.reshape(row_count, features).astype(jnp.float32), 0.0
    )
    branch_low = grad_out.astype(jnp.bfloat16)
    shrink_grad = outer_sum(activation, branch_low)
    shrink_bias_grad = jnp.sum(branch_low.astype(jnp.float32), axis=0)
    grad_act = back_product(branch_low, shrink_w)
    gelu_value, gelu_back = jax.vjp(partial(jax.nn.gelu, approximate=False), preact)
    grad_pre = gelu_back(grad_act)[0].astype(jnp.bfloat16)
    expand_grad = outer_sum(normed2, grad_pre)
    expand_bias_grad = jnp.sum(grad_pre.astype(jnp.float32), axis=0)
    grad_normed2 = back_product(grad_pre, expand_w)
    norm2_value, norm2_back = jax.vjp(layer_norm, attended, vector_w[2], vector_w[3])
    grad_through2, gain2_grad, shift2_grad = norm2_back(grad_normed2)
    grad_attended = grad_out + grad_through2
    mix_low = grad_attended.astype(jnp.bfloat16)
    mixing_grad = outer_sum(mixed, mix_low)
    mixing_bias_grad = jnp.sum(mix_low.astype(jnp.float32), axis=0)
    grad_mixed_flat = (
        back_product(mix_low, mixing_w).astype(jnp.bfloat16).reshape(groups, slot_count, features)
    )
    grad_mixed = grad_mixed_flat.reshape(groups, slot_count, head_count, HD)
    scores = masked_scores(queries, key_all, live_all)
    probs = jnp.exp(scores - peak) / total
    prob_low = probs.astype(jnp.bfloat16)
    grad_probs = jnp.einsum(
        "gshe,gthe->ghst", grad_mixed, value_all, preferred_element_type=jnp.float32
    )
    delta = jnp.sum(probs * grad_probs, axis=-1, keepdims=True)
    grad_scores = (probs * (grad_probs - delta)).astype(jnp.bfloat16)
    score_scale = 1.0 / math.sqrt(HD)
    grad_queries = (
        jnp.einsum("ghst,gthe->gshe", grad_scores, key_all, preferred_element_type=jnp.float32)
        * score_scale
    )
    term_keys = (
        jnp.einsum("ghst,gshe->gthe", grad_scores, queries, preferred_element_type=jnp.float32)
        * score_scale
    )
    term_values = jnp.einsum(
        "ghst,gshe->gthe", prob_low, grad_mixed, preferred_element_type=jnp.float32
    )
    grad_keys, grad_values = (
        lax.psum_scatter(
            term_keys.reshape(groups, -1, features), "blk", scatter_dimension=1, tiled=True
        ),
        lax.psum_scatter(
            term_values.reshape(groups, -1, features), "blk", scatter_dimension=1, tiled=True
        ),
    )
    grad_triple = jnp.concatenate(
        [
            grad_queries.reshape(row_count, features),
            grad_keys.reshape(row_count, features),
            grad_values.reshape(row_count, features),
        ],
        axis=1,
    ).astype(jnp.bfloat16)
    triple_grad = outer_sum(normed1, grad_triple)
    triple_sums = jnp.sum(grad_triple.astype(jnp.float32), axis=0)
    grad_normed1 = back_product(grad_triple, triple_w)
    norm1_value, norm1_back = jax.vjp(layer_norm, flat_tokens, vector_w[0], vector_w[1])
    grad_through1, gain1_grad, shift1_grad = norm1_back(grad_normed1)
    grad_tokens = (grad_attended + grad_through1).reshape(groups, slot_count, features)
    cube_rows = jnp.arange(groups, dtype=jnp.int32)[:, None]
    token_grads = (
        jnp.zeros(cube_tokens.shape, jnp.float32)
        .at[cube_rows, local_index]
        .add(grad_tokens)
        .astype(jnp.bfloat16)
    )
    leading_rows = jnp.stack(
        [
            gain1_grad,
            shift1_grad,
            gain2_grad,
            shift2_grad,
            triple_sums[:features],
            triple_sums[2 * features :],
            mixing_bias_grad,
            shrink_bias_grad,
        ]
    )
    vector_grad = jnp.concatenate([leading_rows, expand_bias_grad.reshape(-1, features)], axis=0)
    reduced = group_section(triple_grad, mixing_grad, expand_grad, shrink_grad, vector_grad)
    reduced = cycle_section(reduced[0], reduced[1], reduced[2], reduced[3], reduced[4])
    masters = (triple_master, mixing_master, expand_master, shrink_master, vector_master)
    firsts = (triple_first, mixing_first, expand_first, shrink_first, vector_first)
    seconds = (triple_second, mixing_second, expand_second, shrink_second, vector_second)
    outputs = [block_output, token_grads]
    for master, first, second, grad, rate, decay in zip(
        masters, firsts, seconds, reduced, RATES, DECAYS
    ):
        outputs.extend(adamw(master, first, second, grad, rate, decay))
    return tuple(outputs)


def solution(mesh):
    groups, blocks = mesh.shape["batch"], mesh.shape["blk"]
    if (groups, blocks) == (4, 8):
        mesh = Mesh(mesh.devices.reshape(2, 2, 8), FINE)
        batch, body = ("y", "core"), per_device
    else:
        batch, body = "batch", per_device_any
    rows = P(batch, "blk", None)
    part = P("blk", batch)
    table = P(None, "blk")
    in_specs = (rows, P(batch, "blk"), P(batch, "blk"), rows) + (part,) * 12 + (table,) * 3
    out_specs = (rows, rows) + (part,) * 16 + (table,) * 4
    return jax.shard_map(body, mesh=mesh, in_specs=in_specs, out_specs=out_specs, check_vma=False)
```

```python
from functools import partial
import math

import jax
import jax.numpy as jnp
from jax import lax
from jax.experimental import pallas as pl
from jax.experimental.pallas import tpu as pltpu
from jax.sharding import Mesh, PartitionSpec as P

HD = 64
STEP = 10
BF = jnp.bfloat16
F32 = jnp.float32

RATES = (0.04, 0.3, 0.04, 0.02, 0.25)
DECAYS = (0.05, 0.05, 0.05, 0.05, 0.0)


def adamw(master, first, second, grad, rate, decay):
    first_new = 0.9 * first + 0.1 * grad
    second_new = 0.999 * second + 0.001 * grad * grad
    corrected = first_new / (1.0 - 0.9**STEP) / (jnp.sqrt(second_new / (1.0 - 0.999**STEP)) + 1e-08)
    master_new = master - rate * (corrected + decay * master)
    return (first_new, second_new, master_new, master_new.astype(BF))


FINE = ("y", "core", "blk")


def place(y, c, b):
    return (y * 2 + c) * 8 + b


def swap(x, dy=0, dc=0, db=0):
    pairs = [
        (place(y, c, b), place(y ^ dy, c ^ dc, b ^ db))
        for y in range(2)
        for c in range(2)
        for b in range(8)
    ]
    return lax.ppermute(x, FINE, pairs)


def trade(x):
    return lax.all_to_all(x, "core", 0, 0, tiled=True)


def cube_pairs(step, back):
    pairs = []
    for y in range(2):
        for c in range(2):
            for b in range(8):
                r, q = b // 4, b % 4
                far = place(y, r, 4 * c + (q + step) % 4)
                near = place(y, c, b)
                pairs.append((far, near) if back else (near, far))
    return pairs


def pick(x, index, axis):
    return lax.dynamic_index_in_dim(x, index, axis, keepdims=False)


def add_low(a, b):
    return (a.astype(F32) + b.astype(F32)).astype(BF)


def tie(*parts):
    return lax.optimization_barrier(parts)


def dot_nn(a, b):
    return jnp.dot(a, b, preferred_element_type=F32)


def dot_nt(a, b):
    return lax.dot_general(a, b, (((1,), (1,)), ((), ())), preferred_element_type=F32)


def dot_tn(a, b):
    return lax.dot_general(a, b, (((0,), (0,)), ((), ())), preferred_element_type=F32)


def call(kernel, outs, name, flops=0, moved=0, vmem=16, **kw):
    return pl.pallas_call(
        kernel,
        out_shape=outs,
        name=name,
        cost_estimate=pl.CostEstimate(flops=int(flops), bytes_accessed=int(moved), transcendentals=0),
        compiler_params=pltpu.CompilerParams(vmem_limit_bytes=vmem * 2**20),
        **kw,
    )


def shape(*dims, dtype=F32):
    return jax.ShapeDtypeStruct(dims, dtype)


VM = pl.BlockSpec(memory_space=pltpu.VMEM)
SM = pl.BlockSpec(memory_space=pltpu.SMEM)


def normalize(rows):
    center = rows - jnp.mean(rows, axis=-1, keepdims=True)
    spread = lax.rsqrt(jnp.mean(center * center, axis=-1, keepdims=True) + 1e-06)
    return center * spread, spread


def norm_back(xhat, spread, gain, grad):
    q = grad * gain
    mean_q = jnp.mean(q, axis=-1, keepdims=True)
    mean_x = jnp.mean(q * xhat, axis=-1, keepdims=True)
    return spread * (q - mean_q - xhat * mean_x)


def lanes(ref_rows, unit):
    return ref_rows[:, 192 * unit : 192 * unit + 192]


def give_kernel(ids, triple, expand, shrink_t, give):
    first = ids[0] == 0
    e = expand[...].astype(BF)
    give[0:96] = jnp.where(first, lanes(e, 1), lanes(e, 0))
    give[96:192] = jnp.where(first, lanes(e, 3), lanes(e, 2))
    s = shrink_t[...].T.astype(BF)
    give[192:384] = jnp.where(first, s[192:], s[:192])
    give[384:480] = lanes(triple, 1).astype(BF)


def pack_kernel(ids, took, triple, mixing, expand, shrink_t, vector, tvm, es, last):
    first, t = ids[0] == 0, ids[1]
    e = expand[...].astype(BF)
    for j in range(2):
        mine = jnp.where(first, lanes(e, 2 * j), lanes(e, 2 * j + 1))
        far = took[96 * j : 96 * j + 96]
        es[0:96, 192 * j : 192 * j + 192] = jnp.where(first, mine, far)
        es[144:240, 192 * j : 192 * j + 192] = jnp.where(first, far, mine)
    s = shrink_t[...].T.astype(BF)
    mine, far = jnp.where(first, s[:192], s[192:]), took[192:384]
    left, right = jnp.where(first, mine, far), jnp.where(first, far, mine)
    for out, at, rows in ((es, 96, slice(0, 48)), (es, 240, slice(48, 96)), (last, 0, slice(96, 192))):
        to = slice(at, at + rows.stop - rows.start)
        out[to, :192] = left[rows]
        out[to, 192:] = right[rows]
    low = triple[...].astype(BF)
    t0, t2, far = lanes(low, 0), lanes(low, 2), took[384:480]
    tvm[0:96, :192] = jnp.where(t == 1, far, jnp.where(t == 2, t2, t0))
    tvm[0:96, 192:] = jnp.where(t == 1, t0, jnp.where(t == 2, far, t2))
    key = jnp.where(t == 1, t2, jnp.where(t == 2, t0, far))
    tvm[96:144, :192] = key[:48]
    tvm[96:144, 192:] = key[48:]
    m = mixing[...].astype(BF)
    tvm[144:192, :192] = m[:48]
    tvm[144:192, 192:] = m[48:]
    tvm[192:208] = jnp.zeros((16, 384), BF)
    tvm[192:204, 0:96] = vector[...].astype(BF)


def qkv_kernel(ids, tok_own, tok_far, qv_own, qv_far, rest_own, rest_far,
               n1_out, x3_out, t3_out, mix_out, vec_out, eb_out, bias, n1):
    first, my, mx, mz = ids[0] == 0, ids[2], ids[3], ids[4]
    for b in range(8):
        iz = ((b >> 1 & 1) ^ (mz & 1)) * 2 + ((b >> 2) ^ (mz >> 1))
        here = (b & 1) ^ mx
        for y in range(2):
            there = y ^ my
            iq, ir = here * 4 + iz, there * 4 + iz
            t3_out[y, 96 * b : 96 * b + 96, :] = jnp.where(there == 0, qv_own[iq], qv_far[iq])
            block = jnp.where(here == 0, rest_own[ir], rest_far[ir])
            t3_out[2, 96 * b : 96 * b + 48, 192 * y : 192 * y + 192] = block[0:48, :192]
            t3_out[2, 96 * b + 48 : 96 * b + 96, 192 * y : 192 * y + 192] = block[0:48, 192:]
            at = 2 * QB + 48 * (y * 8 + b)
            mix_out[0, at : at + 48] = block[48:96]
            mix_out[1, at : at + 48] = block[48:96]
            if y == 0:
                vec_out[0:16, 96 * b : 96 * b + 96] = block[96:112, 0:96].astype(F32)
    half = tok_own.shape[0]
    for at, tok in ((0, tok_own), (half, tok_far)):
        xhat, _ = normalize(tok[...].astype(F32))
        low = (xhat * vec_out[0:1, :] + vec_out[1:2, :]).astype(BF)
        n1[at : at + half, :] = low
        n1_out[:, at : at + half] = low.astype(F32).T.astype(BF)
    mix_out[:, 0 : 2 * QB] = jnp.zeros((2, 2 * QB, 384), BF)
    bias[...] = jnp.zeros_like(bias)
    for j in range(2):
        for k in range(2):
            row = vec_out[4 + j : 5 + j, 384 * k : 384 * k + 384]
            bias[j : j + 1, 192 * k : 192 * k + 192] = jnp.where(first, lanes(row, 0), lanes(row, 1))
    for n in range(4):
        for k in range(2):
            row = vec_out[8 + n : 9 + n, 384 * k : 384 * k + 384]
            eb_out[n, 0:1, 192 * k : 192 * k + 192] = jnp.where(first, lanes(row, 0), lanes(row, 1))
    for j in range(3):
        x3_out[j] = (dot_nn(n1[...], t3_out[j]) + bias[j : j + 1, :]).astype(BF)


def head_masks():
    lane = lax.broadcasted_iota(jnp.int32, (1, 2 * HD), 1)
    return [lane < HD, lane >= HD]


def soft(keys, query, live, width):
    raw = dot_nt(keys, query) * (1.0 / math.sqrt(HD))
    raw = jnp.where(jnp.concatenate([live] * (width // 128), axis=1) > 0, raw, -1e30)
    expo = jnp.exp(raw - jnp.max(raw, axis=0, keepdims=True))
    return expo * (1.0 / jnp.sum(expo, axis=0, keepdims=True))


QB = 256


def attn_kernel(ids, x3, live, _, out):
    q, v, k = x3[0], x3[1], x3[2]
    c = ids[0]
    lv = live[...]
    vt = v.astype(F32).T.astype(BF)
    row = lax.broadcasted_iota(jnp.int32, (2 * HD, 1), 0)
    masks = head_masks()
    for s, core in ((0, c), (QB, 1 - c)):
        total = jnp.zeros((2 * HD, QB), F32)
        for h in range(2):
            qh = jnp.where(masks[h], q[s : s + QB], jnp.zeros((), BF))
            low = soft(k, qh, lv, QB).astype(BF)
            vh = jnp.where(row < HD if h == 0 else row >= HD, vt, jnp.zeros((), BF))
            total += dot_nn(vh, low)
        mixed = total.T.astype(BF)
        at = pl.ds(pl.multiple_of(core * QB, QB), QB)
        out[0, at, :] = mixed
        out[1, at, :] = mixed


def attn_back_kernel(x3, gm_ref, live, d3):
    q, v, k = x3[0], x3[1], x3[2]
    slots = q.shape[0]
    lv = live[...]
    kt = k.astype(F32).T.astype(BF)
    row = lax.broadcasted_iota(jnp.int32, (2 * HD, 1), 0)
    masks = head_masks()
    scale = 1.0 / math.sqrt(HD)
    zero = jnp.zeros((), BF)
    dk = jnp.zeros((slots, 2 * HD), F32)
    dv = jnp.zeros((slots, 2 * HD), F32)
    for s in range(0, slots, QB):
        gm = gm_ref[s : s + QB, :]
        dqt = jnp.zeros((2 * HD, QB), F32)
        for h in range(2):
            qh = jnp.where(masks[h], q[s : s + QB], zero)
            gh = jnp.where(masks[h], gm, zero)
            probs = soft(k, qh, lv, QB)
            gp = dot_nt(v, gh)
            delta = jnp.sum(probs * gp, axis=0, keepdims=True)
            ds = (probs * (gp - delta)).astype(BF)
            kh = jnp.where(row < HD if h == 0 else row >= HD, kt, zero)
            dqt += dot_nn(kh, ds)
            dk += dot_nn(ds, qh)
            dv += dot_nn(probs.astype(BF), gh)
        d3[0, s : s + QB, :] = (dqt.T * scale).astype(BF)
    d3[1] = dv.astype(BF)
    d3[2] = (dk * scale).astype(BF)


def mid_kernel(ids, tok_own, tok_far, traded, vec, att_own, att_far, n2_out, n2t_out, m_out, mixed_t, mixed_out):
    c = ids[0]
    half = tok_own.shape[0]
    for p in range(2):
        for y in range(2):
            at = 192 * (2 * y + p)
            for b in range(8):
                block = traded[p, 2 * half + 48 * (y * 8 + b) : 2 * half + 48 * (y * 8 + b) + 48]
                m_out[96 * b : 96 * b + 48, at : at + 192] = block[:, :192]
                m_out[96 * b + 48 : 96 * b + 96, at : at + 192] = block[:, 192:]
            for to, core in ((0, c), (half, 1 - c)):
                rows = traded[p, pl.ds(pl.multiple_of(core * half, half), half), :]
                mixed_out[to : to + half, at : at + 192] = lanes(rows, y)
    for to, tok, out in ((0, tok_own, att_own), (half, tok_far, att_far)):
        att = tok[...].astype(F32) + (dot_nn(mixed_out[to : to + half, :], m_out[...]) + vec[6:7, :])
        out[...] = att
        xhat, _ = normalize(att)
        n2 = (xhat * vec[2:3, :] + vec[3:4, :]).astype(BF)
        n2_out[to : to + half, :] = n2
        n2t_out[:, to : to + half] = n2.astype(F32).T.astype(BF)
        mixed_t[:, to : to + half] = mixed_out[to : to + half, :].astype(F32).T.astype(BF)


def ffn_kernel(ids, n2, n2t, br_own, br_far, ea, ea_far, eb, eb_far, el, el_far, bias,
               part_own, part_far, gn2, d_e, d_s, d_bias, br, e_ref, s_ref):
    my, mx, mz = ids[2], ids[3], ids[4]
    n = pl.program_id(0)

    def layer(z):
        return ((z & 1) ^ (mz & 1)) * 2 + ((z >> 1) ^ (mz >> 1))

    def x_first(at, y, x, z):
        i, rows = (x ^ mx) * 4 + layer(z), pl.ds(at, 96 if at == 0 else 48)
        return jnp.where(y == my, ea[i, rows, :], ea_far[i, rows, :])

    def y_first(at, y, x, z):
        i, rows = (y ^ my) * 4 + layer(z), pl.ds(at, 96 if at == 0 else 48)
        return jnp.where(x == mx, eb[i, rows, :], eb_far[i, rows, :])

    def z_last(y, x, z):
        i = (((z >> 1) ^ (mz >> 1)) * 2 + (y ^ my)) * 2 + (x ^ mx)
        return jnp.where((z & 1) == (mz & 1), el[i], el_far[i])

    for b in range(8):
        e_ref[96 * b : 96 * b + 96, :384] = x_first(0, n, b & 1, b >> 1)
        e_ref[96 * b : 96 * b + 96, 384:] = y_first(0, n, b & 1, b >> 1)
    for y in range(2):
        for k in range(2):
            for x in range(2):
                at = 384 * k + 192 * x
                s_ref[at : at + 48, 384 * y : 384 * y + 384] = x_first(96, y, x, 2 * n + k)
                s_ref[at + 48 : at + 96, 384 * y : 384 * y + 384] = y_first(96, y, x, 2 * n + k)
                s_ref[at + 96 : at + 192, 384 * y : 384 * y + 384] = z_last(y, x, 2 * n + k)
    half = br_own.shape[0]

    @pl.when(pl.program_id(0) == 0)
    def _():
        for out in (part_own, part_far, gn2):
            out[...] = jnp.zeros_like(out)
        br[0:half], br[half:] = br_own[...], br_far[...]

    e, s = e_ref[...], s_ref[...]
    pre = dot_nn(n2[...], e) + bias[0]
    grad_act = dot_nt(br[...], s)
    cdf = 0.5 * (1.0 + lax.erf(pre * math.sqrt(0.5)))
    act = (pre * cdf).astype(BF)
    slope = cdf + pre * (jnp.exp(-0.5 * pre * pre) * (1.0 / math.sqrt(2.0 * math.pi)))
    grad_pre = (grad_act * slope).astype(BF)
    y = dot_nn(act, s)
    part_own[...] += y[:half]
    part_far[...] += y[half:]
    gn2[...] += dot_nt(grad_pre, e)
    grad = dot_nn(act.astype(F32).T.astype(BF), br[...]).astype(BF)
    for y in range(2):
        d_s[y] = grad[:, 384 * y : 384 * y + 384].reshape(2, 2, 192, 384)
    grad = dot_nn(n2t[...], grad_pre).astype(BF)
    for p in range(2):
        d_e[0, :, p] = grad[:, 384 * p : 384 * p + 384].reshape(8, 96, 384)
    d_bias[0] = jnp.sum(grad_pre.astype(F32), axis=0, keepdims=True)


def mid_back_kernel(ids, gn_here, gn_there, att_own, att_far, br_own, br_far, mixed_t, m, vec, gatt, gm, dm, sums, low):
    first, c = ids[0] == 0, ids[0]
    half = att_own.shape[0]
    for to, att, br_ref in ((0, att_own, br_own), (half, att_far, br_far)):
        gn = gn_here[to : to + half, :] + gn_there[half - to : 2 * half - to, :]
        br = br_ref[...].astype(F32)
        xhat, spread = normalize(att[...])
        grad = br + norm_back(xhat, spread, vec[2:3, :], gn)
        low[to : to + half, :] = grad.astype(BF)
        if to == 0:
            gatt[...] = grad
            sums[0:1] = jnp.sum(gn * xhat, axis=0, keepdims=True)
            sums[1:2] = jnp.sum(gn, axis=0, keepdims=True)
            sums[2:3] = jnp.sum(grad.astype(BF).astype(F32), axis=0, keepdims=True)
            sums[3:4] = jnp.sum(br, axis=0, keepdims=True)
            sums[4:8] = jnp.zeros((4, sums.shape[1]), F32)
    for k in range(2):
        rows = m[pl.ds(pl.multiple_of(192 * (2 * k + c), 192), 192), :]
        gm[:, 192 * k : 192 * k + 192] = dot_nt(low[...], rows).astype(BF)
        both = low[:, 384 * k : 384 * k + 384]
        mine = jnp.where(first, lanes(both, 0), lanes(both, 1))
        weight = dot_nn(mixed_t[...], mine).astype(BF)
        for b in range(8):
            dm[8 * k + b, :, :192] = weight[96 * b : 96 * b + 48]
            dm[8 * k + b, :, 192:] = weight[96 * b + 48 : 96 * b + 96]


def triple_back_kernel(ids, n1_ref, d3, t3, d_qv, d_k, gn, sums):
    c = ids[0]
    j = pl.program_id(0)
    d = d3[0]
    half = gn.shape[1]
    weight = dot_nn(n1_ref[...], d).astype(BF)
    part = dot_nt(d, t3[0])
    sums[0] = jnp.sum(d.astype(F32), axis=0, keepdims=True)

    @pl.when(j == 0)
    def _():
        gn[c] = part[:half]
        gn[1 - c] = part[half:]

    @pl.when(j > 0)
    def _():
        gn[c] += part[:half]
        gn[1 - c] += part[half:]

    @pl.when(j < 2)
    def _():
        d_qv[0] = weight

    @pl.when(j == 2)
    def _():
        for b in range(8):
            for y in range(2):
                d_k[y, b, :, :192] = weight[96 * b : 96 * b + 48, 192 * y : 192 * y + 192]
                d_k[y, b, :, 192:] = weight[96 * b + 48 : 96 * b + 96, 192 * y : 192 * y + 192]


def first_back_kernel(ids, gn_both, tok, gatt, vec, sums2, sums1, d_bias, out, blocks, table):
    c = ids[0]
    gn = gn_both[0] + gn_both[1]
    xhat, spread = normalize(tok[...].astype(F32))
    out[...] = (gatt[...] + norm_back(xhat, spread, vec[0:1, :], gn)).astype(BF)
    table[12:16] = jnp.zeros((4, table.shape[1]), F32)
    table[0:1] = jnp.sum(gn * xhat, axis=0, keepdims=True)
    table[1:2] = jnp.sum(gn, axis=0, keepdims=True)
    table[2:4] = sums2[0:2]
    table[6:8] = sums2[2:4]
    for row, sums in [(4, sums1[0]), (5, sums1[1])] + [(8 + n, d_bias[n]) for n in range(4)]:
        for k in range(2):
            for p in range(2):
                at = 192 * (2 * k + p)
                table[row : row + 1, at : at + 192] = jnp.where(c == p, lanes(sums, k), 0.0)
    blocks[...] = jnp.zeros_like(blocks)
    for b in range(8):
        blocks[b, :, 0:96] = table[:, 96 * b : 96 * b + 96].astype(BF)


def halves(rows):
    return rows[:, :192], rows[:, 192:]


def fetch(refs, places, sems):
    copies = [pltpu.make_async_copy(ref, place, sems.at[i]) for i, (ref, place) in enumerate(zip(refs, places))]
    for copy in copies:
        copy.start()
    for copy in copies:
        copy.wait()


def adam_into(state, outs, rate, decay, at, grad):
    new = adamw(state[0][at], state[1][at], state[2][at], grad, rate, decay)
    for out, value in zip(outs, new):
        out[at] = value


def triple_units(t, total):
    a, b = halves(total[0:96])
    k = jnp.concatenate(halves(total[96:144]), axis=0)
    return a, b, k


def give_back_kernel(ids, t_own, t_far, es_own, es_far, give):
    first, t = ids[0] == 0, ids[1]
    total = t_own[...].astype(F32) + t_far[...].astype(F32)
    a, b, k = triple_units(t, total)
    give[0:96] = jnp.where(t == 1, a, jnp.where(t == 2, b, k))
    give[96:112] = jnp.zeros((16, 192), F32)
    give[96:112, 0:96] = total[192:208, 0:96]
    total = es_own[...].astype(F32) + es_far[...].astype(F32)
    give[112:208], give[208:304] = halves(jnp.where(first, total[96:192], total[0:96]))
    s0, s1 = halves(total[192:])
    give[304:496] = jnp.where(first, s1, s0)


def prefetch_kernel(_, *refs):
    fetch(refs[: len(refs) // 2], refs[len(refs) // 2 : -1], refs[-1])


def update_kernel(ids, t_own, t_far, es_own, es_far, took, *refs):
    state, outs = refs[:15], refs[15:]
    first, c, t = ids[0] == 0, ids[0], ids[1]
    every = slice(None)
    total = t_own[...].astype(F32) + t_far[...].astype(F32)
    a, b, k = triple_units(t, total)
    units = (
        jnp.where(t == 1, b, jnp.where(t == 2, k, a)),
        took[0:96],
        jnp.where(t == 1, k, jnp.where(t == 2, a, b)),
    )
    for i, unit in enumerate(units):
        adam_into(state[0:3], outs[0:4], RATES[0], DECAYS[0], (every, slice(192 * i, 192 * i + 192)), unit)
    for i, part in enumerate(halves(total[144:192])):
        adam_into(state[3:6], outs[4:8], RATES[1], DECAYS[1], (slice(48 * i, 48 * i + 48), every), part)
    total_es = es_own[...].astype(F32) + es_far[...].astype(F32)
    e = halves(jnp.where(first, total_es[0:96], total_es[96:192]))
    s0, s1 = halves(total_es[192:])
    s = jnp.where(first, s0, s1)
    for p in range(2):
        for j in range(2):
            grad = jnp.where(c == p, e[j], took[112 + 96 * j : 208 + 96 * j])
            at = 384 * j + 192 * p
            adam_into(state[6:9], outs[8:12], RATES[2], DECAYS[2], (every, slice(at, at + 192)), grad)
        grad = jnp.where(c == p, s, took[304:496]).T
        adam_into(state[9:12], outs[12:16], RATES[3], DECAYS[3], (every, slice(192 * p, 192 * p + 192)), grad)
    adam_into(state[12:15], outs[16:20], RATES[4], DECAYS[4], (every, every), total[192:204, 0:96] + took[96:108, 0:96])


def by_core(c, own, far):
    return jnp.where(c == 0, jnp.stack([own, far]), jnp.stack([far, own]))


def per_device(
    cube_tokens, visible, live_counts, block_cotangent,
    triple_master, triple_first, triple_second,
    mixing_master, mixing_first, mixing_second,
    expand_master, expand_first, expand_second,
    shrink_master, shrink_first, shrink_second,
    vector_master, vector_first, vector_second,
):
    y, c, b = lax.axis_index("y"), lax.axis_index("core"), lax.axis_index("blk")
    bits = (y, b & 1, b >> 1 & 1, b >> 2)
    turn = b % 4
    unturn = (4 - turn) % 4
    region, feats = cube_tokens.shape[1:]
    slots = visible.shape[1]
    slot_axis = jnp.arange(slots, dtype=jnp.int32)

    t_id = 2 * y + c
    ids = jnp.stack([c, t_id, y, bits[1], b >> 1]).astype(jnp.int32)
    shrink_t = shrink_master.T
    took = swap(call(
        give_kernel, shape(480, 192, dtype=BF), "give", 1e10, 1e3, in_specs=[SM, VM, VM, VM], out_specs=VM,
    )(ids, triple_master, expand_master, shrink_t), dc=1)
    tvm, es, last = call(
        pack_kernel, (shape(208, 384, dtype=BF), shape(288, 384, dtype=BF), shape(96, 384, dtype=BF)), "pack", 1e10, 1e3,
        in_specs=[SM] + [VM] * 6, out_specs=(VM, VM, VM),
    )(ids, took, triple_master, mixing_master, expand_master, shrink_t, vector_master)

    t_far = swap(tvm, db=4)
    last_in = swap(last, db=1)

    visible, block_cotangent, tvm, es, last = tie(visible, block_cotangent, tvm, es, last)
    def turned(x):
        return lax.dynamic_slice_in_dim(jnp.concatenate([x, x]), turn, 4, 0)

    local = visible % region
    flat_index = turned(local + region * jnp.arange(4, dtype=jnp.int32)[:, None])
    picked = jnp.take(cube_tokens.reshape(-1, feats), flat_index.reshape(-1), axis=0).reshape(4, slots, feats)
    counts = jnp.broadcast_to(turned(live_counts)[:, :, None].astype(BF), (4, 16, feats))
    live_here = slot_axis[None, :] < live_counts
    masked = turned(jnp.where(live_here[:, :, None], block_cotangent, jnp.zeros((), BF)))
    packet = jnp.concatenate([picked, masked, counts], axis=1)

    def packets(*steps):
        return [lax.ppermute(packet[s], FINE, cube_pairs(s, False)) for s in steps]

    last = jnp.stack([last, last_in])
    last_in = swap(last, dy=1)
    t_far, packet, es, last_in = tie(t_far, packet, es, last_in)
    tvm = jnp.stack([tvm, t_far])
    t_far = swap(tvm, db=2)
    last = jnp.stack([last, last_in]).reshape(384, 384)
    es_far = swap(jnp.concatenate([es, last], axis=0), db=4)
    own = packets(0, 1)

    t_far, packet = tie(t_far, packet)
    tvm = jnp.stack([tvm, t_far]).reshape(4, 208, 384)
    qv, rest = tvm[:, :96], tvm[:, 96:]
    qv_x, rest_y = swap(qv, db=1), swap(rest, dy=1)

    qv_x, rest_y, own, packet = tie(qv_x, rest_y, own, packet)
    qv = jnp.stack([qv, qv_x]).reshape(8, 96, 384)
    rest = jnp.stack([rest, rest_y]).reshape(8, 112, 384)
    qv_far, rest_far = swap(qv, dy=1), swap(rest, db=1)
    es_far, last = tie(es_far, last)
    el = jnp.stack([last, es_far[288:]]).reshape(8, 96, 384)
    es = jnp.stack([es, es_far[:288]])
    es_far = swap(es, db=2)
    own = own + packets(2, 3)

    qv_far, rest_far, es_far, own = tie(qv_far, rest_far, es_far, own)
    es = jnp.stack([es, es_far]).reshape(4, 288, 384)
    ea, eb = es[:, :144], es[:, 144:]
    ea_in, eb_in = swap(ea, db=1), swap(eb, dy=1)
    el_far = swap(el, db=2)
    own = jnp.stack(own)
    far = swap(own, dc=1)

    rows = 4 * slots
    tok_own, tok_far = [p[:, :slots].reshape(rows, feats) for p in (own, far)]
    br_own, br_far = [p[:, slots : 2 * slots].reshape(rows, feats) for p in (own, far)]
    cnt = jnp.concatenate([own[:, 2 * slots, :1], far[:, 2 * slots, :1]]).astype(jnp.int32)
    live = (slot_axis[None, :] < cnt).reshape(2 * rows, 1)
    live_cols = jnp.broadcast_to(live.astype(F32), (2 * rows, 128))

    n1, x3, t3, mix, vec, e_bias = call(
        qkv_kernel,
        (shape(feats, 2 * rows, dtype=BF), shape(3, 2 * rows, 384, dtype=BF), shape(3, feats, 384, dtype=BF),
         shape(2, 2 * rows + feats, 384, dtype=BF), shape(16, feats), shape(4, 1, 384)),
        "qkv", 2 * 512 * 768 * 1152, 8e6,
        in_specs=[SM] + [VM] * 6, out_specs=(VM,) * 6, scratch_shapes=[pltpu.VMEM((8, 384), F32), pltpu.VMEM((2 * rows, feats), BF)],
    )(ids, tok_own, tok_far, qv, qv_far, rest, rest_far)
    x3, mix, ea_in, eb_in, el_far = tie(x3, mix, ea_in, eb_in, el_far)
    ea = jnp.stack([ea, ea_in]).reshape(8, 144, 384)
    eb = jnp.stack([eb, eb_in]).reshape(8, 144, 384)
    ea_far, eb_far = swap(ea, dy=1), swap(eb, db=1)

    pairs3 = pl.BlockSpec((3, 2 * rows, 128), lambda i: (0, 0, i))
    col = pl.BlockSpec((2 * rows, 128), lambda i: (0, i))
    same = pl.BlockSpec((2 * rows, 128), lambda i: (0, 0))
    traded = trade(call(
        attn_kernel, shape(2, 2 * rows + feats, 384, dtype=BF), "attention", 6e9, 2e6,
        grid=(3,), in_specs=[SM, pairs3, same, pl.BlockSpec(memory_space=pl.ANY)],
        out_specs=pl.BlockSpec((2, 2 * rows, 128), lambda i: (0, 0, i)), input_output_aliases={3: 0},
    )(ids, x3, live_cols, mix))
    att, att_far, n2, n2t, mix, mixed = call(
        mid_kernel,
        (shape(rows, feats), shape(rows, feats), shape(2 * rows, feats, dtype=BF), shape(feats, 2 * rows, dtype=BF),
         shape(feats, feats, dtype=BF), shape(feats, 2 * rows, dtype=BF)),
        "mixing", 3e9, 5e6, in_specs=[SM] + [VM] * 4, out_specs=(VM,) * 6,
        scratch_shapes=[pltpu.VMEM((2 * rows, feats), BF)],
    )(ids, tok_own, tok_far, traded, vec)

    whole = pl.BlockSpec((rows, feats), lambda i: (0, 0))

    gathered = [pl.BlockSpec((8, r, 384), lambda n: (0, 0, 0)) for r in (144, 144, 144, 144, 96, 96)]
    every = pl.BlockSpec((2 * rows, feats), lambda i: (0, 0))
    part_own, part_give, gn2, d_e, d_s, d_b = call(
        ffn_kernel,
        (shape(rows, feats),) * 2
        + (shape(2 * rows, feats), shape(2, 8, 2, 96, 384, dtype=BF), shape(2, 4, 2, 192, 384, dtype=BF), shape(2, 1, 768)),
        "feed_forward", 18e9, 20e6, 46,
        grid=(2,),
        in_specs=[SM, every, pl.BlockSpec((feats, 2 * rows), lambda n: (0, 0))] + [whole] * 2 + gathered
        + [pl.BlockSpec((1, 1, 768), lambda n: (n, 0, 0))],
        out_specs=(
            whole, whole, every,
            pl.BlockSpec((1, 8, 2, 96, 384), lambda n: (n, 0, 0, 0, 0)),
            pl.BlockSpec((2, 2, 2, 192, 384), lambda n: (0, n, 0, 0, 0)),
            pl.BlockSpec((1, 1, 768), lambda n: (n, 0, 0)),
        ),
        scratch_shapes=[pltpu.VMEM((2 * rows, feats), BF), pltpu.VMEM((feats, 768), BF), pltpu.VMEM((768, feats), BF)],
    )(ids, n2, n2t, br_own, br_far, ea, ea_far, eb, eb_far, el, el_far, e_bias.reshape(2, 1, 768))

    z0, z1 = bits[2], bits[3]
    gn2_far = swap(gn2, dc=1)
    d_e = d_e.reshape(2, 4, 2, 192, 384)
    e_in = swap(pick(d_e, 1 - bits[1], 2), db=1)
    s_in = swap(pick(d_s, 1 - y, 0), dy=1)

    gatt, gm, dm, sums2 = call(
        mid_back_kernel,
        (shape(rows, feats), shape(2 * rows, 384, dtype=BF), shape(16, 48, 384, dtype=BF), shape(8, feats)),
        "mixing_back", 6e9, 8e6, in_specs=[SM] + [VM] * 9, out_specs=(VM,) * 4,
        scratch_shapes=[pltpu.VMEM((2 * rows, feats), BF)],
    )(ids, gn2, gn2_far, att, att_far, br_own, br_far, mixed, mix, vec)
    d3 = call(
        attn_back_kernel, shape(3, 2 * rows, 384, dtype=BF), "attention_back", 9e9, 5e6,
        grid=(3,), in_specs=[pairs3, col, same], out_specs=pairs3,
    )(x3, gm, live_cols)

    third = pl.BlockSpec((1, 2 * rows, 384), lambda j: (j, 0, 0))
    d_qv, d_k, gn1, sums1 = call(
        triple_back_kernel,
        (shape(2, feats, 384, dtype=BF), shape(2, 8, 48, 384, dtype=BF), shape(2, rows, feats), shape(3, 1, 384)),
        "triple_back", 5e9, 5e6,
        grid=(3,),
        in_specs=[SM, pl.BlockSpec((feats, 2 * rows), lambda j: (0, 0)), third, pl.BlockSpec((1, feats, 384), lambda j: (j, 0, 0))],
        out_specs=(
            pl.BlockSpec((1, feats, 384), lambda j: (jnp.minimum(j, 1), 0, 0)),
            pl.BlockSpec((2, 8, 48, 384), lambda j: (0, 0, 0, 0)),
            pl.BlockSpec((2, rows, feats), lambda j: (0, 0, 0)),
            pl.BlockSpec((1, 1, 384), lambda j: (j, 0, 0)),
        ),
    )(ids, n1, d3, t3)

    gn1 = trade(gn1)
    grad_tok, blocks = call(
        first_back_kernel, (shape(rows, feats, dtype=BF), shape(8, 16, 384, dtype=BF)), "first_back", 1e9, 1e6,
        in_specs=[SM] + [VM] * 7, out_specs=(VM, VM), scratch_shapes=[pltpu.VMEM((16, feats), F32)],
    )(ids, gn1, tok_own, gatt, vec, sums2, sums1, d_b.reshape(4, 1, 384))

    blocks = jnp.broadcast_to(blocks, (2, 8, 16, 384))
    d_qv = d_qv.reshape(2, 4, 2, 96, 384)
    d_km = jnp.concatenate([d_k, dm.reshape(2, 8, 48, 384), blocks], axis=2).reshape(2, 4, 2, 112, 384)
    qv_in = swap(pick(d_qv, 1 - bits[1], 2), db=1)
    km_in = swap(pick(d_km, 1 - y, 0), dy=1)

    e_in, s_in, grad_tok, part_give = tie(e_in, s_in, grad_tok, part_give)
    d_e = add_low(pick(d_e, bits[1], 2), e_in)
    d_s = add_low(pick(d_s, y, 0), s_in)
    e_in = swap(pick(d_e, 1 - y, 0), dy=1)
    s_in = swap(pick(d_s, 1 - bits[1], 1), db=1)

    part_far = swap(part_give, dc=1)
    result = att + (part_own + part_far + vec[7])
    result = jnp.where(live[:rows], result, 0.0).astype(BF).reshape(4, slots, feats)
    packet = jnp.concatenate([result, grad_tok.reshape(4, slots, feats)], axis=1)

    def go_back(step, *after):
        part = tie(packet[step], *after)[0]
        return lax.ppermute(part, FINE, cube_pairs(step, True))

    back = [go_back(0)]
    back += [go_back(1, back[0])]

    qv_in, km_in, back, packet = tie(qv_in, km_in, back, packet)
    d_qv = add_low(pick(d_qv, bits[1], 2), qv_in)
    d_km = add_low(pick(d_km, y, 0), km_in)
    qv_in = swap(pick(d_qv, 1 - y, 0), dy=1)
    km_in = swap(pick(d_km, 1 - bits[1], 1), db=1)
    back += [go_back(2)]

    e_in, s_in, packet = tie(e_in, s_in, packet)
    d_es = jnp.concatenate(
        [add_low(pick(d_e, y, 0), e_in), add_low(pick(d_s, bits[1], 1), s_in)], axis=1
    ).reshape(2, 2, 384, 384)
    es_in = swap(pick(d_es, 1 - z0, 1), db=2)
    back += [go_back(3)]

    qv_in, km_in = tie(qv_in, km_in)
    d_t = jnp.concatenate(
        [add_low(pick(d_qv, y, 0), qv_in), add_low(pick(d_km, bits[1], 1), km_in)], axis=1
    ).reshape(2, 2, 208, 384)
    t_in = swap(pick(d_t, 1 - z0, 1), db=2)

    es_in, qv_in = tie(es_in, qv_in)
    es_keep = d_es = add_low(pick(d_es, z0, 1), es_in)
    es_in = swap(pick(d_es, 1 - z1, 0), db=4)
    d_t = add_low(pick(d_t, z0, 1), t_in)
    t_in = swap(pick(d_t, 1 - z1, 0), db=4)

    state = (triple_master, triple_first, triple_second, mixing_master, mixing_first, mixing_second,
             expand_master, expand_first, expand_second, shrink_t, shrink_first.T, shrink_second.T,
             vector_master, vector_first, vector_second)
    ids_late = tie(ids, es_keep)[0]
    ready = call(
        prefetch_kernel, tuple(shape(*a.shape) for a in state), "prefetch", 1e10, 1e3,
        in_specs=[SM] + [pl.BlockSpec(memory_space=pltpu.HBM)] * len(state), out_specs=(VM,) * len(state),
        scratch_shapes=[pltpu.SemaphoreType.DMA((len(state),))],
    )(ids_late, *state)

    back = jnp.stack(back)
    back = lax.dynamic_slice_in_dim(jnp.concatenate([back, back]), unturn, 4, 0)
    block_output = back[:, :slots]
    spread = (jnp.arange(region, dtype=jnp.int32)[None, :, None] == local[:, None, :]).astype(BF)
    token_grads = jnp.einsum("grs,gsf->grf", spread, back[:, slots:], preferred_element_type=F32).astype(BF)

    t_in, es_in, token_grads, block_output, ready = tie(t_in, es_in, token_grads, block_output, ready)
    grads = (pick(d_t, z1, 0), t_in, pick(d_es, z1, 0), es_in)
    took = swap(call(
        give_back_kernel, shape(496, 192), "give_back", 1e6, 1e6, in_specs=[SM] + [VM] * 4, out_specs=VM,
    )(ids, *grads), dc=1)

    def whole_of(a):
        return pl.BlockSpec(a.shape, lambda i: (0,) * len(a.shape))

    outs = tuple(shape(*a.shape, dtype=d) for a in state[::3] for d in (F32, F32, F32, BF))
    new = call(
        update_kernel, outs, "update", 1e8, 4e6, grid=(1,),
        in_specs=[SM] + [whole_of(a) for a in (*grads, took, *state)], out_specs=tuple(whole_of(o) for o in outs),
    )(ids, *grads, took, *ready)
    return (block_output, token_grads, *new[:12], *(o.T for o in new[12:16]), *new[16:])


def layer_norm(rows, gain, shift):
    center = rows - jnp.mean(rows, axis=-1, keepdims=True)
    spread = lax.rsqrt(jnp.mean(center * center, axis=-1, keepdims=True) + 1e-06)
    return center * spread * gain + shift


def outer_sum(left, right):
    return lax.dot_general(
        left, right, (((0,), (0,)), ((), ())), preferred_element_type=jnp.float32
    )


def back_product(grads, weight):
    return lax.dot_general(
        grads, weight, (((1,), (1,)), ((), ())), preferred_element_type=jnp.float32
    )


def masked_scores(queries, key_all, live_all):
    raw = jnp.einsum("gshe,gthe->ghst", queries, key_all, preferred_element_type=jnp.float32) * (
        1.0 / math.sqrt(HD)
    )
    return jnp.where(live_all[:, None, None, :] > 0, raw, -1e30)


def cycle_section(triple_grad, mixing_grad, expand_grad, shrink_grad, vector_grad):
    summed = (
        lax.psum_scatter(triple_grad, "blk", scatter_dimension=0, tiled=True),
        lax.psum_scatter(mixing_grad, "blk", scatter_dimension=0, tiled=True),
        lax.psum_scatter(expand_grad, "blk", scatter_dimension=0, tiled=True),
        lax.psum_scatter(shrink_grad, "blk", scatter_dimension=0, tiled=True),
        lax.psum_scatter(vector_grad, "blk", scatter_dimension=1, tiled=True),
    )
    return (summed[0], summed[1], summed[2], summed[3], summed[4])


def group_section(triple_grad, mixing_grad, expand_grad, shrink_grad, vector_grad):
    summed = (
        lax.psum_scatter(triple_grad, "batch", scatter_dimension=1, tiled=True),
        lax.psum_scatter(mixing_grad, "batch", scatter_dimension=1, tiled=True),
        lax.psum_scatter(expand_grad, "batch", scatter_dimension=1, tiled=True),
        lax.psum_scatter(shrink_grad, "batch", scatter_dimension=1, tiled=True),
    )
    vector_sum = lax.psum(vector_grad, "batch")
    return (summed[0], summed[1], summed[2], summed[3], vector_sum)


def per_device_any(
    cube_tokens,
    visible,
    live_counts,
    block_cotangent,
    triple_master,
    triple_first,
    triple_second,
    mixing_master,
    mixing_first,
    mixing_second,
    expand_master,
    expand_first,
    expand_second,
    shrink_master,
    shrink_first,
    shrink_second,
    vector_master,
    vector_first,
    vector_second,
):
    low_copies = (
        lax.all_gather(triple_master.astype(jnp.bfloat16), "blk", axis=0, tiled=True),
        lax.all_gather(mixing_master.astype(jnp.bfloat16), "blk", axis=0, tiled=True),
        lax.all_gather(expand_master.astype(jnp.bfloat16), "blk", axis=0, tiled=True),
        lax.all_gather(shrink_master.astype(jnp.bfloat16), "blk", axis=0, tiled=True),
        lax.all_gather(vector_master.astype(jnp.bfloat16), "blk", axis=1, tiled=True),
    )
    triple_w, mixing_w, expand_w, shrink_w = (
        lax.all_gather(low_copies[0], "batch", axis=1, tiled=True),
        lax.all_gather(low_copies[1], "batch", axis=1, tiled=True),
        lax.all_gather(low_copies[2], "batch", axis=1, tiled=True),
        lax.all_gather(low_copies[3], "batch", axis=1, tiled=True),
    )
    vector_w = low_copies[4].astype(jnp.float32)
    groups, slot_count = visible.shape
    region = cube_tokens.shape[1]
    features = cube_tokens.shape[2]
    row_count = groups * slot_count
    head_count = features // HD
    local_index = visible % region
    tokens = jnp.take_along_axis(cube_tokens, local_index[:, :, None], axis=1).astype(jnp.float32)
    flat_tokens = tokens.reshape(row_count, features)
    live_mask = jnp.arange(slot_count, dtype=jnp.int32)[None, :] < live_counts
    live_rows = live_mask.reshape(row_count, 1)
    normed1 = layer_norm(flat_tokens, vector_w[0], vector_w[1]).astype(jnp.bfloat16)
    zero_bias = jnp.zeros((features,), jnp.float32)
    triple_bias = jnp.concatenate([vector_w[4], zero_bias, vector_w[5]])
    triple = (jnp.dot(normed1, triple_w, preferred_element_type=jnp.float32) + triple_bias).astype(
        jnp.bfloat16
    )
    triple = triple.reshape(groups, slot_count, 3 * features)
    query_flat = triple[:, :, :features]
    queries = query_flat.reshape(groups, slot_count, head_count, HD)
    key_rows = triple[:, :, features : 2 * features]
    value_rows = triple[:, :, 2 * features :]
    key_all, value_all, live_all = (
        lax.all_gather(key_rows, "blk", axis=1, tiled=True),
        lax.all_gather(value_rows, "blk", axis=1, tiled=True),
        lax.all_gather(live_mask.astype(jnp.bfloat16), "blk", axis=1, tiled=True),
    )
    key_all = key_all.reshape(groups, -1, head_count, HD)
    value_all = value_all.reshape(groups, -1, head_count, HD)
    scores = masked_scores(queries, key_all, live_all)
    peak = jnp.max(scores, axis=-1, keepdims=True)
    expo = jnp.exp(scores - peak)
    total = jnp.sum(expo, axis=-1, keepdims=True)
    prob_low = (expo / total).astype(jnp.bfloat16)
    mixed = jnp.einsum("ghst,gthe->gshe", prob_low, value_all, preferred_element_type=jnp.float32)
    mixed = mixed.astype(jnp.bfloat16).reshape(row_count, features)
    attended = flat_tokens + (
        jnp.dot(mixed, mixing_w, preferred_element_type=jnp.float32) + vector_w[6]
    )
    normed2 = layer_norm(attended, vector_w[2], vector_w[3]).astype(jnp.bfloat16)
    preact = jnp.dot(normed2, expand_w, preferred_element_type=jnp.float32) + vector_w[8:].reshape(
        -1
    )
    activation = jax.nn.gelu(preact, approximate=False).astype(jnp.bfloat16)
    result = attended + (
        jnp.dot(activation, shrink_w, preferred_element_type=jnp.float32) + vector_w[7]
    )
    result = jnp.where(live_rows, result, 0.0)
    block_output = result.astype(jnp.bfloat16).reshape(groups, slot_count, features)
    grad_out = jnp.where(
        live_rows, block_cotangent.reshape(row_count, features).astype(jnp.float32), 0.0
    )
    branch_low = grad_out.astype(jnp.bfloat16)
    shrink_grad = outer_sum(activation, branch_low)
    shrink_bias_grad = jnp.sum(branch_low.astype(jnp.float32), axis=0)
    grad_act = back_product(branch_low, shrink_w)
    gelu_value, gelu_back = jax.vjp(partial(jax.nn.gelu, approximate=False), preact)
    grad_pre = gelu_back(grad_act)[0].astype(jnp.bfloat16)
    expand_grad = outer_sum(normed2, grad_pre)
    expand_bias_grad = jnp.sum(grad_pre.astype(jnp.float32), axis=0)
    grad_normed2 = back_product(grad_pre, expand_w)
    norm2_value, norm2_back = jax.vjp(layer_norm, attended, vector_w[2], vector_w[3])
    grad_through2, gain2_grad, shift2_grad = norm2_back(grad_normed2)
    grad_attended = grad_out + grad_through2
    mix_low = grad_attended.astype(jnp.bfloat16)
    mixing_grad = outer_sum(mixed, mix_low)
    mixing_bias_grad = jnp.sum(mix_low.astype(jnp.float32), axis=0)
    grad_mixed_flat = (
        back_product(mix_low, mixing_w).astype(jnp.bfloat16).reshape(groups, slot_count, features)
    )
    grad_mixed = grad_mixed_flat.reshape(groups, slot_count, head_count, HD)
    scores = masked_scores(queries, key_all, live_all)
    probs = jnp.exp(scores - peak) / total
    prob_low = probs.astype(jnp.bfloat16)
    grad_probs = jnp.einsum(
        "gshe,gthe->ghst", grad_mixed, value_all, preferred_element_type=jnp.float32
    )
    delta = jnp.sum(probs * grad_probs, axis=-1, keepdims=True)
    grad_scores = (probs * (grad_probs - delta)).astype(jnp.bfloat16)
    score_scale = 1.0 / math.sqrt(HD)
    grad_queries = (
        jnp.einsum("ghst,gthe->gshe", grad_scores, key_all, preferred_element_type=jnp.float32)
        * score_scale
    )
    term_keys = (
        jnp.einsum("ghst,gshe->gthe", grad_scores, queries, preferred_element_type=jnp.float32)
        * score_scale
    )
    term_values = jnp.einsum(
        "ghst,gshe->gthe", prob_low, grad_mixed, preferred_element_type=jnp.float32
    )
    grad_keys, grad_values = (
        lax.psum_scatter(
            term_keys.reshape(groups, -1, features), "blk", scatter_dimension=1, tiled=True
        ),
        lax.psum_scatter(
            term_values.reshape(groups, -1, features), "blk", scatter_dimension=1, tiled=True
        ),
    )
    grad_triple = jnp.concatenate(
        [
            grad_queries.reshape(row_count, features),
            grad_keys.reshape(row_count, features),
            grad_values.reshape(row_count, features),
        ],
        axis=1,
    ).astype(jnp.bfloat16)
    triple_grad = outer_sum(normed1, grad_triple)
    triple_sums = jnp.sum(grad_triple.astype(jnp.float32), axis=0)
    grad_normed1 = back_product(grad_triple, triple_w)
    norm1_value, norm1_back = jax.vjp(layer_norm, flat_tokens, vector_w[0], vector_w[1])
    grad_through1, gain1_grad, shift1_grad = norm1_back(grad_normed1)
    grad_tokens = (grad_attended + grad_through1).reshape(groups, slot_count, features)
    cube_rows = jnp.arange(groups, dtype=jnp.int32)[:, None]
    token_grads = (
        jnp.zeros(cube_tokens.shape, jnp.float32)
        .at[cube_rows, local_index]
        .add(grad_tokens)
        .astype(jnp.bfloat16)
    )
    leading_rows = jnp.stack(
        [
            gain1_grad,
            shift1_grad,
            gain2_grad,
            shift2_grad,
            triple_sums[:features],
            triple_sums[2 * features :],
            mixing_bias_grad,
            shrink_bias_grad,
        ]
    )
    vector_grad = jnp.concatenate([leading_rows, expand_bias_grad.reshape(-1, features)], axis=0)
    reduced = group_section(triple_grad, mixing_grad, expand_grad, shrink_grad, vector_grad)
    reduced = cycle_section(reduced[0], reduced[1], reduced[2], reduced[3], reduced[4])
    masters = (triple_master, mixing_master, expand_master, shrink_master, vector_master)
    firsts = (triple_first, mixing_first, expand_first, shrink_first, vector_first)
    seconds = (triple_second, mixing_second, expand_second, shrink_second, vector_second)
    outputs = [block_output, token_grads]
    for master, first, second, grad, rate, decay in zip(
        masters, firsts, seconds, reduced, RATES, DECAYS
    ):
        outputs.extend(adamw(master, first, second, grad, rate, decay))
    return tuple(outputs)


def solution(mesh):
    groups, blocks = mesh.shape["batch"], mesh.shape["blk"]
    if (groups, blocks) == (4, 8):
        mesh = Mesh(mesh.devices.reshape(2, 2, 8), FINE)
        batch, body = ("y", "core"), per_device
    else:
        batch, body = "batch", per_device_any
    rows = P(batch, "blk", None)
    part = P("blk", batch)
    table = P(None, "blk")
    in_specs = (rows, P(batch, "blk"), P(batch, "blk"), rows) + (part,) * 12 + (table,) * 3
    out_specs = (rows, rows) + (part,) * 16 + (table,) * 4
    return jax.shard_map(body, mesh=mesh, in_specs=in_specs, out_specs=out_specs, check_vma=False)
```

```python
from functools import partial
import math

import jax
import jax.numpy as jnp
from jax import lax
from jax.experimental import pallas as pl
from jax.experimental.pallas import tpu as pltpu
from jax.sharding import Mesh, PartitionSpec as P

HD = 64
STEP = 10
BF = jnp.bfloat16
F32 = jnp.float32

RATES = (0.04, 0.3, 0.04, 0.02, 0.25)
DECAYS = (0.05, 0.05, 0.05, 0.05, 0.0)


def adamw(master, first, second, grad, rate, decay):
    first_new = 0.9 * first + 0.1 * grad
    second_new = 0.999 * second + 0.001 * grad * grad
    corrected = first_new / (1.0 - 0.9**STEP) / (jnp.sqrt(second_new / (1.0 - 0.999**STEP)) + 1e-08)
    master_new = master - rate * (corrected + decay * master)
    return (first_new, second_new, master_new, master_new.astype(BF))


FINE = ("y", "core", "blk")


def place(y, c, b):
    return (y * 2 + c) * 8 + b


def swap(x, dy=0, dc=0, db=0):
    pairs = [
        (place(y, c, b), place(y ^ dy, c ^ dc, b ^ db))
        for y in range(2)
        for c in range(2)
        for b in range(8)
    ]
    return lax.ppermute(x, FINE, pairs)


def trade(x):
    return lax.all_to_all(x, "core", 0, 0, tiled=True)


def cube_pairs(step, back):
    pairs = []
    for y in range(2):
        for c in range(2):
            for b in range(8):
                r, q = b // 4, b % 4
                far = place(y, r, 4 * c + (q + step) % 4)
                near = place(y, c, b)
                pairs.append((far, near) if back else (near, far))
    return pairs


def pick(x, index, axis):
    return lax.dynamic_index_in_dim(x, index, axis, keepdims=False)


def add_low(a, b):
    return (a.astype(F32) + b.astype(F32)).astype(BF)


def tie(*parts):
    return lax.optimization_barrier(parts)


def dot_nn(a, b):
    return jnp.dot(a, b, preferred_element_type=F32)


def dot_nt(a, b):
    return lax.dot_general(a, b, (((1,), (1,)), ((), ())), preferred_element_type=F32)


def dot_tn(a, b):
    return lax.dot_general(a, b, (((0,), (0,)), ((), ())), preferred_element_type=F32)


def call(kernel, outs, name, flops=0, moved=0, vmem=16, **kw):
    return pl.pallas_call(
        kernel,
        out_shape=outs,
        name=name,
        cost_estimate=pl.CostEstimate(flops=int(flops), bytes_accessed=int(moved), transcendentals=0),
        compiler_params=pltpu.CompilerParams(vmem_limit_bytes=vmem * 2**20),
        **kw,
    )


def shape(*dims, dtype=F32):
    return jax.ShapeDtypeStruct(dims, dtype)


VM = pl.BlockSpec(memory_space=pltpu.VMEM)
SM = pl.BlockSpec(memory_space=pltpu.SMEM)


def normalize(rows):
    center = rows - jnp.mean(rows, axis=-1, keepdims=True)
    spread = lax.rsqrt(jnp.mean(center * center, axis=-1, keepdims=True) + 1e-06)
    return center * spread, spread


def norm_back(xhat, spread, gain, grad):
    q = grad * gain
    mean_q = jnp.mean(q, axis=-1, keepdims=True)
    mean_x = jnp.mean(q * xhat, axis=-1, keepdims=True)
    return spread * (q - mean_q - xhat * mean_x)


def lanes(ref_rows, unit):
    return ref_rows[:, 192 * unit : 192 * unit + 192]


def give_kernel(ids, triple, expand, shrink_t, give):
    first = ids[0] == 0
    e = expand[...].astype(BF)
    give[0:96] = jnp.where(first, lanes(e, 1), lanes(e, 0))
    give[96:192] = jnp.where(first, lanes(e, 3), lanes(e, 2))
    s = shrink_t[...].T.astype(BF)
    give[192:384] = jnp.where(first, s[192:], s[:192])
    give[384:480] = lanes(triple, 1).astype(BF)


def pack_kernel(ids, took, triple, mixing, expand, shrink_t, vector, tvm, es, last):
    first, t = ids[0] == 0, ids[1]
    e = expand[...].astype(BF)
    for j in range(2):
        mine = jnp.where(first, lanes(e, 2 * j), lanes(e, 2 * j + 1))
        far = took[96 * j : 96 * j + 96]
        es[0:96, 192 * j : 192 * j + 192] = jnp.where(first, mine, far)
        es[144:240, 192 * j : 192 * j + 192] = jnp.where(first, far, mine)
    s = shrink_t[...].T.astype(BF)
    mine, far = jnp.where(first, s[:192], s[192:]), took[192:384]
    left, right = jnp.where(first, mine, far), jnp.where(first, far, mine)
    for out, at, rows in ((es, 96, slice(0, 48)), (es, 240, slice(48, 96)), (last, 0, slice(96, 192))):
        to = slice(at, at + rows.stop - rows.start)
        out[to, :192] = left[rows]
        out[to, 192:] = right[rows]
    low = triple[...].astype(BF)
    t0, t2, far = lanes(low, 0), lanes(low, 2), took[384:480]
    tvm[0:96, :192] = jnp.where(t == 1, far, jnp.where(t == 2, t2, t0))
    tvm[0:96, 192:] = jnp.where(t == 1, t0, jnp.where(t == 2, far, t2))
    key = jnp.where(t == 1, t2, jnp.where(t == 2, t0, far))
    tvm[96:144, :192] = key[:48]
    tvm[96:144, 192:] = key[48:]
    m = mixing[...].astype(BF)
    tvm[144:192, :192] = m[:48]
    tvm[144:192, 192:] = m[48:]
    tvm[192:208] = jnp.zeros((16, 384), BF)
    tvm[192:204, 0:96] = vector[...].astype(BF)


def qkv_kernel(ids, tok_own, tok_far, qv_own, qv_far, rest_own, rest_far,
               n1_out, x3_out, t3_out, mix_out, vec_out, eb_out, bias, n1):
    first, my, mx, mz = ids[0] == 0, ids[2], ids[3], ids[4]
    for b in range(8):
        iz = ((b >> 1 & 1) ^ (mz & 1)) * 2 + ((b >> 2) ^ (mz >> 1))
        here = (b & 1) ^ mx
        for y in range(2):
            there = y ^ my
            iq, ir = here * 4 + iz, there * 4 + iz
            t3_out[y, 96 * b : 96 * b + 96, :] = jnp.where(there == 0, qv_own[iq], qv_far[iq])
            block = jnp.where(here == 0, rest_own[ir], rest_far[ir])
            t3_out[2, 96 * b : 96 * b + 48, 192 * y : 192 * y + 192] = block[0:48, :192]
            t3_out[2, 96 * b + 48 : 96 * b + 96, 192 * y : 192 * y + 192] = block[0:48, 192:]
            at = 2 * QB + 48 * (y * 8 + b)
            mix_out[0, at : at + 48] = block[48:96]
            mix_out[1, at : at + 48] = block[48:96]
            if y == 0:
                vec_out[0:16, 96 * b : 96 * b + 96] = block[96:112, 0:96].astype(F32)
    half = tok_own.shape[0]
    for at, tok in ((0, tok_own), (half, tok_far)):
        xhat, _ = normalize(tok[...].astype(F32))
        low = (xhat * vec_out[0:1, :] + vec_out[1:2, :]).astype(BF)
        n1[at : at + half, :] = low
        n1_out[:, at : at + half] = low.astype(F32).T.astype(BF)
    mix_out[:, 0 : 2 * QB] = jnp.zeros((2, 2 * QB, 384), BF)
    bias[...] = jnp.zeros_like(bias)
    for j in range(2):
        for k in range(2):
            row = vec_out[4 + j : 5 + j, 384 * k : 384 * k + 384]
            bias[j : j + 1, 192 * k : 192 * k + 192] = jnp.where(first, lanes(row, 0), lanes(row, 1))
    for n in range(4):
        for k in range(2):
            row = vec_out[8 + n : 9 + n, 384 * k : 384 * k + 384]
            eb_out[n, 0:1, 192 * k : 192 * k + 192] = jnp.where(first, lanes(row, 0), lanes(row, 1))
    for j in range(3):
        x3_out[j] = (dot_nn(n1[...], t3_out[j]) + bias[j : j + 1, :]).astype(BF)


def head_masks():
    lane = lax.broadcasted_iota(jnp.int32, (1, 2 * HD), 1)
    return [lane < HD, lane >= HD]


def soft(keys, query, live, width):
    raw = dot_nt(keys, query) * (1.0 / math.sqrt(HD))
    raw = jnp.where(jnp.concatenate([live] * (width // 128), axis=1) > 0, raw, -1e30)
    expo = jnp.exp(raw - jnp.max(raw, axis=0, keepdims=True))
    return expo * (1.0 / jnp.sum(expo, axis=0, keepdims=True))


QB = 256


def attn_kernel(ids, x3, live, _, out):
    q, v, k = x3[0], x3[1], x3[2]
    c = ids[0]
    lv = live[...]
    vt = v.astype(F32).T.astype(BF)
    row = lax.broadcasted_iota(jnp.int32, (2 * HD, 1), 0)
    masks = head_masks()
    for s, core in ((0, c), (QB, 1 - c)):
        total = jnp.zeros((2 * HD, QB), F32)
        for h in range(2):
            qh = jnp.where(masks[h], q[s : s + QB], jnp.zeros((), BF))
            low = soft(k, qh, lv, QB).astype(BF)
            vh = jnp.where(row < HD if h == 0 else row >= HD, vt, jnp.zeros((), BF))
            total += dot_nn(vh, low)
        mixed = total.T.astype(BF)
        at = pl.ds(pl.multiple_of(core * QB, QB), QB)
        out[0, at, :] = mixed
        out[1, at, :] = mixed


def attn_back_kernel(x3, gm_ref, live, d3):
    q, v, k = x3[0], x3[1], x3[2]
    slots = q.shape[0]
    lv = live[...]
    kt = k.astype(F32).T.astype(BF)
    row = lax.broadcasted_iota(jnp.int32, (2 * HD, 1), 0)
    masks = head_masks()
    scale = 1.0 / math.sqrt(HD)
    zero = jnp.zeros((), BF)
    dk = jnp.zeros((slots, 2 * HD), F32)
    dv = jnp.zeros((slots, 2 * HD), F32)
    for s in range(0, slots, QB):
        gm = gm_ref[s : s + QB, :]
        dqt = jnp.zeros((2 * HD, QB), F32)
        for h in range(2):
            qh = jnp.where(masks[h], q[s : s + QB], zero)
            gh = jnp.where(masks[h], gm, zero)
            probs = soft(k, qh, lv, QB)
            gp = dot_nt(v, gh)
            delta = jnp.sum(probs * gp, axis=0, keepdims=True)
            ds = (probs * (gp - delta)).astype(BF)
            kh = jnp.where(row < HD if h == 0 else row >= HD, kt, zero)
            dqt += dot_nn(kh, ds)
            dk += dot_nn(ds, qh)
            dv += dot_nn(probs.astype(BF), gh)
        d3[0, s : s + QB, :] = (dqt.T * scale).astype(BF)
    d3[1] = dv.astype(BF)
    d3[2] = (dk * scale).astype(BF)


def mid_kernel(ids, tok_own, tok_far, traded, vec, att_own, att_far, n2_out, n2t_out, m_out, mixed_t, mixed_out):
    c = ids[0]
    half = tok_own.shape[0]
    for p in range(2):
        for y in range(2):
            at = 192 * (2 * y + p)
            for b in range(8):
                block = traded[p, 2 * half + 48 * (y * 8 + b) : 2 * half + 48 * (y * 8 + b) + 48]
                m_out[96 * b : 96 * b + 48, at : at + 192] = block[:, :192]
                m_out[96 * b + 48 : 96 * b + 96, at : at + 192] = block[:, 192:]
            for to, core in ((0, c), (half, 1 - c)):
                rows = traded[p, pl.ds(pl.multiple_of(core * half, half), half), :]
                mixed_out[to : to + half, at : at + 192] = lanes(rows, y)
    for to, tok, out in ((0, tok_own, att_own), (half, tok_far, att_far)):
        att = tok[...].astype(F32) + (dot_nn(mixed_out[to : to + half, :], m_out[...]) + vec[6:7, :])
        out[...] = att
        xhat, _ = normalize(att)
        n2 = (xhat * vec[2:3, :] + vec[3:4, :]).astype(BF)
        n2_out[to : to + half, :] = n2
        n2t_out[:, to : to + half] = n2.astype(F32).T.astype(BF)
        mixed_t[:, to : to + half] = mixed_out[to : to + half, :].astype(F32).T.astype(BF)


def ffn_kernel(ids, n2, n2t, br_own, br_far, ea, ea_far, eb, eb_far, el, el_far, bias,
               part_own, part_far, gn2, e_x, e_y, s_x, s_y, s_z, d_bias, br, e_ref, s_ref):
    my, mx, mz = ids[2], ids[3], ids[4]
    n = pl.program_id(0)

    def layer(z):
        return ((z & 1) ^ (mz & 1)) * 2 + ((z >> 1) ^ (mz >> 1))

    def x_first(at, y, x, z):
        i, rows = (x ^ mx) * 4 + layer(z), pl.ds(at, 96 if at == 0 else 48)
        return jnp.where(y == my, ea[i, rows, :], ea_far[i, rows, :])

    def y_first(at, y, x, z):
        i, rows = (y ^ my) * 4 + layer(z), pl.ds(at, 96 if at == 0 else 48)
        return jnp.where(x == mx, eb[i, rows, :], eb_far[i, rows, :])

    def z_last(y, x, z):
        i = (((z >> 1) ^ (mz >> 1)) * 2 + (y ^ my)) * 2 + (x ^ mx)
        return jnp.where((z & 1) == (mz & 1), el[i], el_far[i])

    for b in range(8):
        e_ref[96 * b : 96 * b + 96, :384] = x_first(0, n, b & 1, b >> 1)
        e_ref[96 * b : 96 * b + 96, 384:] = y_first(0, n, b & 1, b >> 1)
    for y in range(2):
        for k in range(2):
            for x in range(2):
                at = 384 * k + 192 * x
                s_ref[at : at + 48, 384 * y : 384 * y + 384] = x_first(96, y, x, 2 * n + k)
                s_ref[at + 48 : at + 96, 384 * y : 384 * y + 384] = y_first(96, y, x, 2 * n + k)
                s_ref[at + 96 : at + 192, 384 * y : 384 * y + 384] = z_last(y, x, 2 * n + k)
    half = br_own.shape[0]

    @pl.when(pl.program_id(0) == 0)
    def _():
        for out in (part_own, part_far, gn2):
            out[...] = jnp.zeros_like(out)
        br[0:half], br[half:] = br_own[...], br_far[...]

    e, s = e_ref[...], s_ref[...]
    pre = dot_nn(n2[...], e) + bias[0]
    grad_act = dot_nt(br[...], s)
    cdf = 0.5 * (1.0 + lax.erf(pre * math.sqrt(0.5)))
    act = (pre * cdf).astype(BF)
    slope = cdf + pre * (jnp.exp(-0.5 * pre * pre) * (1.0 / math.sqrt(2.0 * math.pi)))
    grad_pre = (grad_act * slope).astype(BF)
    y = dot_nn(act, s)
    part_own[...] += y[:half]
    part_far[...] += y[half:]
    gn2[...] += dot_nt(grad_pre, e)
    grad = dot_nn(act.astype(F32).T.astype(BF), br[...]).astype(BF)
    for y in range(2):
        for b in range(4):
            block = grad[192 * b : 192 * b + 192, 384 * y : 384 * y + 384]
            s_x[y, b], s_y[y, b], s_z[y, b] = block[0:48], block[48:96], block[96:192]
    grad = dot_nn(n2t[...], grad_pre).astype(BF)
    for p, out in ((0, e_x), (1, e_y)):
        out[0] = grad[:, 384 * p : 384 * p + 384].reshape(8, 96, 384)
    d_bias[0] = jnp.sum(grad_pre.astype(F32), axis=0, keepdims=True)


def mid_back_kernel(ids, gn_here, gn_there, att_own, att_far, br_own, br_far, mixed_t, m, vec, gatt, gm, dm, sums, low):
    first, c = ids[0] == 0, ids[0]
    half = att_own.shape[0]
    for to, att, br_ref in ((0, att_own, br_own), (half, att_far, br_far)):
        gn = gn_here[to : to + half, :] + gn_there[half - to : 2 * half - to, :]
        br = br_ref[...].astype(F32)
        xhat, spread = normalize(att[...])
        grad = br + norm_back(xhat, spread, vec[2:3, :], gn)
        low[to : to + half, :] = grad.astype(BF)
        if to == 0:
            gatt[...] = grad
            sums[0:1] = jnp.sum(gn * xhat, axis=0, keepdims=True)
            sums[1:2] = jnp.sum(gn, axis=0, keepdims=True)
            sums[2:3] = jnp.sum(grad.astype(BF).astype(F32), axis=0, keepdims=True)
            sums[3:4] = jnp.sum(br, axis=0, keepdims=True)
            sums[4:8] = jnp.zeros((4, sums.shape[1]), F32)
    for k in range(2):
        rows = m[pl.ds(pl.multiple_of(192 * (2 * k + c), 192), 192), :]
        gm[:, 192 * k : 192 * k + 192] = dot_nt(low[...], rows).astype(BF)
        both = low[:, 384 * k : 384 * k + 384]
        mine = jnp.where(first, lanes(both, 0), lanes(both, 1))
        weight = dot_nn(mixed_t[...], mine).astype(BF)
        for b in range(8):
            dm[8 * k + b, :, :192] = weight[96 * b : 96 * b + 48]
            dm[8 * k + b, :, 192:] = weight[96 * b + 48 : 96 * b + 96]


def triple_back_kernel(ids, n1_ref, d3, t3, d_qv, d_k, gn, sums):
    c = ids[0]
    j = pl.program_id(0)
    d = d3[0]
    half = gn.shape[1]
    weight = dot_nn(n1_ref[...], d).astype(BF)
    part = dot_nt(d, t3[0])
    sums[0] = jnp.sum(d.astype(F32), axis=0, keepdims=True)

    @pl.when(j == 0)
    def _():
        gn[c] = part[:half]
        gn[1 - c] = part[half:]

    @pl.when(j > 0)
    def _():
        gn[c] += part[:half]
        gn[1 - c] += part[half:]

    @pl.when(j < 2)
    def _():
        d_qv[0] = weight

    @pl.when(j == 2)
    def _():
        for b in range(8):
            for y in range(2):
                d_k[y, b, :, :192] = weight[96 * b : 96 * b + 48, 192 * y : 192 * y + 192]
                d_k[y, b, :, 192:] = weight[96 * b + 48 : 96 * b + 96, 192 * y : 192 * y + 192]


def first_back_kernel(ids, gn_both, tok, gatt, vec, sums2, sums1, d_bias, out, blocks, table):
    c = ids[0]
    gn = gn_both[0] + gn_both[1]
    xhat, spread = normalize(tok[...].astype(F32))
    out[...] = (gatt[...] + norm_back(xhat, spread, vec[0:1, :], gn)).astype(BF)
    table[12:16] = jnp.zeros((4, table.shape[1]), F32)
    table[0:1] = jnp.sum(gn * xhat, axis=0, keepdims=True)
    table[1:2] = jnp.sum(gn, axis=0, keepdims=True)
    table[2:4] = sums2[0:2]
    table[6:8] = sums2[2:4]
    for row, sums in [(4, sums1[0]), (5, sums1[1])] + [(8 + n, d_bias[n]) for n in range(4)]:
        for k in range(2):
            for p in range(2):
                at = 192 * (2 * k + p)
                table[row : row + 1, at : at + 192] = jnp.where(c == p, lanes(sums, k), 0.0)
    blocks[...] = jnp.zeros_like(blocks)
    for b in range(8):
        blocks[b, :, 0:96] = table[:, 96 * b : 96 * b + 96].astype(BF)


def halves(rows):
    return rows[:, :192], rows[:, 192:]


def fetch(refs, places, sems):
    copies = [pltpu.make_async_copy(ref, place, sems.at[i]) for i, (ref, place) in enumerate(zip(refs, places))]
    for copy in copies:
        copy.start()
    for copy in copies:
        copy.wait()


def adam_into(state, outs, rate, decay, at, grad):
    new = adamw(state[0][at], state[1][at], state[2][at], grad, rate, decay)
    for out, value in zip(outs, new):
        out[at] = value


def triple_units(t, total):
    a, b = halves(total[0:96])
    k = jnp.concatenate(halves(total[96:144]), axis=0)
    return a, b, k


def forward_total(own, far):
    total = own[...].astype(F32) + far[...].astype(F32)
    return jnp.concatenate([total[0:96], total[144:240], total[96:144], total[240:288], total[288:384]], axis=0)


def give_back_kernel(ids, t_own, t_far, es_own, es_far, give):
    first, t = ids[0] == 0, ids[1]
    total = t_own[...].astype(F32) + t_far[...].astype(F32)
    a, b, k = triple_units(t, total)
    give[0:96] = jnp.where(t == 1, a, jnp.where(t == 2, b, k))
    give[96:112] = jnp.zeros((16, 192), F32)
    give[96:112, 0:96] = total[192:208, 0:96]
    total = forward_total(es_own, es_far)
    give[112:208], give[208:304] = halves(jnp.where(first, total[96:192], total[0:96]))
    s0, s1 = halves(total[192:])
    give[304:496] = jnp.where(first, s1, s0)


def prefetch_kernel(_, *refs):
    fetch(refs[: len(refs) // 2], refs[len(refs) // 2 : -1], refs[-1])


def update_kernel(ids, t_own, t_far, es_own, es_far, took, *refs):
    state, outs = refs[:15], refs[15:]
    first, c, t = ids[0] == 0, ids[0], ids[1]
    every = slice(None)
    total = t_own[...].astype(F32) + t_far[...].astype(F32)
    a, b, k = triple_units(t, total)
    units = (
        jnp.where(t == 1, b, jnp.where(t == 2, k, a)),
        took[0:96],
        jnp.where(t == 1, k, jnp.where(t == 2, a, b)),
    )
    for i, unit in enumerate(units):
        adam_into(state[0:3], outs[0:4], RATES[0], DECAYS[0], (every, slice(192 * i, 192 * i + 192)), unit)
    for i, part in enumerate(halves(total[144:192])):
        adam_into(state[3:6], outs[4:8], RATES[1], DECAYS[1], (slice(48 * i, 48 * i + 48), every), part)
    total_es = forward_total(es_own, es_far)
    e = halves(jnp.where(first, total_es[0:96], total_es[96:192]))
    s0, s1 = halves(total_es[192:])
    s = jnp.where(first, s0, s1)
    for p in range(2):
        for j in range(2):
            grad = jnp.where(c == p, e[j], took[112 + 96 * j : 208 + 96 * j])
            at = 384 * j + 192 * p
            adam_into(state[6:9], outs[8:12], RATES[2], DECAYS[2], (every, slice(at, at + 192)), grad)
        grad = jnp.where(c == p, s, took[304:496]).T
        adam_into(state[9:12], outs[12:16], RATES[3], DECAYS[3], (every, slice(192 * p, 192 * p + 192)), grad)
    adam_into(state[12:15], outs[16:20], RATES[4], DECAYS[4], (every, every), total[192:204, 0:96] + took[96:108, 0:96])


def by_core(c, own, far):
    return jnp.where(c == 0, jnp.stack([own, far]), jnp.stack([far, own]))


def per_device(
    cube_tokens, visible, live_counts, block_cotangent,
    triple_master, triple_first, triple_second,
    mixing_master, mixing_first, mixing_second,
    expand_master, expand_first, expand_second,
    shrink_master, shrink_first, shrink_second,
    vector_master, vector_first, vector_second,
):
    y, c, b = lax.axis_index("y"), lax.axis_index("core"), lax.axis_index("blk")
    bits = (y, b & 1, b >> 1 & 1, b >> 2)
    turn = b % 4
    unturn = (4 - turn) % 4
    region, feats = cube_tokens.shape[1:]
    slots = visible.shape[1]
    slot_axis = jnp.arange(slots, dtype=jnp.int32)

    t_id = 2 * y + c
    ids = jnp.stack([c, t_id, y, bits[1], b >> 1]).astype(jnp.int32)
    shrink_t = shrink_master.T
    took = swap(call(
        give_kernel, shape(480, 192, dtype=BF), "give", 1e10, 1e3, in_specs=[SM, VM, VM, VM], out_specs=VM,
    )(ids, triple_master, expand_master, shrink_t), dc=1)
    tvm, es, last = call(
        pack_kernel, (shape(208, 384, dtype=BF), shape(288, 384, dtype=BF), shape(96, 384, dtype=BF)), "pack", 1e10, 1e3,
        in_specs=[SM] + [VM] * 6, out_specs=(VM, VM, VM),
    )(ids, took, triple_master, mixing_master, expand_master, shrink_t, vector_master)

    t_far = swap(tvm, db=4)
    last_in = swap(last, db=1)

    visible, block_cotangent, tvm, es, last = tie(visible, block_cotangent, tvm, es, last)
    def turned(x):
        return lax.dynamic_slice_in_dim(jnp.concatenate([x, x]), turn, 4, 0)

    local = visible % region
    flat_index = turned(local + region * jnp.arange(4, dtype=jnp.int32)[:, None])
    picked = jnp.take(cube_tokens.reshape(-1, feats), flat_index.reshape(-1), axis=0).reshape(4, slots, feats)
    counts = jnp.broadcast_to(turned(live_counts)[:, :, None].astype(BF), (4, 16, feats))
    live_here = slot_axis[None, :] < live_counts
    masked = turned(jnp.where(live_here[:, :, None], block_cotangent, jnp.zeros((), BF)))
    packet = jnp.concatenate([picked, masked, counts], axis=1)

    def packets(*steps):
        return [lax.ppermute(packet[s], FINE, cube_pairs(s, False)) for s in steps]

    last = jnp.stack([last, last_in])
    last_in = swap(last, dy=1)
    t_far, packet, es, last_in = tie(t_far, packet, es, last_in)
    tvm = jnp.stack([tvm, t_far])
    t_far = swap(tvm, db=2)
    last = jnp.stack([last, last_in]).reshape(384, 384)
    es_far = swap(jnp.concatenate([es, last], axis=0), db=4)
    own = packets(0, 1)

    t_far, packet = tie(t_far, packet)
    tvm = jnp.stack([tvm, t_far]).reshape(4, 208, 384)
    qv, rest = tvm[:, :96], tvm[:, 96:]
    qv_x, rest_y = swap(qv, db=1), swap(rest, dy=1)

    qv_x, rest_y, own, packet = tie(qv_x, rest_y, own, packet)
    qv = jnp.stack([qv, qv_x]).reshape(8, 96, 384)
    rest = jnp.stack([rest, rest_y]).reshape(8, 112, 384)
    qv_far, rest_far = swap(qv, dy=1), swap(rest, db=1)
    es_far, last = tie(es_far, last)
    el = jnp.stack([last, es_far[288:]]).reshape(8, 96, 384)
    es = jnp.stack([es, es_far[:288]])
    es_far = swap(es, db=2)
    own = own + packets(2, 3)

    qv_far, rest_far, es_far, own = tie(qv_far, rest_far, es_far, own)
    es = jnp.stack([es, es_far]).reshape(4, 288, 384)
    ea, eb = es[:, :144], es[:, 144:]
    ea_in, eb_in = swap(ea, db=1), swap(eb, dy=1)
    el_far = swap(el, db=2)
    own = jnp.stack(own)
    far = swap(own, dc=1)

    rows = 4 * slots
    tok_own, tok_far = [p[:, :slots].reshape(rows, feats) for p in (own, far)]
    br_own, br_far = [p[:, slots : 2 * slots].reshape(rows, feats) for p in (own, far)]
    cnt = jnp.concatenate([own[:, 2 * slots, :1], far[:, 2 * slots, :1]]).astype(jnp.int32)
    live = (slot_axis[None, :] < cnt).reshape(2 * rows, 1)
    live_cols = jnp.broadcast_to(live.astype(F32), (2 * rows, 128))

    n1, x3, t3, mix, vec, e_bias = call(
        qkv_kernel,
        (shape(feats, 2 * rows, dtype=BF), shape(3, 2 * rows, 384, dtype=BF), shape(3, feats, 384, dtype=BF),
         shape(2, 2 * rows + feats, 384, dtype=BF), shape(16, feats), shape(4, 1, 384)),
        "qkv", 2 * 512 * 768 * 1152, 8e6,
        in_specs=[SM] + [VM] * 6, out_specs=(VM,) * 6, scratch_shapes=[pltpu.VMEM((8, 384), F32), pltpu.VMEM((2 * rows, feats), BF)],
    )(ids, tok_own, tok_far, qv, qv_far, rest, rest_far)
    x3, mix, ea_in, eb_in = tie(x3, mix, ea_in, eb_in)
    ea = jnp.stack([ea, ea_in]).reshape(8, 144, 384)
    eb = jnp.stack([eb, eb_in]).reshape(8, 144, 384)
    ea_far, eb_far = swap(ea, dy=1), swap(eb, db=1)

    pairs3 = pl.BlockSpec((3, 2 * rows, 128), lambda i: (0, 0, i))
    col = pl.BlockSpec((2 * rows, 128), lambda i: (0, i))
    same = pl.BlockSpec((2 * rows, 128), lambda i: (0, 0))
    traded = trade(call(
        attn_kernel, shape(2, 2 * rows + feats, 384, dtype=BF), "attention", 6e9, 2e6,
        grid=(3,), in_specs=[SM, pairs3, same, pl.BlockSpec(memory_space=pl.ANY)],
        out_specs=pl.BlockSpec((2, 2 * rows, 128), lambda i: (0, 0, i)), input_output_aliases={3: 0},
    )(ids, x3, live_cols, mix))
    att, att_far, n2, n2t, mix, mixed = call(
        mid_kernel,
        (shape(rows, feats), shape(rows, feats), shape(2 * rows, feats, dtype=BF), shape(feats, 2 * rows, dtype=BF),
         shape(feats, feats, dtype=BF), shape(feats, 2 * rows, dtype=BF)),
        "mixing", 3e9, 5e6, in_specs=[SM] + [VM] * 4, out_specs=(VM,) * 6,
        scratch_shapes=[pltpu.VMEM((2 * rows, feats), BF)],
    )(ids, tok_own, tok_far, traded, vec)

    whole = pl.BlockSpec((rows, feats), lambda i: (0, 0))

    gathered = [pl.BlockSpec((8, r, 384), lambda n: (0, 0, 0)) for r in (144, 144, 144, 144, 96, 96)]
    every = pl.BlockSpec((2 * rows, feats), lambda i: (0, 0))
    part_own, part_give, gn2, e_x, e_y, s_x, s_y, d_z, d_b = call(
        ffn_kernel,
        (shape(rows, feats),) * 2
        + (shape(2 * rows, feats),) + (shape(2, 8, 96, 384, dtype=BF),) * 2 + (shape(2, 8, 48, 384, dtype=BF),) * 2
        + (shape(2, 8, 96, 384, dtype=BF), shape(2, 1, 768)),
        "feed_forward", 18e9, 20e6, 46,
        grid=(2,),
        in_specs=[SM, every, pl.BlockSpec((feats, 2 * rows), lambda n: (0, 0))] + [whole] * 2 + gathered
        + [pl.BlockSpec((1, 1, 768), lambda n: (n, 0, 0))],
        out_specs=(
            whole, whole, every,
            pl.BlockSpec((1, 8, 96, 384), lambda n: (n, 0, 0, 0)),
            pl.BlockSpec((1, 8, 96, 384), lambda n: (n, 0, 0, 0)),
            pl.BlockSpec((2, 4, 48, 384), lambda n: (0, n, 0, 0)),
            pl.BlockSpec((2, 4, 48, 384), lambda n: (0, n, 0, 0)),
            pl.BlockSpec((2, 4, 96, 384), lambda n: (0, n, 0, 0)),
            pl.BlockSpec((1, 1, 768), lambda n: (n, 0, 0)),
        ),
        scratch_shapes=[pltpu.VMEM((2 * rows, feats), BF), pltpu.VMEM((feats, 768), BF), pltpu.VMEM((768, feats), BF)],
    )(ids, n2, n2t, br_own, br_far, ea, ea_far, eb, eb_far, el, el_far, e_bias.reshape(2, 1, 768))

    mx, z0, z1 = bits[1], bits[2], bits[3]
    gn2_far = swap(gn2, dc=1)
    d_z = d_z.reshape(2, 2, 2, 2, 96, 384)

    def x_part(at):
        return jnp.concatenate([pick(e_x.reshape(2, 4, 2, 96, 384), at, 2), pick(s_x.reshape(2, 4, 2, 48, 384), at, 2)], axis=2)

    def y_part(at):
        return jnp.concatenate([pick(e_y, at, 0), pick(s_y, at, 0)], axis=1)

    x_in = swap(x_part(1 - mx), db=1)
    y_in = swap(y_part(1 - y), dy=1)
    z_in = swap(pick(d_z, 1 - z0, 2), db=2)

    gatt, gm, dm, sums2 = call(
        mid_back_kernel,
        (shape(rows, feats), shape(2 * rows, 384, dtype=BF), shape(16, 48, 384, dtype=BF), shape(8, feats)),
        "mixing_back", 6e9, 8e6, in_specs=[SM] + [VM] * 9, out_specs=(VM,) * 4,
        scratch_shapes=[pltpu.VMEM((2 * rows, feats), BF)],
    )(ids, gn2, gn2_far, att, att_far, br_own, br_far, mixed, mix, vec)
    d3 = call(
        attn_back_kernel, shape(3, 2 * rows, 384, dtype=BF), "attention_back", 9e9, 5e6,
        grid=(3,), in_specs=[pairs3, col, same], out_specs=pairs3,
    )(x3, gm, live_cols)

    third = pl.BlockSpec((1, 2 * rows, 384), lambda j: (j, 0, 0))
    d_qv, d_k, gn1, sums1 = call(
        triple_back_kernel,
        (shape(2, feats, 384, dtype=BF), shape(2, 8, 48, 384, dtype=BF), shape(2, rows, feats), shape(3, 1, 384)),
        "triple_back", 5e9, 5e6,
        grid=(3,),
        in_specs=[SM, pl.BlockSpec((feats, 2 * rows), lambda j: (0, 0)), third, pl.BlockSpec((1, feats, 384), lambda j: (j, 0, 0))],
        out_specs=(
            pl.BlockSpec((1, feats, 384), lambda j: (jnp.minimum(j, 1), 0, 0)),
            pl.BlockSpec((2, 8, 48, 384), lambda j: (0, 0, 0, 0)),
            pl.BlockSpec((2, rows, feats), lambda j: (0, 0, 0)),
            pl.BlockSpec((1, 1, 384), lambda j: (j, 0, 0)),
        ),
    )(ids, n1, d3, t3)

    gn1 = trade(gn1)
    grad_tok, blocks = call(
        first_back_kernel, (shape(rows, feats, dtype=BF), shape(8, 16, 384, dtype=BF)), "first_back", 1e9, 1e6,
        in_specs=[SM] + [VM] * 7, out_specs=(VM, VM), scratch_shapes=[pltpu.VMEM((16, feats), F32)],
    )(ids, gn1, tok_own, gatt, vec, sums2, sums1, d_b.reshape(4, 1, 384))

    blocks = jnp.broadcast_to(blocks, (2, 8, 16, 384))
    d_qv = d_qv.reshape(2, 4, 2, 96, 384)
    d_km = jnp.concatenate([d_k, dm.reshape(2, 8, 48, 384), blocks], axis=2).reshape(2, 4, 2, 112, 384)
    qv_in = swap(pick(d_qv, 1 - bits[1], 2), db=1)
    km_in = swap(pick(d_km, 1 - y, 0), dy=1)

    x_in, y_in, z_in, grad_tok, part_give = tie(x_in, y_in, z_in, grad_tok, part_give)
    d_x = add_low(x_part(mx), x_in)
    d_y = add_low(y_part(y), y_in).reshape(4, 2, 144, 384)
    x_in = swap(pick(d_x, 1 - y, 0), dy=1)
    y_in = swap(pick(d_y, 1 - mx, 1), db=1)

    part_far = swap(part_give, dc=1)
    result = att + (part_own + part_far + vec[7])
    result = jnp.where(live[:rows], result, 0.0).astype(BF).reshape(4, slots, feats)
    packet = jnp.concatenate([result, grad_tok.reshape(4, slots, feats)], axis=1)

    def go_back(step, *after):
        part = tie(packet[step], *after)[0]
        return lax.ppermute(part, FINE, cube_pairs(step, True))

    back = [go_back(0)]
    back += [go_back(1, back[0])]

    qv_in, km_in, back, packet = tie(qv_in, km_in, back, packet)
    d_qv = add_low(pick(d_qv, mx, 2), qv_in)
    d_km = add_low(pick(d_km, y, 0), km_in)
    qv_in = swap(pick(d_qv, 1 - y, 0), dy=1)
    km_in = swap(pick(d_km, 1 - mx, 1), db=1)
    back += [go_back(2)]
    back += [go_back(3)]

    x_in, y_in, z_in, packet = tie(x_in, y_in, z_in, packet)
    d_es = jnp.concatenate(
        [add_low(pick(d_x, y, 0), x_in), add_low(pick(d_y, mx, 1), y_in)], axis=1
    ).reshape(2, 2, 288, 384)
    es_in = swap(pick(d_es, 1 - z0, 1), db=2)
    d_z = add_low(pick(d_z, z0, 2), z_in)
    z_in = swap(pick(d_z, 1 - y, 0), dy=1)

    qv_in, km_in, z_in = tie(qv_in, km_in, z_in)
    d_t = jnp.concatenate(
        [add_low(pick(d_qv, y, 0), qv_in), add_low(pick(d_km, mx, 1), km_in)], axis=1
    ).reshape(2, 2, 208, 384)
    t_in = swap(pick(d_t, 1 - z0, 1), db=2)
    d_z = add_low(pick(d_z, y, 0), z_in)
    z_in = swap(pick(d_z, 1 - mx, 1), db=1)

    es_in, t_keep = tie(es_in, d_t)
    es_keep = d_es = add_low(pick(d_es, z0, 1), es_in)
    es_in = swap(pick(d_es, 1 - z1, 0), db=4)
    t_in, z_in = tie(t_in, z_in)
    d_t = add_low(pick(d_t, z0, 1), t_in)
    t_in = swap(pick(d_t, 1 - z1, 0), db=4)
    d_z = add_low(pick(d_z, mx, 1), z_in)
    z_in = swap(pick(d_z, 1 - z1, 0), db=4)

    state = (triple_master, triple_first, triple_second, mixing_master, mixing_first, mixing_second,
             expand_master, expand_first, expand_second, shrink_t, shrink_first.T, shrink_second.T,
             vector_master, vector_first, vector_second)
    ids_late = ids + jnp.isnan(es_keep[0, 0, 0]).astype(jnp.int32)
    ready = call(
        prefetch_kernel, tuple(shape(*a.shape) for a in state), "prefetch", 1e10, 1e3,
        in_specs=[SM] + [pl.BlockSpec(memory_space=pltpu.HBM)] * len(state), out_specs=(VM,) * len(state),
        scratch_shapes=[pltpu.SemaphoreType.DMA((len(state),))],
    )(ids_late, *state)

    back = jnp.stack(back)
    back = lax.dynamic_slice_in_dim(jnp.concatenate([back, back]), unturn, 4, 0)
    block_output = back[:, :slots]
    spread = (jnp.arange(region, dtype=jnp.int32)[None, :, None] == local[:, None, :]).astype(BF)
    token_grads = jnp.einsum("grs,gsf->grf", spread, back[:, slots:], preferred_element_type=F32).astype(BF)

    t_in, es_in, z_in, token_grads, block_output, ready = tie(t_in, es_in, z_in, token_grads, block_output, ready)
    grads = (pick(d_t, z1, 0), t_in, jnp.concatenate([pick(d_es, z1, 0), pick(d_z, z1, 0)]), jnp.concatenate([es_in, z_in]))
    took = swap(call(
        give_back_kernel, shape(496, 192), "give_back", 1e6, 1e6, in_specs=[SM] + [VM] * 4, out_specs=VM,
    )(ids, *grads), dc=1)

    def whole_of(a):
        return pl.BlockSpec(a.shape, lambda i: (0,) * len(a.shape))

    outs = tuple(shape(*a.shape, dtype=d) for a in state[::3] for d in (F32, F32, F32, BF))
    new = call(
        update_kernel, outs, "update", 1e8, 4e6, grid=(1,),
        in_specs=[SM] + [whole_of(a) for a in (*grads, took, *state)], out_specs=tuple(whole_of(o) for o in outs),
    )(ids, *grads, took, *ready)
    return (block_output, token_grads, *new[:12], *(o.T for o in new[12:16]), *new[16:])


def layer_norm(rows, gain, shift):
    center = rows - jnp.mean(rows, axis=-1, keepdims=True)
    spread = lax.rsqrt(jnp.mean(center * center, axis=-1, keepdims=True) + 1e-06)
    return center * spread * gain + shift


def outer_sum(left, right):
    return lax.dot_general(
        left, right, (((0,), (0,)), ((), ())), preferred_element_type=jnp.float32
    )


def back_product(grads, weight):
    return lax.dot_general(
        grads, weight, (((1,), (1,)), ((), ())), preferred_element_type=jnp.float32
    )


def masked_scores(queries, key_all, live_all):
    raw = jnp.einsum("gshe,gthe->ghst", queries, key_all, preferred_element_type=jnp.float32) * (
        1.0 / math.sqrt(HD)
    )
    return jnp.where(live_all[:, None, None, :] > 0, raw, -1e30)


def cycle_section(triple_grad, mixing_grad, expand_grad, shrink_grad, vector_grad):
    summed = (
        lax.psum_scatter(triple_grad, "blk", scatter_dimension=0, tiled=True),
        lax.psum_scatter(mixing_grad, "blk", scatter_dimension=0, tiled=True),
        lax.psum_scatter(expand_grad, "blk", scatter_dimension=0, tiled=True),
        lax.psum_scatter(shrink_grad, "blk", scatter_dimension=0, tiled=True),
        lax.psum_scatter(vector_grad, "blk", scatter_dimension=1, tiled=True),
    )
    return (summed[0], summed[1], summed[2], summed[3], summed[4])


def group_section(triple_grad, mixing_grad, expand_grad, shrink_grad, vector_grad):
    summed = (
        lax.psum_scatter(triple_grad, "batch", scatter_dimension=1, tiled=True),
        lax.psum_scatter(mixing_grad, "batch", scatter_dimension=1, tiled=True),
        lax.psum_scatter(expand_grad, "batch", scatter_dimension=1, tiled=True),
        lax.psum_scatter(shrink_grad, "batch", scatter_dimension=1, tiled=True),
    )
    vector_sum = lax.psum(vector_grad, "batch")
    return (summed[0], summed[1], summed[2], summed[3], vector_sum)


def per_device_any(
    cube_tokens,
    visible,
    live_counts,
    block_cotangent,
    triple_master,
    triple_first,
    triple_second,
    mixing_master,
    mixing_first,
    mixing_second,
    expand_master,
    expand_first,
    expand_second,
    shrink_master,
    shrink_first,
    shrink_second,
    vector_master,
    vector_first,
    vector_second,
):
    low_copies = (
        lax.all_gather(triple_master.astype(jnp.bfloat16), "blk", axis=0, tiled=True),
        lax.all_gather(mixing_master.astype(jnp.bfloat16), "blk", axis=0, tiled=True),
        lax.all_gather(expand_master.astype(jnp.bfloat16), "blk", axis=0, tiled=True),
        lax.all_gather(shrink_master.astype(jnp.bfloat16), "blk", axis=0, tiled=True),
        lax.all_gather(vector_master.astype(jnp.bfloat16), "blk", axis=1, tiled=True),
    )
    triple_w, mixing_w, expand_w, shrink_w = (
        lax.all_gather(low_copies[0], "batch", axis=1, tiled=True),
        lax.all_gather(low_copies[1], "batch", axis=1, tiled=True),
        lax.all_gather(low_copies[2], "batch", axis=1, tiled=True),
        lax.all_gather(low_copies[3], "batch", axis=1, tiled=True),
    )
    vector_w = low_copies[4].astype(jnp.float32)
    groups, slot_count = visible.shape
    region = cube_tokens.shape[1]
    features = cube_tokens.shape[2]
    row_count = groups * slot_count
    head_count = features // HD
    local_index = visible % region
    tokens = jnp.take_along_axis(cube_tokens, local_index[:, :, None], axis=1).astype(jnp.float32)
    flat_tokens = tokens.reshape(row_count, features)
    live_mask = jnp.arange(slot_count, dtype=jnp.int32)[None, :] < live_counts
    live_rows = live_mask.reshape(row_count, 1)
    normed1 = layer_norm(flat_tokens, vector_w[0], vector_w[1]).astype(jnp.bfloat16)
    zero_bias = jnp.zeros((features,), jnp.float32)
    triple_bias = jnp.concatenate([vector_w[4], zero_bias, vector_w[5]])
    triple = (jnp.dot(normed1, triple_w, preferred_element_type=jnp.float32) + triple_bias).astype(
        jnp.bfloat16
    )
    triple = triple.reshape(groups, slot_count, 3 * features)
    query_flat = triple[:, :, :features]
    queries = query_flat.reshape(groups, slot_count, head_count, HD)
    key_rows = triple[:, :, features : 2 * features]
    value_rows = triple[:, :, 2 * features :]
    key_all, value_all, live_all = (
        lax.all_gather(key_rows, "blk", axis=1, tiled=True),
        lax.all_gather(value_rows, "blk", axis=1, tiled=True),
        lax.all_gather(live_mask.astype(jnp.bfloat16), "blk", axis=1, tiled=True),
    )
    key_all = key_all.reshape(groups, -1, head_count, HD)
    value_all = value_all.reshape(groups, -1, head_count, HD)
    scores = masked_scores(queries, key_all, live_all)
    peak = jnp.max(scores, axis=-1, keepdims=True)
    expo = jnp.exp(scores - peak)
    total = jnp.sum(expo, axis=-1, keepdims=True)
    prob_low = (expo / total).astype(jnp.bfloat16)
    mixed = jnp.einsum("ghst,gthe->gshe", prob_low, value_all, preferred_element_type=jnp.float32)
    mixed = mixed.astype(jnp.bfloat16).reshape(row_count, features)
    attended = flat_tokens + (
        jnp.dot(mixed, mixing_w, preferred_element_type=jnp.float32) + vector_w[6]
    )
    normed2 = layer_norm(attended, vector_w[2], vector_w[3]).astype(jnp.bfloat16)
    preact = jnp.dot(normed2, expand_w, preferred_element_type=jnp.float32) + vector_w[8:].reshape(
        -1
    )
    activation = jax.nn.gelu(preact, approximate=False).astype(jnp.bfloat16)
    result = attended + (
        jnp.dot(activation, shrink_w, preferred_element_type=jnp.float32) + vector_w[7]
    )
    result = jnp.where(live_rows, result, 0.0)
    block_output = result.astype(jnp.bfloat16).reshape(groups, slot_count, features)
    grad_out = jnp.where(
        live_rows, block_cotangent.reshape(row_count, features).astype(jnp.float32), 0.0
    )
    branch_low = grad_out.astype(jnp.bfloat16)
    shrink_grad = outer_sum(activation, branch_low)
    shrink_bias_grad = jnp.sum(branch_low.astype(jnp.float32), axis=0)
    grad_act = back_product(branch_low, shrink_w)
    gelu_value, gelu_back = jax.vjp(partial(jax.nn.gelu, approximate=False), preact)
    grad_pre = gelu_back(grad_act)[0].astype(jnp.bfloat16)
    expand_grad = outer_sum(normed2, grad_pre)
    expand_bias_grad = jnp.sum(grad_pre.astype(jnp.float32), axis=0)
    grad_normed2 = back_product(grad_pre, expand_w)
    norm2_value, norm2_back = jax.vjp(layer_norm, attended, vector_w[2], vector_w[3])
    grad_through2, gain2_grad, shift2_grad = norm2_back(grad_normed2)
    grad_attended = grad_out + grad_through2
    mix_low = grad_attended.astype(jnp.bfloat16)
    mixing_grad = outer_sum(mixed, mix_low)
    mixing_bias_grad = jnp.sum(mix_low.astype(jnp.float32), axis=0)
    grad_mixed_flat = (
        back_product(mix_low, mixing_w).astype(jnp.bfloat16).reshape(groups, slot_count, features)
    )
    grad_mixed = grad_mixed_flat.reshape(groups, slot_count, head_count, HD)
    scores = masked_scores(queries, key_all, live_all)
    probs = jnp.exp(scores - peak) / total
    prob_low = probs.astype(jnp.bfloat16)
    grad_probs = jnp.einsum(
        "gshe,gthe->ghst", grad_mixed, value_all, preferred_element_type=jnp.float32
    )
    delta = jnp.sum(probs * grad_probs, axis=-1, keepdims=True)
    grad_scores = (probs * (grad_probs - delta)).astype(jnp.bfloat16)
    score_scale = 1.0 / math.sqrt(HD)
    grad_queries = (
        jnp.einsum("ghst,gthe->gshe", grad_scores, key_all, preferred_element_type=jnp.float32)
        * score_scale
    )
    term_keys = (
        jnp.einsum("ghst,gshe->gthe", grad_scores, queries, preferred_element_type=jnp.float32)
        * score_scale
    )
    term_values = jnp.einsum(
        "ghst,gshe->gthe", prob_low, grad_mixed, preferred_element_type=jnp.float32
    )
    grad_keys, grad_values = (
        lax.psum_scatter(
            term_keys.reshape(groups, -1, features), "blk", scatter_dimension=1, tiled=True
        ),
        lax.psum_scatter(
            term_values.reshape(groups, -1, features), "blk", scatter_dimension=1, tiled=True
        ),
    )
    grad_triple = jnp.concatenate(
        [
            grad_queries.reshape(row_count, features),
            grad_keys.reshape(row_count, features),
            grad_values.reshape(row_count, features),
        ],
        axis=1,
    ).astype(jnp.bfloat16)
    triple_grad = outer_sum(normed1, grad_triple)
    triple_sums = jnp.sum(grad_triple.astype(jnp.float32), axis=0)
    grad_normed1 = back_product(grad_triple, triple_w)
    norm1_value, norm1_back = jax.vjp(layer_norm, flat_tokens, vector_w[0], vector_w[1])
    grad_through1, gain1_grad, shift1_grad = norm1_back(grad_normed1)
    grad_tokens = (grad_attended + grad_through1).reshape(groups, slot_count, features)
    cube_rows = jnp.arange(groups, dtype=jnp.int32)[:, None]
    token_grads = (
        jnp.zeros(cube_tokens.shape, jnp.float32)
        .at[cube_rows, local_index]
        .add(grad_tokens)
        .astype(jnp.bfloat16)
    )
    leading_rows = jnp.stack(
        [
            gain1_grad,
            shift1_grad,
            gain2_grad,
            shift2_grad,
            triple_sums[:features],
            triple_sums[2 * features :],
            mixing_bias_grad,
            shrink_bias_grad,
        ]
    )
    vector_grad = jnp.concatenate([leading_rows, expand_bias_grad.reshape(-1, features)], axis=0)
    reduced = group_section(triple_grad, mixing_grad, expand_grad, shrink_grad, vector_grad)
    reduced = cycle_section(reduced[0], reduced[1], reduced[2], reduced[3], reduced[4])
    masters = (triple_master, mixing_master, expand_master, shrink_master, vector_master)
    firsts = (triple_first, mixing_first, expand_first, shrink_first, vector_first)
    seconds = (triple_second, mixing_second, expand_second, shrink_second, vector_second)
    outputs = [block_output, token_grads]
    for master, first, second, grad, rate, decay in zip(
        masters, firsts, seconds, reduced, RATES, DECAYS
    ):
        outputs.extend(adamw(master, first, second, grad, rate, decay))
    return tuple(outputs)


def solution(mesh):
    groups, blocks = mesh.shape["batch"], mesh.shape["blk"]
    if (groups, blocks) == (4, 8):
        mesh = Mesh(mesh.devices.reshape(2, 2, 8), FINE)
        batch, body = ("y", "core"), per_device
    else:
        batch, body = "batch", per_device_any
    rows = P(batch, "blk", None)
    part = P("blk", batch)
    table = P(None, "blk")
    in_specs = (rows, P(batch, "blk"), P(batch, "blk"), rows) + (part,) * 12 + (table,) * 3
    out_specs = (rows, rows) + (part,) * 16 + (table,) * 4
    return jax.shard_map(body, mesh=mesh, in_specs=in_specs, out_specs=out_specs, check_vma=False)
```

```python
from functools import partial
import math

import jax
import jax.numpy as jnp
from jax import lax
from jax.experimental import pallas as pl
from jax.experimental.pallas import tpu as pltpu
from jax.sharding import Mesh, PartitionSpec as P

HD = 64
STEP = 10
BF = jnp.bfloat16
F32 = jnp.float32

RATES = (0.04, 0.3, 0.04, 0.02, 0.25)
DECAYS = (0.05, 0.05, 0.05, 0.05, 0.0)


def adamw(master, first, second, grad, rate, decay):
    first_new = 0.9 * first + 0.1 * grad
    second_new = 0.999 * second + 0.001 * grad * grad
    corrected = first_new / (1.0 - 0.9**STEP) / (jnp.sqrt(second_new / (1.0 - 0.999**STEP)) + 1e-08)
    master_new = master - rate * (corrected + decay * master)
    return (first_new, second_new, master_new, master_new.astype(BF))


FINE = ("y", "core", "blk")


def place(y, c, b):
    return (y * 2 + c) * 8 + b


def swap(x, dy=0, dc=0, db=0):
    pairs = [
        (place(y, c, b), place(y ^ dy, c ^ dc, b ^ db))
        for y in range(2)
        for c in range(2)
        for b in range(8)
    ]
    return lax.ppermute(x, FINE, pairs)


def trade(x):
    return lax.all_to_all(x, "core", 0, 0, tiled=True)


def cube_pairs(step, back):
    pairs = []
    for y in range(2):
        for c in range(2):
            for b in range(8):
                r, q = b // 4, b % 4
                far = place(y, r, 4 * c + (q + step) % 4)
                near = place(y, c, b)
                pairs.append((far, near) if back else (near, far))
    return pairs


def pick(x, index, axis):
    return lax.dynamic_index_in_dim(x, index, axis, keepdims=False)


def add_low(a, b):
    return (a.astype(F32) + b.astype(F32)).astype(BF)


def tie(*parts):
    return lax.optimization_barrier(parts)


def dot_nn(a, b):
    return jnp.dot(a, b, preferred_element_type=F32)


def dot_nt(a, b):
    return lax.dot_general(a, b, (((1,), (1,)), ((), ())), preferred_element_type=F32)


def dot_tn(a, b):
    return lax.dot_general(a, b, (((0,), (0,)), ((), ())), preferred_element_type=F32)


def call(kernel, outs, name, flops=0, moved=0, vmem=16, **kw):
    return pl.pallas_call(
        kernel,
        out_shape=outs,
        name=name,
        cost_estimate=pl.CostEstimate(flops=int(flops), bytes_accessed=int(moved), transcendentals=0),
        compiler_params=pltpu.CompilerParams(vmem_limit_bytes=vmem * 2**20),
        **kw,
    )


def shape(*dims, dtype=F32):
    return jax.ShapeDtypeStruct(dims, dtype)


VM = pl.BlockSpec(memory_space=pltpu.VMEM)
SM = pl.BlockSpec(memory_space=pltpu.SMEM)


def normalize(rows):
    center = rows - jnp.mean(rows, axis=-1, keepdims=True)
    spread = lax.rsqrt(jnp.mean(center * center, axis=-1, keepdims=True) + 1e-06)
    return center * spread, spread


def norm_back(xhat, spread, gain, grad):
    q = grad * gain
    mean_q = jnp.mean(q, axis=-1, keepdims=True)
    mean_x = jnp.mean(q * xhat, axis=-1, keepdims=True)
    return spread * (q - mean_q - xhat * mean_x)


def lanes(ref_rows, unit):
    return ref_rows[:, 192 * unit : 192 * unit + 192]


def give_kernel(ids, triple, expand, shrink_t, give):
    first = ids[0] == 0
    e = expand[...].astype(BF)
    give[0:96] = jnp.where(first, lanes(e, 1), lanes(e, 0))
    give[96:192] = jnp.where(first, lanes(e, 3), lanes(e, 2))
    s = shrink_t[...].T.astype(BF)
    give[192:384] = jnp.where(first, s[192:], s[:192])
    give[384:480] = lanes(triple, 1).astype(BF)


def pack_kernel(ids, took, triple, mixing, expand, shrink_t, vector, tvm, es, last):
    first, t = ids[0] == 0, ids[1]
    e = expand[...].astype(BF)
    for j in range(2):
        mine = jnp.where(first, lanes(e, 2 * j), lanes(e, 2 * j + 1))
        far = took[96 * j : 96 * j + 96]
        es[0:96, 192 * j : 192 * j + 192] = jnp.where(first, mine, far)
        es[144:240, 192 * j : 192 * j + 192] = jnp.where(first, far, mine)
    s = shrink_t[...].T.astype(BF)
    mine, far = jnp.where(first, s[:192], s[192:]), took[192:384]
    left, right = jnp.where(first, mine, far), jnp.where(first, far, mine)
    for out, at, rows in ((es, 96, slice(0, 48)), (es, 240, slice(48, 96)), (last, 0, slice(96, 192))):
        to = slice(at, at + rows.stop - rows.start)
        out[to, :192] = left[rows]
        out[to, 192:] = right[rows]
    low = triple[...].astype(BF)
    t0, t2, far = lanes(low, 0), lanes(low, 2), took[384:480]
    tvm[0:96, :192] = jnp.where(t == 1, far, jnp.where(t == 2, t2, t0))
    tvm[0:96, 192:] = jnp.where(t == 1, t0, jnp.where(t == 2, far, t2))
    key = jnp.where(t == 1, t2, jnp.where(t == 2, t0, far))
    tvm[96:144, :192] = key[:48]
    tvm[96:144, 192:] = key[48:]
    m = mixing[...].astype(BF)
    tvm[144:192, :192] = m[:48]
    tvm[144:192, 192:] = m[48:]
    tvm[192:208] = jnp.zeros((16, 384), BF)
    tvm[192:204, 0:96] = vector[...].astype(BF)


def qkv_kernel(ids, tok_own, tok_far, qv_own, qv_far, rest_own, rest_far,
               n1_out, x3_out, t3_out, mix_out, vec_out, eb_out, bias, n1):
    first, my, mx, mz = ids[0] == 0, ids[2], ids[3], ids[4]
    for b in range(8):
        iz = ((b >> 1 & 1) ^ (mz & 1)) * 2 + ((b >> 2) ^ (mz >> 1))
        here = (b & 1) ^ mx
        for y in range(2):
            there = y ^ my
            iq, ir = here * 4 + iz, there * 4 + iz
            t3_out[y, 96 * b : 96 * b + 96, :] = jnp.where(there == 0, qv_own[iq], qv_far[iq])
            block = jnp.where(here == 0, rest_own[ir], rest_far[ir])
            t3_out[2, 96 * b : 96 * b + 48, 192 * y : 192 * y + 192] = block[0:48, :192]
            t3_out[2, 96 * b + 48 : 96 * b + 96, 192 * y : 192 * y + 192] = block[0:48, 192:]
            at = 2 * QB + 48 * (y * 8 + b)
            mix_out[0, at : at + 48] = block[48:96]
            mix_out[1, at : at + 48] = block[48:96]
            if y == 0:
                vec_out[0:16, 96 * b : 96 * b + 96] = block[96:112, 0:96].astype(F32)
    half = tok_own.shape[0]
    for at, tok in ((0, tok_own), (half, tok_far)):
        xhat, _ = normalize(tok[...].astype(F32))
        low = (xhat * vec_out[0:1, :] + vec_out[1:2, :]).astype(BF)
        n1[at : at + half, :] = low
        n1_out[:, at : at + half] = low.astype(F32).T.astype(BF)
    mix_out[:, 0 : 2 * QB] = jnp.zeros((2, 2 * QB, 384), BF)
    bias[...] = jnp.zeros_like(bias)
    for j in range(2):
        for k in range(2):
            row = vec_out[4 + j : 5 + j, 384 * k : 384 * k + 384]
            bias[j : j + 1, 192 * k : 192 * k + 192] = jnp.where(first, lanes(row, 0), lanes(row, 1))
    for n in range(4):
        for k in range(2):
            row = vec_out[8 + n : 9 + n, 384 * k : 384 * k + 384]
            eb_out[n, 0:1, 192 * k : 192 * k + 192] = jnp.where(first, lanes(row, 0), lanes(row, 1))
    for j in range(3):
        x3_out[j] = (dot_nn(n1[...], t3_out[j]) + bias[j : j + 1, :]).astype(BF)


def head_masks():
    lane = lax.broadcasted_iota(jnp.int32, (1, 2 * HD), 1)
    return [lane < HD, lane >= HD]


def soft(keys, query, live, width):
    raw = dot_nt(keys, query) * (1.0 / math.sqrt(HD))
    raw = jnp.where(jnp.concatenate([live] * (width // 128), axis=1) > 0, raw, -1e30)
    expo = jnp.exp(raw - jnp.max(raw, axis=0, keepdims=True))
    return expo * (1.0 / jnp.sum(expo, axis=0, keepdims=True))


QB = 256


def attn_kernel(ids, x3, live, _, out):
    q, v, k = x3[0], x3[1], x3[2]
    c = ids[0]
    lv = live[...]
    vt = v.astype(F32).T.astype(BF)
    row = lax.broadcasted_iota(jnp.int32, (2 * HD, 1), 0)
    masks = head_masks()
    for s, core in ((0, c), (QB, 1 - c)):
        total = jnp.zeros((2 * HD, QB), F32)
        for h in range(2):
            qh = jnp.where(masks[h], q[s : s + QB], jnp.zeros((), BF))
            low = soft(k, qh, lv, QB).astype(BF)
            vh = jnp.where(row < HD if h == 0 else row >= HD, vt, jnp.zeros((), BF))
            total += dot_nn(vh, low)
        mixed = total.T.astype(BF)
        at = pl.ds(pl.multiple_of(core * QB, QB), QB)
        out[0, at, :] = mixed
        out[1, at, :] = mixed


def attn_back_kernel(x3, gm_ref, live, d3):
    q, v, k = x3[0], x3[1], x3[2]
    slots = q.shape[0]
    lv = live[...]
    kt = k.astype(F32).T.astype(BF)
    row = lax.broadcasted_iota(jnp.int32, (2 * HD, 1), 0)
    masks = head_masks()
    scale = 1.0 / math.sqrt(HD)
    zero = jnp.zeros((), BF)
    dk = jnp.zeros((slots, 2 * HD), F32)
    dv = jnp.zeros((slots, 2 * HD), F32)
    for s in range(0, slots, QB):
        gm = gm_ref[s : s + QB, :]
        dqt = jnp.zeros((2 * HD, QB), F32)
        for h in range(2):
            qh = jnp.where(masks[h], q[s : s + QB], zero)
            gh = jnp.where(masks[h], gm, zero)
            probs = soft(k, qh, lv, QB)
            gp = dot_nt(v, gh)
            delta = jnp.sum(probs * gp, axis=0, keepdims=True)
            ds = (probs * (gp - delta)).astype(BF)
            kh = jnp.where(row < HD if h == 0 else row >= HD, kt, zero)
            dqt += dot_nn(kh, ds)
            dk += dot_nn(ds, qh)
            dv += dot_nn(probs.astype(BF), gh)
        d3[0, s : s + QB, :] = (dqt.T * scale).astype(BF)
    d3[1] = dv.astype(BF)
    d3[2] = (dk * scale).astype(BF)


def mid_kernel(ids, tok_own, tok_far, traded, vec, att_own, att_far, n2_out, n2t_out, m_out, mixed_t, mixed_out):
    c = ids[0]
    half = tok_own.shape[0]
    for p in range(2):
        for y in range(2):
            at = 192 * (2 * y + p)
            for b in range(8):
                block = traded[p, 2 * half + 48 * (y * 8 + b) : 2 * half + 48 * (y * 8 + b) + 48]
                m_out[96 * b : 96 * b + 48, at : at + 192] = block[:, :192]
                m_out[96 * b + 48 : 96 * b + 96, at : at + 192] = block[:, 192:]
            for to, core in ((0, c), (half, 1 - c)):
                rows = traded[p, pl.ds(pl.multiple_of(core * half, half), half), :]
                mixed_out[to : to + half, at : at + 192] = lanes(rows, y)
    for to, tok, out in ((0, tok_own, att_own), (half, tok_far, att_far)):
        att = tok[...].astype(F32) + (dot_nn(mixed_out[to : to + half, :], m_out[...]) + vec[6:7, :])
        out[...] = att
        xhat, _ = normalize(att)
        n2 = (xhat * vec[2:3, :] + vec[3:4, :]).astype(BF)
        n2_out[to : to + half, :] = n2
        n2t_out[:, to : to + half] = n2.astype(F32).T.astype(BF)
        mixed_t[:, to : to + half] = mixed_out[to : to + half, :].astype(F32).T.astype(BF)


def ffn_kernel(ids, n2, n2t, br_own, br_far, ea, ea_far, eb, eb_far, el, el_far, bias,
               part_own, part_far, gn2, e_x, e_y, s_x, s_y, s_z, d_bias, br, e_ref, s_ref):
    my, mx, mz = ids[2], ids[3], ids[4]
    n = pl.program_id(0)

    def layer(z):
        return ((z & 1) ^ (mz & 1)) * 2 + ((z >> 1) ^ (mz >> 1))

    def x_first(at, y, x, z):
        i, rows = (x ^ mx) * 4 + layer(z), pl.ds(at, 96 if at == 0 else 48)
        return jnp.where(y == my, ea[i, rows, :], ea_far[i, rows, :])

    def y_first(at, y, x, z):
        i, rows = (y ^ my) * 4 + layer(z), pl.ds(at, 96 if at == 0 else 48)
        return jnp.where(x == mx, eb[i, rows, :], eb_far[i, rows, :])

    def z_last(y, x, z):
        i = (((z >> 1) ^ (mz >> 1)) * 2 + (y ^ my)) * 2 + (x ^ mx)
        return jnp.where((z & 1) == (mz & 1), el[i], el_far[i])

    for b in range(8):
        e_ref[96 * b : 96 * b + 96, :384] = x_first(0, n, b & 1, b >> 1)
        e_ref[96 * b : 96 * b + 96, 384:] = y_first(0, n, b & 1, b >> 1)
    for y in range(2):
        for k in range(2):
            for x in range(2):
                at = 384 * k + 192 * x
                s_ref[at : at + 48, 384 * y : 384 * y + 384] = x_first(96, y, x, 2 * n + k)
                s_ref[at + 48 : at + 96, 384 * y : 384 * y + 384] = y_first(96, y, x, 2 * n + k)
                s_ref[at + 96 : at + 192, 384 * y : 384 * y + 384] = z_last(y, x, 2 * n + k)
    half = br_own.shape[0]

    @pl.when(pl.program_id(0) == 0)
    def _():
        for out in (part_own, part_far, gn2):
            out[...] = jnp.zeros_like(out)
        br[0:half], br[half:] = br_own[...], br_far[...]

    e, s = e_ref[...], s_ref[...]
    pre = dot_nn(n2[...], e) + bias[0]
    grad_act = dot_nt(br[...], s)
    cdf = 0.5 * (1.0 + lax.erf(pre * math.sqrt(0.5)))
    act = (pre * cdf).astype(BF)
    slope = cdf + pre * (jnp.exp(-0.5 * pre * pre) * (1.0 / math.sqrt(2.0 * math.pi)))
    grad_pre = (grad_act * slope).astype(BF)
    y = dot_nn(act, s)
    part_own[...] += y[:half]
    part_far[...] += y[half:]
    gn2[...] += dot_nt(grad_pre, e)
    grad = dot_nn(act.astype(F32).T.astype(BF), br[...]).astype(BF)
    for y in range(2):
        for b in range(4):
            block = grad[192 * b : 192 * b + 192, 384 * y : 384 * y + 384]
            s_x[y, b], s_y[y, b], s_z[y, b] = block[0:48], block[48:96], block[96:192]
    grad = dot_nn(n2t[...], grad_pre).astype(BF)
    for p, out in ((0, e_x), (1, e_y)):
        out[0] = grad[:, 384 * p : 384 * p + 384].reshape(8, 96, 384)
    d_bias[0] = jnp.sum(grad_pre.astype(F32), axis=0, keepdims=True)


def mid_back_kernel(ids, gn_here, gn_there, att_own, att_far, br_own, br_far, mixed_t, m, vec, gatt, gm, dm, sums, low):
    first, c = ids[0] == 0, ids[0]
    half = att_own.shape[0]
    for to, att, br_ref in ((0, att_own, br_own), (half, att_far, br_far)):
        gn = gn_here[to : to + half, :] + gn_there[half - to : 2 * half - to, :]
        br = br_ref[...].astype(F32)
        xhat, spread = normalize(att[...])
        grad = br + norm_back(xhat, spread, vec[2:3, :], gn)
        low[to : to + half, :] = grad.astype(BF)
        if to == 0:
            gatt[...] = grad
            sums[0:1] = jnp.sum(gn * xhat, axis=0, keepdims=True)
            sums[1:2] = jnp.sum(gn, axis=0, keepdims=True)
            sums[2:3] = jnp.sum(grad.astype(BF).astype(F32), axis=0, keepdims=True)
            sums[3:4] = jnp.sum(br, axis=0, keepdims=True)
            sums[4:8] = jnp.zeros((4, sums.shape[1]), F32)
    for k in range(2):
        rows = m[pl.ds(pl.multiple_of(192 * (2 * k + c), 192), 192), :]
        gm[:, 192 * k : 192 * k + 192] = dot_nt(low[...], rows).astype(BF)
        both = low[:, 384 * k : 384 * k + 384]
        mine = jnp.where(first, lanes(both, 0), lanes(both, 1))
        weight = dot_nn(mixed_t[...], mine).astype(BF)
        for b in range(8):
            dm[8 * k + b, :, :192] = weight[96 * b : 96 * b + 48]
            dm[8 * k + b, :, 192:] = weight[96 * b + 48 : 96 * b + 96]


def triple_back_kernel(ids, n1_ref, d3, t3, d_qv, d_k, gn, sums):
    c = ids[0]
    j = pl.program_id(0)
    d = d3[0]
    half = gn.shape[1]
    weight = dot_nn(n1_ref[...], d).astype(BF)
    part = dot_nt(d, t3[0])
    sums[0] = jnp.sum(d.astype(F32), axis=0, keepdims=True)

    @pl.when(j == 0)
    def _():
        gn[c] = part[:half]
        gn[1 - c] = part[half:]

    @pl.when(j > 0)
    def _():
        gn[c] += part[:half]
        gn[1 - c] += part[half:]

    @pl.when(j < 2)
    def _():
        d_qv[0] = weight

    @pl.when(j == 2)
    def _():
        for b in range(8):
            for y in range(2):
                d_k[y, b, :, :192] = weight[96 * b : 96 * b + 48, 192 * y : 192 * y + 192]
                d_k[y, b, :, 192:] = weight[96 * b + 48 : 96 * b + 96, 192 * y : 192 * y + 192]


def first_back_kernel(ids, gn_both, tok, gatt, vec, sums2, sums1, d_bias, out, blocks, table):
    c = ids[0]
    gn = gn_both[0] + gn_both[1]
    xhat, spread = normalize(tok[...].astype(F32))
    out[...] = (gatt[...] + norm_back(xhat, spread, vec[0:1, :], gn)).astype(BF)
    table[12:16] = jnp.zeros((4, table.shape[1]), F32)
    table[0:1] = jnp.sum(gn * xhat, axis=0, keepdims=True)
    table[1:2] = jnp.sum(gn, axis=0, keepdims=True)
    table[2:4] = sums2[0:2]
    table[6:8] = sums2[2:4]
    for row, sums in [(4, sums1[0]), (5, sums1[1])] + [(8 + n, d_bias[n]) for n in range(4)]:
        for k in range(2):
            for p in range(2):
                at = 192 * (2 * k + p)
                table[row : row + 1, at : at + 192] = jnp.where(c == p, lanes(sums, k), 0.0)
    blocks[...] = jnp.zeros_like(blocks)
    for b in range(8):
        blocks[b, :, 0:96] = table[:, 96 * b : 96 * b + 96].astype(BF)


def halves(rows):
    return rows[:, :192], rows[:, 192:]


def fetch(refs, places, sems):
    copies = [pltpu.make_async_copy(ref, place, sems.at[i]) for i, (ref, place) in enumerate(zip(refs, places))]
    for copy in copies:
        copy.start()
    for copy in copies:
        copy.wait()


def adam_into(state, outs, rate, decay, at, grad):
    new = adamw(state[0][at], state[1][at], state[2][at], grad, rate, decay)
    for out, value in zip(outs, new):
        out[at] = value


def triple_units(t, total):
    a, b = halves(total[0:96])
    k = jnp.concatenate(halves(total[96:144]), axis=0)
    return a, b, k


def forward_total(own, far, last):
    total = own[...].astype(F32) + far[...].astype(F32)
    return jnp.concatenate([total[0:96], total[144:240], total[96:144], total[240:288], last], axis=0)


def give_back_kernel(ids, t_own, t_far, es_own, es_far, give):
    first, t = ids[0] == 0, ids[1]
    total = t_own[...].astype(F32) + t_far[...].astype(F32)
    a, b, k = triple_units(t, total)
    give[0:96] = jnp.where(t == 1, a, jnp.where(t == 2, b, k))
    give[96:112] = jnp.zeros((16, 192), F32)
    give[96:112, 0:96] = total[144:160, 0:96]
    total = forward_total(es_own, es_far, total[160:256])
    give[112:208], give[208:304] = halves(jnp.where(first, total[96:192], total[0:96]))
    s0, s1 = halves(total[192:])
    give[304:496] = jnp.where(first, s1, s0)


def prefetch_kernel(_, *refs):
    fetch(refs[: len(refs) // 2], refs[len(refs) // 2 : -1], refs[-1])


def update_kernel(ids, t_own, t_far, es_own, es_far, took, *refs):
    state, outs = refs[:15], refs[15:]
    first, c, t = ids[0] == 0, ids[0], ids[1]
    every = slice(None)
    total = t_own[...].astype(F32) + t_far[...].astype(F32)
    a, b, k = triple_units(t, total)
    units = (
        jnp.where(t == 1, b, jnp.where(t == 2, k, a)),
        took[0:96],
        jnp.where(t == 1, k, jnp.where(t == 2, a, b)),
    )
    for i, unit in enumerate(units):
        adam_into(state[0:3], outs[0:4], RATES[0], DECAYS[0], (every, slice(192 * i, 192 * i + 192)), unit)
    for i, part in enumerate(halves(total[256:304])):
        adam_into(state[3:6], outs[4:8], RATES[1], DECAYS[1], (slice(48 * i, 48 * i + 48), every), part)
    total_es = forward_total(es_own, es_far, total[160:256])
    e = halves(jnp.where(first, total_es[0:96], total_es[96:192]))
    s0, s1 = halves(total_es[192:])
    s = jnp.where(first, s0, s1)
    for p in range(2):
        for j in range(2):
            grad = jnp.where(c == p, e[j], took[112 + 96 * j : 208 + 96 * j])
            at = 384 * j + 192 * p
            adam_into(state[6:9], outs[8:12], RATES[2], DECAYS[2], (every, slice(at, at + 192)), grad)
        grad = jnp.where(c == p, s, took[304:496]).T
        adam_into(state[9:12], outs[12:16], RATES[3], DECAYS[3], (every, slice(192 * p, 192 * p + 192)), grad)
    adam_into(state[12:15], outs[16:20], RATES[4], DECAYS[4], (every, every), total[144:156, 0:96] + took[96:108, 0:96])


def by_core(c, own, far):
    return jnp.where(c == 0, jnp.stack([own, far]), jnp.stack([far, own]))


def per_device(
    cube_tokens, visible, live_counts, block_cotangent,
    triple_master, triple_first, triple_second,
    mixing_master, mixing_first, mixing_second,
    expand_master, expand_first, expand_second,
    shrink_master, shrink_first, shrink_second,
    vector_master, vector_first, vector_second,
):
    y, c, b = lax.axis_index("y"), lax.axis_index("core"), lax.axis_index("blk")
    bits = (y, b & 1, b >> 1 & 1, b >> 2)
    turn = b % 4
    unturn = (4 - turn) % 4
    region, feats = cube_tokens.shape[1:]
    slots = visible.shape[1]
    slot_axis = jnp.arange(slots, dtype=jnp.int32)

    t_id = 2 * y + c
    ids = jnp.stack([c, t_id, y, bits[1], b >> 1]).astype(jnp.int32)
    shrink_t = shrink_master.T
    took = swap(call(
        give_kernel, shape(480, 192, dtype=BF), "give", 1e10, 1e3, in_specs=[SM, VM, VM, VM], out_specs=VM,
    )(ids, triple_master, expand_master, shrink_t), dc=1)
    tvm, es, last = call(
        pack_kernel, (shape(208, 384, dtype=BF), shape(288, 384, dtype=BF), shape(96, 384, dtype=BF)), "pack", 1e10, 1e3,
        in_specs=[SM] + [VM] * 6, out_specs=(VM, VM, VM),
    )(ids, took, triple_master, mixing_master, expand_master, shrink_t, vector_master)

    t_far = swap(tvm, db=4)
    last_in = swap(last, db=1)

    visible, block_cotangent, tvm, es, last = tie(visible, block_cotangent, tvm, es, last)
    def turned(x):
        return lax.dynamic_slice_in_dim(jnp.concatenate([x, x]), turn, 4, 0)

    local = visible % region
    flat_index = turned(local + region * jnp.arange(4, dtype=jnp.int32)[:, None])
    picked = jnp.take(cube_tokens.reshape(-1, feats), flat_index.reshape(-1), axis=0).reshape(4, slots, feats)
    counts = jnp.broadcast_to(turned(live_counts)[:, :, None].astype(BF), (4, 16, feats))
    live_here = slot_axis[None, :] < live_counts
    masked = turned(jnp.where(live_here[:, :, None], block_cotangent, jnp.zeros((), BF)))
    packet = jnp.concatenate([picked, masked, counts], axis=1)

    def packets(*steps):
        return [lax.ppermute(packet[s], FINE, cube_pairs(s, False)) for s in steps]

    last = jnp.stack([last, last_in])
    last_in = swap(last, dy=1)
    t_far, packet, es, last_in = tie(t_far, packet, es, last_in)
    tvm = jnp.stack([tvm, t_far])
    t_far = swap(tvm, db=2)
    last = jnp.stack([last, last_in]).reshape(384, 384)
    es_far = swap(jnp.concatenate([es, last], axis=0), db=4)
    own = packets(0, 1)

    t_far, packet = tie(t_far, packet)
    tvm = jnp.stack([tvm, t_far]).reshape(4, 208, 384)
    qv, rest = tvm[:, :96], tvm[:, 96:]
    qv_x, rest_y = swap(qv, db=1), swap(rest, dy=1)

    qv_x, rest_y, own, packet = tie(qv_x, rest_y, own, packet)
    qv = jnp.stack([qv, qv_x]).reshape(8, 96, 384)
    rest = jnp.stack([rest, rest_y]).reshape(8, 112, 384)
    qv_far, rest_far = swap(qv, dy=1), swap(rest, db=1)
    es_far, last = tie(es_far, last)
    el = jnp.stack([last, es_far[288:]]).reshape(8, 96, 384)
    es = jnp.stack([es, es_far[:288]])
    es_far = swap(es, db=2)
    own = own + packets(2, 3)

    qv_far, rest_far, es_far, own = tie(qv_far, rest_far, es_far, own)
    es = jnp.stack([es, es_far]).reshape(4, 288, 384)
    ea, eb = es[:, :144], es[:, 144:]
    ea_in, eb_in = swap(ea, db=1), swap(eb, dy=1)
    el_far = swap(el, db=2)
    own = jnp.stack(own)
    far = swap(own, dc=1)

    rows = 4 * slots
    tok_own, tok_far = [p[:, :slots].reshape(rows, feats) for p in (own, far)]
    br_own, br_far = [p[:, slots : 2 * slots].reshape(rows, feats) for p in (own, far)]
    cnt = jnp.concatenate([own[:, 2 * slots, :1], far[:, 2 * slots, :1]]).astype(jnp.int32)
    live = (slot_axis[None, :] < cnt).reshape(2 * rows, 1)
    live_cols = jnp.broadcast_to(live.astype(F32), (2 * rows, 128))

    n1, x3, t3, mix, vec, e_bias = call(
        qkv_kernel,
        (shape(feats, 2 * rows, dtype=BF), shape(3, 2 * rows, 384, dtype=BF), shape(3, feats, 384, dtype=BF),
         shape(2, 2 * rows + feats, 384, dtype=BF), shape(16, feats), shape(4, 1, 384)),
        "qkv", 2 * 512 * 768 * 1152, 8e6,
        in_specs=[SM] + [VM] * 6, out_specs=(VM,) * 6, scratch_shapes=[pltpu.VMEM((8, 384), F32), pltpu.VMEM((2 * rows, feats), BF)],
    )(ids, tok_own, tok_far, qv, qv_far, rest, rest_far)
    x3, mix, ea_in, eb_in = tie(x3, mix, ea_in, eb_in)
    ea = jnp.stack([ea, ea_in]).reshape(8, 144, 384)
    eb = jnp.stack([eb, eb_in]).reshape(8, 144, 384)
    ea_far, eb_far = swap(ea, dy=1), swap(eb, db=1)

    pairs3 = pl.BlockSpec((3, 2 * rows, 128), lambda i: (0, 0, i))
    col = pl.BlockSpec((2 * rows, 128), lambda i: (0, i))
    same = pl.BlockSpec((2 * rows, 128), lambda i: (0, 0))
    traded = trade(call(
        attn_kernel, shape(2, 2 * rows + feats, 384, dtype=BF), "attention", 6e9, 2e6,
        grid=(3,), in_specs=[SM, pairs3, same, pl.BlockSpec(memory_space=pl.ANY)],
        out_specs=pl.BlockSpec((2, 2 * rows, 128), lambda i: (0, 0, i)), input_output_aliases={3: 0},
    )(ids, x3, live_cols, mix))
    att, att_far, n2, n2t, mix, mixed = call(
        mid_kernel,
        (shape(rows, feats), shape(rows, feats), shape(2 * rows, feats, dtype=BF), shape(feats, 2 * rows, dtype=BF),
         shape(feats, feats, dtype=BF), shape(feats, 2 * rows, dtype=BF)),
        "mixing", 3e9, 5e6, in_specs=[SM] + [VM] * 4, out_specs=(VM,) * 6,
        scratch_shapes=[pltpu.VMEM((2 * rows, feats), BF)],
    )(ids, tok_own, tok_far, traded, vec)

    whole = pl.BlockSpec((rows, feats), lambda i: (0, 0))

    gathered = [pl.BlockSpec((8, r, 384), lambda n: (0, 0, 0)) for r in (144, 144, 144, 144, 96, 96)]
    every = pl.BlockSpec((2 * rows, feats), lambda i: (0, 0))
    part_own, part_give, gn2, e_x, e_y, s_x, s_y, d_z, d_b = call(
        ffn_kernel,
        (shape(rows, feats),) * 2
        + (shape(2 * rows, feats),) + (shape(2, 8, 96, 384, dtype=BF),) * 2 + (shape(2, 8, 48, 384, dtype=BF),) * 2
        + (shape(2, 8, 96, 384, dtype=BF), shape(2, 1, 768)),
        "feed_forward", 18e9, 20e6, 46,
        grid=(2,),
        in_specs=[SM, every, pl.BlockSpec((feats, 2 * rows), lambda n: (0, 0))] + [whole] * 2 + gathered
        + [pl.BlockSpec((1, 1, 768), lambda n: (n, 0, 0))],
        out_specs=(
            whole, whole, every,
            pl.BlockSpec((1, 8, 96, 384), lambda n: (n, 0, 0, 0)),
            pl.BlockSpec((1, 8, 96, 384), lambda n: (n, 0, 0, 0)),
            pl.BlockSpec((2, 4, 48, 384), lambda n: (0, n, 0, 0)),
            pl.BlockSpec((2, 4, 48, 384), lambda n: (0, n, 0, 0)),
            pl.BlockSpec((2, 4, 96, 384), lambda n: (0, n, 0, 0)),
            pl.BlockSpec((1, 1, 768), lambda n: (n, 0, 0)),
        ),
        scratch_shapes=[pltpu.VMEM((2 * rows, feats), BF), pltpu.VMEM((feats, 768), BF), pltpu.VMEM((768, feats), BF)],
    )(ids, n2, n2t, br_own, br_far, ea, ea_far, eb, eb_far, el, el_far, e_bias.reshape(2, 1, 768))

    mx, z0, z1 = bits[1], bits[2], bits[3]
    gn2_far = swap(gn2, dc=1)
    d_z = d_z.reshape(2, 2, 2, 2, 96, 384)

    def x_part(at):
        return jnp.concatenate([pick(e_x.reshape(2, 4, 2, 96, 384), at, 2), pick(s_x.reshape(2, 4, 2, 48, 384), at, 2)], axis=2)

    def y_part(at):
        return jnp.concatenate([pick(e_y, at, 0), pick(s_y, at, 0)], axis=1)

    x_in = swap(x_part(1 - mx), db=1)
    y_in = swap(y_part(1 - y), dy=1)

    gatt, gm, dm, sums2 = call(
        mid_back_kernel,
        (shape(rows, feats), shape(2 * rows, 384, dtype=BF), shape(16, 48, 384, dtype=BF), shape(8, feats)),
        "mixing_back", 6e9, 8e6, in_specs=[SM] + [VM] * 9, out_specs=(VM,) * 4,
        scratch_shapes=[pltpu.VMEM((2 * rows, feats), BF)],
    )(ids, gn2, gn2_far, att, att_far, br_own, br_far, mixed, mix, vec)
    d_z = jnp.concatenate([d_z, dm.reshape(2, 2, 2, 2, 48, 384)], axis=4)
    z_in = swap(pick(d_z, 1 - z0, 2), db=2)
    d3 = call(
        attn_back_kernel, shape(3, 2 * rows, 384, dtype=BF), "attention_back", 9e9, 5e6,
        grid=(3,), in_specs=[pairs3, col, same], out_specs=pairs3,
    )(x3, gm, live_cols)

    third = pl.BlockSpec((1, 2 * rows, 384), lambda j: (j, 0, 0))
    d_qv, d_k, gn1, sums1 = call(
        triple_back_kernel,
        (shape(2, feats, 384, dtype=BF), shape(2, 8, 48, 384, dtype=BF), shape(2, rows, feats), shape(3, 1, 384)),
        "triple_back", 5e9, 5e6,
        grid=(3,),
        in_specs=[SM, pl.BlockSpec((feats, 2 * rows), lambda j: (0, 0)), third, pl.BlockSpec((1, feats, 384), lambda j: (j, 0, 0))],
        out_specs=(
            pl.BlockSpec((1, feats, 384), lambda j: (jnp.minimum(j, 1), 0, 0)),
            pl.BlockSpec((2, 8, 48, 384), lambda j: (0, 0, 0, 0)),
            pl.BlockSpec((2, rows, feats), lambda j: (0, 0, 0)),
            pl.BlockSpec((1, 1, 384), lambda j: (j, 0, 0)),
        ),
    )(ids, n1, d3, t3)

    gn1 = trade(gn1)
    grad_tok, blocks = call(
        first_back_kernel, (shape(rows, feats, dtype=BF), shape(8, 16, 384, dtype=BF)), "first_back", 1e9, 1e6,
        in_specs=[SM] + [VM] * 7, out_specs=(VM, VM), scratch_shapes=[pltpu.VMEM((16, feats), F32)],
    )(ids, gn1, tok_own, gatt, vec, sums2, sums1, d_b.reshape(4, 1, 384))

    blocks = jnp.broadcast_to(blocks, (2, 8, 16, 384))
    d_qv = d_qv.reshape(2, 4, 2, 96, 384)
    d_km = jnp.concatenate([d_k, blocks], axis=2).reshape(2, 4, 2, 64, 384)
    qv_in = swap(pick(d_qv, 1 - bits[1], 2), db=1)
    km_in = swap(pick(d_km, 1 - y, 0), dy=1)

    x_in, y_in, z_in, grad_tok, part_give = tie(x_in, y_in, z_in, grad_tok, part_give)
    d_x = add_low(x_part(mx), x_in)
    d_y = add_low(y_part(y), y_in).reshape(4, 2, 144, 384)
    x_in = swap(pick(d_x, 1 - y, 0), dy=1)
    y_in = swap(pick(d_y, 1 - mx, 1), db=1)
    d_z = add_low(pick(d_z, z0, 2), z_in)
    z_in = swap(pick(d_z, 1 - y, 0), dy=1)

    part_far = swap(part_give, dc=1)
    result = att + (part_own + part_far + vec[7])
    result = jnp.where(live[:rows], result, 0.0).astype(BF).reshape(4, slots, feats)
    packet = jnp.concatenate([result, grad_tok.reshape(4, slots, feats)], axis=1)

    def go_back(step, *after):
        part = tie(packet[step], *after)[0]
        return lax.ppermute(part, FINE, cube_pairs(step, True))

    back = [go_back(0)]
    back += [go_back(1, back[0])]

    qv_in, km_in, back, packet = tie(qv_in, km_in, back, packet)
    d_qv = add_low(pick(d_qv, mx, 2), qv_in)
    d_km = add_low(pick(d_km, y, 0), km_in)
    qv_in = swap(pick(d_qv, 1 - y, 0), dy=1)
    km_in = swap(pick(d_km, 1 - mx, 1), db=1)
    back += [go_back(2)]
    back += [go_back(3)]

    x_in, y_in, z_in, packet = tie(x_in, y_in, z_in, packet)
    d_es = jnp.concatenate(
        [add_low(pick(d_x, y, 0), x_in), add_low(pick(d_y, mx, 1), y_in)], axis=1
    ).reshape(2, 2, 288, 384)
    es_in = swap(pick(d_es, 1 - z0, 1), db=2)

    qv_in, km_in, z_in = tie(qv_in, km_in, z_in)
    d_t = jnp.concatenate(
        [add_low(pick(d_qv, y, 0), qv_in), add_low(pick(d_km, mx, 1), km_in)], axis=1
    ).reshape(2, 2, 160, 384)
    t_in = swap(pick(d_t, 1 - z0, 1), db=2)
    d_z = add_low(pick(d_z, y, 0), z_in)
    z_in = swap(pick(d_z, 1 - mx, 1), db=1)

    es_in, t_keep = tie(es_in, d_t)
    es_keep = d_es = add_low(pick(d_es, z0, 1), es_in)
    es_in = swap(pick(d_es, 1 - z1, 0), db=4)
    t_in, z_in = tie(t_in, z_in)
    d_t = jnp.concatenate([add_low(pick(d_t, z0, 1), t_in), add_low(pick(d_z, mx, 1), z_in)], axis=1)
    t_in = swap(pick(d_t, 1 - z1, 0), db=4)

    state = (triple_master, triple_first, triple_second, mixing_master, mixing_first, mixing_second,
             expand_master, expand_first, expand_second, shrink_t, shrink_first.T, shrink_second.T,
             vector_master, vector_first, vector_second)
    ids_late = ids + jnp.isnan(es_keep[0, 0, 0]).astype(jnp.int32)
    ready = call(
        prefetch_kernel, tuple(shape(*a.shape) for a in state), "prefetch", 1e10, 1e3,
        in_specs=[SM] + [pl.BlockSpec(memory_space=pltpu.HBM)] * len(state), out_specs=(VM,) * len(state),
        scratch_shapes=[pltpu.SemaphoreType.DMA((len(state),))],
    )(ids_late, *state)

    back = jnp.stack(back)
    back = lax.dynamic_slice_in_dim(jnp.concatenate([back, back]), unturn, 4, 0)
    block_output = back[:, :slots]
    spread = (jnp.arange(region, dtype=jnp.int32)[None, :, None] == local[:, None, :]).astype(BF)
    token_grads = jnp.einsum("grs,gsf->grf", spread, back[:, slots:], preferred_element_type=F32).astype(BF)

    t_in, es_in, token_grads, block_output, ready = tie(t_in, es_in, token_grads, block_output, ready)
    grads = (pick(d_t, z1, 0), t_in, pick(d_es, z1, 0), es_in)
    took = swap(call(
        give_back_kernel, shape(496, 192), "give_back", 1e6, 1e6, in_specs=[SM] + [VM] * 4, out_specs=VM,
    )(ids, *grads), dc=1)

    def whole_of(a):
        return pl.BlockSpec(a.shape, lambda i: (0,) * len(a.shape))

    outs = tuple(shape(*a.shape, dtype=d) for a in state[::3] for d in (F32, F32, F32, BF))
    new = call(
        update_kernel, outs, "update", 1e8, 4e6, grid=(1,),
        in_specs=[SM] + [whole_of(a) for a in (*grads, took, *state)], out_specs=tuple(whole_of(o) for o in outs),
    )(ids, *grads, took, *ready)
    return (block_output, token_grads, *new[:12], *(o.T for o in new[12:16]), *new[16:])


def layer_norm(rows, gain, shift):
    center = rows - jnp.mean(rows, axis=-1, keepdims=True)
    spread = lax.rsqrt(jnp.mean(center * center, axis=-1, keepdims=True) + 1e-06)
    return center * spread * gain + shift


def outer_sum(left, right):
    return lax.dot_general(
        left, right, (((0,), (0,)), ((), ())), preferred_element_type=jnp.float32
    )


def back_product(grads, weight):
    return lax.dot_general(
        grads, weight, (((1,), (1,)), ((), ())), preferred_element_type=jnp.float32
    )


def masked_scores(queries, key_all, live_all):
    raw = jnp.einsum("gshe,gthe->ghst", queries, key_all, preferred_element_type=jnp.float32) * (
        1.0 / math.sqrt(HD)
    )
    return jnp.where(live_all[:, None, None, :] > 0, raw, -1e30)


def cycle_section(triple_grad, mixing_grad, expand_grad, shrink_grad, vector_grad):
    summed = (
        lax.psum_scatter(triple_grad, "blk", scatter_dimension=0, tiled=True),
        lax.psum_scatter(mixing_grad, "blk", scatter_dimension=0, tiled=True),
        lax.psum_scatter(expand_grad, "blk", scatter_dimension=0, tiled=True),
        lax.psum_scatter(shrink_grad, "blk", scatter_dimension=0, tiled=True),
        lax.psum_scatter(vector_grad, "blk", scatter_dimension=1, tiled=True),
    )
    return (summed[0], summed[1], summed[2], summed[3], summed[4])


def group_section(triple_grad, mixing_grad, expand_grad, shrink_grad, vector_grad):
    summed = (
        lax.psum_scatter(triple_grad, "batch", scatter_dimension=1, tiled=True),
        lax.psum_scatter(mixing_grad, "batch", scatter_dimension=1, tiled=True),
        lax.psum_scatter(expand_grad, "batch", scatter_dimension=1, tiled=True),
        lax.psum_scatter(shrink_grad, "batch", scatter_dimension=1, tiled=True),
    )
    vector_sum = lax.psum(vector_grad, "batch")
    return (summed[0], summed[1], summed[2], summed[3], vector_sum)


def per_device_any(
    cube_tokens,
    visible,
    live_counts,
    block_cotangent,
    triple_master,
    triple_first,
    triple_second,
    mixing_master,
    mixing_first,
    mixing_second,
    expand_master,
    expand_first,
    expand_second,
    shrink_master,
    shrink_first,
    shrink_second,
    vector_master,
    vector_first,
    vector_second,
):
    low_copies = (
        lax.all_gather(triple_master.astype(jnp.bfloat16), "blk", axis=0, tiled=True),
        lax.all_gather(mixing_master.astype(jnp.bfloat16), "blk", axis=0, tiled=True),
        lax.all_gather(expand_master.astype(jnp.bfloat16), "blk", axis=0, tiled=True),
        lax.all_gather(shrink_master.astype(jnp.bfloat16), "blk", axis=0, tiled=True),
        lax.all_gather(vector_master.astype(jnp.bfloat16), "blk", axis=1, tiled=True),
    )
    triple_w, mixing_w, expand_w, shrink_w = (
        lax.all_gather(low_copies[0], "batch", axis=1, tiled=True),
        lax.all_gather(low_copies[1], "batch", axis=1, tiled=True),
        lax.all_gather(low_copies[2], "batch", axis=1, tiled=True),
        lax.all_gather(low_copies[3], "batch", axis=1, tiled=True),
    )
    vector_w = low_copies[4].astype(jnp.float32)
    groups, slot_count = visible.shape
    region = cube_tokens.shape[1]
    features = cube_tokens.shape[2]
    row_count = groups * slot_count
    head_count = features // HD
    local_index = visible % region
    tokens = jnp.take_along_axis(cube_tokens, local_index[:, :, None], axis=1).astype(jnp.float32)
    flat_tokens = tokens.reshape(row_count, features)
    live_mask = jnp.arange(slot_count, dtype=jnp.int32)[None, :] < live_counts
    live_rows = live_mask.reshape(row_count, 1)
    normed1 = layer_norm(flat_tokens, vector_w[0], vector_w[1]).astype(jnp.bfloat16)
    zero_bias = jnp.zeros((features,), jnp.float32)
    triple_bias = jnp.concatenate([vector_w[4], zero_bias, vector_w[5]])
    triple = (jnp.dot(normed1, triple_w, preferred_element_type=jnp.float32) + triple_bias).astype(
        jnp.bfloat16
    )
    triple = triple.reshape(groups, slot_count, 3 * features)
    query_flat = triple[:, :, :features]
    queries = query_flat.reshape(groups, slot_count, head_count, HD)
    key_rows = triple[:, :, features : 2 * features]
    value_rows = triple[:, :, 2 * features :]
    key_all, value_all, live_all = (
        lax.all_gather(key_rows, "blk", axis=1, tiled=True),
        lax.all_gather(value_rows, "blk", axis=1, tiled=True),
        lax.all_gather(live_mask.astype(jnp.bfloat16), "blk", axis=1, tiled=True),
    )
    key_all = key_all.reshape(groups, -1, head_count, HD)
    value_all = value_all.reshape(groups, -1, head_count, HD)
    scores = masked_scores(queries, key_all, live_all)
    peak = jnp.max(scores, axis=-1, keepdims=True)
    expo = jnp.exp(scores - peak)
    total = jnp.sum(expo, axis=-1, keepdims=True)
    prob_low = (expo / total).astype(jnp.bfloat16)
    mixed = jnp.einsum("ghst,gthe->gshe", prob_low, value_all, preferred_element_type=jnp.float32)
    mixed = mixed.astype(jnp.bfloat16).reshape(row_count, features)
    attended = flat_tokens + (
        jnp.dot(mixed, mixing_w, preferred_element_type=jnp.float32) + vector_w[6]
    )
    normed2 = layer_norm(attended, vector_w[2], vector_w[3]).astype(jnp.bfloat16)
    preact = jnp.dot(normed2, expand_w, preferred_element_type=jnp.float32) + vector_w[8:].reshape(
        -1
    )
    activation = jax.nn.gelu(preact, approximate=False).astype(jnp.bfloat16)
    result = attended + (
        jnp.dot(activation, shrink_w, preferred_element_type=jnp.float32) + vector_w[7]
    )
    result = jnp.where(live_rows, result, 0.0)
    block_output = result.astype(jnp.bfloat16).reshape(groups, slot_count, features)
    grad_out = jnp.where(
        live_rows, block_cotangent.reshape(row_count, features).astype(jnp.float32), 0.0
    )
    branch_low = grad_out.astype(jnp.bfloat16)
    shrink_grad = outer_sum(activation, branch_low)
    shrink_bias_grad = jnp.sum(branch_low.astype(jnp.float32), axis=0)
    grad_act = back_product(branch_low, shrink_w)
    gelu_value, gelu_back = jax.vjp(partial(jax.nn.gelu, approximate=False), preact)
    grad_pre = gelu_back(grad_act)[0].astype(jnp.bfloat16)
    expand_grad = outer_sum(normed2, grad_pre)
    expand_bias_grad = jnp.sum(grad_pre.astype(jnp.float32), axis=0)
    grad_normed2 = back_product(grad_pre, expand_w)
    norm2_value, norm2_back = jax.vjp(layer_norm, attended, vector_w[2], vector_w[3])
    grad_through2, gain2_grad, shift2_grad = norm2_back(grad_normed2)
    grad_attended = grad_out + grad_through2
    mix_low = grad_attended.astype(jnp.bfloat16)
    mixing_grad = outer_sum(mixed, mix_low)
    mixing_bias_grad = jnp.sum(mix_low.astype(jnp.float32), axis=0)
    grad_mixed_flat = (
        back_product(mix_low, mixing_w).astype(jnp.bfloat16).reshape(groups, slot_count, features)
    )
    grad_mixed = grad_mixed_flat.reshape(groups, slot_count, head_count, HD)
    scores = masked_scores(queries, key_all, live_all)
    probs = jnp.exp(scores - peak) / total
    prob_low = probs.astype(jnp.bfloat16)
    grad_probs = jnp.einsum(
        "gshe,gthe->ghst", grad_mixed, value_all, preferred_element_type=jnp.float32
    )
    delta = jnp.sum(probs * grad_probs, axis=-1, keepdims=True)
    grad_scores = (probs * (grad_probs - delta)).astype(jnp.bfloat16)
    score_scale = 1.0 / math.sqrt(HD)
    grad_queries = (
        jnp.einsum("ghst,gthe->gshe", grad_scores, key_all, preferred_element_type=jnp.float32)
        * score_scale
    )
    term_keys = (
        jnp.einsum("ghst,gshe->gthe", grad_scores, queries, preferred_element_type=jnp.float32)
        * score_scale
    )
    term_values = jnp.einsum(
        "ghst,gshe->gthe", prob_low, grad_mixed, preferred_element_type=jnp.float32
    )
    grad_keys, grad_values = (
        lax.psum_scatter(
            term_keys.reshape(groups, -1, features), "blk", scatter_dimension=1, tiled=True
        ),
        lax.psum_scatter(
            term_values.reshape(groups, -1, features), "blk", scatter_dimension=1, tiled=True
        ),
    )
    grad_triple = jnp.concatenate(
        [
            grad_queries.reshape(row_count, features),
            grad_keys.reshape(row_count, features),
            grad_values.reshape(row_count, features),
        ],
        axis=1,
    ).astype(jnp.bfloat16)
    triple_grad = outer_sum(normed1, grad_triple)
    triple_sums = jnp.sum(grad_triple.astype(jnp.float32), axis=0)
    grad_normed1 = back_product(grad_triple, triple_w)
    norm1_value, norm1_back = jax.vjp(layer_norm, flat_tokens, vector_w[0], vector_w[1])
    grad_through1, gain1_grad, shift1_grad = norm1_back(grad_normed1)
    grad_tokens = (grad_attended + grad_through1).reshape(groups, slot_count, features)
    cube_rows = jnp.arange(groups, dtype=jnp.int32)[:, None]
    token_grads = (
        jnp.zeros(cube_tokens.shape, jnp.float32)
        .at[cube_rows, local_index]
        .add(grad_tokens)
        .astype(jnp.bfloat16)
    )
    leading_rows = jnp.stack(
        [
            gain1_grad,
            shift1_grad,
            gain2_grad,
            shift2_grad,
            triple_sums[:features],
            triple_sums[2 * features :],
            mixing_bias_grad,
            shrink_bias_grad,
        ]
    )
    vector_grad = jnp.concatenate([leading_rows, expand_bias_grad.reshape(-1, features)], axis=0)
    reduced = group_section(triple_grad, mixing_grad, expand_grad, shrink_grad, vector_grad)
    reduced = cycle_section(reduced[0], reduced[1], reduced[2], reduced[3], reduced[4])
    masters = (triple_master, mixing_master, expand_master, shrink_master, vector_master)
    firsts = (triple_first, mixing_first, expand_first, shrink_first, vector_first)
    seconds = (triple_second, mixing_second, expand_second, shrink_second, vector_second)
    outputs = [block_output, token_grads]
    for master, first, second, grad, rate, decay in zip(
        masters, firsts, seconds, reduced, RATES, DECAYS
    ):
        outputs.extend(adamw(master, first, second, grad, rate, decay))
    return tuple(outputs)


def solution(mesh):
    groups, blocks = mesh.shape["batch"], mesh.shape["blk"]
    if (groups, blocks) == (4, 8):
        mesh = Mesh(mesh.devices.reshape(2, 2, 8), FINE)
        batch, body = ("y", "core"), per_device
    else:
        batch, body = "batch", per_device_any
    rows = P(batch, "blk", None)
    part = P("blk", batch)
    table = P(None, "blk")
    in_specs = (rows, P(batch, "blk"), P(batch, "blk"), rows) + (part,) * 12 + (table,) * 3
    out_specs = (rows, rows) + (part,) * 16 + (table,) * 4
    return jax.shard_map(body, mesh=mesh, in_specs=in_specs, out_specs=out_specs, check_vma=False)
```

```python
from functools import partial
import math

import jax
import jax.numpy as jnp
from jax import lax
from jax.experimental import pallas as pl
from jax.experimental.pallas import tpu as pltpu
from jax.sharding import Mesh, PartitionSpec as P

HD = 64
STEP = 10
BF = jnp.bfloat16
F32 = jnp.float32

RATES = (0.04, 0.3, 0.04, 0.02, 0.25)
DECAYS = (0.05, 0.05, 0.05, 0.05, 0.0)


def adamw(master, first, second, grad, rate, decay):
    first_new = 0.9 * first + 0.1 * grad
    second_new = 0.999 * second + 0.001 * grad * grad
    corrected = first_new / (1.0 - 0.9**STEP) / (jnp.sqrt(second_new / (1.0 - 0.999**STEP)) + 1e-08)
    master_new = master - rate * (corrected + decay * master)
    return (first_new, second_new, master_new, master_new.astype(BF))


FINE = ("y", "core", "blk")


def place(y, c, b):
    return (y * 2 + c) * 8 + b


def swap(x, dy=0, dc=0, db=0):
    pairs = [
        (place(y, c, b), place(y ^ dy, c ^ dc, b ^ db))
        for y in range(2)
        for c in range(2)
        for b in range(8)
    ]
    return lax.ppermute(x, FINE, pairs)


def trade(x):
    return lax.all_to_all(x, "core", 0, 0, tiled=True)


def cube_pairs(step, back):
    pairs = []
    for y in range(2):
        for c in range(2):
            for b in range(8):
                r, q = b // 4, b % 4
                far = place(y, r, 4 * c + (q + step) % 4)
                near = place(y, c, b)
                pairs.append((far, near) if back else (near, far))
    return pairs


def pick(x, index, axis):
    return lax.dynamic_index_in_dim(x, index, axis, keepdims=False)


def add_low(a, b):
    return (a.astype(F32) + b.astype(F32)).astype(BF)


def tie(*parts):
    return lax.optimization_barrier(parts)


def dot_nn(a, b):
    return jnp.dot(a, b, preferred_element_type=F32)


def dot_nt(a, b):
    return lax.dot_general(a, b, (((1,), (1,)), ((), ())), preferred_element_type=F32)


def dot_tn(a, b):
    return lax.dot_general(a, b, (((0,), (0,)), ((), ())), preferred_element_type=F32)


def call(kernel, outs, name, flops=0, moved=0, vmem=16, **kw):
    return pl.pallas_call(
        kernel,
        out_shape=outs,
        name=name,
        cost_estimate=pl.CostEstimate(flops=int(flops), bytes_accessed=int(moved), transcendentals=0),
        compiler_params=pltpu.CompilerParams(vmem_limit_bytes=vmem * 2**20),
        **kw,
    )


def shape(*dims, dtype=F32):
    return jax.ShapeDtypeStruct(dims, dtype)


VM = pl.BlockSpec(memory_space=pltpu.VMEM)
SM = pl.BlockSpec(memory_space=pltpu.SMEM)


def normalize(rows):
    center = rows - jnp.mean(rows, axis=-1, keepdims=True)
    spread = lax.rsqrt(jnp.mean(center * center, axis=-1, keepdims=True) + 1e-06)
    return center * spread, spread


def norm_back(xhat, spread, gain, grad):
    q = grad * gain
    mean_q = jnp.mean(q, axis=-1, keepdims=True)
    mean_x = jnp.mean(q * xhat, axis=-1, keepdims=True)
    return spread * (q - mean_q - xhat * mean_x)


def lanes(ref_rows, unit):
    return ref_rows[:, 192 * unit : 192 * unit + 192]


def give_kernel(ids, triple, expand, shrink_t, give):
    first = ids[0] == 0
    e = expand[...].astype(BF)
    give[0:96] = jnp.where(first, lanes(e, 1), lanes(e, 0))
    give[96:192] = jnp.where(first, lanes(e, 3), lanes(e, 2))
    s = shrink_t[...].T.astype(BF)
    give[192:384] = jnp.where(first, s[192:], s[:192])
    give[384:480] = lanes(triple, 1).astype(BF)


def pack_kernel(ids, took, triple, mixing, expand, shrink_t, vector, tvm, es, last):
    first, t = ids[0] == 0, ids[1]
    e = expand[...].astype(BF)
    for j in range(2):
        mine = jnp.where(first, lanes(e, 2 * j), lanes(e, 2 * j + 1))
        far = took[96 * j : 96 * j + 96]
        es[0:96, 192 * j : 192 * j + 192] = jnp.where(first, mine, far)
        es[144:240, 192 * j : 192 * j + 192] = jnp.where(first, far, mine)
    s = shrink_t[...].T.astype(BF)
    mine, far = jnp.where(first, s[:192], s[192:]), took[192:384]
    left, right = jnp.where(first, mine, far), jnp.where(first, far, mine)
    for out, at, rows in ((es, 96, slice(0, 48)), (es, 240, slice(48, 96)), (last, 0, slice(96, 192))):
        to = slice(at, at + rows.stop - rows.start)
        out[to, :192] = left[rows]
        out[to, 192:] = right[rows]
    low = triple[...].astype(BF)
    t0, t2, far = lanes(low, 0), lanes(low, 2), took[384:480]
    tvm[0:96, :192] = jnp.where(t == 1, far, jnp.where(t == 2, t2, t0))
    tvm[0:96, 192:] = jnp.where(t == 1, t0, jnp.where(t == 2, far, t2))
    key = jnp.where(t == 1, t2, jnp.where(t == 2, t0, far))
    tvm[96:144, :192] = key[:48]
    tvm[96:144, 192:] = key[48:]
    m = mixing[...].astype(BF)
    tvm[144:192, :192] = m[:48]
    tvm[144:192, 192:] = m[48:]
    tvm[192:208] = jnp.zeros((16, 384), BF)
    tvm[192:204, 0:96] = vector[...].astype(BF)


def qkv_kernel(ids, tok_own, tok_far, qv_own, qv_far, rest_own, rest_far,
               n1_out, x3_out, t3_out, mix_out, vec_out, eb_out, bias, n1):
    first, my, mx, mz = ids[0] == 0, ids[2], ids[3], ids[4]
    for b in range(8):
        iz = ((b >> 1 & 1) ^ (mz & 1)) * 2 + ((b >> 2) ^ (mz >> 1))
        here = (b & 1) ^ mx
        for y in range(2):
            there = y ^ my
            iq, ir = here * 4 + iz, there * 4 + iz
            t3_out[y, 96 * b : 96 * b + 96, :] = jnp.where(there == 0, qv_own[iq], qv_far[iq])
            block = jnp.where(here == 0, rest_own[ir], rest_far[ir])
            t3_out[2, 96 * b : 96 * b + 48, 192 * y : 192 * y + 192] = block[0:48, :192]
            t3_out[2, 96 * b + 48 : 96 * b + 96, 192 * y : 192 * y + 192] = block[0:48, 192:]
            at = 2 * QB + 48 * (y * 8 + b)
            mix_out[0, at : at + 48] = block[48:96]
            mix_out[1, at : at + 48] = block[48:96]
            if y == 0:
                vec_out[0:16, 96 * b : 96 * b + 96] = block[96:112, 0:96].astype(F32)
    half = tok_own.shape[0]
    for at, tok in ((0, tok_own), (half, tok_far)):
        xhat, _ = normalize(tok[...].astype(F32))
        low = (xhat * vec_out[0:1, :] + vec_out[1:2, :]).astype(BF)
        n1[at : at + half, :] = low
        n1_out[:, at : at + half] = low.astype(F32).T.astype(BF)
    mix_out[:, 0 : 2 * QB] = jnp.zeros((2, 2 * QB, 384), BF)
    bias[...] = jnp.zeros_like(bias)
    for j in range(2):
        for k in range(2):
            row = vec_out[4 + j : 5 + j, 384 * k : 384 * k + 384]
            bias[j : j + 1, 192 * k : 192 * k + 192] = jnp.where(first, lanes(row, 0), lanes(row, 1))
    for n in range(4):
        for k in range(2):
            row = vec_out[8 + n : 9 + n, 384 * k : 384 * k + 384]
            eb_out[n, 0:1, 192 * k : 192 * k + 192] = jnp.where(first, lanes(row, 0), lanes(row, 1))
    for j in range(3):
        x3_out[j] = (dot_nn(n1[...], t3_out[j]) + bias[j : j + 1, :]).astype(BF)


def head_masks():
    lane = lax.broadcasted_iota(jnp.int32, (1, 2 * HD), 1)
    return [lane < HD, lane >= HD]


def soft(keys, query, live, width):
    raw = dot_nt(keys, query) * (1.0 / math.sqrt(HD))
    raw = jnp.where(jnp.concatenate([live] * (width // 128), axis=1) > 0, raw, -1e30)
    expo = jnp.exp(raw - jnp.max(raw, axis=0, keepdims=True))
    return expo * (1.0 / jnp.sum(expo, axis=0, keepdims=True))


QB = 256


def attn_kernel(ids, x3, live, _, out):
    q, v, k = x3[0], x3[1], x3[2]
    c = ids[0]
    lv = live[...]
    vt = v.astype(F32).T.astype(BF)
    row = lax.broadcasted_iota(jnp.int32, (2 * HD, 1), 0)
    masks = head_masks()
    for s, core in ((0, c), (QB, 1 - c)):
        total = jnp.zeros((2 * HD, QB), F32)
        for h in range(2):
            qh = jnp.where(masks[h], q[s : s + QB], jnp.zeros((), BF))
            low = soft(k, qh, lv, QB).astype(BF)
            vh = jnp.where(row < HD if h == 0 else row >= HD, vt, jnp.zeros((), BF))
            total += dot_nn(vh, low)
        mixed = total.T.astype(BF)
        at = pl.ds(pl.multiple_of(core * QB, QB), QB)
        out[0, at, :] = mixed
        out[1, at, :] = mixed


def attn_back_kernel(x3, gm_ref, live, d3):
    q, v, k = x3[0], x3[1], x3[2]
    slots = q.shape[0]
    lv = live[...]
    kt = k.astype(F32).T.astype(BF)
    row = lax.broadcasted_iota(jnp.int32, (2 * HD, 1), 0)
    masks = head_masks()
    scale = 1.0 / math.sqrt(HD)
    zero = jnp.zeros((), BF)
    dk = jnp.zeros((slots, 2 * HD), F32)
    dv = jnp.zeros((slots, 2 * HD), F32)
    for s in range(0, slots, QB):
        gm = gm_ref[s : s + QB, :]
        dqt = jnp.zeros((2 * HD, QB), F32)
        for h in range(2):
            qh = jnp.where(masks[h], q[s : s + QB], zero)
            gh = jnp.where(masks[h], gm, zero)
            probs = soft(k, qh, lv, QB)
            gp = dot_nt(v, gh)
            delta = jnp.sum(probs * gp, axis=0, keepdims=True)
            ds = (probs * (gp - delta)).astype(BF)
            kh = jnp.where(row < HD if h == 0 else row >= HD, kt, zero)
            dqt += dot_nn(kh, ds)
            dk += dot_nn(ds, qh)
            dv += dot_nn(probs.astype(BF), gh)
        d3[0, s : s + QB, :] = (dqt.T * scale).astype(BF)
    d3[1] = dv.astype(BF)
    d3[2] = (dk * scale).astype(BF)


def mid_kernel(ids, tok_own, tok_far, traded, vec, att_own, att_far, n2_out, n2t_out, m_out, mixed_t, mixed_out):
    c = ids[0]
    half = tok_own.shape[0]
    for p in range(2):
        for y in range(2):
            at = 192 * (2 * y + p)
            for b in range(8):
                block = traded[p, 2 * half + 48 * (y * 8 + b) : 2 * half + 48 * (y * 8 + b) + 48]
                m_out[96 * b : 96 * b + 48, at : at + 192] = block[:, :192]
                m_out[96 * b + 48 : 96 * b + 96, at : at + 192] = block[:, 192:]
            for to, core in ((0, c), (half, 1 - c)):
                rows = traded[p, pl.ds(pl.multiple_of(core * half, half), half), :]
                mixed_out[to : to + half, at : at + 192] = lanes(rows, y)
    for to, tok, out in ((0, tok_own, att_own), (half, tok_far, att_far)):
        att = tok[...].astype(F32) + (dot_nn(mixed_out[to : to + half, :], m_out[...]) + vec[6:7, :])
        out[...] = att
        xhat, _ = normalize(att)
        n2 = (xhat * vec[2:3, :] + vec[3:4, :]).astype(BF)
        n2_out[to : to + half, :] = n2
        n2t_out[:, to : to + half] = n2.astype(F32).T.astype(BF)
        mixed_t[:, to : to + half] = mixed_out[to : to + half, :].astype(F32).T.astype(BF)


def ffn_kernel(ids, n2, n2t, br_own, br_far, ea, ea_far, eb, eb_far, el, el_far, bias,
               part_own, part_far, gn2, e_x, e_y, s_x, s_y, s_z, d_bias, br, e_ref, s_ref):
    my, mx, mz = ids[2], ids[3], ids[4]
    n = pl.program_id(0)

    def layer(z):
        return ((z & 1) ^ (mz & 1)) * 2 + ((z >> 1) ^ (mz >> 1))

    def x_first(at, y, x, z):
        i, rows = (x ^ mx) * 4 + layer(z), pl.ds(at, 96 if at == 0 else 48)
        return jnp.where(y == my, ea[i, rows, :], ea_far[i, rows, :])

    def y_first(at, y, x, z):
        i, rows = (y ^ my) * 4 + layer(z), pl.ds(at, 96 if at == 0 else 48)
        return jnp.where(x == mx, eb[i, rows, :], eb_far[i, rows, :])

    def z_last(y, x, z):
        i = (((z >> 1) ^ (mz >> 1)) * 2 + (y ^ my)) * 2 + (x ^ mx)
        return jnp.where((z & 1) == (mz & 1), el[i], el_far[i])

    for b in range(8):
        e_ref[96 * b : 96 * b + 96, :384] = x_first(0, n, b & 1, b >> 1)
        e_ref[96 * b : 96 * b + 96, 384:] = y_first(0, n, b & 1, b >> 1)
    for y in range(2):
        for k in range(2):
            for x in range(2):
                at = 384 * k + 192 * x
                s_ref[at : at + 48, 384 * y : 384 * y + 384] = x_first(96, y, x, 2 * n + k)
                s_ref[at + 48 : at + 96, 384 * y : 384 * y + 384] = y_first(96, y, x, 2 * n + k)
                s_ref[at + 96 : at + 192, 384 * y : 384 * y + 384] = z_last(y, x, 2 * n + k)
    half = br_own.shape[0]

    @pl.when(pl.program_id(0) == 0)
    def _():
        for out in (part_own, part_far, gn2):
            out[...] = jnp.zeros_like(out)
        br[0:half], br[half:] = br_own[...], br_far[...]

    e, s = e_ref[...], s_ref[...]
    pre = dot_nn(n2[...], e) + bias[0]
    grad_act = dot_nt(br[...], s)
    cdf = 0.5 * (1.0 + lax.erf(pre * math.sqrt(0.5)))
    act = (pre * cdf).astype(BF)
    slope = cdf + pre * (jnp.exp(-0.5 * pre * pre) * (1.0 / math.sqrt(2.0 * math.pi)))
    grad_pre = (grad_act * slope).astype(BF)
    y = dot_nn(act, s)
    part_own[...] += y[:half]
    part_far[...] += y[half:]
    gn2[...] += dot_nt(grad_pre, e)
    grad = dot_nn(act.astype(F32).T.astype(BF), br[...]).astype(BF)
    for y in range(2):
        for b in range(4):
            block = grad[192 * b : 192 * b + 192, 384 * y : 384 * y + 384]
            s_x[y, b], s_y[y, b], s_z[y, b] = block[0:48], block[48:96], block[96:192]
    grad = dot_nn(n2t[...], grad_pre).astype(BF)
    for p, out in ((0, e_x), (1, e_y)):
        out[0] = grad[:, 384 * p : 384 * p + 384].reshape(8, 96, 384)
    d_bias[0] = jnp.sum(grad_pre.astype(F32), axis=0, keepdims=True)


def mid_back_kernel(ids, gn_here, gn_there, att_own, att_far, br_own, br_far, mixed_t, m, vec, gatt, gm, dm, sums, low):
    first, c = ids[0] == 0, ids[0]
    half = att_own.shape[0]
    for to, att, br_ref in ((0, att_own, br_own), (half, att_far, br_far)):
        gn = gn_here[to : to + half, :] + gn_there[half - to : 2 * half - to, :]
        br = br_ref[...].astype(F32)
        xhat, spread = normalize(att[...])
        grad = br + norm_back(xhat, spread, vec[2:3, :], gn)
        low[to : to + half, :] = grad.astype(BF)
        if to == 0:
            gatt[...] = grad
            sums[0:1] = jnp.sum(gn * xhat, axis=0, keepdims=True)
            sums[1:2] = jnp.sum(gn, axis=0, keepdims=True)
            sums[2:3] = jnp.sum(grad.astype(BF).astype(F32), axis=0, keepdims=True)
            sums[3:4] = jnp.sum(br, axis=0, keepdims=True)
            sums[4:8] = jnp.zeros((4, sums.shape[1]), F32)
    for k in range(2):
        rows = m[pl.ds(pl.multiple_of(192 * (2 * k + c), 192), 192), :]
        gm[:, 192 * k : 192 * k + 192] = dot_nt(low[...], rows).astype(BF)
        both = low[:, 384 * k : 384 * k + 384]
        mine = jnp.where(first, lanes(both, 0), lanes(both, 1))
        weight = dot_nn(mixed_t[...], mine).astype(BF)
        for b in range(8):
            dm[8 * k + b, :, :192] = weight[96 * b : 96 * b + 48]
            dm[8 * k + b, :, 192:] = weight[96 * b + 48 : 96 * b + 96]


def triple_back_kernel(ids, n1_ref, d3, t3, d_qv, d_k, gn, sums):
    c = ids[0]
    j = pl.program_id(0)
    d = d3[0]
    half = gn.shape[1]
    weight = dot_nn(n1_ref[...], d).astype(BF)
    part = dot_nt(d, t3[0])
    sums[0] = jnp.sum(d.astype(F32), axis=0, keepdims=True)

    @pl.when(j == 0)
    def _():
        gn[c] = part[:half]
        gn[1 - c] = part[half:]

    @pl.when(j > 0)
    def _():
        gn[c] += part[:half]
        gn[1 - c] += part[half:]

    @pl.when(j < 2)
    def _():
        d_qv[0] = weight

    @pl.when(j == 2)
    def _():
        for b in range(8):
            for y in range(2):
                d_k[y, b, :, :192] = weight[96 * b : 96 * b + 48, 192 * y : 192 * y + 192]
                d_k[y, b, :, 192:] = weight[96 * b + 48 : 96 * b + 96, 192 * y : 192 * y + 192]


def first_back_kernel(ids, gn_both, tok, gatt, vec, sums2, sums1, d_bias, out, blocks, table):
    c = ids[0]
    gn = gn_both[0] + gn_both[1]
    xhat, spread = normalize(tok[...].astype(F32))
    out[...] = (gatt[...] + norm_back(xhat, spread, vec[0:1, :], gn)).astype(BF)
    table[12:16] = jnp.zeros((4, table.shape[1]), F32)
    table[0:1] = jnp.sum(gn * xhat, axis=0, keepdims=True)
    table[1:2] = jnp.sum(gn, axis=0, keepdims=True)
    table[2:4] = sums2[0:2]
    table[6:8] = sums2[2:4]
    for row, sums in [(4, sums1[0]), (5, sums1[1])] + [(8 + n, d_bias[n]) for n in range(4)]:
        for k in range(2):
            for p in range(2):
                at = 192 * (2 * k + p)
                table[row : row + 1, at : at + 192] = jnp.where(c == p, lanes(sums, k), 0.0)
    blocks[...] = jnp.zeros_like(blocks)
    for b in range(8):
        blocks[b, :, 0:96] = table[:, 96 * b : 96 * b + 96].astype(BF)


def halves(rows):
    return rows[:, :192], rows[:, 192:]


def fetch(refs, places, sems):
    copies = [pltpu.make_async_copy(ref, place, sems.at[i]) for i, (ref, place) in enumerate(zip(refs, places))]
    for copy in copies:
        copy.start()
    for copy in copies:
        copy.wait()


def adam_into(state, outs, rate, decay, at, grad):
    new = adamw(state[0][at], state[1][at], state[2][at], grad, rate, decay)
    for out, value in zip(outs, new):
        out[at] = value


def triple_units(t, total):
    a, b = halves(total[0:96])
    k = jnp.concatenate(halves(total[96:144]), axis=0)
    return a, b, k


def forward_total(own, far, last):
    total = own[...].astype(F32) + far[...].astype(F32)
    return jnp.concatenate([total[0:96], total[144:240], total[96:144], total[240:288], last], axis=0)


def give_back_kernel(ids, t_own, t_far, es_own, es_far, give):
    first, t = ids[0] == 0, ids[1]
    total = t_own[...].astype(F32) + t_far[...].astype(F32)
    a, b, k = triple_units(t, total)
    give[0:96] = jnp.where(t == 1, a, jnp.where(t == 2, b, k))
    give[96:112] = jnp.zeros((16, 192), F32)
    give[96:112, 0:96] = total[144:160, 0:96]
    total = forward_total(es_own, es_far, total[160:256])
    give[112:208], give[208:304] = halves(jnp.where(first, total[96:192], total[0:96]))
    s0, s1 = halves(total[192:])
    give[304:496] = jnp.where(first, s1, s0)


def prefetch_kernel(_, *refs):
    fetch(refs[: len(refs) // 2], refs[len(refs) // 2 : -1], refs[-1])


def update_kernel(ids, t_own, t_far, es_own, es_far, took, *refs):
    state, outs = refs[:15], refs[15:]
    first, c, t = ids[0] == 0, ids[0], ids[1]
    every = slice(None)
    total = t_own[...].astype(F32) + t_far[...].astype(F32)
    a, b, k = triple_units(t, total)
    units = (
        jnp.where(t == 1, b, jnp.where(t == 2, k, a)),
        took[0:96],
        jnp.where(t == 1, k, jnp.where(t == 2, a, b)),
    )
    for i, unit in enumerate(units):
        adam_into(state[0:3], outs[0:4], RATES[0], DECAYS[0], (every, slice(192 * i, 192 * i + 192)), unit)
    for i, part in enumerate(halves(total[256:304])):
        adam_into(state[3:6], outs[4:8], RATES[1], DECAYS[1], (slice(48 * i, 48 * i + 48), every), part)
    total_es = forward_total(es_own, es_far, total[160:256])
    e = halves(jnp.where(first, total_es[0:96], total_es[96:192]))
    s0, s1 = halves(total_es[192:])
    s = jnp.where(first, s0, s1)
    for p in range(2):
        for j in range(2):
            grad = jnp.where(c == p, e[j], took[112 + 96 * j : 208 + 96 * j])
            at = 384 * j + 192 * p
            adam_into(state[6:9], outs[8:12], RATES[2], DECAYS[2], (every, slice(at, at + 192)), grad)
        grad = jnp.where(c == p, s, took[304:496]).T
        adam_into(state[9:12], outs[12:16], RATES[3], DECAYS[3], (every, slice(192 * p, 192 * p + 192)), grad)
    adam_into(state[12:15], outs[16:20], RATES[4], DECAYS[4], (every, every), total[144:156, 0:96] + took[96:108, 0:96])


def by_core(c, own, far):
    return jnp.where(c == 0, jnp.stack([own, far]), jnp.stack([far, own]))


def per_device(
    cube_tokens, visible, live_counts, block_cotangent,
    triple_master, triple_first, triple_second,
    mixing_master, mixing_first, mixing_second,
    expand_master, expand_first, expand_second,
    shrink_master, shrink_first, shrink_second,
    vector_master, vector_first, vector_second,
):
    y, c, b = lax.axis_index("y"), lax.axis_index("core"), lax.axis_index("blk")
    bits = (y, b & 1, b >> 1 & 1, b >> 2)
    turn = b % 4
    unturn = (4 - turn) % 4
    region, feats = cube_tokens.shape[1:]
    slots = visible.shape[1]
    slot_axis = jnp.arange(slots, dtype=jnp.int32)

    t_id = 2 * y + c
    ids = jnp.stack([c, t_id, y, bits[1], b >> 1]).astype(jnp.int32)
    shrink_t = shrink_master.T
    took = swap(call(
        give_kernel, shape(480, 192, dtype=BF), "give", 1e10, 1e3, in_specs=[SM, VM, VM, VM], out_specs=VM,
    )(ids, triple_master, expand_master, shrink_t), dc=1)
    tvm, es, last = call(
        pack_kernel, (shape(208, 384, dtype=BF), shape(288, 384, dtype=BF), shape(96, 384, dtype=BF)), "pack", 1e10, 1e3,
        in_specs=[SM] + [VM] * 6, out_specs=(VM, VM, VM),
    )(ids, took, triple_master, mixing_master, expand_master, shrink_t, vector_master)

    t_far = swap(tvm, db=4)
    last_in = swap(last, db=1)

    visible, block_cotangent, tvm, es, last = tie(visible, block_cotangent, tvm, es, last)
    def turned(x):
        return lax.dynamic_slice_in_dim(jnp.concatenate([x, x]), turn, 4, 0)

    local = visible % region
    flat_index = turned(local + region * jnp.arange(4, dtype=jnp.int32)[:, None])
    picked = jnp.take(cube_tokens.reshape(-1, feats), flat_index.reshape(-1), axis=0).reshape(4, slots, feats)
    counts = jnp.broadcast_to(turned(live_counts)[:, :, None].astype(BF), (4, 16, feats))
    live_here = slot_axis[None, :] < live_counts
    masked = turned(jnp.where(live_here[:, :, None], block_cotangent, jnp.zeros((), BF)))
    packet = jnp.concatenate([picked, masked, counts], axis=1)

    def packets(*steps):
        return [lax.ppermute(packet[s], FINE, cube_pairs(s, False)) for s in steps]

    last = jnp.stack([last, last_in])
    last_in = swap(last, dy=1)
    t_far, packet, es, last_in = tie(t_far, packet, es, last_in)
    tvm = jnp.stack([tvm, t_far])
    t_far = swap(tvm, db=2)
    last = jnp.stack([last, last_in]).reshape(384, 384)
    es_far = swap(jnp.concatenate([es, last], axis=0), db=4)
    own = packets(0, 1)

    t_far, packet = tie(t_far, packet)
    tvm = jnp.stack([tvm, t_far]).reshape(4, 208, 384)
    qv, rest = tvm[:, :96], tvm[:, 96:]
    qv_x, rest_y = swap(qv, db=1), swap(rest, dy=1)

    qv_x, rest_y, own, packet = tie(qv_x, rest_y, own, packet)
    qv = jnp.stack([qv, qv_x]).reshape(8, 96, 384)
    rest = jnp.stack([rest, rest_y]).reshape(8, 112, 384)
    qv_far, rest_far = swap(qv, dy=1), swap(rest, db=1)
    es_far, last = tie(es_far, last)
    el = jnp.stack([last, es_far[288:]]).reshape(8, 96, 384)
    es = jnp.stack([es, es_far[:288]])
    es_far = swap(es, db=2)
    own = own + packets(2, 3)

    qv_far, rest_far, es_far, own = tie(qv_far, rest_far, es_far, own)
    es = jnp.stack([es, es_far]).reshape(4, 288, 384)
    ea, eb = es[:, :144], es[:, 144:]
    ea_in, eb_in = swap(ea, db=1), swap(eb, dy=1)
    el_far = swap(el, db=2)
    own = jnp.stack(own)
    far = swap(own, dc=1)

    rows = 4 * slots
    tok_own, tok_far = [p[:, :slots].reshape(rows, feats) for p in (own, far)]
    br_own, br_far = [p[:, slots : 2 * slots].reshape(rows, feats) for p in (own, far)]
    cnt = jnp.concatenate([own[:, 2 * slots, :1], far[:, 2 * slots, :1]]).astype(jnp.int32)
    live = (slot_axis[None, :] < cnt).reshape(2 * rows, 1)
    live_cols = jnp.broadcast_to(live.astype(F32), (2 * rows, 128))

    n1, x3, t3, mix, vec, e_bias = call(
        qkv_kernel,
        (shape(feats, 2 * rows, dtype=BF), shape(3, 2 * rows, 384, dtype=BF), shape(3, feats, 384, dtype=BF),
         shape(2, 2 * rows + feats, 384, dtype=BF), shape(16, feats), shape(4, 1, 384)),
        "qkv", 2 * 512 * 768 * 1152, 8e6,
        in_specs=[SM] + [VM] * 6, out_specs=(VM,) * 6, scratch_shapes=[pltpu.VMEM((8, 384), F32), pltpu.VMEM((2 * rows, feats), BF)],
    )(ids, tok_own, tok_far, qv, qv_far, rest, rest_far)
    x3, mix, ea_in, eb_in = tie(x3, mix, ea_in, eb_in)
    ea = jnp.stack([ea, ea_in]).reshape(8, 144, 384)
    eb = jnp.stack([eb, eb_in]).reshape(8, 144, 384)
    ea_far, eb_far = swap(ea, dy=1), swap(eb, db=1)

    pairs3 = pl.BlockSpec((3, 2 * rows, 128), lambda i: (0, 0, i))
    col = pl.BlockSpec((2 * rows, 128), lambda i: (0, i))
    same = pl.BlockSpec((2 * rows, 128), lambda i: (0, 0))
    traded = trade(call(
        attn_kernel, shape(2, 2 * rows + feats, 384, dtype=BF), "attention", 6e9, 2e6,
        grid=(3,), in_specs=[SM, pairs3, same, pl.BlockSpec(memory_space=pl.ANY)],
        out_specs=pl.BlockSpec((2, 2 * rows, 128), lambda i: (0, 0, i)), input_output_aliases={3: 0},
    )(ids, x3, live_cols, mix))
    att, att_far, n2, n2t, mix, mixed = call(
        mid_kernel,
        (shape(rows, feats), shape(rows, feats), shape(2 * rows, feats, dtype=BF), shape(feats, 2 * rows, dtype=BF),
         shape(feats, feats, dtype=BF), shape(feats, 2 * rows, dtype=BF)),
        "mixing", 3e9, 5e6, in_specs=[SM] + [VM] * 4, out_specs=(VM,) * 6,
        scratch_shapes=[pltpu.VMEM((2 * rows, feats), BF)],
    )(ids, tok_own, tok_far, traded, vec)

    whole = pl.BlockSpec((rows, feats), lambda i: (0, 0))

    gathered = [pl.BlockSpec((8, r, 384), lambda n: (0, 0, 0)) for r in (144, 144, 144, 144, 96, 96)]
    every = pl.BlockSpec((2 * rows, feats), lambda i: (0, 0))
    part_own, part_give, gn2, e_x, e_y, s_x, s_y, d_z, d_b = call(
        ffn_kernel,
        (pltpu.HBM((rows, feats), F32), shape(rows, feats))
        + (shape(2 * rows, feats),) + (shape(2, 8, 96, 384, dtype=BF),) * 2 + (pltpu.HBM((2, 8, 48, 384), BF),) * 2
        + (shape(2, 8, 96, 384, dtype=BF), shape(2, 1, 768)),
        "feed_forward", 18e9, 20e6, 46,
        grid=(2,),
        in_specs=[SM, every, pl.BlockSpec((feats, 2 * rows), lambda n: (0, 0))] + [whole] * 2 + gathered
        + [pl.BlockSpec((1, 1, 768), lambda n: (n, 0, 0))],
        out_specs=(
            whole, whole, every,
            pl.BlockSpec((1, 8, 96, 384), lambda n: (n, 0, 0, 0)),
            pl.BlockSpec((1, 8, 96, 384), lambda n: (n, 0, 0, 0)),
            pl.BlockSpec((2, 4, 48, 384), lambda n: (0, n, 0, 0)),
            pl.BlockSpec((2, 4, 48, 384), lambda n: (0, n, 0, 0)),
            pl.BlockSpec((2, 4, 96, 384), lambda n: (0, n, 0, 0)),
            pl.BlockSpec((1, 1, 768), lambda n: (n, 0, 0)),
        ),
        scratch_shapes=[pltpu.VMEM((2 * rows, feats), BF), pltpu.VMEM((feats, 768), BF), pltpu.VMEM((768, feats), BF)],
    )(ids, n2, n2t, br_own, br_far, ea, ea_far, eb, eb_far, el, el_far, e_bias.reshape(2, 1, 768))

    mx, z0, z1 = bits[1], bits[2], bits[3]
    gn2_far = swap(gn2, dc=1)
    d_z = d_z.reshape(2, 2, 2, 2, 96, 384)

    def x_part(at):
        return jnp.concatenate([pick(e_x.reshape(2, 4, 2, 96, 384), at, 2), pick(s_x.reshape(2, 4, 2, 48, 384), at, 2)], axis=2)

    def y_part(at):
        return jnp.concatenate([pick(e_y, at, 0), pick(s_y, at, 0)], axis=1)

    x_in = swap(x_part(1 - mx), db=1)
    y_in = swap(y_part(1 - y), dy=1)

    gatt, gm, dm, sums2 = call(
        mid_back_kernel,
        (shape(rows, feats), shape(2 * rows, 384, dtype=BF), shape(16, 48, 384, dtype=BF), shape(8, feats)),
        "mixing_back", 6e9, 8e6, in_specs=[SM] + [VM] * 9, out_specs=(VM,) * 4,
        scratch_shapes=[pltpu.VMEM((2 * rows, feats), BF)],
    )(ids, gn2, gn2_far, att, att_far, br_own, br_far, mixed, mix, vec)
    d_z = jnp.concatenate([d_z, dm.reshape(2, 2, 2, 2, 48, 384)], axis=4)
    z_in = swap(pick(d_z, 1 - z0, 2), db=2)
    d3 = call(
        attn_back_kernel, shape(3, 2 * rows, 384, dtype=BF), "attention_back", 9e9, 5e6,
        grid=(3,), in_specs=[pairs3, col, same], out_specs=pairs3,
    )(x3, gm, live_cols)

    third = pl.BlockSpec((1, 2 * rows, 384), lambda j: (j, 0, 0))
    d_qv, d_k, gn1, sums1 = call(
        triple_back_kernel,
        (shape(2, feats, 384, dtype=BF), shape(2, 8, 48, 384, dtype=BF), shape(2, rows, feats), shape(3, 1, 384)),
        "triple_back", 5e9, 5e6,
        grid=(3,),
        in_specs=[SM, pl.BlockSpec((feats, 2 * rows), lambda j: (0, 0)), third, pl.BlockSpec((1, feats, 384), lambda j: (j, 0, 0))],
        out_specs=(
            pl.BlockSpec((1, feats, 384), lambda j: (jnp.minimum(j, 1), 0, 0)),
            pl.BlockSpec((2, 8, 48, 384), lambda j: (0, 0, 0, 0)),
            pl.BlockSpec((2, rows, feats), lambda j: (0, 0, 0)),
            pl.BlockSpec((1, 1, 384), lambda j: (j, 0, 0)),
        ),
    )(ids, n1, d3, t3)

    gn1 = trade(gn1)
    grad_tok, blocks = call(
        first_back_kernel, (shape(rows, feats, dtype=BF), shape(8, 16, 384, dtype=BF)), "first_back", 1e9, 1e6,
        in_specs=[SM] + [VM] * 7, out_specs=(VM, VM), scratch_shapes=[pltpu.VMEM((16, feats), F32)],
    )(ids, gn1, tok_own, gatt, vec, sums2, sums1, d_b.reshape(4, 1, 384))

    blocks = jnp.broadcast_to(blocks, (2, 8, 16, 384))
    d_qv = d_qv.reshape(2, 4, 2, 96, 384)
    d_km = jnp.concatenate([d_k, blocks], axis=2).reshape(2, 4, 2, 64, 384)
    qv_in = swap(pick(d_qv, 1 - bits[1], 2), db=1)
    km_in = swap(pick(d_km, 1 - y, 0), dy=1)

    x_in, y_in, z_in, grad_tok, part_give = tie(x_in, y_in, z_in, grad_tok, part_give)
    d_x = add_low(x_part(mx), x_in)
    d_y = add_low(y_part(y), y_in).reshape(4, 2, 144, 384)
    x_in = swap(pick(d_x, 1 - y, 0), dy=1)
    y_in = swap(pick(d_y, 1 - mx, 1), db=1)
    d_z = add_low(pick(d_z, z0, 2), z_in)
    z_in = swap(pick(d_z, 1 - y, 0), dy=1)

    part_far = swap(part_give, dc=1)
    result = att + (part_own + part_far + vec[7])
    result = jnp.where(live[:rows], result, 0.0).astype(BF).reshape(4, slots, feats)
    packet = jnp.concatenate([result, grad_tok.reshape(4, slots, feats)], axis=1)

    def go_back(step, *after):
        part = tie(packet[step], *after)[0]
        return lax.ppermute(part, FINE, cube_pairs(step, True))

    back = [go_back(0)]
    back += [go_back(1, back[0])]

    qv_in, km_in, back, packet = tie(qv_in, km_in, back, packet)
    d_qv = add_low(pick(d_qv, mx, 2), qv_in)
    d_km = add_low(pick(d_km, y, 0), km_in)
    qv_in = swap(pick(d_qv, 1 - y, 0), dy=1)
    km_in = swap(pick(d_km, 1 - mx, 1), db=1)
    back += [go_back(2)]
    back += [go_back(3)]

    x_in, y_in, z_in, packet = tie(x_in, y_in, z_in, packet)
    d_es = jnp.concatenate(
        [add_low(pick(d_x, y, 0), x_in), add_low(pick(d_y, mx, 1), y_in)], axis=1
    ).reshape(2, 2, 288, 384)
    es_in = swap(pick(d_es, 1 - z0, 1), db=2)

    qv_in, km_in, z_in = tie(qv_in, km_in, z_in)
    d_t = jnp.concatenate(
        [add_low(pick(d_qv, y, 0), qv_in), add_low(pick(d_km, mx, 1), km_in)], axis=1
    ).reshape(2, 2, 160, 384)
    t_in = swap(pick(d_t, 1 - z0, 1), db=2)
    d_z = add_low(pick(d_z, y, 0), z_in)
    z_in = swap(pick(d_z, 1 - mx, 1), db=1)

    es_in, t_keep = tie(es_in, d_t)
    es_keep = d_es = add_low(pick(d_es, z0, 1), es_in)
    es_in = swap(pick(d_es, 1 - z1, 0), db=4)
    t_in, z_in = tie(t_in, z_in)
    d_t = jnp.concatenate([add_low(pick(d_t, z0, 1), t_in), add_low(pick(d_z, mx, 1), z_in)], axis=1)
    t_in = swap(pick(d_t, 1 - z1, 0), db=4)

    state = (triple_master, triple_first, triple_second, mixing_master, mixing_first, mixing_second,
             expand_master, expand_first, expand_second, shrink_t, shrink_first.T, shrink_second.T,
             vector_master, vector_first, vector_second)
    ids_late = ids + jnp.isnan(es_keep[0, 0, 0]).astype(jnp.int32)
    ready = call(
        prefetch_kernel, tuple(shape(*a.shape) for a in state), "prefetch", 1e10, 1e3,
        in_specs=[SM] + [pl.BlockSpec(memory_space=pltpu.HBM)] * len(state), out_specs=(VM,) * len(state),
        scratch_shapes=[pltpu.SemaphoreType.DMA((len(state),))],
    )(ids_late, *state)

    back = jnp.stack(back)
    back = lax.dynamic_slice_in_dim(jnp.concatenate([back, back]), unturn, 4, 0)
    block_output = back[:, :slots]
    spread = (jnp.arange(region, dtype=jnp.int32)[None, :, None] == local[:, None, :]).astype(BF)
    token_grads = jnp.einsum("grs,gsf->grf", spread, back[:, slots:], preferred_element_type=F32).astype(BF)

    t_in, es_in, token_grads, block_output, ready = tie(t_in, es_in, token_grads, block_output, ready)
    grads = (pick(d_t, z1, 0), t_in, pick(d_es, z1, 0), es_in)
    took = swap(call(
        give_back_kernel, shape(496, 192), "give_back", 1e6, 1e6, in_specs=[SM] + [VM] * 4, out_specs=VM,
    )(ids, *grads), dc=1)

    def whole_of(a):
        return pl.BlockSpec(a.shape, lambda i: (0,) * len(a.shape))

    outs = tuple(shape(*a.shape, dtype=d) for a in state[::3] for d in (F32, F32, F32, BF))
    new = call(
        update_kernel, outs, "update", 1e8, 4e6, grid=(1,),
        in_specs=[SM] + [whole_of(a) for a in (*grads, took, *state)], out_specs=tuple(whole_of(o) for o in outs),
    )(ids, *grads, took, *ready)
    return (block_output, token_grads, *new[:12], *(o.T for o in new[12:16]), *new[16:])


def layer_norm(rows, gain, shift):
    center = rows - jnp.mean(rows, axis=-1, keepdims=True)
    spread = lax.rsqrt(jnp.mean(center * center, axis=-1, keepdims=True) + 1e-06)
    return center * spread * gain + shift


def outer_sum(left, right):
    return lax.dot_general(
        left, right, (((0,), (0,)), ((), ())), preferred_element_type=jnp.float32
    )


def back_product(grads, weight):
    return lax.dot_general(
        grads, weight, (((1,), (1,)), ((), ())), preferred_element_type=jnp.float32
    )


def masked_scores(queries, key_all, live_all):
    raw = jnp.einsum("gshe,gthe->ghst", queries, key_all, preferred_element_type=jnp.float32) * (
        1.0 / math.sqrt(HD)
    )
    return jnp.where(live_all[:, None, None, :] > 0, raw, -1e30)


def cycle_section(triple_grad, mixing_grad, expand_grad, shrink_grad, vector_grad):
    summed = (
        lax.psum_scatter(triple_grad, "blk", scatter_dimension=0, tiled=True),
        lax.psum_scatter(mixing_grad, "blk", scatter_dimension=0, tiled=True),
        lax.psum_scatter(expand_grad, "blk", scatter_dimension=0, tiled=True),
        lax.psum_scatter(shrink_grad, "blk", scatter_dimension=0, tiled=True),
        lax.psum_scatter(vector_grad, "blk", scatter_dimension=1, tiled=True),
    )
    return (summed[0], summed[1], summed[2], summed[3], summed[4])


def group_section(triple_grad, mixing_grad, expand_grad, shrink_grad, vector_grad):
    summed = (
        lax.psum_scatter(triple_grad, "batch", scatter_dimension=1, tiled=True),
        lax.psum_scatter(mixing_grad, "batch", scatter_dimension=1, tiled=True),
        lax.psum_scatter(expand_grad, "batch", scatter_dimension=1, tiled=True),
        lax.psum_scatter(shrink_grad, "batch", scatter_dimension=1, tiled=True),
    )
    vector_sum = lax.psum(vector_grad, "batch")
    return (summed[0], summed[1], summed[2], summed[3], vector_sum)


def per_device_any(
    cube_tokens,
    visible,
    live_counts,
    block_cotangent,
    triple_master,
    triple_first,
    triple_second,
    mixing_master,
    mixing_first,
    mixing_second,
    expand_master,
    expand_first,
    expand_second,
    shrink_master,
    shrink_first,
    shrink_second,
    vector_master,
    vector_first,
    vector_second,
):
    low_copies = (
        lax.all_gather(triple_master.astype(jnp.bfloat16), "blk", axis=0, tiled=True),
        lax.all_gather(mixing_master.astype(jnp.bfloat16), "blk", axis=0, tiled=True),
        lax.all_gather(expand_master.astype(jnp.bfloat16), "blk", axis=0, tiled=True),
        lax.all_gather(shrink_master.astype(jnp.bfloat16), "blk", axis=0, tiled=True),
        lax.all_gather(vector_master.astype(jnp.bfloat16), "blk", axis=1, tiled=True),
    )
    triple_w, mixing_w, expand_w, shrink_w = (
        lax.all_gather(low_copies[0], "batch", axis=1, tiled=True),
        lax.all_gather(low_copies[1], "batch", axis=1, tiled=True),
        lax.all_gather(low_copies[2], "batch", axis=1, tiled=True),
        lax.all_gather(low_copies[3], "batch", axis=1, tiled=True),
    )
    vector_w = low_copies[4].astype(jnp.float32)
    groups, slot_count = visible.shape
    region = cube_tokens.shape[1]
    features = cube_tokens.shape[2]
    row_count = groups * slot_count
    head_count = features // HD
    local_index = visible % region
    tokens = jnp.take_along_axis(cube_tokens, local_index[:, :, None], axis=1).astype(jnp.float32)
    flat_tokens = tokens.reshape(row_count, features)
    live_mask = jnp.arange(slot_count, dtype=jnp.int32)[None, :] < live_counts
    live_rows = live_mask.reshape(row_count, 1)
    normed1 = layer_norm(flat_tokens, vector_w[0], vector_w[1]).astype(jnp.bfloat16)
    zero_bias = jnp.zeros((features,), jnp.float32)
    triple_bias = jnp.concatenate([vector_w[4], zero_bias, vector_w[5]])
    triple = (jnp.dot(normed1, triple_w, preferred_element_type=jnp.float32) + triple_bias).astype(
        jnp.bfloat16
    )
    triple = triple.reshape(groups, slot_count, 3 * features)
    query_flat = triple[:, :, :features]
    queries = query_flat.reshape(groups, slot_count, head_count, HD)
    key_rows = triple[:, :, features : 2 * features]
    value_rows = triple[:, :, 2 * features :]
    key_all, value_all, live_all = (
        lax.all_gather(key_rows, "blk", axis=1, tiled=True),
        lax.all_gather(value_rows, "blk", axis=1, tiled=True),
        lax.all_gather(live_mask.astype(jnp.bfloat16), "blk", axis=1, tiled=True),
    )
    key_all = key_all.reshape(groups, -1, head_count, HD)
    value_all = value_all.reshape(groups, -1, head_count, HD)
    scores = masked_scores(queries, key_all, live_all)
    peak = jnp.max(scores, axis=-1, keepdims=True)
    expo = jnp.exp(scores - peak)
    total = jnp.sum(expo, axis=-1, keepdims=True)
    prob_low = (expo / total).astype(jnp.bfloat16)
    mixed = jnp.einsum("ghst,gthe->gshe", prob_low, value_all, preferred_element_type=jnp.float32)
    mixed = mixed.astype(jnp.bfloat16).reshape(row_count, features)
    attended = flat_tokens + (
        jnp.dot(mixed, mixing_w, preferred_element_type=jnp.float32) + vector_w[6]
    )
    normed2 = layer_norm(attended, vector_w[2], vector_w[3]).astype(jnp.bfloat16)
    preact = jnp.dot(normed2, expand_w, preferred_element_type=jnp.float32) + vector_w[8:].reshape(
        -1
    )
    activation = jax.nn.gelu(preact, approximate=False).astype(jnp.bfloat16)
    result = attended + (
        jnp.dot(activation, shrink_w, preferred_element_type=jnp.float32) + vector_w[7]
    )
    result = jnp.where(live_rows, result, 0.0)
    block_output = result.astype(jnp.bfloat16).reshape(groups, slot_count, features)
    grad_out = jnp.where(
        live_rows, block_cotangent.reshape(row_count, features).astype(jnp.float32), 0.0
    )
    branch_low = grad_out.astype(jnp.bfloat16)
    shrink_grad = outer_sum(activation, branch_low)
    shrink_bias_grad = jnp.sum(branch_low.astype(jnp.float32), axis=0)
    grad_act = back_product(branch_low, shrink_w)
    gelu_value, gelu_back = jax.vjp(partial(jax.nn.gelu, approximate=False), preact)
    grad_pre = gelu_back(grad_act)[0].astype(jnp.bfloat16)
    expand_grad = outer_sum(normed2, grad_pre)
    expand_bias_grad = jnp.sum(grad_pre.astype(jnp.float32), axis=0)
    grad_normed2 = back_product(grad_pre, expand_w)
    norm2_value, norm2_back = jax.vjp(layer_norm, attended, vector_w[2], vector_w[3])
    grad_through2, gain2_grad, shift2_grad = norm2_back(grad_normed2)
    grad_attended = grad_out + grad_through2
    mix_low = grad_attended.astype(jnp.bfloat16)
    mixing_grad = outer_sum(mixed, mix_low)
    mixing_bias_grad = jnp.sum(mix_low.astype(jnp.float32), axis=0)
    grad_mixed_flat = (
        back_product(mix_low, mixing_w).astype(jnp.bfloat16).reshape(groups, slot_count, features)
    )
    grad_mixed = grad_mixed_flat.reshape(groups, slot_count, head_count, HD)
    scores = masked_scores(queries, key_all, live_all)
    probs = jnp.exp(scores - peak) / total
    prob_low = probs.astype(jnp.bfloat16)
    grad_probs = jnp.einsum(
        "gshe,gthe->ghst", grad_mixed, value_all, preferred_element_type=jnp.float32
    )
    delta = jnp.sum(probs * grad_probs, axis=-1, keepdims=True)
    grad_scores = (probs * (grad_probs - delta)).astype(jnp.bfloat16)
    score_scale = 1.0 / math.sqrt(HD)
    grad_queries = (
        jnp.einsum("ghst,gthe->gshe", grad_scores, key_all, preferred_element_type=jnp.float32)
        * score_scale
    )
    term_keys = (
        jnp.einsum("ghst,gshe->gthe", grad_scores, queries, preferred_element_type=jnp.float32)
        * score_scale
    )
    term_values = jnp.einsum(
        "ghst,gshe->gthe", prob_low, grad_mixed, preferred_element_type=jnp.float32
    )
    grad_keys, grad_values = (
        lax.psum_scatter(
            term_keys.reshape(groups, -1, features), "blk", scatter_dimension=1, tiled=True
        ),
        lax.psum_scatter(
            term_values.reshape(groups, -1, features), "blk", scatter_dimension=1, tiled=True
        ),
    )
    grad_triple = jnp.concatenate(
        [
            grad_queries.reshape(row_count, features),
            grad_keys.reshape(row_count, features),
            grad_values.reshape(row_count, features),
        ],
        axis=1,
    ).astype(jnp.bfloat16)
    triple_grad = outer_sum(normed1, grad_triple)
    triple_sums = jnp.sum(grad_triple.astype(jnp.float32), axis=0)
    grad_normed1 = back_product(grad_triple, triple_w)
    norm1_value, norm1_back = jax.vjp(layer_norm, flat_tokens, vector_w[0], vector_w[1])
    grad_through1, gain1_grad, shift1_grad = norm1_back(grad_normed1)
    grad_tokens = (grad_attended + grad_through1).reshape(groups, slot_count, features)
    cube_rows = jnp.arange(groups, dtype=jnp.int32)[:, None]
    token_grads = (
        jnp.zeros(cube_tokens.shape, jnp.float32)
        .at[cube_rows, local_index]
        .add(grad_tokens)
        .astype(jnp.bfloat16)
    )
    leading_rows = jnp.stack(
        [
            gain1_grad,
            shift1_grad,
            gain2_grad,
            shift2_grad,
            triple_sums[:features],
            triple_sums[2 * features :],
            mixing_bias_grad,
            shrink_bias_grad,
        ]
    )
    vector_grad = jnp.concatenate([leading_rows, expand_bias_grad.reshape(-1, features)], axis=0)
    reduced = group_section(triple_grad, mixing_grad, expand_grad, shrink_grad, vector_grad)
    reduced = cycle_section(reduced[0], reduced[1], reduced[2], reduced[3], reduced[4])
    masters = (triple_master, mixing_master, expand_master, shrink_master, vector_master)
    firsts = (triple_first, mixing_first, expand_first, shrink_first, vector_first)
    seconds = (triple_second, mixing_second, expand_second, shrink_second, vector_second)
    outputs = [block_output, token_grads]
    for master, first, second, grad, rate, decay in zip(
        masters, firsts, seconds, reduced, RATES, DECAYS
    ):
        outputs.extend(adamw(master, first, second, grad, rate, decay))
    return tuple(outputs)


def solution(mesh):
    groups, blocks = mesh.shape["batch"], mesh.shape["blk"]
    if (groups, blocks) == (4, 8):
        mesh = Mesh(mesh.devices.reshape(2, 2, 8), FINE)
        batch, body = ("y", "core"), per_device
    else:
        batch, body = "batch", per_device_any
    rows = P(batch, "blk", None)
    part = P("blk", batch)
    table = P(None, "blk")
    in_specs = (rows, P(batch, "blk"), P(batch, "blk"), rows) + (part,) * 12 + (table,) * 3
    out_specs = (rows, rows) + (part,) * 16 + (table,) * 4
    return jax.shard_map(body, mesh=mesh, in_specs=in_specs, out_specs=out_specs, check_vma=False)
```
